32 devices in a mesh: groups: 2 (over x), seq: 16 (over z, y, core).
Axes of the slice: x: 2, y: 2, z: 4, core: 2. Of those that a mesh axis runs over, the one named last changes fastest.
Arguments:
- tokens: bfloat16 [8192, 256], P(('groups', 'seq')), parts along dimension 0, may hold values from -6 to 6
- norm_gain: float32 [256], replicated, may hold values from 0.1 to 1.9
- w_in: bfloat16 [256, 768], replicated, may hold values from -0.375 to 0.375
- short_filter: float32 [3, 768], replicated, may hold values from -0.8 to 0.8
- long_filter: float32 [4096, 256], P('seq'), may hold values from -0.09375 to 0.09375
- medium_filter: float32 [128, 256], replicated, may hold values from -0.5 to 0.5
- skip_gain: float32 [256], replicated, may hold values from -1 to 1
- w_out: bfloat16 [256, 256], replicated, may hold values from -0.375 to 0.375
Outputs:
- result: bfloat16 [8192, 256], P(('groups', 'seq')), parts along dimension 0
The draws below stay inside these ranges and needn't reach their ends.
There are 2 independent parts, one for each index of `groups`. The reference program is written for one: setup_inputs(seed, part) draws one part's arguments, and reference() takes and returns one part's arrays. A program takes and returns all parts, laid end to end along the dimension named above; an argument that names none is the same for every part. Nothing has to cross between parts.
All inputs are finite; a program needn't handle non-finite values.
Results may differ from the reference program's by a relative error of at most 0.015.
Values may be sent and summed in bfloat16 or wider, within the bound.
No kernel may reach another device: no remote copies, remote signals or barrier semaphores. Data moves between devices by JAX's collectives and lax.ppermute only.
A program may use at most 64 MiB of HBM per device.

```python
import jax
import jax.numpy as jnp
from jax import lax

D = 256
TAPS = 3
MED = 128
TOKENS = 4096


def block_levels(own_key, shape, cuts, low, largest):
    def one(position, parts):
        heights = jax.random.uniform(jax.random.fold_in(jax.random.fold_in(own_key, 6), position), (parts,), jnp.float32, low / len(cuts), largest / len(cuts))
        return jnp.repeat(jnp.exp(heights), shape[position] // parts).reshape((-1,) + (1,) * (len(shape) - position - 1))

    gain = one(*cuts[0])
    for cut in cuts[1:]:
        gain = gain * one(*cut)
    return gain


def bell_draw(key, shape, scale, bound, pieces=(), held_as=jnp.bfloat16):
    array = scale * jax.random.normal(key, shape, jnp.float32)
    if pieces:
        array = array * block_levels(key, shape, pieces, -0.22, 0.18)
    return jnp.clip(array, -bound, bound).astype(held_as)


def setup_inputs(seed: int = 0, part: int = 0) -> dict:
    streams_of = jax.random.split(jax.random.key(seed), 9)
    own_keys = jax.random.split(jax.random.fold_in(streams_of[8], part), 9)
    tokens = bell_draw(own_keys[0], (TOKENS, D), 1.0, 6.0, ((0, 16),))
    norm_gain = jnp.clip(1.0 + 0.18 * jax.random.normal(streams_of[1], (D,), jnp.float32), 0.1, 1.9)
    w_in = bell_draw(streams_of[2], (D, 3 * D), D ** -0.5, 0.375)
    short_filter = jnp.clip(jax.random.uniform(streams_of[3], (TAPS, 3 * D), jnp.float32, -0.8, 0.8), -0.8, 0.8)
    long_filter = bell_draw(streams_of[4], (TOKENS, D), TOKENS ** -0.5, 0.09375, ((0, 16),), jnp.float32)
    medium_filter = bell_draw(streams_of[5], (MED, D), MED ** -0.5, 0.5, (), jnp.float32)
    skip_gain = jnp.clip(jax.random.uniform(streams_of[6], (D,), jnp.float32, -1.0, 1.0), -1.0, 1.0)
    w_out = bell_draw(streams_of[7], (D, D), D ** -0.5, 0.375)
    return {"tokens": tokens, "norm_gain": norm_gain, "w_in": w_in, "short_filter": short_filter, "long_filter": long_filter, "medium_filter": medium_filter, "skip_gain": skip_gain, "w_out": w_out}


epsilon = 1e-06

def reference(tokens, norm_gain, w_in, short_filter, long_filter, medium_filter, skip_gain, w_out):
    inputs = tokens.astype(jnp.float32)
    mean_sq = lax.optimization_barrier(jnp.mean(inputs * inputs, axis=-1, keepdims=True))
    normed = (inputs * lax.rsqrt(mean_sq + epsilon) * norm_gain).astype(jnp.bfloat16)
    projected = jnp.dot(normed, w_in, preferred_element_type=jnp.float32).astype(jnp.bfloat16)
    projected = lax.optimization_barrier(projected).astype(jnp.float32)
    taps_count = short_filter.shape[0]
    padded = jnp.pad(projected, ((taps_count - 1, 0), (0, 0)))
    short_mix = jnp.zeros_like(projected)
    for tap_num in range(taps_count):
        begin = taps_count - 1 - tap_num
        short_mix = short_mix + short_filter[tap_num] * padded[begin:begin + TOKENS]
    query_part = short_mix[:, 0:D]
    key_part = short_mix[:, D:2 * D]
    value_part = short_mix[:, 2 * D:3 * D]
    signal = key_part * value_part
    fft_len = 2 * TOKENS
    spectrum = jnp.fft.rfft(signal, n=fft_len, axis=0) * jnp.fft.rfft(long_filter, n=fft_len, axis=0)
    conv_out = jnp.fft.irfft(spectrum, n=fft_len, axis=0)[:TOKENS].astype(signal.dtype)
    med_pad = jnp.pad(signal, ((MED - 1, 0), (0, 0)))

    def add_tap(tap_num, acc):
        weights = lax.dynamic_slice_in_dim(medium_filter, tap_num, 1, 0)
        window = lax.dynamic_slice_in_dim(med_pad, (MED - 1 - tap_num).astype(jnp.int32), TOKENS, 0)
        return acc + weights * window
    med_out = lax.fori_loop(0, MED, add_tap, jnp.zeros_like(signal))
    mixed_out = (query_part * (conv_out + med_out + skip_gain * signal)).astype(jnp.bfloat16)
    return jnp.dot(mixed_out, w_out, preferred_element_type=jnp.float32).astype(jnp.bfloat16)
```

```python
import math

import jax
import jax.numpy as jnp
import numpy as np
from jax import lax
from jax.experimental import pallas as pl
from jax.experimental.pallas import tpu as pltpu
from jax.sharding import PartitionSpec as P

epsilon = 1e-06
rim_pad = 16
vmem_bytes = 32 * 2**20


def from_behind(array, axis, by):
    devices = lax.axis_size(axis)
    pairs = [(i, i + by) for i in range(devices) if 0 <= i + by < devices]
    return lax.ppermute(array, axis, pairs)


def call(body, outs, args, scratch=(), flops=0, moved=0):
    return pl.pallas_call(
        body,
        out_shape=outs,
        in_specs=[pl.BlockSpec(memory_space=pltpu.VMEM)] * len(args),
        out_specs=jax.tree.map(lambda _: pl.BlockSpec(memory_space=pltpu.VMEM), outs),
        scratch_shapes=list(scratch),
        compiler_params=pltpu.CompilerParams(vmem_limit_bytes=vmem_bytes),
        cost_estimate=pl.CostEstimate(flops=flops, bytes_accessed=moved, transcendentals=0),
    )(*args)


def spectral_tables(devices, rows, chans):
    span = 2 * devices
    full_len = span * rows
    freq_count = devices + 1
    height = -(-freq_count * chans // 16) * 16
    freqs = np.arange(freq_count)
    blocks = np.arange(devices)
    offsets = np.arange(rows)
    eye = np.eye(chans)

    def grown(table):
        out = np.zeros((height, table.shape[1]))
        out[: table.shape[0]] = table
        return out

    angle = 2.0 * math.pi / span * (freqs[:, None] * blocks[None, :] % span)
    first = np.concatenate([grown(np.kron(np.cos(angle), eye)), grown(np.kron(-np.sin(angle), eye))])
    weight = np.where((freqs == 0) | (freqs == devices), 1.0, 2.0)[:, None] / full_len
    last = np.concatenate(
        [grown(np.kron(weight * np.cos(angle), eye)), grown(np.kron(-weight * np.sin(angle), eye))]
    ).T
    twist = 2.0 * math.pi / full_len * (freqs[:, None] * offsets[None, :] % full_len)
    tw_cos = grown(np.repeat(np.cos(twist), chans, axis=0))
    tw_sin = grown(np.repeat(np.sin(twist), chans, axis=0))
    turn = 2.0 * math.pi / rows * (offsets[:, None] * offsets[None, :] % rows)
    inner = np.concatenate([np.cos(turn), np.sin(turn)], axis=1)
    return (
        jnp.asarray(first, jnp.bfloat16),
        jnp.asarray(np.concatenate([tw_cos, tw_sin]), jnp.float32),
        jnp.asarray(inner, jnp.bfloat16),
        jnp.asarray(last, jnp.bfloat16),
    )


def filter_body(long_ref, medium_ref, skip_ref, out_ref):
    med_len = medium_ref.shape[0]
    is_first = jnp.where(lax.axis_index("seq") == 0, 1.0, 0.0)
    head = long_ref[0:med_len, :] + is_first * medium_ref[...]
    row = lax.broadcasted_iota(jnp.int32, head.shape, 0)
    head = head + jnp.where(row == 0, is_first * skip_ref[...], 0.0)
    out_ref[:, 0:med_len] = head.T.astype(jnp.bfloat16)
    out_ref[:, med_len:] = long_ref[med_len:, :].T.astype(jnp.bfloat16)


def signal_body(tokens_ref, rim_ref, gain_ref, w_ref, short_ref, signal_ref, query_ref, proj_ref):
    rows, width = tokens_ref.shape
    for src, begin, count in ((rim_ref, 0, rim_pad), (tokens_ref, rim_pad, rows)):
        inputs = src[...].astype(jnp.float32)
        mean_sq = jnp.mean(inputs * inputs, axis=-1, keepdims=True)
        normed = (inputs * lax.rsqrt(mean_sq + epsilon) * gain_ref[...]).astype(jnp.bfloat16)
        projected = jnp.dot(normed, w_ref[...], preferred_element_type=jnp.float32)
        proj_ref[begin : begin + count, :] = projected.astype(jnp.bfloat16).astype(jnp.float32)
    taps_count = short_ref.shape[0]

    def mixed(part):
        cols = slice(part * width, (part + 1) * width)
        acc = short_ref[0:1, cols] * proj_ref[rim_pad : rim_pad + rows, cols]
        for tap_num in range(1, taps_count):
            begin = rim_pad - tap_num
            acc = acc + short_ref[tap_num : tap_num + 1, cols] * proj_ref[begin : begin + rows, cols]
        return acc

    query_ref[...] = mixed(0)
    signal_ref[...] = (mixed(1) * mixed(2)).T.astype(jnp.bfloat16)


def forward(values, first_ref, twist_ref, inner_ref):
    half = twist_ref.shape[0] // 2
    rows = twist_ref.shape[1]
    spread = jnp.dot(first_ref[...], values, preferred_element_type=jnp.float32)
    tw_cos, tw_sin = twist_ref[0:half, :], twist_ref[half:, :]
    real, imag = spread[0:half], spread[half:]
    turned = jnp.concatenate([real * tw_cos + imag * tw_sin, imag * tw_cos - real * tw_sin])
    both = jnp.dot(turned.astype(jnp.bfloat16), inner_ref[...], preferred_element_type=jnp.float32)
    return both[0:half, 0:rows] + both[half:, rows:], both[half:, 0:rows] - both[0:half, rows:]


def filter_spectrum_body(filter_ref, first_ref, twist_ref, inner_ref, out_ref):
    half = twist_ref.shape[0] // 2
    real, imag = forward(filter_ref[...], first_ref, twist_ref, inner_ref)
    out_ref[0:half, :] = real
    out_ref[half:, :] = imag


def convolve_body(signal_ref, spec_ref, first_ref, twist_ref, inner_ref, last_ref, out_ref):
    half = twist_ref.shape[0] // 2
    rows = twist_ref.shape[1]
    real, imag = forward(signal_ref[...], first_ref, twist_ref, inner_ref)
    fil_re, fil_im = spec_ref[0:half, :], spec_ref[half:, :]
    product = jnp.concatenate([real * fil_re - imag * fil_im, real * fil_im + imag * fil_re])
    both = jnp.dot(product.astype(jnp.bfloat16), inner_ref[...], preferred_element_type=jnp.float32)
    real = both[0:half, 0:rows] - both[half:, rows:]
    imag = both[half:, 0:rows] + both[0:half, rows:]
    tw_cos, tw_sin = twist_ref[0:half, :], twist_ref[half:, :]
    turned = jnp.concatenate([real * tw_cos - imag * tw_sin, imag * tw_cos + real * tw_sin])
    out_ref[...] = jnp.dot(
        last_ref[...], turned.astype(jnp.bfloat16), preferred_element_type=jnp.float32
    ).astype(jnp.bfloat16)


def output_body(conv_ref, query_ref, w_ref, out_ref):
    conv = conv_ref[...].astype(jnp.float32).T
    mixed_out = (query_ref[...] * conv).astype(jnp.bfloat16)
    out_ref[...] = jnp.dot(mixed_out, w_ref[...], preferred_element_type=jnp.float32).astype(
        jnp.bfloat16
    )


def local(tokens, norm_gain, w_in, short_filter, long_filter, medium_filter, skip_gain, w_out):
    rows, width = tokens.shape
    devices = lax.axis_size("seq")
    chans = width // devices
    first, twist, inner, last = spectral_tables(devices, rows, chans)
    flat = jax.ShapeDtypeStruct((width, rows), jnp.bfloat16)

    def swap(array):
        return lax.all_to_all(
            array.reshape(devices, chans, rows), "seq", split_axis=0, concat_axis=0
        ).reshape(width, rows)

    rim = from_behind(tokens[rows - rim_pad :], "seq", 1)
    filter_part = call(
        filter_body, flat, (long_filter, medium_filter, skip_gain[None, :]), moved=500_000
    )
    filter_part = swap(filter_part)
    signal, query = call(
        signal_body,
        (flat, jax.ShapeDtypeStruct((rows, width), jnp.float32)),
        (tokens, rim, norm_gain[None, :], w_in, short_filter),
        [pltpu.VMEM((rim_pad + rows, 3 * width), jnp.float32)],
        flops=2 * rows * width * 3 * width,
        moved=1_000_000,
    )
    signal = swap(signal)
    work = 2 * first.shape[0] * width * rows
    spectrum = call(
        filter_spectrum_body,
        jax.ShapeDtypeStruct(twist.shape, jnp.float32),
        (filter_part, first, twist, inner),
        flops=3 * work,
        moved=1_500_000,
    )
    conv = call(
        convolve_body,
        flat,
        (signal, spectrum, first, twist, inner, last),
        flops=6 * work,
        moved=2_000_000,
    )
    conv = swap(conv)
    return call(
        output_body,
        jax.ShapeDtypeStruct((rows, width), jnp.bfloat16),
        (conv, query, w_out),
        flops=2 * rows * width * width,
        moved=600_000,
    )


def solution(mesh):
    placed = (P(("groups", "seq"), None), P(), P(), P(), P("seq", None), P(), P(), P())
    return jax.shard_map(
        local, mesh=mesh, in_specs=placed, out_specs=P(("groups", "seq"), None), check_vma=False
    )
```

```python
import functools
import math

import jax
import jax.numpy as jnp
import numpy as np
from jax import lax
from jax.experimental import pallas as pl
from jax.experimental.pallas import tpu as pltpu
from jax.sharding import PartitionSpec as P

epsilon = 1e-06
edge = 8
rim_step = 32
vmem_bytes = 32 * 2**20


def whole(space):
    return pl.BlockSpec(memory_space=space)


def call(body, outs, args, spaces, scratch=(), flops=0, moved=0):
    return pl.pallas_call(
        body,
        out_shape=outs,
        in_specs=[whole(space) for space in spaces],
        out_specs=jax.tree.map(lambda _: whole(pltpu.VMEM), outs),
        scratch_shapes=list(scratch),
        compiler_params=pltpu.CompilerParams(vmem_limit_bytes=vmem_bytes),
        cost_estimate=pl.CostEstimate(flops=flops, bytes_accessed=moved, transcendentals=0),
    )(*args)


def spectral_tables(devices, rows, chans):
    span = 2 * devices
    full_len = span * rows
    freq_count = devices + 1
    height = -(-freq_count * chans // 16) * 16
    freqs = np.arange(freq_count)
    blocks = np.arange(devices)
    offsets = np.arange(rows)
    eye = np.eye(chans)

    def grown(table):
        out = np.zeros((height, table.shape[1]))
        out[: table.shape[0]] = table
        return out

    angle = 2.0 * math.pi / span * (freqs[:, None] * blocks[None, :] % span)
    first = np.concatenate([grown(np.kron(np.cos(angle), eye)), grown(np.kron(-np.sin(angle), eye))])
    weight = np.where((freqs == 0) | (freqs == devices), 1.0, 2.0)[:, None] / full_len
    last = np.concatenate(
        [grown(np.kron(weight * np.cos(angle), eye)), grown(np.kron(-weight * np.sin(angle), eye))]
    ).T
    twist = 2.0 * math.pi / full_len * (freqs[:, None] * offsets[None, :] % full_len)
    tw_cos = grown(np.repeat(np.cos(twist), chans, axis=0))
    tw_sin = grown(np.repeat(np.sin(twist), chans, axis=0))
    turn = 2.0 * math.pi / rows * (offsets[:, None] * offsets[None, :] % rows)
    inner = np.concatenate([np.cos(turn), np.sin(turn)], axis=1)
    return (
        jnp.asarray(first, jnp.bfloat16),
        jnp.asarray(np.concatenate([tw_cos, tw_sin]), jnp.float32),
        jnp.asarray(inner, jnp.bfloat16),
        jnp.asarray(last, jnp.bfloat16),
    )


def prepare_body(*refs):
    hbm, (packed_ref, query_ref), held, proj_ref, sems = refs[:7], refs[7:9], refs[9:16], *refs[16:]
    copies = [pltpu.make_async_copy(h, v, sems.at[i]) for i, (h, v) in enumerate(zip(hbm, held))]
    for copy in copies:
        copy.start()
    tokens_ref, gain_ref, w_ref, short_ref, long_ref, medium_ref, skip_ref = held
    rows, width = tokens_ref.shape
    proj_ref[0:edge, :] = jnp.zeros((edge, proj_ref.shape[1]), jnp.float32)
    proj_ref[edge + rows :, :] = jnp.zeros((edge, proj_ref.shape[1]), jnp.float32)
    copies[0].wait()
    copies[1].wait()
    inputs = tokens_ref[...].astype(jnp.float32)
    mean_sq = jnp.mean(inputs * inputs, axis=-1, keepdims=True)
    normed = (inputs * lax.rsqrt(mean_sq + epsilon) * gain_ref[...]).astype(jnp.bfloat16)
    copies[2].wait()
    projected = jnp.dot(normed, w_ref[...], preferred_element_type=jnp.float32)
    proj_ref[edge : edge + rows, :] = projected.astype(jnp.bfloat16).astype(jnp.float32)
    copies[3].wait()
    taps_count = short_ref.shape[0]

    def mixed(part):
        cols = slice(part * width, (part + 1) * width)
        acc = short_ref[0:1, cols] * proj_ref[edge : 2 * edge + rows, cols]
        for tap_num in range(1, taps_count):
            begin = edge - tap_num
            acc = acc + short_ref[tap_num : tap_num + 1, cols] * proj_ref[begin : begin + rows + edge, cols]
        return acc

    query, key, value = mixed(0), mixed(1), mixed(2)
    row = lax.broadcasted_iota(jnp.int32, (rows, width), 0)
    query_ref[...] = jnp.where(row < taps_count - 1, 1.0, query[0:rows])
    packed_ref[:, 0:rows] = (key[0:rows] * value[0:rows]).T.astype(jnp.bfloat16)
    rims = []
    for part in (key, value, query):
        rims += [part[0:edge], part[rows:], jnp.zeros((rim_step - 2 * edge, width), jnp.float32)]
    rims.append(jnp.zeros((128 - 3 * rim_step, width), jnp.float32))
    packed_ref[:, 2 * rows :] = jnp.concatenate(rims).T.astype(jnp.bfloat16)
    for copy in copies[4:]:
        copy.wait()
    med_len = medium_ref.shape[0]
    is_first = jnp.where(lax.axis_index("seq") == 0, 1.0, 0.0)
    head = long_ref[0:med_len, :] + is_first * medium_ref[...]
    head_row = lax.broadcasted_iota(jnp.int32, head.shape, 0)
    head = head + jnp.where(head_row == 0, is_first * skip_ref[...], 0.0)
    packed_ref[:, rows : rows + med_len] = head.T.astype(jnp.bfloat16)
    packed_ref[:, rows + med_len : 2 * rows] = long_ref[med_len:, :].T.astype(jnp.bfloat16)


def convolve_body(chans, rim_count, packed_ref, first_ref, twist_ref, inner_ref, last_ref, out_ref):
    half = twist_ref.shape[0] // 2
    rows = twist_ref.shape[1]
    rim = packed_ref[:, 2 * rows :].astype(jnp.float32)
    before = jnp.concatenate([jnp.zeros((chans, 128), jnp.float32), rim[:-chans]])
    rim = rim + pltpu.roll(before, 128 - edge, 1)
    in_rim = lax.broadcasted_iota(jnp.int32, rim.shape, 1) < rim_count
    rim_signal = (rim * pltpu.roll(rim, 128 - rim_step, 1)).astype(jnp.bfloat16)
    rim_query = jnp.where(in_rim, pltpu.roll(rim, 128 - 2 * rim_step, 1), 1.0)
    values = jnp.concatenate(
        [jnp.where(in_rim, rim_signal, packed_ref[:, 0:128]), packed_ref[:, 128 : 2 * rows]], axis=1
    )
    spread = jnp.dot(first_ref[...], values, preferred_element_type=jnp.float32)
    tw_cos, tw_sin = twist_ref[0:half, :], twist_ref[half:, :]
    spectra = []
    for begin in (0, rows):
        real, imag = spread[0:half, begin : begin + rows], spread[half:, begin : begin + rows]
        turned = jnp.concatenate([real * tw_cos + imag * tw_sin, imag * tw_cos - real * tw_sin])
        both = jnp.dot(turned.astype(jnp.bfloat16), inner_ref[...], preferred_element_type=jnp.float32)
        spectra.append(both[0:half, 0:rows] + both[half:, rows:])
        spectra.append(both[half:, 0:rows] - both[0:half, rows:])
    real, imag, fil_re, fil_im = spectra
    product = jnp.concatenate([real * fil_re - imag * fil_im, real * fil_im + imag * fil_re])
    both = jnp.dot(product.astype(jnp.bfloat16), inner_ref[...], preferred_element_type=jnp.float32)
    real = both[0:half, 0:rows] - both[half:, rows:]
    imag = both[half:, 0:rows] + both[0:half, rows:]
    turned = jnp.concatenate([real * tw_cos - imag * tw_sin, imag * tw_cos + real * tw_sin])
    conv = jnp.dot(last_ref[...], turned.astype(jnp.bfloat16), preferred_element_type=jnp.float32)
    out_ref[:, 0:128] = (conv[:, 0:128] * rim_query).astype(jnp.bfloat16)
    out_ref[:, 128:] = conv[:, 128:].astype(jnp.bfloat16)


def output_body(conv_ref, query_ref, w_ref, out_ref):
    conv = conv_ref[...].astype(jnp.float32).T
    mixed_out = (query_ref[...] * conv).astype(jnp.bfloat16)
    out_ref[...] = jnp.dot(mixed_out, w_ref[...], preferred_element_type=jnp.float32).astype(
        jnp.bfloat16
    )


def local(tokens, norm_gain, w_in, short_filter, long_filter, medium_filter, skip_gain, w_out):
    rows, width = tokens.shape
    devices = lax.axis_size("seq")
    chans = width // devices
    first, twist, inner, last = spectral_tables(devices, rows, chans)

    def swap(array):
        pieces = array.reshape(devices, chans, array.shape[1])
        return lax.all_to_all(pieces, "seq", split_axis=0, concat_axis=0).reshape(array.shape)

    args = (tokens, norm_gain[None, :], w_in, short_filter, long_filter, medium_filter, skip_gain[None, :])
    packed, query = call(
        prepare_body,
        (
            jax.ShapeDtypeStruct((width, 2 * rows + 128), jnp.bfloat16),
            jax.ShapeDtypeStruct((rows, width), jnp.float32),
        ),
        args,
        [pltpu.HBM] * len(args),
        [pltpu.VMEM(arg.shape, arg.dtype) for arg in args]
        + [
            pltpu.VMEM((rows + 2 * edge, 3 * width), jnp.float32),
            pltpu.SemaphoreType.DMA((len(args),)),
        ],
        flops=2 * rows * width * 3 * width,
        moved=1_500_000,
    )
    conv = call(
        functools.partial(convolve_body, chans, short_filter.shape[0] - 1),
        jax.ShapeDtypeStruct((width, rows), jnp.bfloat16),
        (swap(packed), first, twist, inner, last),
        [pltpu.VMEM] * 5,
        flops=18 * first.shape[0] * width * rows,
        moved=2_000_000,
    )
    return call(
        output_body,
        jax.ShapeDtypeStruct((rows, width), jnp.bfloat16),
        (swap(conv), query, w_out),
        [pltpu.VMEM] * 3,
        flops=2 * rows * width * width,
        moved=600_000,
    )


def solution(mesh):
    placed = (P(("groups", "seq"), None), P(), P(), P(), P("seq", None), P(), P(), P())
    return jax.shard_map(
        local, mesh=mesh, in_specs=placed, out_specs=P(("groups", "seq"), None), check_vma=False
    )
```

```python
import functools
import math

import jax
import jax.numpy as jnp
import numpy as np
from jax import lax
from jax.experimental import pallas as pl
from jax.experimental.pallas import tpu as pltpu
from jax.sharding import PartitionSpec as P

epsilon = 1e-06
edge = 8
rim_step = 32
vmem_bytes = 32 * 2**20


def whole(space):
    return pl.BlockSpec(memory_space=space)


def call(body, outs, args, spaces, scratch=(), flops=0, moved=0):
    return pl.pallas_call(
        body,
        out_shape=outs,
        in_specs=[whole(space) for space in spaces],
        out_specs=jax.tree.map(lambda _: whole(pltpu.VMEM), outs),
        scratch_shapes=list(scratch),
        compiler_params=pltpu.CompilerParams(vmem_limit_bytes=vmem_bytes),
        cost_estimate=pl.CostEstimate(flops=flops, bytes_accessed=moved, transcendentals=0),
    )(*args)


def spectral_tables(devices, rows, chans):
    span = 2 * devices
    full_len = span * rows
    freq_count = devices + 1
    height = -(-freq_count * chans // 16) * 16
    freqs = np.arange(freq_count)
    blocks = np.arange(devices)
    offsets = np.arange(rows)
    eye = np.eye(chans)

    def grown(table):
        out = np.zeros((height, table.shape[1]))
        out[: table.shape[0]] = table
        return out

    angle = 2.0 * math.pi / span * (freqs[:, None] * blocks[None, :] % span)
    first = np.concatenate([grown(np.kron(np.cos(angle), eye)), grown(np.kron(-np.sin(angle), eye))])
    weight = np.where((freqs == 0) | (freqs == devices), 1.0, 2.0)[:, None] / full_len
    last = np.concatenate(
        [grown(np.kron(weight * np.cos(angle), eye)), grown(np.kron(-weight * np.sin(angle), eye))]
    ).T
    twist = 2.0 * math.pi / full_len * (freqs[:, None] * offsets[None, :] % full_len)
    tw_cos = grown(np.repeat(np.cos(twist), chans, axis=0))
    tw_sin = grown(np.repeat(np.sin(twist), chans, axis=0))
    turn = 2.0 * math.pi / rows * (offsets[:, None] * offsets[None, :] % rows)
    inner = np.concatenate([np.cos(turn), np.sin(turn)], axis=1)
    return (
        jnp.asarray(first, jnp.bfloat16),
        jnp.asarray(np.concatenate([tw_cos, tw_sin]), jnp.float32),
        jnp.asarray(inner, jnp.bfloat16),
        jnp.asarray(last, jnp.bfloat16),
    )


def prepare_body(*refs):
    hbm, (packed_ref, query_ref), held, proj_ref, sems = refs[:7], refs[7:9], refs[9:16], *refs[16:]
    copies = [pltpu.make_async_copy(h, v, sems.at[i]) for i, (h, v) in enumerate(zip(hbm, held))]
    for copy in copies:
        copy.start()
    tokens_ref, gain_ref, w_ref, short_ref, long_ref, medium_ref, skip_ref = held
    rows, width = tokens_ref.shape
    proj_ref[0:edge, :] = jnp.zeros((edge, proj_ref.shape[1]), jnp.float32)
    proj_ref[edge + rows :, :] = jnp.zeros((edge, proj_ref.shape[1]), jnp.float32)
    copies[0].wait()
    copies[1].wait()
    inputs = tokens_ref[...].astype(jnp.float32)
    mean_sq = jnp.mean(inputs * inputs, axis=-1, keepdims=True)
    normed = (inputs * lax.rsqrt(mean_sq + epsilon) * gain_ref[...]).astype(jnp.bfloat16)
    copies[2].wait()
    projected = jnp.dot(normed, w_ref[...], preferred_element_type=jnp.float32)
    proj_ref[edge : edge + rows, :] = projected.astype(jnp.bfloat16).astype(jnp.float32)
    copies[3].wait()
    taps_count = short_ref.shape[0]

    def mixed(part):
        cols = slice(part * width, (part + 1) * width)
        acc = short_ref[0:1, cols] * proj_ref[edge : 2 * edge + rows, cols]
        for tap_num in range(1, taps_count):
            begin = edge - tap_num
            acc = acc + short_ref[tap_num : tap_num + 1, cols] * proj_ref[begin : begin + rows + edge, cols]
        return acc

    query, key, value = mixed(0), mixed(1), mixed(2)
    row = lax.broadcasted_iota(jnp.int32, (rows, width), 0)
    query_ref[...] = jnp.where(row < taps_count - 1, 1.0, query[0:rows])
    packed_ref[:, 0:rows] = (key[0:rows] * value[0:rows]).T.astype(jnp.bfloat16)
    rims = []
    for part in (key, value, query):
        rims += [part[0:edge], part[rows:], jnp.zeros((rim_step - 2 * edge, width), jnp.float32)]
    rims.append(jnp.zeros((128 - 3 * rim_step, width), jnp.float32))
    packed_ref[:, 2 * rows :] = jnp.concatenate(rims).T.astype(jnp.bfloat16)
    for copy in copies[4:]:
        copy.wait()
    med_len = medium_ref.shape[0]
    is_first = jnp.where(lax.axis_index("seq") == 0, 1.0, 0.0)
    head = long_ref[0:med_len, :] + is_first * medium_ref[...]
    head_row = lax.broadcasted_iota(jnp.int32, head.shape, 0)
    head = head + jnp.where(head_row == 0, is_first * skip_ref[...], 0.0)
    packed_ref[:, rows : rows + med_len] = head.T.astype(jnp.bfloat16)
    packed_ref[:, rows + med_len : 2 * rows] = long_ref[med_len:, :].T.astype(jnp.bfloat16)


def convolve_body(chans, rim_count, packed_ref, first_ref, twist_ref, inner_ref, last_ref, out_ref):
    half = twist_ref.shape[0] // 2
    rows = twist_ref.shape[1]
    rim = packed_ref[:, 2 * rows :].astype(jnp.float32)
    before = jnp.concatenate([jnp.zeros((chans, 128), jnp.float32), rim[:-chans]])
    rim = rim + pltpu.roll(before, 128 - edge, 1)
    in_rim = lax.broadcasted_iota(jnp.int32, rim.shape, 1) < rim_count
    rim_signal = (rim * pltpu.roll(rim, 128 - rim_step, 1)).astype(jnp.bfloat16)
    rim_query = jnp.where(in_rim, pltpu.roll(rim, 128 - 2 * rim_step, 1), 1.0)
    values = jnp.concatenate(
        [jnp.where(in_rim, rim_signal, packed_ref[:, 0:128]), packed_ref[:, 128 : 2 * rows]], axis=1
    )
    spread = jnp.dot(first_ref[...], values, preferred_element_type=jnp.float32)
    tw_cos, tw_sin = twist_ref[0:half, :], twist_ref[half:, :]
    spectra = []
    for begin in (0, rows):
        real, imag = spread[0:half, begin : begin + rows], spread[half:, begin : begin + rows]
        turned = jnp.concatenate([real * tw_cos + imag * tw_sin, imag * tw_cos - real * tw_sin])
        both = jnp.dot(turned.astype(jnp.bfloat16), inner_ref[...], preferred_element_type=jnp.float32)
        spectra.append(both[0:half, 0:rows] + both[half:, rows:])
        spectra.append(both[half:, 0:rows] - both[0:half, rows:])
    real, imag, fil_re, fil_im = spectra
    product = jnp.concatenate([real * fil_re - imag * fil_im, real * fil_im + imag * fil_re])
    both = jnp.dot(product.astype(jnp.bfloat16), inner_ref[...], preferred_element_type=jnp.float32)
    real = both[0:half, 0:rows] - both[half:, rows:]
    imag = both[half:, 0:rows] + both[0:half, rows:]
    turned = jnp.concatenate([real * tw_cos - imag * tw_sin, imag * tw_cos + real * tw_sin])
    conv = jnp.dot(last_ref[...], turned.astype(jnp.bfloat16), preferred_element_type=jnp.float32)
    out_ref[:, 0:128] = (conv[:, 0:128] * rim_query).astype(jnp.bfloat16)
    out_ref[:, 128:] = conv[:, 128:].astype(jnp.bfloat16)


def output_body(conv_ref, query_ref, w_ref, out_ref):
    conv = conv_ref[...].astype(jnp.float32).T
    mixed_out = (query_ref[...] * conv).astype(jnp.bfloat16)
    out_ref[...] = jnp.dot(mixed_out, w_ref[...], preferred_element_type=jnp.float32).astype(
        jnp.bfloat16
    )


def local(tokens, norm_gain, w_in, short_filter, long_filter, medium_filter, skip_gain, w_out):
    rows, width = tokens.shape
    devices = lax.axis_size("seq")
    chans = width // devices
    first, twist, inner, last = spectral_tables(devices, rows, chans)

    def swap(array):
        pieces = array.reshape(devices, chans, array.shape[1])
        return lax.all_to_all(pieces, "seq", split_axis=0, concat_axis=0).reshape(array.shape)

    args = (tokens, norm_gain[None, :], w_in, short_filter, long_filter, medium_filter, skip_gain[None, :])
    args = tuple(pltpu.with_memory_space_constraint(arg, pltpu.HBM) for arg in args)
    packed, query = call(
        prepare_body,
        (
            jax.ShapeDtypeStruct((width, 2 * rows + 128), jnp.bfloat16),
            jax.ShapeDtypeStruct((rows, width), jnp.float32),
        ),
        args,
        [pltpu.HBM] * len(args),
        [pltpu.VMEM(arg.shape, arg.dtype) for arg in args]
        + [
            pltpu.VMEM((rows + 2 * edge, 3 * width), jnp.float32),
            pltpu.SemaphoreType.DMA((len(args),)),
        ],
        flops=2 * rows * width * 3 * width,
        moved=1_500_000,
    )
    conv = call(
        functools.partial(convolve_body, chans, short_filter.shape[0] - 1),
        jax.ShapeDtypeStruct((width, rows), jnp.bfloat16),
        (swap(packed), first, twist, inner, last),
        [pltpu.VMEM] * 5,
        flops=18 * first.shape[0] * width * rows,
        moved=2_000_000,
    )
    return call(
        output_body,
        jax.ShapeDtypeStruct((rows, width), jnp.bfloat16),
        (swap(conv), query, w_out),
        [pltpu.VMEM] * 3,
        flops=2 * rows * width * width,
        moved=600_000,
    )


def solution(mesh):
    placed = (P(("groups", "seq"), None), P(), P(), P(), P("seq", None), P(), P(), P())
    return jax.shard_map(
        local, mesh=mesh, in_specs=placed, out_specs=P(("groups", "seq"), None), check_vma=False
    )
```

```python
import functools
import math

import jax
import jax.numpy as jnp
import numpy as np
from jax import lax
from jax.experimental import pallas as pl
from jax.experimental.pallas import tpu as pltpu
from jax.sharding import PartitionSpec as P

epsilon = 1e-06
edge = 8
rim_step = 32
vmem_bytes = 32 * 2**20


def whole(space):
    return pl.BlockSpec(memory_space=space)


def call(body, outs, args, spaces, scratch=(), flops=0, moved=0):
    return pl.pallas_call(
        body,
        out_shape=outs,
        in_specs=[whole(space) for space in spaces],
        out_specs=jax.tree.map(lambda _: whole(pltpu.VMEM), outs),
        scratch_shapes=list(scratch),
        compiler_params=pltpu.CompilerParams(vmem_limit_bytes=vmem_bytes),
        cost_estimate=pl.CostEstimate(flops=flops, bytes_accessed=moved, transcendentals=0),
    )(*args)


def spectral_tables(outer, inner_size, rows, chans):
    devices = outer * inner_size
    span = 2 * devices
    full_len = span * rows
    freq_count = devices + 1
    height = -(-freq_count * chans // 16) * 16
    freqs = np.arange(freq_count)
    blocks = np.arange(devices).reshape(outer, inner_size).T.ravel()
    offsets = np.arange(rows)
    eye = np.eye(chans)

    def grown(table):
        out = np.zeros((height, table.shape[1]))
        out[: table.shape[0]] = table
        return out

    angle = 2.0 * math.pi / span * (freqs[:, None] * blocks[None, :] % span)
    first = np.concatenate([grown(np.kron(np.cos(angle), eye)), grown(np.kron(-np.sin(angle), eye))])
    weight = np.where((freqs == 0) | (freqs == devices), 1.0, 2.0)[:, None] / full_len
    last = np.concatenate(
        [grown(np.kron(weight * np.cos(angle), eye)), grown(np.kron(-weight * np.sin(angle), eye))]
    ).T
    twist = 2.0 * math.pi / full_len * (freqs[:, None] * offsets[None, :] % full_len)
    tw_cos = grown(np.repeat(np.cos(twist), chans, axis=0))
    tw_sin = grown(np.repeat(np.sin(twist), chans, axis=0))
    turn = 2.0 * math.pi / rows * (offsets[:, None] * offsets[None, :] % rows)
    inner = np.concatenate([np.cos(turn), np.sin(turn)], axis=1)
    return (
        jnp.asarray(first, jnp.bfloat16),
        jnp.asarray(np.concatenate([tw_cos, tw_sin]), jnp.float32),
        jnp.asarray(inner, jnp.bfloat16),
        jnp.asarray(last, jnp.bfloat16),
    )


def prepare_body(*refs):
    hbm, (packed_ref, query_ref), held, proj_ref, sems = refs[:7], refs[7:9], refs[9:16], *refs[16:]
    copies = [pltpu.make_async_copy(h, v, sems.at[i]) for i, (h, v) in enumerate(zip(hbm, held))]
    for copy in copies:
        copy.start()
    tokens_ref, gain_ref, w_ref, short_ref, long_ref, medium_ref, skip_ref = held
    rows, width = tokens_ref.shape
    proj_ref[0:edge, :] = jnp.zeros((edge, proj_ref.shape[1]), jnp.float32)
    proj_ref[edge + rows :, :] = jnp.zeros((edge, proj_ref.shape[1]), jnp.float32)
    copies[0].wait()
    copies[1].wait()
    inputs = tokens_ref[...].astype(jnp.float32)
    mean_sq = jnp.mean(inputs * inputs, axis=-1, keepdims=True)
    normed = (inputs * lax.rsqrt(mean_sq + epsilon) * gain_ref[...]).astype(jnp.bfloat16)
    copies[2].wait()
    projected = jnp.dot(normed, w_ref[...], preferred_element_type=jnp.float32)
    proj_ref[edge : edge + rows, :] = projected.astype(jnp.bfloat16).astype(jnp.float32)
    copies[3].wait()
    taps_count = short_ref.shape[0]

    def mixed(part):
        cols = slice(part * width, (part + 1) * width)
        acc = short_ref[0:1, cols] * proj_ref[edge : 2 * edge + rows, cols]
        for tap_num in range(1, taps_count):
            begin = edge - tap_num
            acc = acc + short_ref[tap_num : tap_num + 1, cols] * proj_ref[begin : begin + rows + edge, cols]
        return acc

    query, key, value = mixed(0), mixed(1), mixed(2)
    row = lax.broadcasted_iota(jnp.int32, (rows, width), 0)
    query_ref[...] = jnp.where(row < taps_count - 1, 1.0, query[0:rows])
    packed_ref[:, 0:rows] = (key[0:rows] * value[0:rows]).T.astype(jnp.bfloat16)
    rims = []
    for part in (key, value, query):
        rims += [part[0:edge], part[rows:], jnp.zeros((rim_step - 2 * edge, width), jnp.float32)]
    rims.append(jnp.zeros((128 - 3 * rim_step, width), jnp.float32))
    packed_ref[:, 2 * rows :] = jnp.concatenate(rims).T.astype(jnp.bfloat16)
    for copy in copies[4:]:
        copy.wait()
    med_len = medium_ref.shape[0]
    is_first = jnp.where(lax.axis_index(("outer", "inner")) == 0, 1.0, 0.0)
    head = long_ref[0:med_len, :] + is_first * medium_ref[...]
    head_row = lax.broadcasted_iota(jnp.int32, head.shape, 0)
    head = head + jnp.where(head_row == 0, is_first * skip_ref[...], 0.0)
    packed_ref[:, rows : rows + med_len] = head.T.astype(jnp.bfloat16)
    packed_ref[:, rows + med_len : 2 * rows] = long_ref[med_len:, :].T.astype(jnp.bfloat16)


def convolve_body(chans, outer, rim_count, packed_ref, first_ref, twist_ref, inner_ref, last_ref, out_ref):
    half = twist_ref.shape[0] // 2
    rows = twist_ref.shape[1]
    rim = packed_ref[:, 2 * rows :].astype(jnp.float32)
    turn = outer * chans
    before = [jnp.zeros((chans, 128), jnp.float32), rim[-turn:-chans], rim[:-turn]]
    before = jnp.concatenate(before)
    rim = rim + pltpu.roll(before, 128 - edge, 1)
    in_rim = lax.broadcasted_iota(jnp.int32, rim.shape, 1) < rim_count
    rim_signal = (rim * pltpu.roll(rim, 128 - rim_step, 1)).astype(jnp.bfloat16)
    rim_query = jnp.where(in_rim, pltpu.roll(rim, 128 - 2 * rim_step, 1), 1.0)
    values = jnp.concatenate(
        [jnp.where(in_rim, rim_signal, packed_ref[:, 0:128]), packed_ref[:, 128 : 2 * rows]], axis=1
    )
    spread = jnp.dot(first_ref[...], values, preferred_element_type=jnp.float32)
    tw_cos, tw_sin = twist_ref[0:half, :], twist_ref[half:, :]
    spectra = []
    for begin in (0, rows):
        real, imag = spread[0:half, begin : begin + rows], spread[half:, begin : begin + rows]
        turned = jnp.concatenate([real * tw_cos + imag * tw_sin, imag * tw_cos - real * tw_sin])
        both = jnp.dot(turned.astype(jnp.bfloat16), inner_ref[...], preferred_element_type=jnp.float32)
        spectra.append(both[0:half, 0:rows] + both[half:, rows:])
        spectra.append(both[half:, 0:rows] - both[0:half, rows:])
    real, imag, fil_re, fil_im = spectra
    product = jnp.concatenate([real * fil_re - imag * fil_im, real * fil_im + imag * fil_re])
    both = jnp.dot(product.astype(jnp.bfloat16), inner_ref[...], preferred_element_type=jnp.float32)
    real = both[0:half, 0:rows] - both[half:, rows:]
    imag = both[half:, 0:rows] + both[0:half, rows:]
    turned = jnp.concatenate([real * tw_cos - imag * tw_sin, imag * tw_cos + real * tw_sin])
    conv = jnp.dot(last_ref[...], turned.astype(jnp.bfloat16), preferred_element_type=jnp.float32)
    out_ref[:, 0:128] = (conv[:, 0:128] * rim_query).astype(jnp.bfloat16)
    out_ref[:, 128:] = conv[:, 128:].astype(jnp.bfloat16)


def output_body(conv_ref, query_ref, w_ref, out_ref):
    conv = conv_ref[...].astype(jnp.float32).T
    mixed_out = (query_ref[...] * conv).astype(jnp.bfloat16)
    out_ref[...] = jnp.dot(mixed_out, w_ref[...], preferred_element_type=jnp.float32).astype(
        jnp.bfloat16
    )


def local(tokens, norm_gain, w_in, short_filter, long_filter, medium_filter, skip_gain, w_out):
    rows, width = tokens.shape
    devices = lax.axis_size(("outer", "inner"))
    chans = width // devices
    first, twist, inner, last = spectral_tables(
        lax.axis_size("outer"), lax.axis_size("inner"), rows, chans
    )


    def swap(array, axes):
        sizes = [lax.axis_size(axis) for axis in axes]
        pieces = array.reshape(*sizes, chans, array.shape[1])
        pieces = lax.all_to_all(pieces, axes[0], split_axis=0, concat_axis=0)
        pieces = pieces.transpose(1, 0, 2, 3)
        pieces = lax.all_to_all(pieces, axes[1], split_axis=0, concat_axis=0)
        return pieces.reshape(array.shape)

    args = (tokens, norm_gain[None, :], w_in, short_filter, long_filter, medium_filter, skip_gain[None, :])
    args = tuple(pltpu.with_memory_space_constraint(arg, pltpu.HBM) for arg in args)
    packed, query = call(
        prepare_body,
        (
            jax.ShapeDtypeStruct((width, 2 * rows + 128), jnp.bfloat16),
            jax.ShapeDtypeStruct((rows, width), jnp.float32),
        ),
        args,
        [pltpu.HBM] * len(args),
        [pltpu.VMEM(arg.shape, arg.dtype) for arg in args]
        + [
            pltpu.VMEM((rows + 2 * edge, 3 * width), jnp.float32),
            pltpu.SemaphoreType.DMA((len(args),)),
        ],
        flops=2 * rows * width * 3 * width,
        moved=1_500_000,
    )
    conv = call(
        functools.partial(convolve_body, chans, lax.axis_size("outer"), short_filter.shape[0] - 1),
        jax.ShapeDtypeStruct((width, rows), jnp.bfloat16),
        (swap(packed, ("outer", "inner")), first, twist, inner, last),
        [pltpu.VMEM] * 5,
        flops=18 * first.shape[0] * width * rows,
        moved=2_000_000,
    )
    return call(
        output_body,
        jax.ShapeDtypeStruct((rows, width), jnp.bfloat16),
        (swap(conv, ("inner", "outer")), query, w_out),
        [pltpu.VMEM] * 3,
        flops=2 * rows * width * width,
        moved=600_000,
    )


def solution(mesh):
    groups, devices = mesh.devices.shape
    outer = 2 ** (devices.bit_length() // 2)
    split = jax.sharding.Mesh(
        mesh.devices.reshape(groups, outer, devices // outer), ("groups", "outer", "inner")
    )
    rows = P(("groups", "outer", "inner"), None)
    placed = (rows, P(), P(), P(), P(("outer", "inner"), None), P(), P(), P())
    return jax.shard_map(local, mesh=split, in_specs=placed, out_specs=rows, check_vma=False)
```

```python
import functools
import math

import jax
import jax.numpy as jnp
import numpy as np
from jax import lax
from jax.experimental import pallas as pl
from jax.experimental.pallas import tpu as pltpu
from jax.sharding import PartitionSpec as P

epsilon = 1e-06
edge = 8
rim_step = 32
vmem_bytes = 32 * 2**20


def whole(space):
    return pl.BlockSpec(memory_space=space)


def call(body, outs, args, spaces, scratch=(), flops=0, moved=0):
    return pl.pallas_call(
        body,
        out_shape=outs,
        in_specs=[whole(space) for space in spaces],
        out_specs=jax.tree.map(lambda _: whole(pltpu.VMEM), outs),
        scratch_shapes=list(scratch),
        compiler_params=pltpu.CompilerParams(vmem_limit_bytes=vmem_bytes),
        cost_estimate=pl.CostEstimate(flops=flops, bytes_accessed=moved, transcendentals=0),
    )(*args)


def spectral_tables(devices, rows, chans):
    span = 2 * devices
    full_len = span * rows
    freq_count = devices + 1
    height = -(-freq_count * chans // 16) * 16
    freqs = np.arange(freq_count)
    blocks = np.arange(devices)
    offsets = np.arange(rows)
    eye = np.eye(chans)

    def grown(table):
        out = np.zeros((height, table.shape[1]))
        out[: table.shape[0]] = table
        return out

    angle = 2.0 * math.pi / span * (freqs[:, None] * blocks[None, :] % span)
    first = np.concatenate([grown(np.kron(np.cos(angle), eye)), grown(np.kron(-np.sin(angle), eye))])
    weight = np.where((freqs == 0) | (freqs == devices), 1.0, 2.0)[:, None] / full_len
    last = np.concatenate(
        [grown(np.kron(weight * np.cos(angle), eye)), grown(np.kron(-weight * np.sin(angle), eye))]
    ).T
    twist = 2.0 * math.pi / full_len * (freqs[:, None] * offsets[None, :] % full_len)
    tw_cos = grown(np.repeat(np.cos(twist), chans, axis=0))
    tw_sin = grown(np.repeat(np.sin(twist), chans, axis=0))
    turn = 2.0 * math.pi / rows * (offsets[:, None] * offsets[None, :] % rows)
    inner = np.concatenate([np.cos(turn), np.sin(turn)], axis=1)
    return (
        jnp.asarray(first, jnp.bfloat16),
        jnp.asarray(np.concatenate([tw_cos, tw_sin]), jnp.float32),
        jnp.asarray(inner, jnp.bfloat16),
        jnp.asarray(last, jnp.bfloat16),
    )


def put_pieces(source_ref, piece_refs):
    if len(piece_refs) == 1:
        piece_refs[0][...] = source_ref[...]
        return
    span = piece_refs[0].shape[0]
    mine = lax.axis_index("outer")
    for distance, piece_ref in enumerate(piece_refs):
        piece_ref[...] = source_ref[pl.ds(pl.multiple_of((mine ^ distance) * span, span), span), :]


def take_pieces(piece_refs, target_ref, chans):
    if len(piece_refs) == 1:
        target_ref[...] = piece_refs[0][...]
        return
    mine, mine_inner = lax.axis_index("outer"), lax.axis_index("inner")
    for distance, piece_ref in enumerate(piece_refs):
        for far in range(piece_ref.shape[0] // chans):
            block = (mine ^ far) * len(piece_refs) + (mine_inner ^ distance)
            target_ref[pl.ds(pl.multiple_of(block * chans, chans), chans), :] = piece_ref[
                far * chans : (far + 1) * chans, :
            ]


def regroup_body(chans, outer, *refs):
    mine = lax.axis_index("inner")
    for distance, out_ref in enumerate(refs[outer:]):
        begin = pl.multiple_of((mine ^ distance) * chans, chans)
        for far in range(outer):
            out_ref[far * chans : (far + 1) * chans, :] = refs[far][pl.ds(begin, chans), :]


def prepare_body(outer, *refs):
    hbm, query_ref, piece_refs, refs = refs[:7], refs[7], refs[8 : 8 + outer], refs[8 + outer :]
    held, packed_ref, proj_ref, sems = refs[:7], *refs[7:]
    copies = [pltpu.make_async_copy(h, v, sems.at[i]) for i, (h, v) in enumerate(zip(hbm, held))]
    for copy in copies:
        copy.start()
    tokens_ref, gain_ref, w_ref, short_ref, long_ref, medium_ref, skip_ref = held
    rows, width = tokens_ref.shape
    proj_ref[0:edge, :] = jnp.zeros((edge, proj_ref.shape[1]), jnp.float32)
    proj_ref[edge + rows :, :] = jnp.zeros((edge, proj_ref.shape[1]), jnp.float32)
    copies[0].wait()
    copies[1].wait()
    inputs = tokens_ref[...].astype(jnp.float32)
    mean_sq = jnp.mean(inputs * inputs, axis=-1, keepdims=True)
    normed = (inputs * lax.rsqrt(mean_sq + epsilon) * gain_ref[...]).astype(jnp.bfloat16)
    copies[2].wait()
    projected = jnp.dot(normed, w_ref[...], preferred_element_type=jnp.float32)
    proj_ref[edge : edge + rows, :] = projected.astype(jnp.bfloat16).astype(jnp.float32)
    copies[3].wait()
    taps_count = short_ref.shape[0]

    def mixed(part):
        cols = slice(part * width, (part + 1) * width)
        acc = short_ref[0:1, cols] * proj_ref[edge : 2 * edge + rows, cols]
        for tap_num in range(1, taps_count):
            begin = edge - tap_num
            acc = acc + short_ref[tap_num : tap_num + 1, cols] * proj_ref[begin : begin + rows + edge, cols]
        return acc

    query, key, value = mixed(0), mixed(1), mixed(2)
    row = lax.broadcasted_iota(jnp.int32, (rows, width), 0)
    query_ref[...] = jnp.where(row < taps_count - 1, 1.0, query[0:rows])
    packed_ref[:, 0:rows] = (key[0:rows] * value[0:rows]).T.astype(jnp.bfloat16)
    rims = []
    for part in (key, value, query):
        rims += [part[0:edge], part[rows:], jnp.zeros((rim_step - 2 * edge, width), jnp.float32)]
    rims.append(jnp.zeros((128 - 3 * rim_step, width), jnp.float32))
    packed_ref[:, 2 * rows :] = jnp.concatenate(rims).T.astype(jnp.bfloat16)
    for copy in copies[4:]:
        copy.wait()
    med_len = medium_ref.shape[0]
    is_first = jnp.where(lax.axis_index(("outer", "inner")) == 0, 1.0, 0.0)
    head = long_ref[0:med_len, :] + is_first * medium_ref[...]
    head_row = lax.broadcasted_iota(jnp.int32, head.shape, 0)
    head = head + jnp.where(head_row == 0, is_first * skip_ref[...], 0.0)
    packed_ref[:, rows : rows + med_len] = head.T.astype(jnp.bfloat16)
    packed_ref[:, rows + med_len : 2 * rows] = long_ref[med_len:, :].T.astype(jnp.bfloat16)
    put_pieces(packed_ref, piece_refs)


def convolve_body(chans, inner, outer, rim_count, *refs):
    piece_refs, refs = refs[:inner], refs[inner:]
    (first_ref, twist_ref, inner_ref, last_ref), refs = refs[:4], refs[4:]
    out_refs, packed_ref, conv_ref = refs[:outer], *refs[outer:]
    take_pieces(piece_refs, packed_ref, chans)
    half = twist_ref.shape[0] // 2
    rows = twist_ref.shape[1]
    rim = packed_ref[:, 2 * rows :].astype(jnp.float32)
    before = jnp.concatenate([jnp.zeros((chans, 128), jnp.float32), rim[:-chans]])
    rim = rim + pltpu.roll(before, 128 - edge, 1)
    in_rim = lax.broadcasted_iota(jnp.int32, rim.shape, 1) < rim_count
    rim_signal = (rim * pltpu.roll(rim, 128 - rim_step, 1)).astype(jnp.bfloat16)
    rim_query = jnp.where(in_rim, pltpu.roll(rim, 128 - 2 * rim_step, 1), 1.0)
    values = jnp.concatenate(
        [jnp.where(in_rim, rim_signal, packed_ref[:, 0:128]), packed_ref[:, 128 : 2 * rows]], axis=1
    )
    spread = jnp.dot(first_ref[...], values, preferred_element_type=jnp.float32)
    tw_cos, tw_sin = twist_ref[0:half, :], twist_ref[half:, :]
    spectra = []
    for begin in (0, rows):
        real, imag = spread[0:half, begin : begin + rows], spread[half:, begin : begin + rows]
        turned = jnp.concatenate([real * tw_cos + imag * tw_sin, imag * tw_cos - real * tw_sin])
        both = jnp.dot(turned.astype(jnp.bfloat16), inner_ref[...], preferred_element_type=jnp.float32)
        spectra.append(both[0:half, 0:rows] + both[half:, rows:])
        spectra.append(both[half:, 0:rows] - both[0:half, rows:])
    real, imag, fil_re, fil_im = spectra
    product = jnp.concatenate([real * fil_re - imag * fil_im, real * fil_im + imag * fil_re])
    both = jnp.dot(product.astype(jnp.bfloat16), inner_ref[...], preferred_element_type=jnp.float32)
    real = both[0:half, 0:rows] - both[half:, rows:]
    imag = both[half:, 0:rows] + both[0:half, rows:]
    turned = jnp.concatenate([real * tw_cos - imag * tw_sin, imag * tw_cos + real * tw_sin])
    conv = jnp.dot(last_ref[...], turned.astype(jnp.bfloat16), preferred_element_type=jnp.float32)
    conv_ref[:, 0:128] = (conv[:, 0:128] * rim_query).astype(jnp.bfloat16)
    conv_ref[:, 128:] = conv[:, 128:].astype(jnp.bfloat16)
    put_pieces(conv_ref, out_refs)


def output_body(chans, inner, *refs):
    piece_refs, (query_ref, w_ref, out_ref, conv_ref) = refs[:inner], refs[inner:]
    take_pieces(piece_refs, conv_ref, chans)
    conv = conv_ref[...].astype(jnp.float32).T
    mixed_out = (query_ref[...] * conv).astype(jnp.bfloat16)
    out_ref[...] = jnp.dot(mixed_out, w_ref[...], preferred_element_type=jnp.float32).astype(
        jnp.bfloat16
    )


def away(array, axis, distance):
    return lax.ppermute(array, axis, [(i, i ^ distance) for i in range(lax.axis_size(axis))])


def exchange(pieces, axis):
    order = sorted(range(1, len(pieces)), key=lambda d: -d.bit_length())
    moved = {distance: away(pieces[distance], axis, distance) for distance in order}
    return [moved.get(distance, pieces[distance]) for distance in range(len(pieces))]


def local(tokens, norm_gain, w_in, short_filter, long_filter, medium_filter, skip_gain, w_out):
    rows, width = tokens.shape
    devices = lax.axis_size(("outer", "inner"))
    chans = width // devices
    first, twist, inner_table, last = spectral_tables(devices, rows, chans)
    staged = chans % 16 == 0
    outer, inner = (lax.axis_size("outer"), lax.axis_size("inner")) if staged else (1, 1)

    def bf16(*shape):
        return jax.ShapeDtypeStruct(shape, jnp.bfloat16)

    def swap(pieces):
        lanes = pieces[0].shape[1]
        if not staged:
            blocks = pieces[0].reshape(devices, chans, lanes)
            blocks = lax.all_to_all(blocks, ("outer", "inner"), split_axis=0, concat_axis=0)
            return [blocks.reshape(width, lanes)]
        pieces = exchange(pieces, "outer")
        pieces = call(
            functools.partial(regroup_body, chans, outer),
            (bf16(outer * chans, lanes),) * inner,
            pieces,
            [pltpu.VMEM] * outer,
            moved=4 * width * lanes,
        )
        return exchange(pieces, "inner")

    args = (tokens, norm_gain[None, :], w_in, short_filter, long_filter, medium_filter, skip_gain[None, :])
    args = tuple(pltpu.with_memory_space_constraint(arg, pltpu.HBM) for arg in args)
    lanes = 2 * rows + 128
    query, *pieces = call(
        functools.partial(prepare_body, outer),
        (jax.ShapeDtypeStruct((rows, width), jnp.float32),) + (bf16(width // outer, lanes),) * outer,
        args,
        [pltpu.HBM] * len(args),
        [pltpu.VMEM(arg.shape, arg.dtype) for arg in args]
        + [
            pltpu.VMEM((width, lanes), jnp.bfloat16),
            pltpu.VMEM((rows + 2 * edge, 3 * width), jnp.float32),
            pltpu.SemaphoreType.DMA((len(args),)),
        ],
        flops=2 * rows * width * 3 * width,
        moved=1_500_000,
    )
    pieces = call(
        functools.partial(convolve_body, chans, inner, outer, short_filter.shape[0] - 1),
        (bf16(width // outer, rows),) * outer,
        (*swap(pieces), first, twist, inner_table, last),
        [pltpu.VMEM] * (inner + 4),
        [pltpu.VMEM((width, lanes), jnp.bfloat16), pltpu.VMEM((width, rows), jnp.bfloat16)],
        flops=18 * first.shape[0] * width * rows,
        moved=2_000_000,
    )
    return call(
        functools.partial(output_body, chans, inner),
        bf16(rows, width),
        (*swap(pieces), query, w_out),
        [pltpu.VMEM] * (inner + 2),
        [pltpu.VMEM((width, rows), jnp.bfloat16)],
        flops=2 * rows * width * width,
        moved=600_000,
    )


def solution(mesh):
    groups, devices = mesh.devices.shape
    outer = 2 ** (devices.bit_length() // 2)
    split = jax.sharding.Mesh(
        mesh.devices.reshape(groups, outer, devices // outer), ("groups", "outer", "inner")
    )
    rows = P(("groups", "outer", "inner"), None)
    placed = (rows, P(), P(), P(), P(("outer", "inner"), None), P(), P(), P())
    return jax.shard_map(local, mesh=split, in_specs=placed, out_specs=rows, check_vma=False)
```

```python
import functools
import math

import jax
import jax.numpy as jnp
import numpy as np
from jax import lax
from jax.experimental import pallas as pl
from jax.experimental.pallas import tpu as pltpu
from jax.sharding import PartitionSpec as P

epsilon = 1e-06
edge = 8
lane = 128
rim_step = 2 * edge
vmem_bytes = 32 * 2**20


def whole(space):
    return pl.BlockSpec(memory_space=space)


def call(body, outs, args, spaces, scratch=(), flops=0, moved=0):
    return pl.pallas_call(
        body,
        out_shape=outs,
        in_specs=[whole(space) for space in spaces],
        out_specs=jax.tree.map(lambda _: whole(pltpu.VMEM), outs),
        scratch_shapes=list(scratch),
        compiler_params=pltpu.CompilerParams(vmem_limit_bytes=vmem_bytes),
        cost_estimate=pl.CostEstimate(flops=flops, bytes_accessed=moved, transcendentals=0),
    )(*args)


def spectral_tables(devices, rows, chans):
    span = 2 * devices
    full_len = span * rows
    freq_count = devices + 1
    height = -(-freq_count * chans // 16) * 16
    freqs = np.arange(freq_count)
    blocks = np.arange(devices)
    offsets = np.arange(rows)
    eye = np.eye(chans)

    def grown(table):
        out = np.zeros((height, table.shape[1]))
        out[: table.shape[0]] = table
        return out

    angle = 2.0 * math.pi / span * (freqs[:, None] * blocks[None, :] % span)
    first = np.concatenate([grown(np.kron(np.cos(angle), eye)), grown(np.kron(-np.sin(angle), eye))])
    weight = np.where((freqs == 0) | (freqs == devices), 1.0, 2.0)[:, None] / full_len
    last = np.concatenate(
        [grown(np.kron(weight * np.cos(angle), eye)), grown(np.kron(-weight * np.sin(angle), eye))]
    ).T
    twist = 2.0 * math.pi / full_len * (freqs[:, None] * offsets[None, :] % full_len)
    tw_cos = grown(np.repeat(np.cos(twist), chans, axis=0))
    tw_sin = grown(np.repeat(np.sin(twist), chans, axis=0))
    turn = 2.0 * math.pi / rows * (offsets[:, None] * offsets[None, :] % rows)
    inner = np.concatenate([np.cos(turn), np.sin(turn)], axis=1)
    return (
        jnp.asarray(first, jnp.bfloat16),
        jnp.asarray(np.concatenate([tw_cos, tw_sin]), jnp.float32),
        jnp.asarray(inner, jnp.bfloat16),
        jnp.asarray(last, jnp.bfloat16),
    )


def prepare_body(*refs):
    hbm, (packed_ref, query_ref), held, proj_ref, sems = refs[:7], refs[7:9], refs[9:16], *refs[16:]
    copies = [pltpu.make_async_copy(h, v, sems.at[i]) for i, (h, v) in enumerate(zip(hbm, held))]
    for copy in copies:
        copy.start()
    tokens_ref, gain_ref, w_ref, short_ref, long_ref, medium_ref, skip_ref = held
    rows, width = tokens_ref.shape
    proj_ref[0:edge, :] = jnp.zeros((edge, proj_ref.shape[1]), jnp.float32)
    proj_ref[edge + rows :, :] = jnp.zeros((edge, proj_ref.shape[1]), jnp.float32)
    copies[0].wait()
    copies[1].wait()
    inputs = tokens_ref[...].astype(jnp.float32)
    mean_sq = jnp.mean(inputs * inputs, axis=-1, keepdims=True)
    normed = (inputs * lax.rsqrt(mean_sq + epsilon) * gain_ref[...]).astype(jnp.bfloat16)
    copies[2].wait()
    projected = jnp.dot(normed, w_ref[...], preferred_element_type=jnp.float32)
    proj_ref[edge : edge + rows, :] = projected.astype(jnp.bfloat16).astype(jnp.float32)
    copies[3].wait()
    taps_count = short_ref.shape[0]

    def mixed(part):
        cols = slice(part * width, (part + 1) * width)
        acc = short_ref[0:1, cols] * proj_ref[edge : 2 * edge + rows, cols]
        for tap_num in range(1, taps_count):
            begin = edge - tap_num
            acc = acc + short_ref[tap_num : tap_num + 1, cols] * proj_ref[begin : begin + rows + edge, cols]
        return acc

    query, key, value = mixed(0), mixed(1), mixed(2)
    row = lax.broadcasted_iota(jnp.int32, (rows, width), 0)
    query_ref[...] = jnp.where(row < taps_count - 1, 1.0, query[0:rows])
    signal = (key[0:rows] * value[0:rows]).astype(jnp.bfloat16).T
    rims = []
    for part in (key, value, query):
        rims += [part[0:edge], part[rows:]]
    rims.append(jnp.zeros((lane - 3 * rim_step, width), jnp.float32))
    rim = jnp.concatenate(rims).T
    for copy in copies[4:]:
        copy.wait()
    med_len = medium_ref.shape[0]
    is_first = jnp.where(lax.axis_index("seq") == 0, 1.0, 0.0)
    head = long_ref[0:med_len, :] + is_first * medium_ref[...]
    head_row = lax.broadcasted_iota(jnp.int32, head.shape, 0)
    head = head + jnp.where(head_row == 0, is_first * skip_ref[...], 0.0)
    taps = jnp.concatenate([head, long_ref[med_len:, :]]).astype(jnp.bfloat16).T
    put_blocks(packed_ref, signal, taps, rim)


def put_blocks(packed_ref, signal, taps, rim):
    devices = packed_ref.shape[0]
    chans = signal.shape[0] // devices
    if chans % 16:
        packed_ref[...] = jnp.concatenate([signal, taps, rim.astype(jnp.bfloat16)], axis=1)
        return
    begin = 0
    for part in (signal, taps):
        part = part.reshape(devices, chans, -1)
        for column in range(part.shape[2] // lane):
            packed_ref[:, begin : begin + chans, :] = part[:, :, column * lane : (column + 1) * lane]
            begin += chans
    rim = rim.reshape(devices, chans, lane)
    both = rim[:, : chans // 2] + pltpu.roll(rim[:, chans // 2 :], lane // 2, 2)
    packed_ref[:, begin:, :] = both.astype(jnp.bfloat16)


def take_blocks(packed_ref, chans, rows):
    if chans % 16:
        return packed_ref[:, : 2 * rows], packed_ref[:, 2 * rows :].astype(jnp.float32)
    width = packed_ref.shape[0] * chans
    count = 2 * rows // lane
    columns = [
        packed_ref[:, i * chans : (i + 1) * chans, :].reshape(width, lane) for i in range(count)
    ]
    both = packed_ref[:, count * chans :, :].astype(jnp.float32)
    rim = jnp.concatenate([both, pltpu.roll(both, lane // 2, 2)], axis=1).reshape(width, lane)
    return jnp.concatenate(columns, axis=1), rim


def convolve_body(chans, rim_count, packed_ref, first_ref, twist_ref, inner_ref, last_ref, out_ref):
    half = twist_ref.shape[0] // 2
    rows = twist_ref.shape[1]
    values, rim = take_blocks(packed_ref, chans, rows)
    before = jnp.concatenate([jnp.zeros((chans, lane), jnp.float32), rim[:-chans]])
    rim = rim + pltpu.roll(before, lane - edge, 1)
    in_rim = lax.broadcasted_iota(jnp.int32, rim.shape, 1) < rim_count
    rim_signal = (rim * pltpu.roll(rim, lane - rim_step, 1)).astype(jnp.bfloat16)
    rim_query = jnp.where(in_rim, pltpu.roll(rim, lane - 2 * rim_step, 1), 1.0)
    values = jnp.concatenate(
        [jnp.where(in_rim, rim_signal, values[:, 0:lane]), values[:, lane:]], axis=1
    )
    spread = jnp.dot(first_ref[...], values, preferred_element_type=jnp.float32)
    tw_cos, tw_sin = twist_ref[0:half, :], twist_ref[half:, :]
    spectra = []
    for begin in (0, rows):
        real, imag = spread[0:half, begin : begin + rows], spread[half:, begin : begin + rows]
        turned = jnp.concatenate([real * tw_cos + imag * tw_sin, imag * tw_cos - real * tw_sin])
        both = jnp.dot(turned.astype(jnp.bfloat16), inner_ref[...], preferred_element_type=jnp.float32)
        spectra.append(both[0:half, 0:rows] + both[half:, rows:])
        spectra.append(both[half:, 0:rows] - both[0:half, rows:])
    real, imag, fil_re, fil_im = spectra
    product = jnp.concatenate([real * fil_re - imag * fil_im, real * fil_im + imag * fil_re])
    both = jnp.dot(product.astype(jnp.bfloat16), inner_ref[...], preferred_element_type=jnp.float32)
    real = both[0:half, 0:rows] - both[half:, rows:]
    imag = both[half:, 0:rows] + both[0:half, rows:]
    turned = jnp.concatenate([real * tw_cos - imag * tw_sin, imag * tw_cos + real * tw_sin])
    conv = jnp.dot(last_ref[...], turned.astype(jnp.bfloat16), preferred_element_type=jnp.float32)
    out_ref[:, 0:lane] = (conv[:, 0:lane] * rim_query).astype(jnp.bfloat16)
    out_ref[:, lane:] = conv[:, lane:].astype(jnp.bfloat16)


def output_body(conv_ref, query_ref, w_ref, out_ref):
    conv = conv_ref[...].astype(jnp.float32).T
    mixed_out = (query_ref[...] * conv).astype(jnp.bfloat16)
    out_ref[...] = jnp.dot(mixed_out, w_ref[...], preferred_element_type=jnp.float32).astype(
        jnp.bfloat16
    )


def local(tokens, norm_gain, w_in, short_filter, long_filter, medium_filter, skip_gain, w_out):
    rows, width = tokens.shape
    devices = lax.axis_size("seq")
    chans = width // devices
    first, twist, inner, last = spectral_tables(devices, rows, chans)

    if chans % 16:
        packed_shape = (width, 2 * rows + lane)
    else:
        packed_shape = (devices, 2 * rows // lane * chans + chans // 2, lane)

    def swap(array):
        pieces = array.reshape(devices, -1, array.shape[-1])
        return lax.all_to_all(pieces, "seq", split_axis=0, concat_axis=0).reshape(array.shape)

    args = (tokens, norm_gain[None, :], w_in, short_filter, long_filter, medium_filter, skip_gain[None, :])
    args = tuple(pltpu.with_memory_space_constraint(arg, pltpu.HBM) for arg in args)
    packed, query = call(
        prepare_body,
        (
            jax.ShapeDtypeStruct(packed_shape, jnp.bfloat16),
            jax.ShapeDtypeStruct((rows, width), jnp.float32),
        ),
        args,
        [pltpu.HBM] * len(args),
        [pltpu.VMEM(arg.shape, arg.dtype) for arg in args]
        + [
            pltpu.VMEM((rows + 2 * edge, 3 * width), jnp.float32),
            pltpu.SemaphoreType.DMA((len(args),)),
        ],
        flops=2 * rows * width * 3 * width,
        moved=1_500_000,
    )
    conv = call(
        functools.partial(convolve_body, chans, short_filter.shape[0] - 1),
        jax.ShapeDtypeStruct((width, rows), jnp.bfloat16),
        (swap(packed), first, twist, inner, last),
        [pltpu.VMEM] * 5,
        flops=18 * first.shape[0] * width * rows,
        moved=2_000_000,
    )
    return call(
        output_body,
        jax.ShapeDtypeStruct((rows, width), jnp.bfloat16),
        (swap(conv), query, w_out),
        [pltpu.VMEM] * 3,
        flops=2 * rows * width * width,
        moved=600_000,
    )


def solution(mesh):
    placed = (P(("groups", "seq"), None), P(), P(), P(), P("seq", None), P(), P(), P())
    return jax.shard_map(
        local, mesh=mesh, in_specs=placed, out_specs=P(("groups", "seq"), None), check_vma=False
    )
```

```python
import functools
import math

import jax
import jax.numpy as jnp
import numpy as np
from jax import lax
from jax.experimental import pallas as pl
from jax.experimental.pallas import tpu as pltpu
from jax.sharding import PartitionSpec as P

epsilon = 1e-06
edge = 8
lane = 128
rim_step = 2 * edge
vmem_bytes = 32 * 2**20


def whole(space):
    return pl.BlockSpec(memory_space=space)


def call(body, outs, args, spaces, scratch=(), flops=0, moved=0):
    return pl.pallas_call(
        body,
        out_shape=outs,
        in_specs=[whole(space) for space in spaces],
        out_specs=jax.tree.map(lambda _: whole(pltpu.VMEM), outs),
        scratch_shapes=list(scratch),
        compiler_params=pltpu.CompilerParams(vmem_limit_bytes=vmem_bytes),
        cost_estimate=pl.CostEstimate(flops=flops, bytes_accessed=moved, transcendentals=0),
    )(*args)


def spectral_tables(devices, rows, chans):
    full_len = devices * rows
    freqs = 4 * np.arange(devices) + 1
    eye = np.eye(chans)
    angle = 2.0 * math.pi / (4 * devices) * (freqs[:, None] * np.arange(devices)[None, :] % (4 * devices))
    cosine, sine = np.kron(np.cos(angle), eye), np.kron(np.sin(angle), eye)
    first = np.concatenate([cosine, -sine])
    last = np.concatenate([cosine, -sine]).T / full_len
    offsets = np.arange(rows)
    twist = 2.0 * math.pi / (4 * full_len) * (freqs[:, None] * offsets[None, :] % (4 * full_len))
    twist = np.repeat(np.concatenate([np.cos(twist), np.sin(twist)]), chans, axis=0)
    turn = 2.0 * math.pi / rows * (offsets[:, None] * offsets[None, :] % rows)
    cosine, sine = np.cos(turn), np.sin(turn)
    inner = np.block([[cosine, -sine], [sine, cosine]])
    return (
        jnp.asarray(first, jnp.bfloat16),
        jnp.asarray(twist, jnp.float32),
        jnp.asarray(inner, jnp.bfloat16),
        jnp.asarray(last, jnp.bfloat16),
    )


def prepare_body(*refs):
    hbm, (packed_ref, query_ref), held, sems = refs[:7], refs[7:9], refs[9:16], refs[16]
    copies = [pltpu.make_async_copy(h, v, sems.at[i]) for i, (h, v) in enumerate(zip(hbm, held))]
    for copy in copies:
        copy.start()
    tokens_ref, gain_ref, w_ref, short_ref, long_ref, medium_ref, skip_ref = held
    rows, width = tokens_ref.shape
    copies[0].wait()
    copies[1].wait()
    inputs = tokens_ref[...].astype(jnp.float32)
    mean_sq = jnp.mean(inputs * inputs, axis=-1, keepdims=True)
    normed = (inputs * lax.rsqrt(mean_sq + epsilon) * gain_ref[...]).astype(jnp.bfloat16)
    copies[2].wait()
    projected = jnp.dot(normed, w_ref[...], preferred_element_type=jnp.float32)
    projected = projected.astype(jnp.bfloat16).astype(jnp.float32)
    projected = jnp.concatenate([projected, jnp.zeros((edge, 3 * width), jnp.float32)])
    copies[3].wait()
    taps_count = short_ref.shape[0]

    def mixed(part):
        cols = slice(part * width, (part + 1) * width)
        acc = short_ref[0:1, cols] * projected[:, cols]
        for tap_num in range(1, taps_count):
            acc = acc + short_ref[tap_num : tap_num + 1, cols] * pltpu.roll(projected[:, cols], tap_num, 0)
        return acc

    query, key, value = mixed(0), mixed(1), mixed(2)
    row = lax.broadcasted_iota(jnp.int32, (rows, width), 0)
    query_ref[...] = jnp.where(row < taps_count - 1, 1.0, query[0:rows])
    signal = (key[0:rows] * value[0:rows]).astype(jnp.bfloat16).T
    rims = []
    for part in (key, value, query):
        rims += [part[0:edge], part[rows:]]
    rims.append(jnp.zeros((lane - 3 * rim_step, width), jnp.float32))
    rim = jnp.concatenate(rims).T
    for copy in copies[4:]:
        copy.wait()
    med_len = medium_ref.shape[0]
    is_first = jnp.where(lax.axis_index("seq") == 0, 1.0, 0.0)
    head = long_ref[0:med_len, :] + is_first * medium_ref[...]
    head_row = lax.broadcasted_iota(jnp.int32, head.shape, 0)
    head = head + jnp.where(head_row == 0, is_first * skip_ref[...], 0.0)
    taps = jnp.concatenate([head, long_ref[med_len:, :]]).astype(jnp.bfloat16).T
    put_blocks(packed_ref, signal, taps, rim)


def put_blocks(packed_ref, signal, taps, rim):
    devices = packed_ref.shape[0]
    chans = signal.shape[0] // devices
    if chans % 16:
        packed_ref[...] = jnp.concatenate([signal, taps, rim.astype(jnp.bfloat16)], axis=1)
        return
    begin = 0
    for part in (signal, taps):
        part = part.reshape(devices, chans, -1)
        for column in range(part.shape[2] // lane):
            packed_ref[:, begin : begin + chans, :] = part[:, :, column * lane : (column + 1) * lane]
            begin += chans
    rim = rim.reshape(devices, chans, lane)
    both = rim[:, : chans // 2] + pltpu.roll(rim[:, chans // 2 :], lane // 2, 2)
    packed_ref[:, begin:, :] = both.astype(jnp.bfloat16)


def take_blocks(packed_ref, chans, rows):
    if chans % 16:
        return packed_ref[:, : 2 * rows], packed_ref[:, 2 * rows :].astype(jnp.float32)
    width = packed_ref.shape[0] * chans
    count = 2 * rows // lane
    columns = [
        packed_ref[:, i * chans : (i + 1) * chans, :].reshape(width, lane) for i in range(count)
    ]
    both = packed_ref[:, count * chans :, :].astype(jnp.float32)
    rim = jnp.concatenate([both, pltpu.roll(both, lane // 2, 2)], axis=1).reshape(width, lane)
    return jnp.concatenate(columns, axis=1), rim


def convolve_body(chans, rim_count, packed_ref, first_ref, twist_ref, inner_ref, last_ref, out_ref):
    half = twist_ref.shape[0] // 2
    rows = twist_ref.shape[1]
    values, rim = take_blocks(packed_ref, chans, rows)
    before = jnp.concatenate([jnp.zeros((chans, lane), jnp.float32), rim[:-chans]])
    rim = rim + pltpu.roll(before, lane - edge, 1)
    in_rim = lax.broadcasted_iota(jnp.int32, rim.shape, 1) < rim_count
    rim_signal = (rim * pltpu.roll(rim, lane - rim_step, 1)).astype(jnp.bfloat16)
    rim_query = jnp.where(in_rim, pltpu.roll(rim, lane - 2 * rim_step, 1), 1.0)
    values = jnp.concatenate(
        [jnp.where(in_rim, rim_signal, values[:, 0:lane]), values[:, lane:]], axis=1
    )
    spread = jnp.dot(first_ref[...], values, preferred_element_type=jnp.float32)
    tw_cos, tw_sin = twist_ref[0:half, :], twist_ref[half:, :]
    turned = []
    for begin in (0, rows):
        real, imag = spread[0:half, begin : begin + rows], spread[half:, begin : begin + rows]
        turned.append([real * tw_cos + imag * tw_sin, imag * tw_cos - real * tw_sin])
    turned = jnp.concatenate([jnp.concatenate(pair, axis=1).astype(jnp.bfloat16) for pair in turned])
    spectra = jnp.dot(turned, inner_ref[...], preferred_element_type=jnp.float32)
    real, imag = spectra[0:half, 0:rows], spectra[0:half, rows:]
    fil_re, fil_im = spectra[half:, 0:rows], spectra[half:, rows:]
    product = [real * fil_im + imag * fil_re, real * fil_re - imag * fil_im]
    product = jnp.concatenate(product, axis=1).astype(jnp.bfloat16)
    back = jnp.dot(product, inner_ref[...], preferred_element_type=jnp.float32)
    imag, real = back[:, 0:rows], back[:, rows:]
    turned = jnp.concatenate([real * tw_cos - imag * tw_sin, imag * tw_cos + real * tw_sin])
    conv = jnp.dot(last_ref[...], turned.astype(jnp.bfloat16), preferred_element_type=jnp.float32)
    out_ref[:, 0:lane] = (conv[:, 0:lane] * rim_query).astype(jnp.bfloat16)
    out_ref[:, lane:] = conv[:, lane:].astype(jnp.bfloat16)


def output_body(conv_ref, query_ref, w_ref, out_ref):
    conv = conv_ref[...].T.astype(jnp.float32)
    mixed_out = (query_ref[...] * conv).astype(jnp.bfloat16)
    out_ref[...] = jnp.dot(mixed_out, w_ref[...], preferred_element_type=jnp.float32).astype(
        jnp.bfloat16
    )


def local(tokens, norm_gain, w_in, short_filter, long_filter, medium_filter, skip_gain, w_out):
    rows, width = tokens.shape
    devices = lax.axis_size("seq")
    chans = width // devices
    first, twist, inner, last = spectral_tables(devices, rows, chans)

    if chans % 16:
        packed_shape = (width, 2 * rows + lane)
    else:
        packed_shape = (devices, 2 * rows // lane * chans + chans // 2, lane)

    def swap(array):
        pieces = array.reshape(devices, -1, array.shape[-1])
        return lax.all_to_all(pieces, "seq", split_axis=0, concat_axis=0).reshape(array.shape)

    args = (tokens, norm_gain[None, :], w_in, short_filter, long_filter, medium_filter, skip_gain[None, :])
    args = tuple(pltpu.with_memory_space_constraint(arg, pltpu.HBM) for arg in args)
    packed, query = call(
        prepare_body,
        (
            jax.ShapeDtypeStruct(packed_shape, jnp.bfloat16),
            jax.ShapeDtypeStruct((rows, width), jnp.float32),
        ),
        args,
        [pltpu.HBM] * len(args),
        [pltpu.VMEM(arg.shape, arg.dtype) for arg in args]
        + [pltpu.SemaphoreType.DMA((len(args),))],
        flops=2 * rows * width * 3 * width,
        moved=1_500_000,
    )
    conv = call(
        functools.partial(convolve_body, chans, short_filter.shape[0] - 1),
        jax.ShapeDtypeStruct((width, rows), jnp.bfloat16),
        (swap(packed), first, twist, inner, last),
        [pltpu.VMEM] * 5,
        flops=18 * first.shape[0] * width * rows,
        moved=2_000_000,
    )
    return call(
        output_body,
        jax.ShapeDtypeStruct((rows, width), jnp.bfloat16),
        (swap(conv), query, w_out),
        [pltpu.VMEM] * 3,
        flops=2 * rows * width * width,
        moved=600_000,
    )


def solution(mesh):
    placed = (P(("groups", "seq"), None), P(), P(), P(), P("seq", None), P(), P(), P())
    return jax.shard_map(
        local, mesh=mesh, in_specs=placed, out_specs=P(("groups", "seq"), None), check_vma=False
    )
```

```python
import functools
import math

import jax
import jax.numpy as jnp
import numpy as np
from jax import lax
from jax.experimental import pallas as pl
from jax.experimental.pallas import tpu as pltpu
from jax.sharding import PartitionSpec as P

epsilon = 1e-06
edge = 8
lane = 128
rim_step = 2 * edge
vmem_bytes = 32 * 2**20


def whole(space):
    return pl.BlockSpec(memory_space=space)


def call(body, outs, args, spaces, scratch=(), flops=0, moved=0):
    return pl.pallas_call(
        body,
        out_shape=outs,
        in_specs=[whole(space) for space in spaces],
        out_specs=jax.tree.map(lambda _: whole(pltpu.VMEM), outs),
        scratch_shapes=list(scratch),
        compiler_params=pltpu.CompilerParams(vmem_limit_bytes=vmem_bytes),
        cost_estimate=pl.CostEstimate(flops=flops, bytes_accessed=moved, transcendentals=0),
    )(*args)


def spectral_tables(devices, rows, chans):
    full_len = devices * rows
    freqs = 4 * np.arange(devices) + 1
    eye = np.eye(chans)
    angle = 2.0 * math.pi / (4 * devices) * (freqs[:, None] * np.arange(devices)[None, :] % (4 * devices))
    cosine, sine = np.kron(np.cos(angle), eye), np.kron(np.sin(angle), eye)
    first = np.concatenate([cosine, -sine])
    last = np.concatenate([cosine, -sine]).T / full_len
    offsets = np.arange(rows)
    twist = 2.0 * math.pi / (4 * full_len) * (freqs[:, None] * offsets[None, :] % (4 * full_len))
    twist = np.concatenate([np.cos(twist), np.sin(twist)])
    if chans % 8:
        twist = np.repeat(twist, chans, axis=0)
    turn = 2.0 * math.pi / rows * (offsets[:, None] * offsets[None, :] % rows)
    cosine, sine = np.cos(turn), np.sin(turn)
    inner = np.block([[cosine, -sine], [sine, cosine]])
    return (
        jnp.asarray(first, jnp.bfloat16),
        jnp.asarray(twist, jnp.float32),
        jnp.asarray(inner, jnp.bfloat16),
        jnp.asarray(last, jnp.bfloat16),
    )


def prepare_body(*refs):
    hbm, (packed_ref, query_ref), held, sems = refs[:7], refs[7:9], refs[9:16], refs[16]
    tokens_ref, gain_ref, w_ref, short_ref, long_ref, medium_ref, skip_ref = held
    rows, width = tokens_ref.shape
    is_first = lax.axis_index("seq") == 0
    parts = [slice(part * width, (part + 1) * width) for part in range(3)]

    def copy_of(index, cols=None, sem=None):
        source, target = hbm[index], held[index]
        if cols is not None:
            source, target = source.at[:, cols], target.at[:, cols]
        return pltpu.make_async_copy(source, target, sems.at[index if sem is None else sem])

    tokens_copy, gain_copy, short_copy, long_copy = (copy_of(index) for index in (0, 1, 3, 4))
    medium_copy, skip_copy = copy_of(5), copy_of(6)
    w_copies = [copy_of(2, cols, 6 + part if part else 2) for part, cols in enumerate(parts)]
    for copy in (tokens_copy, gain_copy, w_copies[1], w_copies[2], short_copy, long_copy, w_copies[0]):
        copy.start()

    @pl.when(is_first)
    def _():
        medium_copy.start()
        skip_copy.start()

    tokens_copy.wait()
    gain_copy.wait()
    inputs = tokens_ref[...].astype(jnp.float32)
    mean_sq = jnp.mean(inputs * inputs, axis=-1, keepdims=True)
    normed = (inputs * lax.rsqrt(mean_sq + epsilon) * gain_ref[...]).astype(jnp.bfloat16)
    taps_count = short_ref.shape[0]

    def mixed(part):
        w_copies[part].wait()
        cols = parts[part]
        projected = jnp.dot(normed, w_ref[:, cols], preferred_element_type=jnp.float32)
        projected = projected.astype(jnp.bfloat16).astype(jnp.float32)
        projected = jnp.concatenate([projected, jnp.zeros((edge, width), jnp.float32)])
        acc = short_ref[0:1, cols] * projected
        for tap_num in range(1, taps_count):
            acc = acc + short_ref[tap_num : tap_num + 1, cols] * pltpu.roll(projected, tap_num, 0)
        return acc

    short_copy.wait()
    key, value = mixed(1), mixed(2)
    put_columns(packed_ref, 0, (key[0:rows] * value[0:rows]).astype(jnp.bfloat16).T)
    long_copy.wait()

    @pl.when(is_first)
    def _():
        medium_copy.wait()
        skip_copy.wait()
        med_len = medium_ref.shape[0]
        head_row = lax.broadcasted_iota(jnp.int32, medium_ref.shape, 0)
        direct = jnp.where(head_row == 0, skip_ref[...], 0.0)
        long_ref[0:med_len, :] = long_ref[0:med_len, :] + medium_ref[...] + direct

    put_columns(packed_ref, rows, long_ref[...].astype(jnp.bfloat16).T)
    query = mixed(0)
    row = lax.broadcasted_iota(jnp.int32, (rows, width), 0)
    query_ref[...] = jnp.where(row < taps_count - 1, 1.0, query[0:rows])
    rims = []
    for part in (key, value, query):
        rims += [part[0:edge], part[rows:]]
    rims.append(jnp.zeros((lane - 3 * rim_step, width), jnp.float32))
    put_rim(packed_ref, 2 * rows, jnp.concatenate(rims).T)


def put_columns(packed_ref, begin, values):
    if len(packed_ref.shape) == 2:
        packed_ref[:, begin : begin + values.shape[1]] = values
        return
    devices = packed_ref.shape[0]
    values = values.reshape(devices, -1, values.shape[1])
    chans = values.shape[1]
    for column in range(values.shape[2] // lane):
        place = (begin // lane + column) * chans
        packed_ref[:, place : place + chans, :] = values[:, :, column * lane : (column + 1) * lane]


def put_rim(packed_ref, begin, rim):
    if len(packed_ref.shape) == 2:
        packed_ref[:, begin:] = rim.astype(jnp.bfloat16)
        return
    rim = rim.reshape(packed_ref.shape[0], -1, lane)
    chans = rim.shape[1]
    both = rim[:, : chans // 2] + pltpu.roll(rim[:, chans // 2 :], lane // 2, 2)
    packed_ref[:, begin // lane * chans :, :] = both.astype(jnp.bfloat16)


def take_blocks(packed_ref, chans, rows):
    if chans % 16:
        return packed_ref[:, : 2 * rows], packed_ref[:, 2 * rows :].astype(jnp.float32)
    width = packed_ref.shape[0] * chans
    count = 2 * rows // lane
    columns = [
        packed_ref[:, i * chans : (i + 1) * chans, :].reshape(width, lane) for i in range(count)
    ]
    both = packed_ref[:, count * chans :, :].astype(jnp.float32)
    rim = jnp.concatenate([both, pltpu.roll(both, lane // 2, 2)], axis=1).reshape(width, lane)
    return jnp.concatenate(columns, axis=1), rim


def twist_rows(twist_ref, chans):
    half, rows = twist_ref.shape[0] // 2, twist_ref.shape[1]
    tables = twist_ref[0:half, :], twist_ref[half:, :]
    if chans % 8:
        return tables
    return tuple(
        jnp.broadcast_to(table[:, None, :], (half, chans, rows)).reshape(half * chans, rows)
        for table in tables
    )


def convolve_body(chans, rim_count, packed_ref, first_ref, twist_ref, inner_ref, last_ref, out_ref):
    rows = twist_ref.shape[1]
    half = first_ref.shape[0] // 2
    values, rim = take_blocks(packed_ref, chans, rows)
    before = jnp.concatenate([jnp.zeros((chans, lane), jnp.float32), rim[:-chans]])
    rim = rim + pltpu.roll(before, lane - edge, 1)
    in_rim = lax.broadcasted_iota(jnp.int32, rim.shape, 1) < rim_count
    rim_signal = (rim * pltpu.roll(rim, lane - rim_step, 1)).astype(jnp.bfloat16)
    rim_query = jnp.where(in_rim, pltpu.roll(rim, lane - 2 * rim_step, 1), 1.0)
    values = jnp.concatenate(
        [jnp.where(in_rim, rim_signal, values[:, 0:lane]), values[:, lane:]], axis=1
    )
    spread = jnp.dot(first_ref[...], values, preferred_element_type=jnp.float32)
    tw_cos, tw_sin = twist_rows(twist_ref, chans)
    turned = []
    for begin in (0, rows):
        real, imag = spread[0:half, begin : begin + rows], spread[half:, begin : begin + rows]
        turned.append([real * tw_cos + imag * tw_sin, imag * tw_cos - real * tw_sin])
    turned = jnp.concatenate([jnp.concatenate(pair, axis=1).astype(jnp.bfloat16) for pair in turned])
    spectra = jnp.dot(turned, inner_ref[...], preferred_element_type=jnp.float32)
    real, imag = spectra[0:half, 0:rows], spectra[0:half, rows:]
    fil_re, fil_im = spectra[half:, 0:rows], spectra[half:, rows:]
    product = [real * fil_im + imag * fil_re, real * fil_re - imag * fil_im]
    product = jnp.concatenate(product, axis=1).astype(jnp.bfloat16)
    back = jnp.dot(product, inner_ref[...], preferred_element_type=jnp.float32)
    imag, real = back[:, 0:rows], back[:, rows:]
    turned = jnp.concatenate([real * tw_cos - imag * tw_sin, imag * tw_cos + real * tw_sin])
    conv = jnp.dot(last_ref[...], turned.astype(jnp.bfloat16), preferred_element_type=jnp.float32)
    out_ref[:, 0:lane] = (conv[:, 0:lane] * rim_query).astype(jnp.bfloat16)
    out_ref[:, lane:] = conv[:, lane:].astype(jnp.bfloat16)


def output_body(conv_ref, query_ref, w_ref, out_ref):
    conv = conv_ref[...].T.astype(jnp.float32)
    mixed_out = (query_ref[...] * conv).astype(jnp.bfloat16)
    out_ref[...] = jnp.dot(mixed_out, w_ref[...], preferred_element_type=jnp.float32).astype(
        jnp.bfloat16
    )


def local(tokens, norm_gain, w_in, short_filter, long_filter, medium_filter, skip_gain, w_out):
    rows, width = tokens.shape
    devices = lax.axis_size("seq")
    chans = width // devices
    first, twist, inner, last = spectral_tables(devices, rows, chans)

    if chans % 16:
        packed_shape = (width, 2 * rows + lane)
    else:
        packed_shape = (devices, 2 * rows // lane * chans + chans // 2, lane)

    def swap(array):
        pieces = array.reshape(devices, -1, array.shape[-1])
        return lax.all_to_all(pieces, "seq", split_axis=0, concat_axis=0).reshape(array.shape)

    args = (tokens, norm_gain[None, :], w_in, short_filter, long_filter, medium_filter, skip_gain[None, :])
    args = tuple(pltpu.with_memory_space_constraint(arg, pltpu.HBM) for arg in args)
    packed, query = call(
        prepare_body,
        (
            jax.ShapeDtypeStruct(packed_shape, jnp.bfloat16),
            jax.ShapeDtypeStruct((rows, width), jnp.float32),
        ),
        args,
        [pltpu.HBM] * len(args),
        [pltpu.VMEM(arg.shape, arg.dtype) for arg in args]
        + [pltpu.SemaphoreType.DMA((len(args) + 2,))],
        flops=2 * rows * width * 3 * width,
        moved=1_500_000,
    )
    conv = call(
        functools.partial(convolve_body, chans, short_filter.shape[0] - 1),
        jax.ShapeDtypeStruct((width, rows), jnp.bfloat16),
        (swap(packed), first, twist, inner, last),
        [pltpu.VMEM] * 5,
        flops=18 * first.shape[0] * width * rows,
        moved=2_000_000,
    )
    return call(
        output_body,
        jax.ShapeDtypeStruct((rows, width), jnp.bfloat16),
        (swap(conv), query, w_out),
        [pltpu.VMEM] * 3,
        flops=2 * rows * width * width,
        moved=600_000,
    )


def solution(mesh):
    placed = (P(("groups", "seq"), None), P(), P(), P(), P("seq", None), P(), P(), P())
    return jax.shard_map(
        local, mesh=mesh, in_specs=placed, out_specs=P(("groups", "seq"), None), check_vma=False
    )
```

```python
import functools
import math

import jax
import jax.numpy as jnp
import numpy as np
from jax import lax
from jax.experimental import pallas as pl
from jax.experimental.pallas import tpu as pltpu
from jax.sharding import PartitionSpec as P

epsilon = 1e-06
edge = 8
lane = 128
rim_step = 2 * edge
vmem_bytes = 32 * 2**20


def whole(space):
    return pl.BlockSpec(memory_space=space)


def call(body, outs, args, spaces, scratch=(), flops=0, moved=0):
    return pl.pallas_call(
        body,
        out_shape=outs,
        in_specs=[whole(space) for space in spaces],
        out_specs=jax.tree.map(lambda _: whole(pltpu.VMEM), outs),
        scratch_shapes=list(scratch),
        compiler_params=pltpu.CompilerParams(vmem_limit_bytes=vmem_bytes),
        cost_estimate=pl.CostEstimate(flops=flops, bytes_accessed=moved, transcendentals=0),
    )(*args)


def spectral_tables(devices, rows, chans):
    full_len = devices * rows
    freqs = 4 * np.arange(devices) + 1
    eye = np.eye(chans)
    angle = 2.0 * math.pi / (4 * devices) * (freqs[:, None] * np.arange(devices)[None, :] % (4 * devices))
    cosine, sine = np.kron(np.cos(angle), eye), np.kron(np.sin(angle), eye)
    first = np.concatenate([cosine, -sine])
    last = np.concatenate([cosine, -sine]).T / full_len
    offsets = np.arange(rows)
    twist = 2.0 * math.pi / (4 * full_len) * (freqs[:, None] * offsets[None, :] % (4 * full_len))
    twist = np.concatenate([np.cos(twist), np.sin(twist)])
    if chans % 8:
        twist = np.repeat(twist, chans, axis=0)
    turn = 2.0 * math.pi / rows * (offsets[:, None] * offsets[None, :] % rows)
    cosine, sine = np.cos(turn), np.sin(turn)
    inner = np.block([[cosine, -sine], [sine, cosine]])
    return (
        jnp.asarray(first, jnp.bfloat16),
        jnp.asarray(twist, jnp.float32),
        jnp.asarray(inner, jnp.bfloat16),
        jnp.asarray(last, jnp.bfloat16),
    )


def prepare_body(*refs):
    hbm, (packed_ref, query_ref), held, sems = refs[:7], refs[7:9], refs[9:16], refs[16]
    tokens_ref, gain_ref, w_ref, short_ref, long_ref, medium_ref, skip_ref = held
    rows, width = tokens_ref.shape
    copies = [pltpu.make_async_copy(h, v, sems.at[i]) for i, (h, v) in enumerate(zip(hbm, held))]
    for index in (4, 5, 6, 0, 1, 2, 3):
        copies[index].start()
    for copy in copies[4:]:
        copy.wait()
    med_len = medium_ref.shape[0]
    is_first = jnp.where(lax.axis_index("seq") == 0, 1.0, 0.0)
    head = long_ref[0:med_len, :] + is_first * medium_ref[...]
    head_row = lax.broadcasted_iota(jnp.int32, head.shape, 0)
    head = head + jnp.where(head_row == 0, is_first * skip_ref[...], 0.0)
    taps = jnp.concatenate([head, long_ref[med_len:, :]]).astype(jnp.bfloat16)
    put_columns(packed_ref, rows, taps.T)
    copies[0].wait()
    copies[1].wait()
    inputs = tokens_ref[...].astype(jnp.float32)
    mean_sq = jnp.mean(inputs * inputs, axis=-1, keepdims=True)
    normed = (inputs * lax.rsqrt(mean_sq + epsilon) * gain_ref[...]).astype(jnp.bfloat16)
    copies[2].wait()
    copies[3].wait()
    projected = jnp.dot(normed, w_ref[...], preferred_element_type=jnp.float32)
    projected = projected.astype(jnp.bfloat16).astype(jnp.float32)
    projected = jnp.concatenate([projected, jnp.zeros((edge, 3 * width), jnp.float32)])
    taps_count = short_ref.shape[0]

    def mixed(part):
        cols = slice(part * width, (part + 1) * width)
        acc = short_ref[0:1, cols] * projected[:, cols]
        for tap_num in range(1, taps_count):
            acc = acc + short_ref[tap_num : tap_num + 1, cols] * pltpu.roll(projected[:, cols], tap_num, 0)
        return acc

    query, key, value = mixed(0), mixed(1), mixed(2)
    row = lax.broadcasted_iota(jnp.int32, (rows, width), 0)
    query_ref[...] = jnp.where(row < taps_count - 1, 1.0, query[0:rows])
    put_columns(packed_ref, 0, (key[0:rows] * value[0:rows]).astype(jnp.bfloat16).T)
    rims = []
    for part in (key, value, query):
        rims += [part[0:edge], part[rows:]]
    rims.append(jnp.zeros((lane - 3 * rim_step, width), jnp.float32))
    put_rim(packed_ref, 2 * rows, jnp.concatenate(rims).T)


def put_columns(packed_ref, begin, values):
    if len(packed_ref.shape) == 2:
        packed_ref[:, begin : begin + values.shape[1]] = values
        return
    devices = packed_ref.shape[0]
    values = values.reshape(devices, -1, values.shape[1])
    chans = values.shape[1]
    for column in range(values.shape[2] // lane):
        place = (begin // lane + column) * chans
        packed_ref[:, place : place + chans, :] = values[:, :, column * lane : (column + 1) * lane]


def put_rim(packed_ref, begin, rim):
    if len(packed_ref.shape) == 2:
        packed_ref[:, begin:] = rim.astype(jnp.bfloat16)
        return
    rim = rim.reshape(packed_ref.shape[0], -1, lane)
    chans = rim.shape[1]
    both = rim[:, : chans // 2] + pltpu.roll(rim[:, chans // 2 :], lane // 2, 2)
    packed_ref[:, begin // lane * chans :, :] = both.astype(jnp.bfloat16)


def take_blocks(packed_ref, chans, rows):
    if chans % 16:
        return packed_ref[:, : 2 * rows], packed_ref[:, 2 * rows :].astype(jnp.float32)
    width = packed_ref.shape[0] * chans
    count = 2 * rows // lane
    columns = [
        packed_ref[:, i * chans : (i + 1) * chans, :].reshape(width, lane) for i in range(count)
    ]
    both = packed_ref[:, count * chans :, :].astype(jnp.float32)
    rim = jnp.concatenate([both, pltpu.roll(both, lane // 2, 2)], axis=1).reshape(width, lane)
    return jnp.concatenate(columns, axis=1), rim


def twist_rows(twist_ref, chans):
    half, rows = twist_ref.shape[0] // 2, twist_ref.shape[1]
    tables = twist_ref[0:half, :], twist_ref[half:, :]
    if chans % 8:
        return tables
    return tuple(
        jnp.broadcast_to(table[:, None, :], (half, chans, rows)).reshape(half * chans, rows)
        for table in tables
    )


def convolve_body(chans, rim_count, packed_ref, first_ref, twist_ref, inner_ref, last_ref, out_ref):
    rows = twist_ref.shape[1]
    half = first_ref.shape[0] // 2
    values, rim = take_blocks(packed_ref, chans, rows)
    before = jnp.concatenate([jnp.zeros((chans, lane), jnp.float32), rim[:-chans]])
    rim = rim + pltpu.roll(before, lane - edge, 1)
    in_rim = lax.broadcasted_iota(jnp.int32, rim.shape, 1) < rim_count
    rim_signal = (rim * pltpu.roll(rim, lane - rim_step, 1)).astype(jnp.bfloat16)
    rim_query = jnp.where(in_rim, pltpu.roll(rim, lane - 2 * rim_step, 1), 1.0)
    values = jnp.concatenate(
        [jnp.where(in_rim, rim_signal, values[:, 0:lane]), values[:, lane:]], axis=1
    )
    tw_cos, tw_sin = twist_rows(twist_ref, chans)
    span = half // 2
    conv = 0.0
    for begin in range(0, half, span):
        own, other = slice(begin, begin + span), slice(half + begin, half + begin + span)
        table = jnp.concatenate([first_ref[own, :], first_ref[other, :]])
        spread = jnp.dot(table, values, preferred_element_type=jnp.float32)
        cosine, sine = tw_cos[own], tw_sin[own]
        turned = []
        for cols in (slice(0, rows), slice(rows, 2 * rows)):
            real, imag = spread[0:span, cols], spread[span:, cols]
            pair = [real * cosine + imag * sine, imag * cosine - real * sine]
            turned.append(jnp.concatenate(pair, axis=1).astype(jnp.bfloat16))
        spectra = jnp.dot(
            jnp.concatenate(turned), inner_ref[...], preferred_element_type=jnp.float32
        )
        real, imag = spectra[0:span, 0:rows], spectra[0:span, rows:]
        fil_re, fil_im = spectra[span:, 0:rows], spectra[span:, rows:]
        product = [real * fil_im + imag * fil_re, real * fil_re - imag * fil_im]
        product = jnp.concatenate(product, axis=1).astype(jnp.bfloat16)
        back = jnp.dot(product, inner_ref[...], preferred_element_type=jnp.float32)
        imag, real = back[:, 0:rows], back[:, rows:]
        turned = jnp.concatenate([real * cosine - imag * sine, imag * cosine + real * sine])
        table = jnp.concatenate([last_ref[:, own], last_ref[:, other]], axis=1)
        conv = conv + jnp.dot(table, turned.astype(jnp.bfloat16), preferred_element_type=jnp.float32)
    out_ref[:, 0:lane] = (conv[:, 0:lane] * rim_query).astype(jnp.bfloat16)
    out_ref[:, lane:] = conv[:, lane:].astype(jnp.bfloat16)


def output_body(conv_ref, query_ref, w_ref, out_ref):
    conv = conv_ref[...].T.astype(jnp.float32)
    mixed_out = (query_ref[...] * conv).astype(jnp.bfloat16)
    out_ref[...] = jnp.dot(mixed_out, w_ref[...], preferred_element_type=jnp.float32).astype(
        jnp.bfloat16
    )


def local(tokens, norm_gain, w_in, short_filter, long_filter, medium_filter, skip_gain, w_out):
    rows, width = tokens.shape
    devices = lax.axis_size("seq")
    chans = width // devices
    first, twist, inner, last = spectral_tables(devices, rows, chans)

    if chans % 16:
        packed_shape = (width, 2 * rows + lane)
    else:
        packed_shape = (devices, 2 * rows // lane * chans + chans // 2, lane)

    def swap(array):
        pieces = array.reshape(devices, -1, array.shape[-1])
        return lax.all_to_all(pieces, "seq", split_axis=0, concat_axis=0).reshape(array.shape)

    args = (tokens, norm_gain[None, :], w_in, short_filter, long_filter, medium_filter, skip_gain[None, :])
    args = tuple(pltpu.with_memory_space_constraint(arg, pltpu.HBM) for arg in args)
    packed, query = call(
        prepare_body,
        (
            jax.ShapeDtypeStruct(packed_shape, jnp.bfloat16),
            jax.ShapeDtypeStruct((rows, width), jnp.float32),
        ),
        args,
        [pltpu.HBM] * len(args),
        [pltpu.VMEM(arg.shape, arg.dtype) for arg in args]
        + [pltpu.SemaphoreType.DMA((len(args),))],
        flops=2 * rows * width * 3 * width,
        moved=1_500_000,
    )
    conv = call(
        functools.partial(convolve_body, chans, short_filter.shape[0] - 1),
        jax.ShapeDtypeStruct((width, rows), jnp.bfloat16),
        (swap(packed), first, twist, inner, last),
        [pltpu.VMEM] * 5,
        flops=18 * first.shape[0] * width * rows,
        moved=2_000_000,
    )
    return call(
        output_body,
        jax.ShapeDtypeStruct((rows, width), jnp.bfloat16),
        (swap(conv), query, w_out),
        [pltpu.VMEM] * 3,
        flops=2 * rows * width * width,
        moved=600_000,
    )


def solution(mesh):
    placed = (P(("groups", "seq"), None), P(), P(), P(), P("seq", None), P(), P(), P())
    return jax.shard_map(
        local, mesh=mesh, in_specs=placed, out_specs=P(("groups", "seq"), None), check_vma=False
    )
```

```python
import functools
import math

import jax
import jax.numpy as jnp
import numpy as np
from jax import lax
from jax.experimental import pallas as pl
from jax.experimental.pallas import tpu as pltpu
from jax.sharding import PartitionSpec as P

epsilon = 1e-06
edge = 8
lane = 128
rim_step = 2 * edge
vmem_bytes = 32 * 2**20


def whole(space):
    return pl.BlockSpec(memory_space=space)


def call(body, outs, args, spaces, scratch=(), flops=0, moved=0):
    return pl.pallas_call(
        body,
        out_shape=outs,
        in_specs=[whole(space) for space in spaces],
        out_specs=jax.tree.map(lambda _: whole(pltpu.VMEM), outs),
        scratch_shapes=list(scratch),
        compiler_params=pltpu.CompilerParams(vmem_limit_bytes=vmem_bytes),
        cost_estimate=pl.CostEstimate(flops=flops, bytes_accessed=moved, transcendentals=0),
    )(*args)


def spectral_tables(devices, rows, chans):
    full_len = devices * rows
    freqs = 4 * np.arange(devices) + 1
    eye = np.eye(chans)
    angle = 2.0 * math.pi / (4 * devices) * (freqs[:, None] * np.arange(devices)[None, :] % (4 * devices))
    cosine, sine = np.kron(np.cos(angle), eye), np.kron(np.sin(angle), eye)
    first = np.concatenate([cosine, -sine])
    last = np.concatenate([cosine, -sine]).T / full_len
    offsets = np.arange(rows)
    twist = 2.0 * math.pi / (4 * full_len) * (freqs[:, None] * offsets[None, :] % (4 * full_len))
    twist = np.concatenate([np.cos(twist), np.sin(twist)])
    if chans % 8:
        twist = np.repeat(twist, chans, axis=0)
    turn = 2.0 * math.pi / rows * (offsets[:, None] * offsets[None, :] % rows)
    cosine, sine = np.cos(turn), np.sin(turn)
    inner = np.block([[cosine, -sine], [sine, cosine]])
    return (
        jnp.asarray(first, jnp.bfloat16),
        jnp.asarray(twist, jnp.float32),
        jnp.asarray(inner, jnp.bfloat16),
        jnp.asarray(last, jnp.bfloat16),
    )


def prepare_body(*refs):
    hbm, (packed_ref, query_ref), held, sems = refs[:7], refs[7:9], refs[9:16], refs[16]
    tokens_ref, gain_ref, w_ref, short_ref, long_ref, medium_ref, skip_ref = held
    rows, width = tokens_ref.shape
    copies = [pltpu.make_async_copy(h, v, sems.at[i]) for i, (h, v) in enumerate(zip(hbm, held))]
    for copy in copies:
        copy.start()
    copies[0].wait()
    copies[1].wait()
    inputs = tokens_ref[...].astype(jnp.float32)
    mean_sq = jnp.mean(inputs * inputs, axis=-1, keepdims=True)
    normed = (inputs * lax.rsqrt(mean_sq + epsilon) * gain_ref[...]).astype(jnp.bfloat16)
    copies[2].wait()
    copies[3].wait()
    projected = jnp.dot(normed, w_ref[...], preferred_element_type=jnp.float32)
    projected = projected.astype(jnp.bfloat16).astype(jnp.float32)
    projected = jnp.concatenate([projected, jnp.zeros((edge, 3 * width), jnp.float32)])
    taps_count = short_ref.shape[0]

    def mixed(part):
        cols = slice(part * width, (part + 1) * width)
        acc = short_ref[0:1, cols] * projected[:, cols]
        for tap_num in range(1, taps_count):
            acc = acc + short_ref[tap_num : tap_num + 1, cols] * pltpu.roll(projected[:, cols], tap_num, 0)
        return acc

    query, key, value = mixed(0), mixed(1), mixed(2)
    row = lax.broadcasted_iota(jnp.int32, (rows, width), 0)
    query_ref[...] = jnp.where(row < taps_count - 1, 1.0, query[0:rows])
    put_columns(packed_ref, 0, (key[0:rows] * value[0:rows]).astype(jnp.bfloat16).T)
    rims = []
    for part in (key, value, query):
        rims += [part[0:edge], part[rows:]]
    rims.append(jnp.zeros((lane - 3 * rim_step, width), jnp.float32))
    put_rim(packed_ref, 2 * rows, jnp.concatenate(rims).T)
    for copy in copies[4:]:
        copy.wait()
    med_len = medium_ref.shape[0]
    is_first = jnp.where(lax.axis_index("seq") == 0, 1.0, 0.0)
    head = long_ref[0:med_len, :] + is_first * medium_ref[...]
    head_row = lax.broadcasted_iota(jnp.int32, head.shape, 0)
    head = head + jnp.where(head_row == 0, is_first * skip_ref[...], 0.0)
    taps = jnp.concatenate([head, long_ref[med_len:, :]]).astype(jnp.bfloat16)
    put_columns(packed_ref, rows, taps.T)


def put_columns(packed_ref, begin, values):
    if len(packed_ref.shape) == 2:
        packed_ref[:, begin : begin + values.shape[1]] = values
        return
    devices = packed_ref.shape[0]
    values = values.reshape(devices, -1, values.shape[1])
    chans = values.shape[1]
    for column in range(values.shape[2] // lane):
        place = (begin // lane + column) * chans
        packed_ref[:, place : place + chans, :] = values[:, :, column * lane : (column + 1) * lane]


def put_rim(packed_ref, begin, rim):
    if len(packed_ref.shape) == 2:
        packed_ref[:, begin:] = rim.astype(jnp.bfloat16)
        return
    rim = rim.reshape(packed_ref.shape[0], -1, lane)
    chans = rim.shape[1]
    both = rim[:, : chans // 2] + pltpu.roll(rim[:, chans // 2 :], lane // 2, 2)
    packed_ref[:, begin // lane * chans :, :] = both.astype(jnp.bfloat16)


def take_blocks(packed_ref, chans, rows):
    if chans % 16:
        return packed_ref[:, : 2 * rows], packed_ref[:, 2 * rows :].astype(jnp.float32)
    width = packed_ref.shape[0] * chans
    count = 2 * rows // lane
    columns = [
        packed_ref[:, i * chans : (i + 1) * chans, :].reshape(width, lane) for i in range(count)
    ]
    both = packed_ref[:, count * chans :, :].astype(jnp.float32)
    rim = jnp.concatenate([both, pltpu.roll(both, lane // 2, 2)], axis=1).reshape(width, lane)
    return jnp.concatenate(columns, axis=1), rim


def twist_rows(twist_ref, chans):
    half, rows = twist_ref.shape[0] // 2, twist_ref.shape[1]
    tables = twist_ref[0:half, :], twist_ref[half:, :]
    if chans % 8:
        return tables
    return tuple(
        jnp.broadcast_to(table[:, None, :], (half, chans, rows)).reshape(half * chans, rows)
        for table in tables
    )


def convolve_body(chans, rim_count, packed_ref, first_ref, twist_ref, inner_ref, last_ref, out_ref):
    rows = twist_ref.shape[1]
    half = first_ref.shape[0] // 2
    values, rim = take_blocks(packed_ref, chans, rows)
    before = jnp.concatenate([jnp.zeros((chans, lane), jnp.float32), rim[:-chans]])
    rim = rim + pltpu.roll(before, lane - edge, 1)
    in_rim = lax.broadcasted_iota(jnp.int32, rim.shape, 1) < rim_count
    rim_signal = (rim * pltpu.roll(rim, lane - rim_step, 1)).astype(jnp.bfloat16)
    rim_query = jnp.where(in_rim, pltpu.roll(rim, lane - 2 * rim_step, 1), 1.0)
    values = jnp.concatenate(
        [jnp.where(in_rim, rim_signal, values[:, 0:lane]), values[:, lane:]], axis=1
    )
    spread = jnp.dot(first_ref[...], values, preferred_element_type=jnp.float32)
    tw_cos, tw_sin = twist_rows(twist_ref, chans)
    turned = []
    for begin in (0, rows):
        real, imag = spread[0:half, begin : begin + rows], spread[half:, begin : begin + rows]
        turned.append([real * tw_cos + imag * tw_sin, imag * tw_cos - real * tw_sin])
    turned = jnp.concatenate([jnp.concatenate(pair, axis=1).astype(jnp.bfloat16) for pair in turned])
    spectra = jnp.dot(turned, inner_ref[...], preferred_element_type=jnp.float32)
    real, imag = spectra[0:half, 0:rows], spectra[0:half, rows:]
    fil_re, fil_im = spectra[half:, 0:rows], spectra[half:, rows:]
    product = [real * fil_im + imag * fil_re, real * fil_re - imag * fil_im]
    product = jnp.concatenate(product, axis=1).astype(jnp.bfloat16)
    back = jnp.dot(product, inner_ref[...], preferred_element_type=jnp.float32)
    imag, real = back[:, 0:rows], back[:, rows:]
    turned = jnp.concatenate([real * tw_cos - imag * tw_sin, imag * tw_cos + real * tw_sin])
    conv = jnp.dot(last_ref[...], turned.astype(jnp.bfloat16), preferred_element_type=jnp.float32)
    out_ref[:, 0:lane] = (conv[:, 0:lane] * rim_query).astype(jnp.bfloat16)
    out_ref[:, lane:] = conv[:, lane:].astype(jnp.bfloat16)


def output_body(conv_ref, query_ref, w_ref, out_ref):
    conv = conv_ref[...].T.astype(jnp.float32)
    mixed_out = (query_ref[...] * conv).astype(jnp.bfloat16)
    out_ref[...] = jnp.dot(mixed_out, w_ref[...], preferred_element_type=jnp.float32).astype(
        jnp.bfloat16
    )


def local(tokens, norm_gain, w_in, short_filter, long_filter, medium_filter, skip_gain, w_out):
    rows, width = tokens.shape
    devices = lax.axis_size("seq")
    chans = width // devices
    first, twist, inner, last = spectral_tables(devices, rows, chans)

    if chans % 16:
        packed_shape = (width, 2 * rows + lane)
    else:
        packed_shape = (devices, 2 * rows // lane * chans + chans // 2, lane)

    def swap(array):
        pieces = array.reshape(devices, -1, array.shape[-1])
        return lax.all_to_all(pieces, "seq", split_axis=0, concat_axis=0).reshape(array.shape)

    args = (tokens, norm_gain[None, :], w_in, short_filter, long_filter, medium_filter, skip_gain[None, :])
    args = tuple(pltpu.with_memory_space_constraint(arg, pltpu.HBM) for arg in args)
    packed, query = call(
        prepare_body,
        (
            jax.ShapeDtypeStruct(packed_shape, jnp.bfloat16),
            jax.ShapeDtypeStruct((rows, width), jnp.float32),
        ),
        args,
        [pltpu.HBM] * len(args),
        [pltpu.VMEM(arg.shape, arg.dtype) for arg in args]
        + [pltpu.SemaphoreType.DMA((len(args),))],
        flops=2 * rows * width * 3 * width,
        moved=1_500_000,
    )
    packed, tables = lax.optimization_barrier((packed, (first, twist, inner, last)))
    conv = call(
        functools.partial(convolve_body, chans, short_filter.shape[0] - 1),
        jax.ShapeDtypeStruct((width, rows), jnp.bfloat16),
        (swap(packed), *tables),
        [pltpu.VMEM] * 5,
        flops=18 * first.shape[0] * width * rows,
        moved=2_000_000,
    )
    return call(
        output_body,
        jax.ShapeDtypeStruct((rows, width), jnp.bfloat16),
        (swap(conv), query, w_out),
        [pltpu.VMEM] * 3,
        flops=2 * rows * width * width,
        moved=600_000,
    )


def solution(mesh):
    placed = (P(("groups", "seq"), None), P(), P(), P(), P("seq", None), P(), P(), P())
    return jax.shard_map(
        local, mesh=mesh, in_specs=placed, out_specs=P(("groups", "seq"), None), check_vma=False
    )
```

```python
import functools
import math

import jax
import jax.numpy as jnp
import numpy as np
from jax import lax
from jax.experimental import pallas as pl
from jax.experimental.pallas import tpu as pltpu
from jax.sharding import PartitionSpec as P

epsilon = 1e-06
edge = 8
lane = 128
rim_step = 2 * edge
vmem_bytes = 32 * 2**20


def whole(space):
    return pl.BlockSpec(memory_space=space)


def call(body, outs, args, spaces, scratch=(), flops=0, moved=0):
    return pl.pallas_call(
        body,
        out_shape=outs,
        in_specs=[whole(space) for space in spaces],
        out_specs=jax.tree.map(lambda _: whole(pltpu.VMEM), outs),
        scratch_shapes=list(scratch),
        compiler_params=pltpu.CompilerParams(vmem_limit_bytes=vmem_bytes),
        cost_estimate=pl.CostEstimate(flops=flops, bytes_accessed=moved, transcendentals=0),
    )(*args)


def spectral_tables(devices, rows, chans):
    full_len = devices * rows
    freqs = 4 * np.arange(devices) + 1
    eye = np.eye(chans)
    angle = 2.0 * math.pi / (4 * devices) * (freqs[:, None] * np.arange(devices)[None, :] % (4 * devices))
    cosine, sine = np.kron(np.cos(angle), eye), np.kron(np.sin(angle), eye)
    first = np.concatenate([cosine, -sine])
    offsets = np.arange(rows)
    twist = 2.0 * math.pi / (4 * full_len) * (freqs[:, None] * offsets[None, :] % (4 * full_len))
    twist = np.concatenate([np.cos(twist), np.sin(twist)])
    if chans % 8:
        twist = np.repeat(twist, chans, axis=0)
    turn = 2.0 * math.pi / rows * (offsets[:, None] * offsets[None, :] % rows)
    inner = np.concatenate([np.cos(turn), np.sin(turn)], axis=1)
    return (
        jnp.asarray(first, jnp.bfloat16),
        jnp.asarray(twist, jnp.float32),
        jnp.asarray(inner, jnp.bfloat16),
    )


def prepare_body(*refs):
    hbm, (packed_ref, query_ref), held, sems = refs[:7], refs[7:9], refs[9:16], refs[16]
    tokens_ref, gain_ref, w_ref, short_ref, long_ref, medium_ref, skip_ref = held
    rows, width = tokens_ref.shape
    copies = [pltpu.make_async_copy(h, v, sems.at[i]) for i, (h, v) in enumerate(zip(hbm, held))]
    for copy in copies:
        copy.start()
    copies[0].wait()
    copies[1].wait()
    inputs = tokens_ref[...].astype(jnp.float32)
    mean_sq = jnp.mean(inputs * inputs, axis=-1, keepdims=True)
    normed = (inputs * lax.rsqrt(mean_sq + epsilon) * gain_ref[...]).astype(jnp.bfloat16)
    copies[2].wait()
    copies[3].wait()
    projected = jnp.dot(normed, w_ref[...], preferred_element_type=jnp.float32)
    projected = projected.astype(jnp.bfloat16).astype(jnp.float32)
    projected = jnp.concatenate([projected, jnp.zeros((edge, 3 * width), jnp.float32)])
    taps_count = short_ref.shape[0]

    def mixed(part):
        cols = slice(part * width, (part + 1) * width)
        acc = short_ref[0:1, cols] * projected[:, cols]
        for tap_num in range(1, taps_count):
            acc = acc + short_ref[tap_num : tap_num + 1, cols] * pltpu.roll(projected[:, cols], tap_num, 0)
        return acc

    query, key, value = mixed(0), mixed(1), mixed(2)
    query_ref[...] = query[0:rows]
    row = lax.broadcasted_iota(jnp.int32, (edge, width), 0)
    query_ref[0:edge, :] = jnp.where(row < taps_count - 1, 1.0, query[0:edge])
    put_columns(packed_ref, 0, (key[0:rows] * value[0:rows]).astype(jnp.bfloat16).T)
    rims = []
    for part in (key, value, query):
        rims += [part[0:edge], part[rows:]]
    rims.append(jnp.zeros((lane - 3 * rim_step, width), jnp.float32))
    put_rim(packed_ref, 2 * rows, jnp.concatenate(rims).T)
    for copy in copies[4:]:
        copy.wait()
    med_len = medium_ref.shape[0]
    is_first = jnp.where(lax.axis_index("seq") == 0, 1.0, 0.0)
    head = long_ref[0:med_len, :] + is_first * medium_ref[...]
    head_row = lax.broadcasted_iota(jnp.int32, head.shape, 0)
    head = head + jnp.where(head_row == 0, is_first * skip_ref[...], 0.0)
    taps = jnp.concatenate([head, long_ref[med_len:, :]]).astype(jnp.bfloat16)
    put_columns(packed_ref, rows, taps.T)


def put_columns(packed_ref, begin, values):
    if len(packed_ref.shape) == 2:
        packed_ref[:, begin : begin + values.shape[1]] = values
        return
    devices = packed_ref.shape[0]
    values = values.reshape(devices, -1, values.shape[1])
    chans = values.shape[1]
    for column in range(values.shape[2] // lane):
        place = (begin // lane + column) * chans
        packed_ref[:, place : place + chans, :] = values[:, :, column * lane : (column + 1) * lane]


def put_rim(packed_ref, begin, rim):
    if len(packed_ref.shape) == 2:
        packed_ref[:, begin:] = rim.astype(jnp.bfloat16)
        return
    rim = rim.reshape(packed_ref.shape[0], -1, lane)
    chans = rim.shape[1]
    both = rim[:, : chans // 2] + pltpu.roll(rim[:, chans // 2 :], lane // 2, 2)
    packed_ref[:, begin // lane * chans :, :] = both.astype(jnp.bfloat16)


def take_blocks(packed_ref, chans, rows):
    if chans % 16:
        return packed_ref[:, : 2 * rows], packed_ref[:, 2 * rows :].astype(jnp.float32)
    width = packed_ref.shape[0] * chans
    count = 2 * rows // lane
    columns = [
        packed_ref[:, i * chans : (i + 1) * chans, :].reshape(width, lane) for i in range(count)
    ]
    both = packed_ref[:, count * chans :, :].astype(jnp.float32)
    rim = jnp.concatenate([both, pltpu.roll(both, lane // 2, 2)], axis=1).reshape(width, lane)
    return jnp.concatenate(columns, axis=1), rim


def twist_rows(twist_ref, chans):
    half, rows = twist_ref.shape[0] // 2, twist_ref.shape[1]
    tables = twist_ref[0:half, :], twist_ref[half:, :]
    if chans % 8:
        return tables
    return tuple(
        jnp.broadcast_to(table[:, None, :], (half, chans, rows)).reshape(half * chans, rows)
        for table in tables
    )


def convolve_body(chans, rim_count, packed_ref, first_ref, twist_ref, inner_ref, out_ref):
    rows = twist_ref.shape[1]
    half = first_ref.shape[0] // 2
    scale = chans / (half * rows)
    values, rim = take_blocks(packed_ref, chans, rows)
    before = jnp.concatenate([jnp.zeros((chans, lane), jnp.float32), rim[:-chans]])
    rim = rim + pltpu.roll(before, lane - edge, 1)
    in_rim = lax.broadcasted_iota(jnp.int32, rim.shape, 1) < rim_count
    rim_signal = (rim * pltpu.roll(rim, lane - rim_step, 1)).astype(jnp.bfloat16)
    rim_query = scale * jnp.where(in_rim, pltpu.roll(rim, lane - 2 * rim_step, 1), 1.0)
    values = jnp.concatenate(
        [jnp.where(in_rim, rim_signal, values[:, 0:lane]), values[:, lane:]], axis=1
    )
    cosine, sine = inner_ref[:, 0:rows], inner_ref[:, rows:]
    inner = jnp.concatenate(
        [jnp.concatenate([cosine, -sine], axis=1), jnp.concatenate([sine, cosine], axis=1)]
    )
    spread = jnp.dot(first_ref[...], values, preferred_element_type=jnp.float32)
    tw_cos, tw_sin = twist_rows(twist_ref, chans)
    turned = []
    for begin in (0, rows):
        real, imag = spread[0:half, begin : begin + rows], spread[half:, begin : begin + rows]
        turned.append([real * tw_cos + imag * tw_sin, imag * tw_cos - real * tw_sin])
    turned = jnp.concatenate([jnp.concatenate(pair, axis=1).astype(jnp.bfloat16) for pair in turned])
    spectra = jnp.dot(turned, inner, preferred_element_type=jnp.float32)
    real, imag = spectra[0:half, 0:rows], spectra[0:half, rows:]
    fil_re, fil_im = spectra[half:, 0:rows], spectra[half:, rows:]
    product = [real * fil_im + imag * fil_re, real * fil_re - imag * fil_im]
    product = jnp.concatenate(product, axis=1).astype(jnp.bfloat16)
    back = jnp.dot(product, inner, preferred_element_type=jnp.float32)
    imag, real = back[:, 0:rows], back[:, rows:]
    turned = jnp.concatenate([real * tw_cos - imag * tw_sin, imag * tw_cos + real * tw_sin])
    last = jnp.concatenate([first_ref[0:half, :].T, first_ref[half:, :].T], axis=1)
    conv = jnp.dot(last, turned.astype(jnp.bfloat16), preferred_element_type=jnp.float32)
    out_ref[:, 0:lane] = (conv[:, 0:lane] * rim_query).astype(jnp.bfloat16)
    out_ref[:, lane:] = (conv[:, lane:] * scale).astype(jnp.bfloat16)


def output_body(conv_ref, query_ref, w_ref, out_ref):
    conv = conv_ref[...].T.astype(jnp.float32)
    mixed_out = (query_ref[...] * conv).astype(jnp.bfloat16)
    out_ref[...] = jnp.dot(mixed_out, w_ref[...], preferred_element_type=jnp.float32).astype(
        jnp.bfloat16
    )


def local(tokens, norm_gain, w_in, short_filter, long_filter, medium_filter, skip_gain, w_out):
    rows, width = tokens.shape
    devices = lax.axis_size("seq")
    chans = width // devices
    first, twist, inner = spectral_tables(devices, rows, chans)

    if chans % 16:
        packed_shape = (width, 2 * rows + lane)
    else:
        packed_shape = (devices, 2 * rows // lane * chans + chans // 2, lane)

    def swap(array):
        pieces = array.reshape(devices, -1, array.shape[-1])
        return lax.all_to_all(pieces, "seq", split_axis=0, concat_axis=0).reshape(array.shape)

    args = (tokens, norm_gain[None, :], w_in, short_filter, long_filter, medium_filter, skip_gain[None, :])
    args = tuple(pltpu.with_memory_space_constraint(arg, pltpu.HBM) for arg in args)
    packed, query = call(
        prepare_body,
        (
            jax.ShapeDtypeStruct(packed_shape, jnp.bfloat16),
            jax.ShapeDtypeStruct((rows, width), jnp.float32),
        ),
        args,
        [pltpu.HBM] * len(args),
        [pltpu.VMEM(arg.shape, arg.dtype) for arg in args]
        + [pltpu.SemaphoreType.DMA((len(args),))],
        flops=2 * rows * width * 3 * width,
        moved=1_500_000,
    )
    conv = call(
        functools.partial(convolve_body, chans, short_filter.shape[0] - 1),
        jax.ShapeDtypeStruct((width, rows), jnp.bfloat16),
        (swap(packed), first, twist, inner),
        [pltpu.VMEM] * 4,
        flops=18 * first.shape[0] * width * rows,
        moved=2_000_000,
    )
    return call(
        output_body,
        jax.ShapeDtypeStruct((rows, width), jnp.bfloat16),
        (swap(conv), query, w_out),
        [pltpu.VMEM] * 3,
        flops=2 * rows * width * width,
        moved=600_000,
    )


def solution(mesh):
    placed = (P(("groups", "seq"), None), P(), P(), P(), P("seq", None), P(), P(), P())
    return jax.shard_map(
        local, mesh=mesh, in_specs=placed, out_specs=P(("groups", "seq"), None), check_vma=False
    )
```

```python
import functools
import math

import jax
import jax.numpy as jnp
import numpy as np
from jax import lax
from jax.experimental import pallas as pl
from jax.experimental.pallas import tpu as pltpu
from jax.sharding import PartitionSpec as P

epsilon = 1e-06
edge = 8
lane = 128
seq = ("chip", "core")
rim_step = 2 * edge
vmem_bytes = 32 * 2**20


def whole(space):
    return pl.BlockSpec(memory_space=space)


def call(body, outs, args, spaces, scratch=(), flops=0, moved=0):
    return pl.pallas_call(
        body,
        out_shape=outs,
        in_specs=[whole(space) for space in spaces],
        out_specs=jax.tree.map(lambda _: whole(pltpu.VMEM), outs),
        scratch_shapes=list(scratch),
        compiler_params=pltpu.CompilerParams(vmem_limit_bytes=vmem_bytes),
        cost_estimate=pl.CostEstimate(flops=flops, bytes_accessed=moved, transcendentals=0),
    )(*args)


def spectral_tables(devices, rows, chans):
    full_len = devices * rows
    freqs = 4 * np.arange(devices) + 1
    eye = np.eye(chans)
    angle = 2.0 * math.pi / (4 * devices) * (freqs[:, None] * np.arange(devices)[None, :] % (4 * devices))
    cosine, sine = np.kron(np.cos(angle), eye), np.kron(np.sin(angle), eye)
    first = np.concatenate([cosine, -sine])
    offsets = np.arange(rows)
    twist = 2.0 * math.pi / (4 * full_len) * (freqs[:, None] * offsets[None, :] % (4 * full_len))
    twist = np.concatenate([np.cos(twist), np.sin(twist)])
    if chans % 8:
        twist = np.repeat(twist, chans, axis=0)
    turn = 2.0 * math.pi / rows * (offsets[:, None] * offsets[None, :] % rows)
    inner = np.concatenate([np.cos(turn), np.sin(turn)], axis=1)
    return (
        jnp.asarray(first, jnp.bfloat16),
        jnp.asarray(twist, jnp.float32),
        jnp.asarray(inner, jnp.bfloat16),
    )


def routes_of(chips):
    far = sorted(range(2, chips, 2), key=lambda d: (-d.bit_length(), d))
    return [(d + 1, d) if turn % 2 == 0 else (d, d + 1) for turn, d in enumerate(far)]


def carried(route, core):
    mine, others = route
    return jnp.where(core == 0, mine, others), jnp.where(core == 0, others, mine)


def put_routes(source_ref, keep_ref, give_ref, near_ref, home_ref):
    chip, core = lax.axis_index("chip"), lax.axis_index("core")

    def blocks(distance):
        return source_ref[pl.ds((chip ^ distance) * 2, 2)]

    for turn, route in enumerate(routes_of(source_ref.shape[0] // 2)):
        own, other = carried(route, core)
        keep_ref[turn] = blocks(own)
        give_ref[turn] = blocks(other)
    near_ref[...] = blocks(1)
    home_ref[...] = blocks(0)


def merge_body(keep_ref, got_ref, *out_refs):
    for turn, out_ref in enumerate(out_refs):
        out_ref[0] = keep_ref[turn]
        out_ref[1] = got_ref[turn]


def split_body(*refs):
    far_refs, (near_ref, home_ref, keep_ref, give_ref) = refs[:-4], refs[-4:]
    core = lax.axis_index("core")
    for out_ref, target in ((keep_ref, core), (give_ref, 1 - core)):
        for turn, far_ref in enumerate(far_refs):
            for sender in range(2):
                out_ref[2 * turn + sender] = far_ref[sender, target]
        out_ref[2 * len(far_refs)] = near_ref[target]
        out_ref[2 * len(far_refs) + 1] = home_ref[target]


def take_routes(keep_ref, got_ref, target_ref):
    chip, core = lax.axis_index("chip"), lax.axis_index("core")
    routes = routes_of(target_ref.shape[0] // 2)
    for turn, route in enumerate(routes):
        own, other = carried(route, core)
        target_ref[(chip ^ own) * 2 + core] = keep_ref[2 * turn]
        target_ref[(chip ^ own) * 2 + 1 - core] = keep_ref[2 * turn + 1]
        target_ref[(chip ^ other) * 2 + 1 - core] = got_ref[2 * turn]
        target_ref[(chip ^ other) * 2 + core] = got_ref[2 * turn + 1]
    for place, distance in ((2 * len(routes), 1), (2 * len(routes) + 1, 0)):
        target_ref[(chip ^ distance) * 2 + core] = keep_ref[place]
        target_ref[(chip ^ distance) * 2 + 1 - core] = got_ref[place]


def prepare_body(*refs):
    hbm, query_ref, outs, held, sems = refs[:7], refs[7], refs[8:-8], refs[-8:-1], refs[-1]
    staged = len(outs) > 1
    outs, packed_ref = (outs[:-1], outs[-1]) if staged else (outs, outs[0])
    tokens_ref, gain_ref, w_ref, short_ref, long_ref, medium_ref, skip_ref = held
    rows, width = tokens_ref.shape
    copies = [pltpu.make_async_copy(h, v, sems.at[i]) for i, (h, v) in enumerate(zip(hbm, held))]
    for copy in copies:
        copy.start()
    copies[0].wait()
    copies[1].wait()
    inputs = tokens_ref[...].astype(jnp.float32)
    mean_sq = jnp.mean(inputs * inputs, axis=-1, keepdims=True)
    normed = (inputs * lax.rsqrt(mean_sq + epsilon) * gain_ref[...]).astype(jnp.bfloat16)
    copies[2].wait()
    copies[3].wait()
    projected = jnp.dot(normed, w_ref[...], preferred_element_type=jnp.float32)
    projected = projected.astype(jnp.bfloat16).astype(jnp.float32)
    projected = jnp.concatenate([projected, jnp.zeros((edge, 3 * width), jnp.float32)])
    taps_count = short_ref.shape[0]

    def mixed(part):
        cols = slice(part * width, (part + 1) * width)
        acc = short_ref[0:1, cols] * projected[:, cols]
        for tap_num in range(1, taps_count):
            acc = acc + short_ref[tap_num : tap_num + 1, cols] * pltpu.roll(projected[:, cols], tap_num, 0)
        return acc

    query, key, value = mixed(0), mixed(1), mixed(2)
    query_ref[...] = query[0:rows]
    row = lax.broadcasted_iota(jnp.int32, (edge, width), 0)
    query_ref[0:edge, :] = jnp.where(row < taps_count - 1, 1.0, query[0:edge])
    put_columns(packed_ref, 0, (key[0:rows] * value[0:rows]).astype(jnp.bfloat16).T)
    rims = []
    for part in (key, value, query):
        rims += [part[0:edge], part[rows:]]
    rims.append(jnp.zeros((lane - 3 * rim_step, width), jnp.float32))
    put_rim(packed_ref, 2 * rows, jnp.concatenate(rims).T)
    for copy in copies[4:]:
        copy.wait()
    med_len = medium_ref.shape[0]
    is_first = jnp.where(lax.axis_index(seq) == 0, 1.0, 0.0)
    head = long_ref[0:med_len, :] + is_first * medium_ref[...]
    head_row = lax.broadcasted_iota(jnp.int32, head.shape, 0)
    head = head + jnp.where(head_row == 0, is_first * skip_ref[...], 0.0)
    taps = jnp.concatenate([head, long_ref[med_len:, :]]).astype(jnp.bfloat16)
    put_columns(packed_ref, rows, taps.T)
    if staged:
        put_routes(packed_ref, *outs)


def put_columns(packed_ref, begin, values):
    if len(packed_ref.shape) == 2:
        packed_ref[:, begin : begin + values.shape[1]] = values
        return
    devices = packed_ref.shape[0]
    values = values.reshape(devices, -1, values.shape[1])
    chans = values.shape[1]
    for column in range(values.shape[2] // lane):
        place = (begin // lane + column) * chans
        packed_ref[:, place : place + chans, :] = values[:, :, column * lane : (column + 1) * lane]


def put_rim(packed_ref, begin, rim):
    if len(packed_ref.shape) == 2:
        packed_ref[:, begin:] = rim.astype(jnp.bfloat16)
        return
    rim = rim.reshape(packed_ref.shape[0], -1, lane)
    chans = rim.shape[1]
    both = rim[:, : chans // 2] + pltpu.roll(rim[:, chans // 2 :], lane // 2, 2)
    packed_ref[:, begin // lane * chans :, :] = both.astype(jnp.bfloat16)


def take_blocks(packed_ref, chans, rows):
    if chans % 16:
        return packed_ref[:, : 2 * rows], packed_ref[:, 2 * rows :].astype(jnp.float32)
    width = packed_ref.shape[0] * chans
    count = 2 * rows // lane
    columns = [
        packed_ref[:, i * chans : (i + 1) * chans, :].reshape(width, lane) for i in range(count)
    ]
    both = packed_ref[:, count * chans :, :].astype(jnp.float32)
    rim = jnp.concatenate([both, pltpu.roll(both, lane // 2, 2)], axis=1).reshape(width, lane)
    return jnp.concatenate(columns, axis=1), rim


def twist_rows(twist_ref, chans):
    half, rows = twist_ref.shape[0] // 2, twist_ref.shape[1]
    tables = twist_ref[0:half, :], twist_ref[half:, :]
    if chans % 8:
        return tables
    return tuple(
        jnp.broadcast_to(table[:, None, :], (half, chans, rows)).reshape(half * chans, rows)
        for table in tables
    )


def convolve_body(chans, rim_count, first_ref, twist_ref, inner_ref, *refs):
    staged = len(refs) > 2
    if staged:
        keep_ref, got_ref, *outs, packed_ref, out_ref = refs
        take_routes(keep_ref, got_ref, packed_ref)
    else:
        packed_ref, out_ref = refs
    rows = twist_ref.shape[1]
    half = first_ref.shape[0] // 2
    scale = chans / (half * rows)
    values, rim = take_blocks(packed_ref, chans, rows)
    before = jnp.concatenate([jnp.zeros((chans, lane), jnp.float32), rim[:-chans]])
    rim = rim + pltpu.roll(before, lane - edge, 1)
    in_rim = lax.broadcasted_iota(jnp.int32, rim.shape, 1) < rim_count
    rim_signal = (rim * pltpu.roll(rim, lane - rim_step, 1)).astype(jnp.bfloat16)
    rim_query = scale * jnp.where(in_rim, pltpu.roll(rim, lane - 2 * rim_step, 1), 1.0)
    values = jnp.concatenate(
        [jnp.where(in_rim, rim_signal, values[:, 0:lane]), values[:, lane:]], axis=1
    )
    cosine, sine = inner_ref[:, 0:rows], inner_ref[:, rows:]
    inner = jnp.concatenate(
        [jnp.concatenate([cosine, -sine], axis=1), jnp.concatenate([sine, cosine], axis=1)]
    )
    spread = jnp.dot(first_ref[...], values, preferred_element_type=jnp.float32)
    tw_cos, tw_sin = twist_rows(twist_ref, chans)
    turned = []
    for begin in (0, rows):
        real, imag = spread[0:half, begin : begin + rows], spread[half:, begin : begin + rows]
        turned.append([real * tw_cos + imag * tw_sin, imag * tw_cos - real * tw_sin])
    turned = jnp.concatenate([jnp.concatenate(pair, axis=1).astype(jnp.bfloat16) for pair in turned])
    spectra = jnp.dot(turned, inner, preferred_element_type=jnp.float32)
    real, imag = spectra[0:half, 0:rows], spectra[0:half, rows:]
    fil_re, fil_im = spectra[half:, 0:rows], spectra[half:, rows:]
    product = [real * fil_im + imag * fil_re, real * fil_re - imag * fil_im]
    product = jnp.concatenate(product, axis=1).astype(jnp.bfloat16)
    back = jnp.dot(product, inner, preferred_element_type=jnp.float32)
    imag, real = back[:, 0:rows], back[:, rows:]
    turned = jnp.concatenate([real * tw_cos - imag * tw_sin, imag * tw_cos + real * tw_sin])
    last = jnp.concatenate([first_ref[0:half, :].T, first_ref[half:, :].T], axis=1)
    conv = jnp.dot(last, turned.astype(jnp.bfloat16), preferred_element_type=jnp.float32)
    conv = jnp.concatenate([conv[:, 0:lane] * rim_query, conv[:, lane:] * scale], axis=1)
    out_ref[...] = conv.astype(jnp.bfloat16).reshape(out_ref.shape)
    if staged:
        put_routes(out_ref, *outs)


def output_body(query_ref, w_ref, *refs):
    if len(refs) > 2:
        keep_ref, got_ref, out_ref, conv_ref = refs
        take_routes(keep_ref, got_ref, conv_ref)
    else:
        conv_ref, out_ref = refs
    conv = conv_ref[...].reshape(w_ref.shape[0], query_ref.shape[0]).T.astype(jnp.float32)
    mixed_out = (query_ref[...] * conv).astype(jnp.bfloat16)
    out_ref[...] = jnp.dot(mixed_out, w_ref[...], preferred_element_type=jnp.float32).astype(
        jnp.bfloat16
    )


def permute(array, partner):
    return lax.ppermute(array, seq, [(i, partner(i)) for i in range(lax.axis_size(seq))])


def bf16(*shape):
    return jax.ShapeDtypeStruct(shape, jnp.bfloat16)


def exchange(keep, give, near, home):
    block, turns = keep.shape[2:], keep.shape[0]
    got = permute(give, lambda i: i ^ 1)
    near = permute(near, lambda i: i ^ 2)
    far = call(
        merge_body, (bf16(2, 2, *block),) * turns, (keep, got), [pltpu.VMEM] * 2, moved=4 * keep.size
    )
    routes = routes_of(lax.axis_size("chip"))
    far = [permute(part, lambda i: i ^ 2 * route[i % 2]) for part, route in zip(far, routes)]
    half = bf16(2 * turns + 2, *block)
    keep, give = call(
        split_body, (half, half), (*far, near, home), [pltpu.VMEM] * (turns + 2), moved=4 * keep.size
    )
    return keep, permute(give, lambda i: i ^ 1)


def local(tokens, norm_gain, w_in, short_filter, long_filter, medium_filter, skip_gain, w_out):
    rows, width = tokens.shape
    devices, chips = lax.axis_size(seq), lax.axis_size("chip")
    chans = width // devices
    first, twist, inner = spectral_tables(devices, rows, chans)
    staged = chans % 16 == 0 and chips >= 4
    if chans % 16:
        packed_shape, conv_shape = (width, 2 * rows + lane), (width, rows)
    else:
        packed_shape = (devices, 2 * rows // lane * chans + chans // 2, lane)
        conv_shape = (devices, chans, rows)

    def pieces(shape):
        if not staged:
            return (bf16(*shape),), []
        block, turns = shape[1:], len(routes_of(chips))
        outs = [bf16(turns, 2, *block)] * 2 + [bf16(2, *block)] * 2
        return tuple(outs), [pltpu.VMEM(shape, jnp.bfloat16)]

    def swap(parts):
        if staged:
            return exchange(*parts)
        (array,) = parts
        blocks = array.reshape(devices, -1, array.shape[-1])
        return (lax.all_to_all(blocks, seq, split_axis=0, concat_axis=0).reshape(array.shape),)

    args = (tokens, norm_gain[None, :], w_in, short_filter, long_filter, medium_filter, skip_gain[None, :])
    args = tuple(pltpu.with_memory_space_constraint(arg, pltpu.HBM) for arg in args)
    outs, packed_scratch = pieces(packed_shape)
    query, *parts = call(
        prepare_body,
        (jax.ShapeDtypeStruct((rows, width), jnp.float32), *outs),
        args,
        [pltpu.HBM] * len(args),
        packed_scratch
        + [pltpu.VMEM(arg.shape, arg.dtype) for arg in args]
        + [pltpu.SemaphoreType.DMA((len(args),))],
        flops=2 * rows * width * 3 * width,
        moved=1_500_000,
    )
    outs, conv_scratch = pieces(conv_shape)
    parts = swap(parts)
    parts = call(
        functools.partial(convolve_body, chans, short_filter.shape[0] - 1),
        outs,
        (first, twist, inner, *parts),
        [pltpu.VMEM] * (3 + len(parts)),
        packed_scratch + conv_scratch,
        flops=18 * first.shape[0] * width * rows,
        moved=2_000_000,
    )
    parts = swap(parts)
    return call(
        output_body,
        bf16(rows, width),
        (query, w_out, *parts),
        [pltpu.VMEM] * (2 + len(parts)),
        conv_scratch,
        flops=2 * rows * width * width,
        moved=600_000,
    )


def solution(mesh):
    groups, devices = mesh.devices.shape
    split = jax.sharding.Mesh(mesh.devices.reshape(groups, devices // 2, 2), ("groups", *seq))
    rows = P(("groups", *seq), None)
    placed = (rows, P(), P(), P(), P(seq, None), P(), P(), P())
    return jax.shard_map(local, mesh=split, in_specs=placed, out_specs=rows, check_vma=False)
```

```python
import functools
import math

import jax
import jax.numpy as jnp
import numpy as np
from jax import lax
from jax.experimental import pallas as pl
from jax.experimental.pallas import tpu as pltpu
from jax.sharding import PartitionSpec as P

epsilon = 1e-06
edge = 8
lane = 128
seq = ("chip", "core")
rim_step = 2 * edge
vmem_bytes = 32 * 2**20


def whole(space):
    return pl.BlockSpec(memory_space=space)


def call(body, outs, args, spaces, scratch=(), flops=0, moved=0):
    return pl.pallas_call(
        body,
        out_shape=outs,
        in_specs=[whole(space) for space in spaces],
        out_specs=jax.tree.map(lambda _: whole(pltpu.VMEM), outs),
        scratch_shapes=list(scratch),
        compiler_params=pltpu.CompilerParams(vmem_limit_bytes=vmem_bytes),
        cost_estimate=pl.CostEstimate(flops=flops, bytes_accessed=moved, transcendentals=0),
    )(*args)


def spectral_tables(devices, rows, chans):
    full_len = devices * rows
    freqs = 4 * np.arange(devices) + 1
    eye = np.eye(chans)
    angle = 2.0 * math.pi / (4 * devices) * (freqs[:, None] * np.arange(devices)[None, :] % (4 * devices))
    cosine, sine = np.kron(np.cos(angle), eye), np.kron(np.sin(angle), eye)
    first = np.concatenate([cosine, -sine])
    offsets = np.arange(rows)
    twist = 2.0 * math.pi / (4 * full_len) * (freqs[:, None] * offsets[None, :] % (4 * full_len))
    twist = np.concatenate([np.cos(twist), np.sin(twist)])
    if chans % 8:
        twist = np.repeat(twist, chans, axis=0)
    turn = 2.0 * math.pi / rows * (offsets[:, None] * offsets[None, :] % rows)
    inner = np.concatenate([np.cos(turn), np.sin(turn)], axis=1)
    return (
        jnp.asarray(first, jnp.bfloat16),
        jnp.asarray(twist, jnp.float32),
        jnp.asarray(inner, jnp.bfloat16),
    )


def routes_of(chips):
    far = sorted(range(2, chips, 2), key=lambda d: (-d.bit_length(), d))
    return [(d + 1, d) if turn % 2 == 0 else (d, d + 1) for turn, d in enumerate(far)]


def carried(route, core):
    mine, others = route
    return jnp.where(core == 0, mine, others), jnp.where(core == 0, others, mine)


def put_routes(source_ref, keep_ref, give_ref, home_ref):
    chip, core = lax.axis_index("chip"), lax.axis_index("core")

    def blocks(distance):
        return source_ref[pl.ds((chip ^ distance) * 2, 2)]

    routes = routes_of(source_ref.shape[0] // 2)
    for turn, route in enumerate(routes):
        own, other = carried(route, core)
        keep_ref[turn] = blocks(own)
        give_ref[turn] = blocks(other)
    keep_ref[len(routes)] = blocks(1)
    give_ref[len(routes)] = blocks(1)
    home_ref[...] = blocks(0)


def merge_body(keep_ref, got_ref, *out_refs):
    for turn, out_ref in enumerate(out_refs):
        out_ref[0] = keep_ref[turn]
        out_ref[1] = got_ref[turn]


def split_body(*refs):
    moved_refs, (home_ref, keep_ref, give_ref) = refs[:-3], refs[-3:]
    core = lax.axis_index("core")
    for out_ref, target in ((keep_ref, core), (give_ref, 1 - core)):
        for turn, moved_ref in enumerate(moved_refs):
            for sender in range(2):
                out_ref[2 * turn + sender] = moved_ref[sender, target]
        out_ref[2 * len(moved_refs)] = home_ref[target]


def take_routes(keep_ref, got_ref, target_ref):
    chip, core = lax.axis_index("chip"), lax.axis_index("core")
    routes = routes_of(target_ref.shape[0] // 2)
    for turn, route in enumerate(routes):
        own, other = carried(route, core)
        target_ref[(chip ^ own) * 2 + core] = keep_ref[2 * turn]
        target_ref[(chip ^ own) * 2 + 1 - core] = keep_ref[2 * turn + 1]
        target_ref[(chip ^ other) * 2 + 1 - core] = got_ref[2 * turn]
        target_ref[(chip ^ other) * 2 + core] = got_ref[2 * turn + 1]
    near, home = 2 * len(routes), 2 * len(routes) + 2
    for sender in range(2):
        block = jnp.where(core == 1, keep_ref[near + sender], got_ref[near + sender])
        target_ref[(chip ^ 1) * 2 + 1 - sender] = block
    target_ref[chip * 2 + core] = keep_ref[home]
    target_ref[chip * 2 + 1 - core] = got_ref[home]


def normed_of(tokens_ref, gain_ref):
    inputs = tokens_ref[...].astype(jnp.float32)
    mean_sq = jnp.mean(inputs * inputs, axis=-1, keepdims=True)
    return (inputs * lax.rsqrt(mean_sq + epsilon) * gain_ref[...]).astype(jnp.bfloat16)


def projected_of(normed, weights):
    projected = jnp.dot(normed, weights, preferred_element_type=jnp.float32)
    projected = projected.astype(jnp.bfloat16).astype(jnp.float32)
    return jnp.concatenate([projected, jnp.zeros((edge, projected.shape[1]), jnp.float32)])


def short_mix(projected, taps):
    acc = taps[0:1] * projected
    for tap_num in range(1, taps.shape[0]):
        acc = acc + taps[tap_num : tap_num + 1] * pltpu.roll(projected, tap_num, 0)
    return acc


def query_body(tokens_ref, gain_ref, w_ref, short_ref, query_ref):
    rows, width = tokens_ref.shape
    cols = slice(0, width)
    query = short_mix(projected_of(normed_of(tokens_ref, gain_ref), w_ref[:, cols]), short_ref[:, cols])
    query_ref[...] = query[0:rows]
    row = lax.broadcasted_iota(jnp.int32, (edge, width), 0)
    query_ref[0:edge, :] = jnp.where(row < short_ref.shape[0] - 1, 1.0, query[0:edge])


def prepare_body(*refs):
    hbm, outs, held, sems = refs[:7], refs[7:-8], refs[-8:-1], refs[-1]
    staged = len(outs) > 1
    outs, packed_ref = (outs[:-1], outs[-1]) if staged else (outs, outs[0])
    tokens_ref, gain_ref, w_ref, short_ref, long_ref, medium_ref, skip_ref = held
    rows, width = tokens_ref.shape
    copies = [pltpu.make_async_copy(h, v, sems.at[i]) for i, (h, v) in enumerate(zip(hbm, held))]
    for copy in copies:
        copy.start()
    copies[0].wait()
    copies[1].wait()
    normed = normed_of(tokens_ref, gain_ref)
    copies[2].wait()
    copies[3].wait()
    query_cols, cols = slice(0, width), slice(width, 3 * width)
    mixed = short_mix(projected_of(normed, w_ref[:, cols]), short_ref[:, cols])
    key, value = mixed[:, 0:width], mixed[:, width:]
    put_columns(packed_ref, 0, (key[0:rows] * value[0:rows]).astype(jnp.bfloat16).T)
    rims = [key[0:edge], key[rows:], value[0:edge], value[rows:]]
    for begin, place in ((0, 0), (rows - 2 * edge, 2 * edge)):
        some = projected_of(normed[begin : begin + 2 * edge], w_ref[:, query_cols])
        rims.append(short_mix(some, short_ref[:, query_cols])[place : place + edge])
    rims.append(jnp.zeros((lane - 3 * rim_step, width), jnp.float32))
    put_rim(packed_ref, 2 * rows, jnp.concatenate(rims).T)
    for copy in copies[4:]:
        copy.wait()
    med_len = medium_ref.shape[0]
    is_first = jnp.where(lax.axis_index(seq) == 0, 1.0, 0.0)
    head = long_ref[0:med_len, :] + is_first * medium_ref[...]
    head_row = lax.broadcasted_iota(jnp.int32, head.shape, 0)
    head = head + jnp.where(head_row == 0, is_first * skip_ref[...], 0.0)
    taps = jnp.concatenate([head, long_ref[med_len:, :]]).astype(jnp.bfloat16)
    put_columns(packed_ref, rows, taps.T)
    if staged:
        put_routes(packed_ref, *outs)


def put_columns(packed_ref, begin, values):
    if len(packed_ref.shape) == 2:
        packed_ref[:, begin : begin + values.shape[1]] = values
        return
    devices = packed_ref.shape[0]
    values = values.reshape(devices, -1, values.shape[1])
    chans = values.shape[1]
    for column in range(values.shape[2] // lane):
        place = (begin // lane + column) * chans
        packed_ref[:, place : place + chans, :] = values[:, :, column * lane : (column + 1) * lane]


def put_rim(packed_ref, begin, rim):
    if len(packed_ref.shape) == 2:
        packed_ref[:, begin:] = rim.astype(jnp.bfloat16)
        return
    rim = rim.reshape(packed_ref.shape[0], -1, lane)
    chans = rim.shape[1]
    both = rim[:, : chans // 2] + pltpu.roll(rim[:, chans // 2 :], lane // 2, 2)
    packed_ref[:, begin // lane * chans :, :] = both.astype(jnp.bfloat16)


def take_blocks(packed_ref, chans, rows):
    if chans % 16:
        return packed_ref[:, : 2 * rows], packed_ref[:, 2 * rows :].astype(jnp.float32)
    width = packed_ref.shape[0] * chans
    count = 2 * rows // lane
    columns = [
        packed_ref[:, i * chans : (i + 1) * chans, :].reshape(width, lane) for i in range(count)
    ]
    both = packed_ref[:, count * chans :, :].astype(jnp.float32)
    rim = jnp.concatenate([both, pltpu.roll(both, lane // 2, 2)], axis=1).reshape(width, lane)
    return jnp.concatenate(columns, axis=1), rim


def twist_rows(twist_ref, chans):
    half, rows = twist_ref.shape[0] // 2, twist_ref.shape[1]
    tables = twist_ref[0:half, :], twist_ref[half:, :]
    if chans % 8:
        return tables
    return tuple(
        jnp.broadcast_to(table[:, None, :], (half, chans, rows)).reshape(half * chans, rows)
        for table in tables
    )


def convolve_body(chans, rim_count, first_ref, twist_ref, inner_ref, *refs):
    staged = len(refs) > 2
    if staged:
        keep_ref, got_ref, *outs, packed_ref, out_ref = refs
        take_routes(keep_ref, got_ref, packed_ref)
    else:
        packed_ref, out_ref = refs
    rows = twist_ref.shape[1]
    half = first_ref.shape[0] // 2
    scale = chans / (half * rows)
    values, rim = take_blocks(packed_ref, chans, rows)
    before = jnp.concatenate([jnp.zeros((chans, lane), jnp.float32), rim[:-chans]])
    rim = rim + pltpu.roll(before, lane - edge, 1)
    in_rim = lax.broadcasted_iota(jnp.int32, rim.shape, 1) < rim_count
    rim_signal = (rim * pltpu.roll(rim, lane - rim_step, 1)).astype(jnp.bfloat16)
    rim_query = scale * jnp.where(in_rim, pltpu.roll(rim, lane - 2 * rim_step, 1), 1.0)
    values = jnp.concatenate(
        [jnp.where(in_rim, rim_signal, values[:, 0:lane]), values[:, lane:]], axis=1
    )
    cosine, sine = inner_ref[:, 0:rows], inner_ref[:, rows:]
    inner = jnp.concatenate(
        [jnp.concatenate([cosine, -sine], axis=1), jnp.concatenate([sine, cosine], axis=1)]
    )
    spread = jnp.dot(first_ref[...], values, preferred_element_type=jnp.float32)
    tw_cos, tw_sin = twist_rows(twist_ref, chans)
    turned = []
    for begin in (0, rows):
        real, imag = spread[0:half, begin : begin + rows], spread[half:, begin : begin + rows]
        turned.append([real * tw_cos + imag * tw_sin, imag * tw_cos - real * tw_sin])
    turned = jnp.concatenate([jnp.concatenate(pair, axis=1).astype(jnp.bfloat16) for pair in turned])
    spectra = jnp.dot(turned, inner, preferred_element_type=jnp.float32)
    real, imag = spectra[0:half, 0:rows], spectra[0:half, rows:]
    fil_re, fil_im = spectra[half:, 0:rows], spectra[half:, rows:]
    product = [real * fil_im + imag * fil_re, real * fil_re - imag * fil_im]
    product = jnp.concatenate(product, axis=1).astype(jnp.bfloat16)
    back = jnp.dot(product, inner, preferred_element_type=jnp.float32)
    imag, real = back[:, 0:rows], back[:, rows:]
    turned = jnp.concatenate([real * tw_cos - imag * tw_sin, imag * tw_cos + real * tw_sin])
    last = jnp.concatenate([first_ref[0:half, :].T, first_ref[half:, :].T], axis=1)
    conv = jnp.dot(last, turned.astype(jnp.bfloat16), preferred_element_type=jnp.float32)
    conv = jnp.concatenate([conv[:, 0:lane] * rim_query, conv[:, lane:] * scale], axis=1)
    out_ref[...] = conv.astype(jnp.bfloat16).reshape(out_ref.shape)
    if staged:
        put_routes(out_ref, *outs)


def output_body(query_ref, w_ref, *refs):
    if len(refs) > 2:
        keep_ref, got_ref, out_ref, conv_ref = refs
        take_routes(keep_ref, got_ref, conv_ref)
    else:
        conv_ref, out_ref = refs
    conv = conv_ref[...].reshape(w_ref.shape[0], query_ref.shape[0]).T.astype(jnp.float32)
    mixed_out = (query_ref[...] * conv).astype(jnp.bfloat16)
    out_ref[...] = jnp.dot(mixed_out, w_ref[...], preferred_element_type=jnp.float32).astype(
        jnp.bfloat16
    )


def permute(array, partner):
    pairs = [(i, partner(i)) for i in range(lax.axis_size(seq))]
    return lax.ppermute(array, seq, [(i, j) for i, j in pairs if j != i])


def bf16(*shape):
    return jax.ShapeDtypeStruct(shape, jnp.bfloat16)


def exchange(keep, give, home):
    block, turns = keep.shape[2:], keep.shape[0]
    got = permute(give, lambda i: i ^ 1)
    moved = call(
        merge_body, (bf16(2, 2, *block),) * turns, (keep, got), [pltpu.VMEM] * 2, moved=4 * keep.size
    )
    routes = routes_of(lax.axis_size("chip")) + [(0, 1)]
    moved = [permute(part, lambda i: i ^ 2 * route[i % 2]) for part, route in zip(moved, routes)]
    half = bf16(2 * turns + 1, *block)
    keep, give = call(
        split_body, (half, half), (*moved, home), [pltpu.VMEM] * (turns + 1), moved=4 * keep.size
    )
    return keep, permute(give, lambda i: i ^ 1)


def local(tokens, norm_gain, w_in, short_filter, long_filter, medium_filter, skip_gain, w_out):
    rows, width = tokens.shape
    devices, chips = lax.axis_size(seq), lax.axis_size("chip")
    chans = width // devices
    first, twist, inner = spectral_tables(devices, rows, chans)
    staged = chans % 16 == 0 and chips >= 4
    if chans % 16:
        packed_shape, conv_shape = (width, 2 * rows + lane), (width, rows)
    else:
        packed_shape = (devices, 2 * rows // lane * chans + chans // 2, lane)
        conv_shape = (devices, chans, rows)

    def pieces(shape):
        if not staged:
            return (bf16(*shape),), []
        block, turns = shape[1:], len(routes_of(chips)) + 1
        outs = [bf16(turns, 2, *block)] * 2 + [bf16(2, *block)]
        return tuple(outs), [pltpu.VMEM(shape, jnp.bfloat16)]

    def swap(parts):
        if staged:
            return exchange(*parts)
        (array,) = parts
        blocks = array.reshape(devices, -1, array.shape[-1])
        return (lax.all_to_all(blocks, seq, split_axis=0, concat_axis=0).reshape(array.shape),)

    query = call(
        query_body,
        jax.ShapeDtypeStruct((rows, width), jnp.float32),
        (tokens, norm_gain[None, :], w_in, short_filter),
        [pltpu.VMEM] * 4,
        flops=2 * rows * width * width,
        moved=800_000,
    )
    args = (tokens, norm_gain[None, :], w_in, short_filter, long_filter, medium_filter, skip_gain[None, :])
    args = tuple(pltpu.with_memory_space_constraint(arg, pltpu.HBM) for arg in args)
    outs, packed_scratch = pieces(packed_shape)
    parts = call(
        prepare_body,
        outs,
        args,
        [pltpu.HBM] * len(args),
        packed_scratch
        + [pltpu.VMEM(arg.shape, arg.dtype) for arg in args]
        + [pltpu.SemaphoreType.DMA((len(args),))],
        flops=2 * rows * width * 3 * width,
        moved=1_500_000,
    )
    outs, conv_scratch = pieces(conv_shape)
    parts = swap(parts)
    parts = call(
        functools.partial(convolve_body, chans, short_filter.shape[0] - 1),
        outs,
        (first, twist, inner, *parts),
        [pltpu.VMEM] * (3 + len(parts)),
        packed_scratch + conv_scratch,
        flops=18 * first.shape[0] * width * rows,
        moved=2_000_000,
    )
    parts = swap(parts)
    return call(
        output_body,
        bf16(rows, width),
        (query, w_out, *parts),
        [pltpu.VMEM] * (2 + len(parts)),
        conv_scratch,
        flops=2 * rows * width * width,
        moved=600_000,
    )


def solution(mesh):
    groups, devices = mesh.devices.shape
    split = jax.sharding.Mesh(mesh.devices.reshape(groups, devices // 2, 2), ("groups", *seq))
    rows = P(("groups", *seq), None)
    placed = (rows, P(), P(), P(), P(seq, None), P(), P(), P())
    return jax.shard_map(local, mesh=split, in_specs=placed, out_specs=rows, check_vma=False)
```

```python
import functools
import math

import jax
import jax.numpy as jnp
import numpy as np
from jax import lax
from jax.experimental import pallas as pl
from jax.experimental.pallas import tpu as pltpu
from jax.sharding import PartitionSpec as P

epsilon = 1e-06
edge = 8
lane = 128
seq = ("chip", "core")
rim_step = 2 * edge
vmem_bytes = 32 * 2**20


def whole(space):
    return pl.BlockSpec(memory_space=space)


def call(body, outs, args, spaces, scratch=(), flops=0, moved=0):
    return pl.pallas_call(
        body,
        out_shape=outs,
        in_specs=[whole(space) for space in spaces],
        out_specs=jax.tree.map(lambda _: whole(pltpu.VMEM), outs),
        scratch_shapes=list(scratch),
        compiler_params=pltpu.CompilerParams(vmem_limit_bytes=vmem_bytes),
        cost_estimate=pl.CostEstimate(flops=flops, bytes_accessed=moved, transcendentals=0),
    )(*args)


def spectral_tables(devices, rows, chans):
    full_len = devices * rows
    freqs = 4 * np.arange(devices) + 1
    eye = np.eye(chans)
    angle = 2.0 * math.pi / (4 * devices) * (freqs[:, None] * np.arange(devices)[None, :] % (4 * devices))
    cosine, sine = np.kron(np.cos(angle), eye), np.kron(np.sin(angle), eye)
    first = np.concatenate([cosine, -sine])
    offsets = np.arange(rows)
    twist = 2.0 * math.pi / (4 * full_len) * (freqs[:, None] * offsets[None, :] % (4 * full_len))
    twist = np.concatenate([np.cos(twist), np.sin(twist)])
    if chans % 8:
        twist = np.repeat(twist, chans, axis=0)
    turn = 2.0 * math.pi / rows * (offsets[:, None] * offsets[None, :] % rows)
    inner = np.concatenate([np.cos(turn), np.sin(turn)], axis=1)
    return (
        jnp.asarray(first, jnp.bfloat16),
        jnp.asarray(twist, jnp.float32),
        jnp.asarray(inner, jnp.bfloat16),
    )


def routes_of(chips):
    far = sorted(range(2, chips, 2), key=lambda d: (-d.bit_length(), d))
    return [(d, d + 1) for d in far]


def carried(route, core):
    mine, others = route
    return jnp.where(core == 0, mine, others), jnp.where(core == 0, others, mine)


def put_routes(source_ref, keep_ref, give_ref, near_ref, home_ref):
    chip, core = lax.axis_index("chip"), lax.axis_index("core")

    def blocks(distance):
        return source_ref[pl.ds((chip ^ distance) * 2, 2)]

    for turn, route in enumerate(routes_of(source_ref.shape[0] // 2)):
        own, other = carried(route, core)
        keep_ref[turn] = blocks(own)
        give_ref[turn] = blocks(other)
    near_ref[...] = blocks(1)
    home_ref[...] = blocks(0)


def merge_body(keep_ref, got_ref, *out_refs):
    for turn, out_ref in enumerate(out_refs):
        out_ref[0] = keep_ref[turn]
        out_ref[1] = got_ref[turn]


def split_body(*refs):
    far_refs, (near_ref, home_ref, keep_ref, give_ref) = refs[:-4], refs[-4:]
    core = lax.axis_index("core")
    for out_ref, target in ((keep_ref, core), (give_ref, 1 - core)):
        for turn, far_ref in enumerate(far_refs):
            for sender in range(2):
                out_ref[2 * turn + sender] = far_ref[sender, target]
        out_ref[2 * len(far_refs)] = near_ref[target]
        out_ref[2 * len(far_refs) + 1] = home_ref[target]


def take_routes(keep_ref, got_ref, target_ref):
    chip, core = lax.axis_index("chip"), lax.axis_index("core")
    routes = routes_of(target_ref.shape[0] // 2)
    for turn, route in enumerate(routes):
        own, other = carried(route, core)
        target_ref[(chip ^ own) * 2 + core] = keep_ref[2 * turn]
        target_ref[(chip ^ own) * 2 + 1 - core] = keep_ref[2 * turn + 1]
        target_ref[(chip ^ other) * 2 + 1 - core] = got_ref[2 * turn]
        target_ref[(chip ^ other) * 2 + core] = got_ref[2 * turn + 1]
    for place, distance in ((2 * len(routes), 1), (2 * len(routes) + 1, 0)):
        target_ref[(chip ^ distance) * 2 + core] = keep_ref[place]
        target_ref[(chip ^ distance) * 2 + 1 - core] = got_ref[place]


def normed_of(tokens_ref, gain_ref):
    inputs = tokens_ref[...].astype(jnp.float32)
    mean_sq = jnp.mean(inputs * inputs, axis=-1, keepdims=True)
    return (inputs * lax.rsqrt(mean_sq + epsilon) * gain_ref[...]).astype(jnp.bfloat16)


def projected_of(normed, weights):
    projected = jnp.dot(normed, weights, preferred_element_type=jnp.float32)
    projected = projected.astype(jnp.bfloat16).astype(jnp.float32)
    return jnp.concatenate([projected, jnp.zeros((edge, projected.shape[1]), jnp.float32)])


def short_mix(projected, taps):
    acc = taps[0:1] * projected
    for tap_num in range(1, taps.shape[0]):
        acc = acc + taps[tap_num : tap_num + 1] * pltpu.roll(projected, tap_num, 0)
    return acc


def query_body(tokens_ref, gain_ref, w_ref, short_ref, query_ref):
    rows, width = tokens_ref.shape
    cols = slice(0, width)
    query = short_mix(projected_of(normed_of(tokens_ref, gain_ref), w_ref[:, cols]), short_ref[:, cols])
    query_ref[...] = query[0:rows]
    row = lax.broadcasted_iota(jnp.int32, (edge, width), 0)
    query_ref[0:edge, :] = jnp.where(row < short_ref.shape[0] - 1, 1.0, query[0:edge])


def prepare_body(*refs):
    hbm, outs, held, sems = refs[:7], refs[7:-8], refs[-8:-1], refs[-1]
    staged = len(outs) > 1
    outs, packed_ref = (outs[:-1], outs[-1]) if staged else (outs, outs[0])
    tokens_ref, gain_ref, w_ref, short_ref, long_ref, medium_ref, skip_ref = held
    rows, width = tokens_ref.shape
    is_first = lax.axis_index(seq) == 0
    query_cols, cols = slice(0, width), slice(width, 3 * width)

    def copy_of(index, sem, part=slice(None)):
        return pltpu.make_async_copy(hbm[index].at[:, part], held[index].at[:, part], sems.at[sem])

    copies = [copy_of(0, 0), copy_of(1, 1), copy_of(2, 2, cols), copy_of(3, 3), copy_of(4, 4)]
    copies.append(copy_of(2, 7, query_cols))
    extra = [copy_of(5, 5), copy_of(6, 6)]
    for copy in copies:
        copy.start()

    @pl.when(is_first)
    def _():
        for copy in extra:
            copy.start()

    copies[0].wait()
    copies[1].wait()
    normed = normed_of(tokens_ref, gain_ref)
    copies[2].wait()
    copies[3].wait()
    mixed = short_mix(projected_of(normed, w_ref[:, cols]), short_ref[:, cols])
    key, value = mixed[:, 0:width], mixed[:, width:]
    put_columns(packed_ref, 0, (key[0:rows] * value[0:rows]).astype(jnp.bfloat16).T)
    copies[5].wait()
    rims = [key[0:edge], key[rows:], value[0:edge], value[rows:]]
    for begin, place in ((0, 0), (rows - 2 * edge, 2 * edge)):
        some = projected_of(normed[begin : begin + 2 * edge], w_ref[:, query_cols])
        rims.append(short_mix(some, short_ref[:, query_cols])[place : place + edge])
    rims.append(jnp.zeros((lane - 3 * rim_step, width), jnp.float32))
    put_rim(packed_ref, 2 * rows, jnp.concatenate(rims).T)
    copies[4].wait()

    @pl.when(is_first)
    def _():
        for copy in extra:
            copy.wait()
        med_len = medium_ref.shape[0]
        head_row = lax.broadcasted_iota(jnp.int32, medium_ref.shape, 0)
        direct = jnp.where(head_row == 0, skip_ref[...], 0.0)
        long_ref[0:med_len, :] = long_ref[0:med_len, :] + medium_ref[...] + direct

    put_columns(packed_ref, rows, long_ref[...].astype(jnp.bfloat16).T)
    if staged:
        put_routes(packed_ref, *outs)


def put_columns(packed_ref, begin, values):
    if len(packed_ref.shape) == 2:
        packed_ref[:, begin : begin + values.shape[1]] = values
        return
    devices = packed_ref.shape[0]
    values = values.reshape(devices, -1, values.shape[1])
    chans = values.shape[1]
    for column in range(values.shape[2] // lane):
        place = (begin // lane + column) * chans
        packed_ref[:, place : place + chans, :] = values[:, :, column * lane : (column + 1) * lane]


def put_rim(packed_ref, begin, rim):
    if len(packed_ref.shape) == 2:
        packed_ref[:, begin:] = rim.astype(jnp.bfloat16)
        return
    rim = rim.reshape(packed_ref.shape[0], -1, lane)
    chans = rim.shape[1]
    both = rim[:, : chans // 2] + pltpu.roll(rim[:, chans // 2 :], lane // 2, 2)
    packed_ref[:, begin // lane * chans :, :] = both.astype(jnp.bfloat16)


def take_blocks(packed_ref, chans, rows):
    if chans % 16:
        return packed_ref[:, : 2 * rows], packed_ref[:, 2 * rows :].astype(jnp.float32)
    width = packed_ref.shape[0] * chans
    count = 2 * rows // lane
    columns = [
        packed_ref[:, i * chans : (i + 1) * chans, :].reshape(width, lane) for i in range(count)
    ]
    both = packed_ref[:, count * chans :, :].astype(jnp.float32)
    rim = jnp.concatenate([both, pltpu.roll(both, lane // 2, 2)], axis=1).reshape(width, lane)
    return jnp.concatenate(columns, axis=1), rim


def twist_rows(twist_ref, chans):
    half, rows = twist_ref.shape[0] // 2, twist_ref.shape[1]
    tables = twist_ref[0:half, :], twist_ref[half:, :]
    if chans % 8:
        return tables
    return tuple(
        jnp.broadcast_to(table[:, None, :], (half, chans, rows)).reshape(half * chans, rows)
        for table in tables
    )


def convolve_body(chans, rim_count, first_ref, twist_ref, inner_ref, *refs):
    staged = len(refs) > 2
    if staged:
        keep_ref, got_ref, *outs, packed_ref, out_ref = refs
        take_routes(keep_ref, got_ref, packed_ref)
    else:
        packed_ref, out_ref = refs
    rows = twist_ref.shape[1]
    half = first_ref.shape[0] // 2
    scale = chans / (half * rows)
    values, rim = take_blocks(packed_ref, chans, rows)
    before = jnp.concatenate([jnp.zeros((chans, lane), jnp.float32), rim[:-chans]])
    rim = rim + pltpu.roll(before, lane - edge, 1)
    in_rim = lax.broadcasted_iota(jnp.int32, rim.shape, 1) < rim_count
    rim_signal = (rim * pltpu.roll(rim, lane - rim_step, 1)).astype(jnp.bfloat16)
    rim_query = scale * jnp.where(in_rim, pltpu.roll(rim, lane - 2 * rim_step, 1), 1.0)
    values = jnp.concatenate(
        [jnp.where(in_rim, rim_signal, values[:, 0:lane]), values[:, lane:]], axis=1
    )
    cosine, sine = inner_ref[:, 0:rows], inner_ref[:, rows:]
    inner = jnp.concatenate(
        [jnp.concatenate([cosine, -sine], axis=1), jnp.concatenate([sine, cosine], axis=1)]
    )
    spread = jnp.dot(first_ref[...], values, preferred_element_type=jnp.float32)
    tw_cos, tw_sin = twist_rows(twist_ref, chans)
    turned = []
    for begin in (0, rows):
        real, imag = spread[0:half, begin : begin + rows], spread[half:, begin : begin + rows]
        turned.append([real * tw_cos + imag * tw_sin, imag * tw_cos - real * tw_sin])
    turned = jnp.concatenate([jnp.concatenate(pair, axis=1).astype(jnp.bfloat16) for pair in turned])
    spectra = jnp.dot(turned, inner, preferred_element_type=jnp.float32)
    real, imag = spectra[0:half, 0:rows], spectra[0:half, rows:]
    fil_re, fil_im = spectra[half:, 0:rows], spectra[half:, rows:]
    product = [real * fil_im + imag * fil_re, real * fil_re - imag * fil_im]
    product = jnp.concatenate(product, axis=1).astype(jnp.bfloat16)
    back = jnp.dot(product, inner, preferred_element_type=jnp.float32)
    imag, real = back[:, 0:rows], back[:, rows:]
    turned = jnp.concatenate([real * tw_cos - imag * tw_sin, imag * tw_cos + real * tw_sin])
    last = jnp.concatenate([first_ref[0:half, :].T, first_ref[half:, :].T], axis=1)
    conv = jnp.dot(last, turned.astype(jnp.bfloat16), preferred_element_type=jnp.float32)
    conv = jnp.concatenate([conv[:, 0:lane] * rim_query, conv[:, lane:] * scale], axis=1)
    out_ref[...] = conv.astype(jnp.bfloat16).reshape(out_ref.shape)
    if staged:
        put_routes(out_ref, *outs)


def output_body(query_ref, w_ref, *refs):
    if len(refs) > 2:
        keep_ref, got_ref, out_ref, conv_ref = refs
        take_routes(keep_ref, got_ref, conv_ref)
    else:
        conv_ref, out_ref = refs
    conv = conv_ref[...].reshape(w_ref.shape[0], query_ref.shape[0]).T.astype(jnp.float32)
    mixed_out = (query_ref[...] * conv).astype(jnp.bfloat16)
    out_ref[...] = jnp.dot(mixed_out, w_ref[...], preferred_element_type=jnp.float32).astype(
        jnp.bfloat16
    )


def permute(array, partner):
    return lax.ppermute(array, seq, [(i, partner(i)) for i in range(lax.axis_size(seq))])


def bf16(*shape):
    return jax.ShapeDtypeStruct(shape, jnp.bfloat16)


def exchange(keep, give, near, home):
    block, turns = keep.shape[2:], keep.shape[0]
    got = permute(give, lambda i: i ^ 1)
    near = permute(near, lambda i: i ^ 2)
    far = call(
        merge_body, (bf16(2, 2, *block),) * turns, (keep, got), [pltpu.VMEM] * 2, moved=4 * keep.size
    )
    routes = routes_of(lax.axis_size("chip"))
    far = [permute(part, lambda i: i ^ 2 * route[i % 2]) for part, route in zip(far, routes)]
    half = bf16(2 * turns + 2, *block)
    keep, give = call(
        split_body, (half, half), (*far, near, home), [pltpu.VMEM] * (turns + 2), moved=4 * keep.size
    )
    return keep, permute(give, lambda i: i ^ 1)


def local(tokens, norm_gain, w_in, short_filter, long_filter, medium_filter, skip_gain, w_out):
    rows, width = tokens.shape
    devices, chips = lax.axis_size(seq), lax.axis_size("chip")
    chans = width // devices
    first, twist, inner = spectral_tables(devices, rows, chans)
    staged = chans % 16 == 0 and chips >= 4
    if chans % 16:
        packed_shape, conv_shape = (width, 2 * rows + lane), (width, rows)
    else:
        packed_shape = (devices, 2 * rows // lane * chans + chans // 2, lane)
        conv_shape = (devices, chans, rows)

    def pieces(shape):
        if not staged:
            return (bf16(*shape),), []
        block, turns = shape[1:], len(routes_of(chips))
        outs = [bf16(turns, 2, *block)] * 2 + [bf16(2, *block)] * 2
        return tuple(outs), [pltpu.VMEM(shape, jnp.bfloat16)]

    def swap(parts):
        if staged:
            return exchange(*parts)
        (array,) = parts
        blocks = array.reshape(devices, -1, array.shape[-1])
        return (lax.all_to_all(blocks, seq, split_axis=0, concat_axis=0).reshape(array.shape),)

    query = call(
        query_body,
        jax.ShapeDtypeStruct((rows, width), jnp.float32),
        (tokens, norm_gain[None, :], w_in, short_filter),
        [pltpu.VMEM] * 4,
        flops=2 * rows * width * width,
        moved=800_000,
    )
    args = (tokens, norm_gain[None, :], w_in, short_filter, long_filter, medium_filter, skip_gain[None, :])
    args = tuple(pltpu.with_memory_space_constraint(arg, pltpu.HBM) for arg in args)
    outs, packed_scratch = pieces(packed_shape)
    parts = call(
        prepare_body,
        outs,
        args,
        [pltpu.HBM] * len(args),
        packed_scratch
        + [pltpu.VMEM(arg.shape, arg.dtype) for arg in args]
        + [pltpu.SemaphoreType.DMA((len(args) + 1,))],
        flops=2 * rows * width * 3 * width,
        moved=1_500_000,
    )
    outs, conv_scratch = pieces(conv_shape)
    parts = swap(parts)
    parts = call(
        functools.partial(convolve_body, chans, short_filter.shape[0] - 1),
        outs,
        (first, twist, inner, *parts),
        [pltpu.VMEM] * (3 + len(parts)),
        packed_scratch + conv_scratch,
        flops=18 * first.shape[0] * width * rows,
        moved=2_000_000,
    )
    parts = swap(parts)
    return call(
        output_body,
        bf16(rows, width),
        (query, w_out, *parts),
        [pltpu.VMEM] * (2 + len(parts)),
        conv_scratch,
        flops=2 * rows * width * width,
        moved=600_000,
    )


def solution(mesh):
    groups, devices = mesh.devices.shape
    split = jax.sharding.Mesh(mesh.devices.reshape(groups, devices // 2, 2), ("groups", *seq))
    rows = P(("groups", *seq), None)
    placed = (rows, P(), P(), P(), P(seq, None), P(), P(), P())
    return jax.shard_map(local, mesh=split, in_specs=placed, out_specs=rows, check_vma=False)
```

```python
import functools
import math

import jax
import jax.numpy as jnp
import numpy as np
from jax import lax
from jax.experimental import pallas as pl
from jax.experimental.pallas import tpu as pltpu
from jax.sharding import PartitionSpec as P

epsilon = 1e-06
edge = 8
lane = 128
seq = ("chip", "core")
rim_step = 2 * edge
chan_tile = 16
vmem_bytes = 32 * 2**20


def whole(space):
    return pl.BlockSpec(memory_space=space)


def call(body, outs, args, spaces, scratch=(), flops=0, moved=0):
    return pl.pallas_call(
        body,
        out_shape=outs,
        in_specs=[whole(space) for space in spaces],
        out_specs=jax.tree.map(lambda _: whole(pltpu.VMEM), outs),
        scratch_shapes=list(scratch),
        compiler_params=pltpu.CompilerParams(vmem_limit_bytes=vmem_bytes),
        cost_estimate=pl.CostEstimate(flops=flops, bytes_accessed=moved, transcendentals=0),
    )(*args)


def spectral_tables(devices, rows, chans):
    full_len = devices * rows
    freqs = 4 * np.arange(devices) + 1
    eye = np.eye(chans)
    angle = 2.0 * math.pi / (4 * devices) * (freqs[:, None] * np.arange(devices)[None, :] % (4 * devices))
    cosine, sine = np.kron(np.cos(angle), eye), np.kron(np.sin(angle), eye)
    first = np.concatenate([cosine, -sine])
    offsets = np.arange(rows)
    twist = 2.0 * math.pi / (4 * full_len) * (freqs[:, None] * offsets[None, :] % (4 * full_len))
    twist = np.concatenate([np.cos(twist), np.sin(twist)])
    if chans % 8:
        twist = np.repeat(twist, chans, axis=0)
    turn = 2.0 * math.pi / rows * (offsets[:, None] * offsets[None, :] % rows)
    inner = np.concatenate([np.cos(turn), np.sin(turn)], axis=1)
    return (
        jnp.asarray(first, jnp.bfloat16),
        jnp.asarray(twist, jnp.float32),
        jnp.asarray(inner, jnp.bfloat16),
    )


def routes_of(chips):
    far = sorted(range(2, chips, 2), key=lambda d: (-d.bit_length(), d))
    return [(d, d + 1) for d in far]


def carried(route, core):
    mine, others = route
    return jnp.where(core == 0, mine, others), jnp.where(core == 0, others, mine)


def put_routes(source_ref, rim_ref, keep_ref, give_ref, near_ref, home_ref):
    chip, core = lax.axis_index("chip"), lax.axis_index("core")
    size = source_ref.shape[0] // 2 // (lax.axis_size("chip"))

    def put(out_ref, distance):
        start = pl.multiple_of((chip ^ distance) * 2 * size, 2 * size)
        out_ref[0 : 2 * size, :] = source_ref[pl.ds(start, 2 * size), :]
        if rim_ref is not None:
            out_ref[2 * size :, :] = rim_ref[chip ^ distance]

    for turn, route in enumerate(routes_of(lax.axis_size("chip"))):
        own, other = carried(route, core)
        put(keep_ref.at[turn], own)
        put(give_ref.at[turn], other)
    put(near_ref, 1)
    put(home_ref, 0)


def half_rims(first_ref, second_ref, begin):
    pair = [ref[begin:, :].astype(jnp.float32)[0 : edge // 2] for ref in (first_ref, second_ref)]
    return jnp.concatenate(pair).astype(jnp.bfloat16)


def merge_body(size, keep_ref, got_ref, *out_refs):
    for turn, out_ref in enumerate(out_refs):
        out_ref[0 : 2 * size, :] = keep_ref[turn, 0 : 2 * size, :]
        out_ref[2 * size : 4 * size, :] = got_ref[turn, 0 : 2 * size, :]
        if out_ref.shape[0] > 4 * size:
            out_ref[4 * size :, :] = half_rims(keep_ref.at[turn], got_ref.at[turn], 2 * size)


def split_body(size, *refs):
    far_refs, (near_ref, home_ref, keep_ref, give_ref) = refs[:-4], refs[-4:]
    core = lax.axis_index("core")
    sources = [(far_ref, 2 * sender) for far_ref in far_refs for sender in range(2)]
    sources += [(near_ref, 0), (home_ref, 0)]
    for out_ref, target in ((keep_ref, core), (give_ref, 1 - core)):
        for place, (source_ref, block) in enumerate(sources):
            start = pl.multiple_of((block + target) * size, size)
            out_ref[place * size : (place + 1) * size, :] = source_ref[pl.ds(start, size), :]
        begin = len(sources) * size
        if out_ref.shape[0] > begin:
            for far_ref in far_refs:
                out_ref[begin : begin + edge, :] = far_ref[4 * size :, :]
                begin += edge
            out_ref[begin:, :] = half_rims(near_ref, home_ref, 2 * size)


def take_routes(keep_ref, got_ref, target_ref, rim_ref=None):
    chip, core = lax.axis_index("chip"), lax.axis_index("core")
    routes = routes_of(lax.axis_size("chip"))
    count = 2 * len(routes) + 2
    size = target_ref.shape[0] // (2 * lax.axis_size("chip"))
    places = [(*carried(route, core), sender) for route in routes for sender in range(2)]
    places += [(1, 1, 0), (0, 0, 0)]
    for place, (own, other, sender) in enumerate(places):
        for ref, distance, carrier in ((keep_ref, own, core), (got_ref, other, 1 - core)):
            device = (chip ^ distance) * 2 + (carrier if sender == 0 else 1 - carrier)
            start = pl.multiple_of(device * size, size)
            target_ref[pl.ds(start, size), :] = ref[place * size : (place + 1) * size, :]
            if rim_ref is not None:
                begin = count * size + place // 2 * edge
                rims = ref[begin : begin + edge, :].astype(jnp.float32)
                rim_ref[device, 0 : edge // 2, :] = rims[place % 2 * edge // 2 : (place % 2 + 1) * edge // 2]


def normed_of(tokens_ref, gain_ref):
    inputs = tokens_ref[...].astype(jnp.float32)
    mean_sq = jnp.mean(inputs * inputs, axis=-1, keepdims=True)
    return (inputs * lax.rsqrt(mean_sq + epsilon) * gain_ref[...]).astype(jnp.bfloat16)


def projected_of(normed, weights):
    projected = jnp.dot(normed, weights, preferred_element_type=jnp.float32)
    projected = projected.astype(jnp.bfloat16).astype(jnp.float32)
    return jnp.concatenate([projected, jnp.zeros((edge, projected.shape[1]), jnp.float32)])


def short_mix(projected, taps):
    acc = taps[0:1] * projected
    for tap_num in range(1, taps.shape[0]):
        acc = acc + taps[tap_num : tap_num + 1] * pltpu.roll(projected, tap_num, 0)
    return acc


def query_body(tokens_ref, gain_ref, w_ref, short_ref, query_ref):
    rows, width = tokens_ref.shape
    cols = slice(0, width)
    query = short_mix(projected_of(normed_of(tokens_ref, gain_ref), w_ref[:, cols]), short_ref[:, cols])
    query_ref[...] = query[0:rows]
    row = lax.broadcasted_iota(jnp.int32, (edge, width), 0)
    query_ref[0:edge, :] = jnp.where(row < short_ref.shape[0] - 1, 1.0, query[0:edge])


def prepare_body(*refs):
    hbm, outs, held, sems = refs[:7], refs[7:-8], refs[-8:-1], refs[-1]
    staged = len(outs) > 1
    outs, (packed_ref, rim_ref) = (outs[:-2], outs[-2:]) if staged else (outs, (outs[0], None))
    tokens_ref, gain_ref, w_ref, short_ref, long_ref, medium_ref, skip_ref = held
    rows, width = tokens_ref.shape
    copies = [pltpu.make_async_copy(h, v, sems.at[i]) for i, (h, v) in enumerate(zip(hbm, held))]
    for copy in copies:
        copy.start()
    copies[0].wait()
    copies[1].wait()
    normed = normed_of(tokens_ref, gain_ref)
    copies[2].wait()
    copies[3].wait()
    query_cols, cols = slice(0, width), slice(width, 3 * width)
    mixed = short_mix(projected_of(normed, w_ref[:, cols]), short_ref[:, cols])
    key, value = mixed[:, 0:width], mixed[:, width:]
    put_columns(packed_ref, 0, (key[0:rows] * value[0:rows]).astype(jnp.bfloat16).T)
    rims = [(key[0:edge], key[rows:]), (value[0:edge], value[rows:])]
    ends = []
    for begin, place in ((0, 0), (rows - 2 * edge, 2 * edge)):
        some = projected_of(normed[begin : begin + 2 * edge], w_ref[:, query_cols])
        ends.append(short_mix(some, short_ref[:, query_cols])[place : place + edge])
    put_rim(packed_ref, rim_ref, [*rims, ends])
    for copy in copies[4:]:
        copy.wait()
    med_len = medium_ref.shape[0]
    is_first = jnp.where(lax.axis_index(seq) == 0, 1.0, 0.0)
    head = long_ref[0:med_len, :] + is_first * medium_ref[...]
    head_row = lax.broadcasted_iota(jnp.int32, head.shape, 0)
    head = head + jnp.where(head_row == 0, is_first * skip_ref[...], 0.0)
    taps = jnp.concatenate([head, long_ref[med_len:, :]]).astype(jnp.bfloat16)
    put_columns(packed_ref, rows, taps.T)
    if staged:
        put_routes(packed_ref, rim_ref, *outs)


def put_columns(packed_ref, begin, values):
    if packed_ref.shape[1] > lane:
        packed_ref[:, begin : begin + values.shape[1]] = values
        return
    devices = lax.axis_size(seq)
    chans = values.shape[0] // devices
    size = packed_ref.shape[0] // devices
    for device in range(devices):
        for column in range(values.shape[1] // lane):
            start = device * size + (begin // lane + column) * chans
            packed_ref[start : start + chans, :] = values[
                device * chans : (device + 1) * chans, column * lane : (column + 1) * lane
            ]


def put_rim(packed_ref, rim_ref, parts):
    width = parts[0][0].shape[1]
    if rim_ref is None:
        rows = [row for part in parts for row in part]
        rows.append(jnp.zeros((lane - 3 * rim_step, width), jnp.float32))
        rim = jnp.concatenate(rows).T
        packed_ref[:, packed_ref.shape[1] - lane :] = rim.astype(jnp.bfloat16)
        return
    chips = rim_ref.shape[0]
    span = width // chips
    half = edge // 4
    group = lax.broadcasted_iota(jnp.int32, (edge // 2, lane), 1) // span
    parts = [jnp.concatenate([own[0:half], after[0:half]]) for own, after in parts]
    for chip in range(chips):
        begin = chip * span // lane * lane
        place = chip * span % lane
        rim = jnp.zeros((edge // 2, lane), jnp.float32)
        for index, part in enumerate(parts):
            shift = (index * span - place) % lane
            moved = part[:, begin : begin + lane]
            moved = pltpu.roll(moved, shift, 1) if shift else moved
            rim = jnp.where(group == index, moved, rim)
        rim = jnp.concatenate([rim, jnp.zeros((edge // 2, lane), jnp.float32)])
        rim_ref[chip] = rim.astype(jnp.bfloat16)


def columns_of(packed_ref, chans, rows):
    devices, count = lax.axis_size(seq), 2 * rows // lane
    blocks = packed_ref[...].reshape(devices, count * chans, lane)
    columns = [blocks[:, i * chans : (i + 1) * chans].reshape(-1, lane) for i in range(count)]
    return jnp.concatenate(columns, axis=1)


def rim_of(rim_ref, turned_ref, chans):
    span = 2 * chans
    rim = rim_ref[...].reshape(-1, lane)
    row = lax.broadcasted_iota(jnp.int32, rim.shape, 0)
    column = lax.broadcasted_iota(jnp.int32, rim.shape, 1)
    before = pltpu.roll(rim, edge - edge // 4, 0)
    rim = rim + jnp.where(row < edge, 0.0, before)
    signal = rim * pltpu.roll(rim, lane - span, 1)
    turned_ref[...] = jnp.where(column < span, signal, rim).T
    found = []
    for begin in (0, 2 * span):
        start = pl.multiple_of(begin + lax.axis_index("core") * chans, chans)
        part = turned_ref[pl.ds(start, chans), :]
        blocks = [part] + [pltpu.roll(part, lane - edge * k, 1) for k in range(1, rim_ref.shape[0])]
        found.append(jnp.concatenate(blocks))
    return found


def twist_rows(twist_ref, chans):
    half, rows = twist_ref.shape[0] // 2, twist_ref.shape[1]
    tables = twist_ref[0:half, :], twist_ref[half:, :]
    if chans % 8:
        return tables
    return tuple(
        jnp.broadcast_to(table[:, None, :], (half, chans, rows)).reshape(half * chans, rows)
        for table in tables
    )


def convolve_body(chans, rim_count, first_ref, twist_ref, inner_ref, *refs):
    rows = twist_ref.shape[1]
    half = first_ref.shape[0] // 2
    scale = chans / (half * rows)
    staged = len(refs) > 2
    if staged:
        keep_ref, got_ref, *outs, packed_ref, rim_ref, turned_ref, out_ref = refs
        rim_ref[...] = jnp.zeros_like(rim_ref)
        take_routes(keep_ref, got_ref, packed_ref, rim_ref)
        values = columns_of(packed_ref, chans, rows)
        rim_signal, rim_query = rim_of(rim_ref, turned_ref, chans)
    else:
        packed_ref, out_ref = refs
        values = packed_ref[:, : 2 * rows]
        rim = packed_ref[:, 2 * rows :].astype(jnp.float32)
        before = jnp.concatenate([jnp.zeros((chans, lane), jnp.float32), rim[:-chans]])
        rim = rim + pltpu.roll(before, lane - edge, 1)
        rim_signal = rim * pltpu.roll(rim, lane - rim_step, 1)
        rim_query = pltpu.roll(rim, lane - 2 * rim_step, 1)
    in_rim = lax.broadcasted_iota(jnp.int32, rim_signal.shape, 1) < rim_count
    rim_signal = rim_signal.astype(jnp.bfloat16)
    rim_query = scale * jnp.where(in_rim, rim_query, 1.0)
    values = jnp.concatenate(
        [jnp.where(in_rim, rim_signal, values[:, 0:lane]), values[:, lane:]], axis=1
    )
    cosine, sine = inner_ref[:, 0:rows], inner_ref[:, rows:]
    inner = jnp.concatenate(
        [jnp.concatenate([cosine, -sine], axis=1), jnp.concatenate([sine, cosine], axis=1)]
    )
    spread = jnp.dot(first_ref[...], values, preferred_element_type=jnp.float32)
    tw_cos, tw_sin = twist_rows(twist_ref, chans)
    turned = []
    for begin in (0, rows):
        real, imag = spread[0:half, begin : begin + rows], spread[half:, begin : begin + rows]
        turned.append([real * tw_cos + imag * tw_sin, imag * tw_cos - real * tw_sin])
    turned = jnp.concatenate([jnp.concatenate(pair, axis=1).astype(jnp.bfloat16) for pair in turned])
    spectra = jnp.dot(turned, inner, preferred_element_type=jnp.float32)
    real, imag = spectra[0:half, 0:rows], spectra[0:half, rows:]
    fil_re, fil_im = spectra[half:, 0:rows], spectra[half:, rows:]
    product = [real * fil_im + imag * fil_re, real * fil_re - imag * fil_im]
    product = jnp.concatenate(product, axis=1).astype(jnp.bfloat16)
    back = jnp.dot(product, inner, preferred_element_type=jnp.float32)
    imag, real = back[:, 0:rows], back[:, rows:]
    turned = jnp.concatenate([real * tw_cos - imag * tw_sin, imag * tw_cos + real * tw_sin])
    last = jnp.concatenate([first_ref[0:half, :].T, first_ref[half:, :].T], axis=1)
    conv = jnp.dot(last, turned.astype(jnp.bfloat16), preferred_element_type=jnp.float32)
    conv = jnp.concatenate([conv[:, 0:lane] * rim_query, conv[:, lane:] * scale], axis=1)
    out_ref[...] = conv.astype(jnp.bfloat16)
    if staged:
        put_routes(out_ref, None, *outs)


def output_body(query_ref, w_ref, *refs):
    if len(refs) > 2:
        keep_ref, got_ref, out_ref, conv_ref = refs
        take_routes(keep_ref, got_ref, conv_ref)
    else:
        conv_ref, out_ref = refs
    conv = conv_ref[...].T.astype(jnp.float32)
    mixed_out = (query_ref[...] * conv).astype(jnp.bfloat16)
    out_ref[...] = jnp.dot(mixed_out, w_ref[...], preferred_element_type=jnp.float32).astype(
        jnp.bfloat16
    )


def permute(array, partner):
    return lax.ppermute(array, seq, [(i, partner(i)) for i in range(lax.axis_size(seq))])


def bf16(*shape):
    return jax.ShapeDtypeStruct(shape, jnp.bfloat16)


def exchange(keep, give, near, home):
    turns, size = keep.shape[0], keep.shape[1] // 2 // chan_tile * chan_tile
    lanes, extra = keep.shape[2], keep.shape[1] - 2 * size
    got = permute(give, lambda i: i ^ 1)
    near = permute(near, lambda i: i ^ 2)
    far = call(
        functools.partial(merge_body, size),
        (bf16(4 * size + extra, lanes),) * turns,
        (keep, got),
        [pltpu.VMEM] * 2,
        moved=4 * keep.size,
    )
    routes = routes_of(lax.axis_size("chip"))
    far = [permute(part, lambda i: i ^ 2 * route[i % 2]) for part, route in zip(far, routes)]
    count = 2 * turns + 2
    half = bf16(count * size + count // 2 * extra, lanes)
    keep, give = call(
        functools.partial(split_body, size),
        (half, half),
        (*far, near, home),
        [pltpu.VMEM] * (turns + 2),
        moved=4 * keep.size,
    )
    return keep, permute(give, lambda i: i ^ 1)


def local(tokens, norm_gain, w_in, short_filter, long_filter, medium_filter, skip_gain, w_out):
    rows, width = tokens.shape
    devices, chips = lax.axis_size(seq), lax.axis_size("chip")
    chans = width // devices
    first, twist, inner = spectral_tables(devices, rows, chans)
    staged = chans == chan_tile and chips >= 4 and short_filter.shape[0] <= 3
    if staged:
        packed_shape = (2 * rows // lane * width, lane)
    else:
        packed_shape = (width, 2 * rows + lane)

    def pieces(shape, extra):
        if not staged:
            return (bf16(*shape),)
        size, turns = 2 * shape[0] // devices + extra, len(routes_of(chips))
        return (bf16(turns, size, shape[1]),) * 2 + (bf16(size, shape[1]),) * 2

    def scratch(*shapes):
        return [pltpu.VMEM(*shape) for shape in shapes] if staged else []

    def swap(parts):
        if staged:
            return exchange(*parts)
        (array,) = parts
        blocks = array.reshape(devices, -1, array.shape[-1])
        return (lax.all_to_all(blocks, seq, split_axis=0, concat_axis=0).reshape(array.shape),)

    query = call(
        query_body,
        jax.ShapeDtypeStruct((rows, width), jnp.float32),
        (tokens, norm_gain[None, :], w_in, short_filter),
        [pltpu.VMEM] * 4,
        flops=2 * rows * width * width,
        moved=800_000,
    )
    args = (tokens, norm_gain[None, :], w_in, short_filter, long_filter, medium_filter, skip_gain[None, :])
    args = tuple(pltpu.with_memory_space_constraint(arg, pltpu.HBM) for arg in args)
    packed = (packed_shape, jnp.bfloat16)
    parts = call(
        prepare_body,
        pieces(packed_shape, edge),
        args,
        [pltpu.HBM] * len(args),
        scratch(packed, ((chips, edge, lane), jnp.bfloat16))
        + [pltpu.VMEM(arg.shape, arg.dtype) for arg in args]
        + [pltpu.SemaphoreType.DMA((len(args),))],
        flops=2 * rows * width * 3 * width,
        moved=1_500_000,
    )
    conv = ((width, rows), jnp.bfloat16)
    parts = swap(parts)
    parts = call(
        functools.partial(convolve_body, chans, short_filter.shape[0] - 1),
        pieces((width, rows), 0),
        (first, twist, inner, *parts),
        [pltpu.VMEM] * (3 + len(parts)),
        scratch(packed, ((devices, edge, lane), jnp.float32), ((lane, lane), jnp.float32), conv),
        flops=18 * first.shape[0] * width * rows,
        moved=2_000_000,
    )
    parts = swap(parts)
    return call(
        output_body,
        bf16(rows, width),
        (query, w_out, *parts),
        [pltpu.VMEM] * (2 + len(parts)),
        scratch(conv),
        flops=2 * rows * width * width,
        moved=600_000,
    )


def solution(mesh):
    groups, devices = mesh.devices.shape
    split = jax.sharding.Mesh(mesh.devices.reshape(groups, devices // 2, 2), ("groups", *seq))
    rows = P(("groups", *seq), None)
    placed = (rows, P(), P(), P(), P(seq, None), P(), P(), P())
    return jax.shard_map(local, mesh=split, in_specs=placed, out_specs=rows, check_vma=False)
```

```python
import functools
import math

import jax
import jax.numpy as jnp
import numpy as np
from jax import lax
from jax.experimental import pallas as pl
from jax.experimental.pallas import tpu as pltpu
from jax.sharding import PartitionSpec as P

epsilon = 1e-06
edge = 8
lane = 128
seq = ("chip", "core")
rim_step = 2 * edge
chan_tile = 16
near_pads = 2
vmem_bytes = 32 * 2**20


def whole(space):
    return pl.BlockSpec(memory_space=space)


def call(body, outs, args, spaces, scratch=(), flops=0, moved=0):
    return pl.pallas_call(
        body,
        out_shape=outs,
        in_specs=[whole(space) for space in spaces],
        out_specs=jax.tree.map(lambda _: whole(pltpu.VMEM), outs),
        scratch_shapes=list(scratch),
        compiler_params=pltpu.CompilerParams(vmem_limit_bytes=vmem_bytes),
        cost_estimate=pl.CostEstimate(flops=flops, bytes_accessed=moved, transcendentals=0),
    )(*args)


def spectral_tables(devices, rows, chans):
    full_len = devices * rows
    freqs = 4 * np.arange(devices) + 1
    eye = np.eye(chans)
    angle = 2.0 * math.pi / (4 * devices) * (freqs[:, None] * np.arange(devices)[None, :] % (4 * devices))
    cosine, sine = np.kron(np.cos(angle), eye), np.kron(np.sin(angle), eye)
    first = np.concatenate([cosine, -sine])
    offsets = np.arange(rows)
    twist = 2.0 * math.pi / (4 * full_len) * (freqs[:, None] * offsets[None, :] % (4 * full_len))
    twist = np.concatenate([np.cos(twist), np.sin(twist)])
    if chans % 8:
        twist = np.repeat(twist, chans, axis=0)
    turn = 2.0 * math.pi / rows * (offsets[:, None] * offsets[None, :] % rows)
    inner = np.concatenate([np.cos(turn), np.sin(turn)], axis=1)
    return (
        jnp.asarray(first, jnp.bfloat16),
        jnp.asarray(twist, jnp.float32),
        jnp.asarray(inner, jnp.bfloat16),
    )


def routes_of(chips):
    far = sorted(range(2, chips, 2), key=lambda d: (-d.bit_length(), d))
    return [(d, d + 1) for d in far]


def carried(route, core):
    mine, others = route
    return jnp.where(core == 0, mine, others), jnp.where(core == 0, others, mine)


def put_routes(source_ref, rim_ref, keep_ref, give_ref, near_ref, home_ref):
    chip, core = lax.axis_index("chip"), lax.axis_index("core")
    size = source_ref.shape[0] // 2 // (lax.axis_size("chip"))
    extra = home_ref.shape[0] - 2 * size

    def put(out_ref, distance):
        start = pl.multiple_of((chip ^ distance) * 2 * size, 2 * size)
        out_ref[0 : 2 * size, :] = source_ref[pl.ds(start, 2 * size), :]
        if extra:
            out_ref[2 * size : 2 * size + extra, :] = rim_ref[chip ^ distance]

    for turn, route in enumerate(routes_of(lax.axis_size("chip"))):
        own, other = carried(route, core)
        put(keep_ref.at[turn], own)
        put(give_ref.at[turn], other)
    put(home_ref, 0)
    put(near_ref, 1)
    for begin in range(2 * size + extra, near_ref.shape[0], 2 * size):
        near_ref[begin : begin + 2 * size, :] = home_ref[0 : 2 * size, :]


def half_rims(first_ref, second_ref, begin):
    pair = [ref[begin : begin + edge, :].astype(jnp.float32) for ref in (first_ref, second_ref)]
    pair = [rims[0 : edge // 2] for rims in pair]
    return jnp.concatenate(pair).astype(jnp.bfloat16)


def merge_body(size, keep_ref, got_ref, *out_refs):
    for turn, out_ref in enumerate(out_refs):
        out_ref[0 : 2 * size, :] = keep_ref[turn, 0 : 2 * size, :]
        out_ref[2 * size : 4 * size, :] = got_ref[turn, 0 : 2 * size, :]
        if out_ref.shape[0] > 4 * size:
            out_ref[4 * size :, :] = half_rims(keep_ref.at[turn], got_ref.at[turn], 2 * size)


def split_body(size, *refs):
    far_refs, (near_ref, home_ref, keep_ref, give_ref) = refs[:-4], refs[-4:]
    core = lax.axis_index("core")
    sources = [(far_ref, 2 * sender) for far_ref in far_refs for sender in range(2)]
    sources += [(near_ref, 0), (home_ref, 0)]
    for out_ref, target in ((keep_ref, core), (give_ref, 1 - core)):
        for place, (source_ref, block) in enumerate(sources):
            start = pl.multiple_of((block + target) * size, size)
            out_ref[place * size : (place + 1) * size, :] = source_ref[pl.ds(start, size), :]
        begin = len(sources) * size
        if out_ref.shape[0] > begin:
            for far_ref in far_refs:
                out_ref[begin : begin + edge, :] = far_ref[4 * size :, :]
                begin += edge
            out_ref[begin:, :] = half_rims(near_ref, home_ref, 2 * size)


def take_routes(keep_ref, got_ref, target_ref, rim_ref=None):
    chip, core = lax.axis_index("chip"), lax.axis_index("core")
    routes = routes_of(lax.axis_size("chip"))
    count = 2 * len(routes) + 2
    size = target_ref.shape[0] // (2 * lax.axis_size("chip"))
    places = [(*carried(route, core), sender) for route in routes for sender in range(2)]
    places += [(1, 1, 0), (0, 0, 0)]
    for place, (own, other, sender) in enumerate(places):
        for ref, distance, carrier in ((keep_ref, own, core), (got_ref, other, 1 - core)):
            device = (chip ^ distance) * 2 + (carrier if sender == 0 else 1 - carrier)
            start = pl.multiple_of(device * size, size)
            target_ref[pl.ds(start, size), :] = ref[place * size : (place + 1) * size, :]
            if rim_ref is not None:
                begin = count * size + place // 2 * edge
                rims = ref[begin : begin + edge, :].astype(jnp.float32)
                rim_ref[device, 0 : edge // 2, :] = rims[place % 2 * edge // 2 : (place % 2 + 1) * edge // 2]


def normed_of(tokens_ref, gain_ref):
    inputs = tokens_ref[...].astype(jnp.float32)
    mean_sq = jnp.mean(inputs * inputs, axis=-1, keepdims=True)
    return (inputs * lax.rsqrt(mean_sq + epsilon) * gain_ref[...]).astype(jnp.bfloat16)


def projected_of(normed, weights):
    projected = jnp.dot(normed, weights, preferred_element_type=jnp.float32)
    projected = projected.astype(jnp.bfloat16).astype(jnp.float32)
    return jnp.concatenate([projected, jnp.zeros((edge, projected.shape[1]), jnp.float32)])


def short_mix(projected, taps):
    acc = taps[0:1] * projected
    for tap_num in range(1, taps.shape[0]):
        acc = acc + taps[tap_num : tap_num + 1] * pltpu.roll(projected, tap_num, 0)
    return acc


def query_body(tokens_ref, gain_ref, w_ref, short_ref, query_ref):
    rows, width = tokens_ref.shape
    cols = slice(0, width)
    query = short_mix(projected_of(normed_of(tokens_ref, gain_ref), w_ref[:, cols]), short_ref[:, cols])
    query_ref[...] = query[0:rows]
    row = lax.broadcasted_iota(jnp.int32, (edge, width), 0)
    query_ref[0:edge, :] = jnp.where(row < short_ref.shape[0] - 1, 1.0, query[0:edge])


def prepare_body(*refs):
    hbm, outs, held, sems = refs[:7], refs[7:-8], refs[-8:-1], refs[-1]
    staged = len(outs) > 1
    outs, (packed_ref, rim_ref) = (outs[:-2], outs[-2:]) if staged else (outs, (outs[0], None))
    tokens_ref, gain_ref, w_ref, short_ref, long_ref, medium_ref, skip_ref = held
    rows, width = tokens_ref.shape
    copies = [pltpu.make_async_copy(h, v, sems.at[i]) for i, (h, v) in enumerate(zip(hbm, held))]
    for copy in copies:
        copy.start()
    copies[0].wait()
    copies[1].wait()
    normed = normed_of(tokens_ref, gain_ref)
    copies[2].wait()
    copies[3].wait()
    query_cols, cols = slice(0, width), slice(width, 3 * width)
    mixed = short_mix(projected_of(normed, w_ref[:, cols]), short_ref[:, cols])
    key, value = mixed[:, 0:width], mixed[:, width:]
    put_columns(packed_ref, 0, (key[0:rows] * value[0:rows]).astype(jnp.bfloat16).T)
    rims = [(key[0:edge], key[rows:]), (value[0:edge], value[rows:])]
    ends = []
    for begin, place in ((0, 0), (rows - 2 * edge, 2 * edge)):
        some = projected_of(normed[begin : begin + 2 * edge], w_ref[:, query_cols])
        ends.append(short_mix(some, short_ref[:, query_cols])[place : place + edge])
    put_rim(packed_ref, rim_ref, [*rims, ends])
    for copy in copies[4:]:
        copy.wait()
    med_len = medium_ref.shape[0]
    is_first = jnp.where(lax.axis_index(seq) == 0, 1.0, 0.0)
    head = long_ref[0:med_len, :] + is_first * medium_ref[...]
    head_row = lax.broadcasted_iota(jnp.int32, head.shape, 0)
    head = head + jnp.where(head_row == 0, is_first * skip_ref[...], 0.0)
    taps = jnp.concatenate([head, long_ref[med_len:, :]]).astype(jnp.bfloat16)
    put_columns(packed_ref, rows, taps.T)
    if staged:
        put_routes(packed_ref, rim_ref, *outs)


def put_columns(packed_ref, begin, values):
    if packed_ref.shape[1] > lane:
        packed_ref[:, begin : begin + values.shape[1]] = values
        return
    devices = lax.axis_size(seq)
    chans = values.shape[0] // devices
    size = packed_ref.shape[0] // devices
    for device in range(devices):
        for column in range(values.shape[1] // lane):
            start = device * size + (begin // lane + column) * chans
            packed_ref[start : start + chans, :] = values[
                device * chans : (device + 1) * chans, column * lane : (column + 1) * lane
            ]


def put_rim(packed_ref, rim_ref, parts):
    width = parts[0][0].shape[1]
    if rim_ref is None:
        rows = [row for part in parts for row in part]
        rows.append(jnp.zeros((lane - 3 * rim_step, width), jnp.float32))
        rim = jnp.concatenate(rows).T
        packed_ref[:, packed_ref.shape[1] - lane :] = rim.astype(jnp.bfloat16)
        return
    chips = rim_ref.shape[0]
    span = width // chips
    half = edge // 4
    group = lax.broadcasted_iota(jnp.int32, (edge // 2, lane), 1) // span
    parts = [jnp.concatenate([own[0:half], after[0:half]]) for own, after in parts]
    for chip in range(chips):
        begin = chip * span // lane * lane
        place = chip * span % lane
        rim = jnp.zeros((edge // 2, lane), jnp.float32)
        for index, part in enumerate(parts):
            shift = (index * span - place) % lane
            moved = part[:, begin : begin + lane]
            moved = pltpu.roll(moved, shift, 1) if shift else moved
            rim = jnp.where(group == index, moved, rim)
        rim = jnp.concatenate([rim, jnp.zeros((edge // 2, lane), jnp.float32)])
        rim_ref[chip] = rim.astype(jnp.bfloat16)


def columns_of(packed_ref, chans, rows):
    devices, count = lax.axis_size(seq), 2 * rows // lane
    blocks = packed_ref[...].reshape(devices, count * chans, lane)
    columns = [blocks[:, i * chans : (i + 1) * chans].reshape(-1, lane) for i in range(count)]
    return jnp.concatenate(columns, axis=1)


def rim_of(rim_ref, turned_ref, chans):
    span = 2 * chans
    rim = rim_ref[...].reshape(-1, lane)
    row = lax.broadcasted_iota(jnp.int32, rim.shape, 0)
    column = lax.broadcasted_iota(jnp.int32, rim.shape, 1)
    before = pltpu.roll(rim, edge - edge // 4, 0)
    rim = rim + jnp.where(row < edge, 0.0, before)
    signal = rim * pltpu.roll(rim, lane - span, 1)
    turned_ref[...] = jnp.where(column < span, signal, rim).T
    found = []
    for begin in (0, 2 * span):
        start = pl.multiple_of(begin + lax.axis_index("core") * chans, chans)
        part = turned_ref[pl.ds(start, chans), :]
        blocks = [part] + [pltpu.roll(part, lane - edge * k, 1) for k in range(1, rim_ref.shape[0])]
        found.append(jnp.concatenate(blocks))
    return found


def twist_rows(twist_ref, chans):
    half, rows = twist_ref.shape[0] // 2, twist_ref.shape[1]
    tables = twist_ref[0:half, :], twist_ref[half:, :]
    if chans % 8:
        return tables
    return tuple(
        jnp.broadcast_to(table[:, None, :], (half, chans, rows)).reshape(half * chans, rows)
        for table in tables
    )


def convolve_body(chans, rim_count, first_ref, twist_ref, inner_ref, *refs):
    rows = twist_ref.shape[1]
    half = first_ref.shape[0] // 2
    scale = chans / (half * rows)
    staged = len(refs) > 2
    if staged:
        keep_ref, got_ref, *outs, packed_ref, rim_ref, turned_ref, out_ref = refs
        rim_ref[...] = jnp.zeros_like(rim_ref)
        take_routes(keep_ref, got_ref, packed_ref, rim_ref)
        values = columns_of(packed_ref, chans, rows)
        rim_signal, rim_query = rim_of(rim_ref, turned_ref, chans)
    else:
        packed_ref, out_ref = refs
        values = packed_ref[:, : 2 * rows]
        rim = packed_ref[:, 2 * rows :].astype(jnp.float32)
        before = jnp.concatenate([jnp.zeros((chans, lane), jnp.float32), rim[:-chans]])
        rim = rim + pltpu.roll(before, lane - edge, 1)
        rim_signal = rim * pltpu.roll(rim, lane - rim_step, 1)
        rim_query = pltpu.roll(rim, lane - 2 * rim_step, 1)
    in_rim = lax.broadcasted_iota(jnp.int32, rim_signal.shape, 1) < rim_count
    rim_signal = rim_signal.astype(jnp.bfloat16)
    rim_query = scale * jnp.where(in_rim, rim_query, 1.0)
    values = jnp.concatenate(
        [jnp.where(in_rim, rim_signal, values[:, 0:lane]), values[:, lane:]], axis=1
    )
    cosine, sine = inner_ref[:, 0:rows], inner_ref[:, rows:]
    inner = jnp.concatenate(
        [jnp.concatenate([cosine, -sine], axis=1), jnp.concatenate([sine, cosine], axis=1)]
    )
    spread = jnp.dot(first_ref[...], values, preferred_element_type=jnp.float32)
    tw_cos, tw_sin = twist_rows(twist_ref, chans)
    turned = []
    for begin in (0, rows):
        real, imag = spread[0:half, begin : begin + rows], spread[half:, begin : begin + rows]
        turned.append([real * tw_cos + imag * tw_sin, imag * tw_cos - real * tw_sin])
    turned = jnp.concatenate([jnp.concatenate(pair, axis=1).astype(jnp.bfloat16) for pair in turned])
    spectra = jnp.dot(turned, inner, preferred_element_type=jnp.float32)
    real, imag = spectra[0:half, 0:rows], spectra[0:half, rows:]
    fil_re, fil_im = spectra[half:, 0:rows], spectra[half:, rows:]
    product = [real * fil_im + imag * fil_re, real * fil_re - imag * fil_im]
    product = jnp.concatenate(product, axis=1).astype(jnp.bfloat16)
    back = jnp.dot(product, inner, preferred_element_type=jnp.float32)
    imag, real = back[:, 0:rows], back[:, rows:]
    turned = jnp.concatenate([real * tw_cos - imag * tw_sin, imag * tw_cos + real * tw_sin])
    last = jnp.concatenate([first_ref[0:half, :].T, first_ref[half:, :].T], axis=1)
    conv = jnp.dot(last, turned.astype(jnp.bfloat16), preferred_element_type=jnp.float32)
    conv = jnp.concatenate([conv[:, 0:lane] * rim_query, conv[:, lane:] * scale], axis=1)
    out_ref[...] = conv.astype(jnp.bfloat16)
    if staged:
        put_routes(out_ref, None, *outs)


def output_body(query_ref, w_ref, *refs):
    if len(refs) > 2:
        keep_ref, got_ref, out_ref, conv_ref = refs
        take_routes(keep_ref, got_ref, conv_ref)
    else:
        conv_ref, out_ref = refs
    conv = conv_ref[...].T.astype(jnp.float32)
    mixed_out = (query_ref[...] * conv).astype(jnp.bfloat16)
    out_ref[...] = jnp.dot(mixed_out, w_ref[...], preferred_element_type=jnp.float32).astype(
        jnp.bfloat16
    )


def permute(array, partner):
    return lax.ppermute(array, seq, [(i, partner(i)) for i in range(lax.axis_size(seq))])


def bf16(*shape):
    return jax.ShapeDtypeStruct(shape, jnp.bfloat16)


def exchange(keep, give, near, home):
    turns, size = keep.shape[0], keep.shape[1] // 2 // chan_tile * chan_tile
    lanes, extra = keep.shape[2], keep.shape[1] - 2 * size
    got = permute(give, lambda i: i ^ 1)
    near = permute(near, lambda i: i ^ 2)
    far = call(
        functools.partial(merge_body, size),
        (bf16(4 * size + extra, lanes),) * turns,
        (keep, got),
        [pltpu.VMEM] * 2,
        moved=4 * keep.size,
    )
    routes = routes_of(lax.axis_size("chip"))
    far = [permute(part, lambda i: i ^ 2 * route[i % 2]) for part, route in zip(far, routes)]
    count = 2 * turns + 2
    half = bf16(count * size + count // 2 * extra, lanes)
    keep, give = call(
        functools.partial(split_body, size),
        (half, half),
        (*far, near, home),
        [pltpu.VMEM] * (turns + 2),
        moved=4 * keep.size,
    )
    return keep, permute(give, lambda i: i ^ 1)


def local(tokens, norm_gain, w_in, short_filter, long_filter, medium_filter, skip_gain, w_out):
    rows, width = tokens.shape
    devices, chips = lax.axis_size(seq), lax.axis_size("chip")
    chans = width // devices
    first, twist, inner = spectral_tables(devices, rows, chans)
    staged = chans == chan_tile and chips >= 4 and short_filter.shape[0] <= 3
    if staged:
        packed_shape = (2 * rows // lane * width, lane)
    else:
        packed_shape = (width, 2 * rows + lane)

    def pieces(shape, extra):
        if not staged:
            return (bf16(*shape),)
        size, turns = 2 * shape[0] // devices + extra, len(routes_of(chips))
        near = size + near_pads * (size - extra)
        return (bf16(turns, size, shape[1]),) * 2 + (bf16(near, shape[1]), bf16(size, shape[1]))

    def scratch(*shapes):
        return [pltpu.VMEM(*shape) for shape in shapes] if staged else []

    def swap(parts):
        if staged:
            return exchange(*parts)
        (array,) = parts
        blocks = array.reshape(devices, -1, array.shape[-1])
        return (lax.all_to_all(blocks, seq, split_axis=0, concat_axis=0).reshape(array.shape),)

    query = call(
        query_body,
        jax.ShapeDtypeStruct((rows, width), jnp.float32),
        (tokens, norm_gain[None, :], w_in, short_filter),
        [pltpu.VMEM] * 4,
        flops=2 * rows * width * width,
        moved=800_000,
    )
    args = (tokens, norm_gain[None, :], w_in, short_filter, long_filter, medium_filter, skip_gain[None, :])
    args = tuple(pltpu.with_memory_space_constraint(arg, pltpu.HBM) for arg in args)
    packed = (packed_shape, jnp.bfloat16)
    parts = call(
        prepare_body,
        pieces(packed_shape, edge),
        args,
        [pltpu.HBM] * len(args),
        scratch(packed, ((chips, edge, lane), jnp.bfloat16))
        + [pltpu.VMEM(arg.shape, arg.dtype) for arg in args]
        + [pltpu.SemaphoreType.DMA((len(args),))],
        flops=2 * rows * width * 3 * width,
        moved=1_500_000,
    )
    conv = ((width, rows), jnp.bfloat16)
    parts = swap(parts)
    parts = call(
        functools.partial(convolve_body, chans, short_filter.shape[0] - 1),
        pieces((width, rows), 0),
        (first, twist, inner, *parts),
        [pltpu.VMEM] * (3 + len(parts)),
        scratch(packed, ((devices, edge, lane), jnp.float32), ((lane, lane), jnp.float32), conv),
        flops=18 * first.shape[0] * width * rows,
        moved=2_000_000,
    )
    parts = swap(parts)
    return call(
        output_body,
        bf16(rows, width),
        (query, w_out, *parts),
        [pltpu.VMEM] * (2 + len(parts)),
        scratch(conv),
        flops=2 * rows * width * width,
        moved=600_000,
    )


def solution(mesh):
    groups, devices = mesh.devices.shape
    split = jax.sharding.Mesh(mesh.devices.reshape(groups, devices // 2, 2), ("groups", *seq))
    rows = P(("groups", *seq), None)
    placed = (rows, P(), P(), P(), P(seq, None), P(), P(), P())
    return jax.shard_map(local, mesh=split, in_specs=placed, out_specs=rows, check_vma=False)
```

```python
import functools
import math

import jax
import jax.numpy as jnp
import numpy as np
from jax import lax
from jax.experimental import pallas as pl
from jax.experimental.pallas import tpu as pltpu
from jax.sharding import PartitionSpec as P

epsilon = 1e-06
edge = 8
lane = 128
seq = ("chip", "core")
rim_step = 2 * edge
chan_tile = 16
vmem_bytes = 32 * 2**20


def whole(space):
    return pl.BlockSpec(memory_space=space)


def call(body, outs, args, spaces, scratch=(), flops=0, moved=0, out_space=pltpu.VMEM):
    return pl.pallas_call(
        body,
        out_shape=outs,
        in_specs=[whole(space) for space in spaces],
        out_specs=jax.tree.map(lambda _: whole(out_space), outs),
        scratch_shapes=list(scratch),
        compiler_params=pltpu.CompilerParams(vmem_limit_bytes=vmem_bytes),
        cost_estimate=pl.CostEstimate(flops=flops, bytes_accessed=moved, transcendentals=0),
    )(*args)


def spectral_tables(devices, rows, chans):
    full_len = devices * rows
    freqs = 4 * np.arange(devices) + 1
    eye = np.eye(chans)
    angle = 2.0 * math.pi / (4 * devices) * (freqs[:, None] * np.arange(devices)[None, :] % (4 * devices))
    cosine, sine = np.kron(np.cos(angle), eye), np.kron(np.sin(angle), eye)
    first = np.concatenate([cosine, -sine])
    offsets = np.arange(rows)
    twist = 2.0 * math.pi / (4 * full_len) * (freqs[:, None] * offsets[None, :] % (4 * full_len))
    twist = np.concatenate([np.cos(twist), np.sin(twist)])
    if chans % 8:
        twist = np.repeat(twist, chans, axis=0)
    turn = 2.0 * math.pi / rows * (offsets[:, None] * offsets[None, :] % rows)
    inner = np.concatenate([np.cos(turn), np.sin(turn)], axis=1)
    return (
        jnp.asarray(first, jnp.bfloat16),
        jnp.asarray(twist, jnp.float32),
        jnp.asarray(inner, jnp.bfloat16),
    )


def routes_of(chips):
    far = sorted(range(2, chips, 2), key=lambda d: (-d.bit_length(), d))
    return [(d, d + 1) for d in far]


def carried(route, core):
    mine, others = route
    return jnp.where(core == 0, mine, others), jnp.where(core == 0, others, mine)


def put_routes(source_ref, rim_ref, keep_ref, give_ref, near_ref, home_ref):
    chip, core = lax.axis_index("chip"), lax.axis_index("core")
    size = source_ref.shape[0] // 2 // (lax.axis_size("chip"))
    extra = home_ref.shape[0] - 2 * size

    def put(out_ref, distance):
        start = pl.multiple_of((chip ^ distance) * 2 * size, 2 * size)
        out_ref[0 : 2 * size, :] = source_ref[pl.ds(start, 2 * size), :]
        if extra:
            out_ref[2 * size : 2 * size + extra, :] = rim_ref[chip ^ distance]

    for turn, route in enumerate(routes_of(lax.axis_size("chip"))):
        own, other = carried(route, core)
        put(keep_ref.at[turn], own)
        put(give_ref.at[turn], other)
    put(home_ref, 0)
    put(near_ref, 1)
    begin = 2 * size + extra
    near_ref[begin : begin + 2 * size, :] = home_ref[0 : 2 * size, :]
    near_ref[begin + 2 * size :, :] = home_ref[0:chan_tile, :]


def half_rims(first_ref, second_ref, begin):
    pair = [ref[begin : begin + edge, :].astype(jnp.float32) for ref in (first_ref, second_ref)]
    pair = [rims[0 : edge // 2] for rims in pair]
    return jnp.concatenate(pair).astype(jnp.bfloat16)


def merge_body(size, keep_ref, got_ref, *out_refs):
    for turn, out_ref in enumerate(out_refs):
        out_ref[0 : 2 * size, :] = keep_ref[turn, 0 : 2 * size, :]
        out_ref[2 * size : 4 * size, :] = got_ref[turn, 0 : 2 * size, :]
        if out_ref.shape[0] > 4 * size:
            out_ref[4 * size :, :] = half_rims(keep_ref.at[turn], got_ref.at[turn], 2 * size)


def split_body(size, *refs):
    far_refs, (near_ref, home_ref, keep_ref, give_ref) = refs[:-4], refs[-4:]
    core = lax.axis_index("core")
    sources = [(far_ref, 2 * sender) for far_ref in far_refs for sender in range(2)]
    sources += [(near_ref, 0), (home_ref, 0)]
    for out_ref, target in ((keep_ref, core), (give_ref, 1 - core)):
        for place, (source_ref, block) in enumerate(sources):
            start = pl.multiple_of((block + target) * size, size)
            out_ref[place * size : (place + 1) * size, :] = source_ref[pl.ds(start, size), :]
        begin = len(sources) * size
        if out_ref.shape[0] > begin:
            for far_ref in far_refs:
                out_ref[begin : begin + edge, :] = far_ref[4 * size :, :]
                begin += edge
            out_ref[begin:, :] = half_rims(near_ref, home_ref, 2 * size)


def take_routes(keep_ref, got_ref, target_ref, rim_ref=None):
    chip, core = lax.axis_index("chip"), lax.axis_index("core")
    routes = routes_of(lax.axis_size("chip"))
    count = 2 * len(routes) + 2
    size = target_ref.shape[0] // (2 * lax.axis_size("chip"))
    places = [(*carried(route, core), sender) for route in routes for sender in range(2)]
    places += [(1, 1, 0), (0, 0, 0)]
    for place, (own, other, sender) in enumerate(places):
        for ref, distance, carrier in ((keep_ref, own, core), (got_ref, other, 1 - core)):
            device = (chip ^ distance) * 2 + (carrier if sender == 0 else 1 - carrier)
            start = pl.multiple_of(device * size, size)
            target_ref[pl.ds(start, size), :] = ref[place * size : (place + 1) * size, :]
            if rim_ref is not None:
                begin = count * size + place // 2 * edge
                rims = ref[begin : begin + edge, :].astype(jnp.float32)
                rim_ref[device, 0 : edge // 2, :] = rims[place % 2 * edge // 2 : (place % 2 + 1) * edge // 2]


def normed_of(tokens_ref, gain_ref):
    inputs = tokens_ref[...].astype(jnp.float32)
    mean_sq = jnp.mean(inputs * inputs, axis=-1, keepdims=True)
    return (inputs * lax.rsqrt(mean_sq + epsilon) * gain_ref[...]).astype(jnp.bfloat16)


def projected_of(normed, weights):
    projected = jnp.dot(normed, weights, preferred_element_type=jnp.float32)
    projected = projected.astype(jnp.bfloat16).astype(jnp.float32)
    return jnp.concatenate([projected, jnp.zeros((edge, projected.shape[1]), jnp.float32)])


def short_mix(projected, taps):
    acc = taps[0:1] * projected
    for tap_num in range(1, taps.shape[0]):
        acc = acc + taps[tap_num : tap_num + 1] * pltpu.roll(projected, tap_num, 0)
    return acc


def query_body(tokens_ref, gain_ref, w_ref, short_ref, query_ref):
    rows, width = tokens_ref.shape
    cols = slice(0, width)
    query = short_mix(projected_of(normed_of(tokens_ref, gain_ref), w_ref[:, cols]), short_ref[:, cols])
    query_ref[...] = query[0:rows]
    row = lax.broadcasted_iota(jnp.int32, (edge, width), 0)
    query_ref[0:edge, :] = jnp.where(row < short_ref.shape[0] - 1, 1.0, query[0:edge])


def prepare_body(*refs):
    hbm, outs, held, sems = refs[:7], refs[7:-8], refs[-8:-1], refs[-1]
    staged = len(outs) > 1
    outs, (packed_ref, rim_ref) = (outs[:-2], outs[-2:]) if staged else (outs, (outs[0], None))
    tokens_ref, gain_ref, w_ref, short_ref, long_ref, medium_ref, skip_ref = held
    rows, width = tokens_ref.shape
    copies = [pltpu.make_async_copy(h, v, sems.at[i]) for i, (h, v) in enumerate(zip(hbm, held))]
    is_first = lax.axis_index(seq) == 0
    for copy in copies[:5]:
        copy.start()

    @pl.when(is_first)
    def _():
        for copy in copies[5:]:
            copy.start()

    copies[0].wait()
    copies[1].wait()
    normed = normed_of(tokens_ref, gain_ref)
    copies[2].wait()
    copies[3].wait()
    query_cols, cols = slice(0, width), slice(width, 3 * width)
    mixed = short_mix(projected_of(normed, w_ref[:, cols]), short_ref[:, cols])
    key, value = mixed[:, 0:width], mixed[:, width:]
    put_columns(packed_ref, 0, (key[0:rows] * value[0:rows]).astype(jnp.bfloat16).T)
    rims = [(key[0:edge], key[rows:]), (value[0:edge], value[rows:])]
    ends = []
    for begin, place in ((0, 0), (rows - 2 * edge, 2 * edge)):
        some = projected_of(normed[begin : begin + 2 * edge], w_ref[:, query_cols])
        ends.append(short_mix(some, short_ref[:, query_cols])[place : place + edge])
    put_rim(packed_ref, rim_ref, [*rims, ends])
    copies[4].wait()

    @pl.when(is_first)
    def _():
        for copy in copies[5:]:
            copy.wait()
        med_len = medium_ref.shape[0]
        head_row = lax.broadcasted_iota(jnp.int32, medium_ref.shape, 0)
        direct = jnp.where(head_row == 0, skip_ref[...], 0.0)
        long_ref[0:med_len, :] = long_ref[0:med_len, :] + medium_ref[...] + direct

    put_columns(packed_ref, rows, long_ref[...].astype(jnp.bfloat16).T)
    if staged:
        put_routes(packed_ref, rim_ref, *outs)


def put_columns(packed_ref, begin, values):
    if packed_ref.shape[1] > lane:
        packed_ref[:, begin : begin + values.shape[1]] = values
        return
    devices = lax.axis_size(seq)
    chans = values.shape[0] // devices
    size = packed_ref.shape[0] // devices
    for device in range(devices):
        for column in range(values.shape[1] // lane):
            start = device * size + (begin // lane + column) * chans
            packed_ref[start : start + chans, :] = values[
                device * chans : (device + 1) * chans, column * lane : (column + 1) * lane
            ]


def put_rim(packed_ref, rim_ref, parts):
    width = parts[0][0].shape[1]
    if rim_ref is None:
        rows = [row for part in parts for row in part]
        rows.append(jnp.zeros((lane - 3 * rim_step, width), jnp.float32))
        rim = jnp.concatenate(rows).T
        packed_ref[:, packed_ref.shape[1] - lane :] = rim.astype(jnp.bfloat16)
        return
    chips = rim_ref.shape[0]
    span = width // chips
    half = edge // 4
    group = lax.broadcasted_iota(jnp.int32, (edge // 2, lane), 1) // span
    parts = [jnp.concatenate([own[0:half], after[0:half]]) for own, after in parts]
    for chip in range(chips):
        begin = chip * span // lane * lane
        place = chip * span % lane
        rim = jnp.zeros((edge // 2, lane), jnp.float32)
        for index, part in enumerate(parts):
            shift = (index * span - place) % lane
            moved = part[:, begin : begin + lane]
            moved = pltpu.roll(moved, shift, 1) if shift else moved
            rim = jnp.where(group == index, moved, rim)
        rim = jnp.concatenate([rim, jnp.zeros((edge // 2, lane), jnp.float32)])
        rim_ref[chip] = rim.astype(jnp.bfloat16)


def columns_of(packed_ref, chans, rows):
    devices, count = lax.axis_size(seq), 2 * rows // lane
    blocks = packed_ref[...].reshape(devices, count * chans, lane)
    columns = [blocks[:, i * chans : (i + 1) * chans].reshape(-1, lane) for i in range(count)]
    return jnp.concatenate(columns, axis=1)


def rim_of(rim_ref, turned_ref, chans):
    span = 2 * chans
    rim = rim_ref[...].reshape(-1, lane)
    row = lax.broadcasted_iota(jnp.int32, rim.shape, 0)
    column = lax.broadcasted_iota(jnp.int32, rim.shape, 1)
    before = pltpu.roll(rim, edge - edge // 4, 0)
    rim = rim + jnp.where(row < edge, 0.0, before)
    signal = rim * pltpu.roll(rim, lane - span, 1)
    turned_ref[...] = jnp.where(column < span, signal, rim).T
    found = []
    for begin in (0, 2 * span):
        start = pl.multiple_of(begin + lax.axis_index("core") * chans, chans)
        part = turned_ref[pl.ds(start, chans), :]
        blocks = [part] + [pltpu.roll(part, lane - edge * k, 1) for k in range(1, rim_ref.shape[0])]
        found.append(jnp.concatenate(blocks))
    return found


def twist_rows(twist_ref, chans):
    half, rows = twist_ref.shape[0] // 2, twist_ref.shape[1]
    tables = twist_ref[0:half, :], twist_ref[half:, :]
    if chans % 8:
        return tables
    return tuple(
        jnp.broadcast_to(table[:, None, :], (half, chans, rows)).reshape(half * chans, rows)
        for table in tables
    )


def convolve_body(chans, rim_count, first_ref, twist_ref, inner_ref, *refs):
    rows = twist_ref.shape[1]
    half = first_ref.shape[0] // 2
    scale = chans / (half * rows)
    staged = len(refs) > 2
    if staged:
        keep_ref, got_ref, *outs, packed_ref, rim_ref, turned_ref, out_ref = refs
        rim_ref[...] = jnp.zeros_like(rim_ref)
        take_routes(keep_ref, got_ref, packed_ref, rim_ref)
        values = columns_of(packed_ref, chans, rows)
        rim_signal, rim_query = rim_of(rim_ref, turned_ref, chans)
    else:
        packed_ref, out_ref = refs
        values = packed_ref[:, : 2 * rows]
        rim = packed_ref[:, 2 * rows :].astype(jnp.float32)
        before = jnp.concatenate([jnp.zeros((chans, lane), jnp.float32), rim[:-chans]])
        rim = rim + pltpu.roll(before, lane - edge, 1)
        rim_signal = rim * pltpu.roll(rim, lane - rim_step, 1)
        rim_query = pltpu.roll(rim, lane - 2 * rim_step, 1)
    in_rim = lax.broadcasted_iota(jnp.int32, rim_signal.shape, 1) < rim_count
    rim_signal = rim_signal.astype(jnp.bfloat16)
    rim_query = scale * jnp.where(in_rim, rim_query, 1.0)
    values = jnp.concatenate(
        [jnp.where(in_rim, rim_signal, values[:, 0:lane]), values[:, lane:]], axis=1
    )
    cosine, sine = inner_ref[:, 0:rows], inner_ref[:, rows:]
    inner = jnp.concatenate(
        [jnp.concatenate([cosine, -sine], axis=1), jnp.concatenate([sine, cosine], axis=1)]
    )
    spread = jnp.dot(first_ref[...], values, preferred_element_type=jnp.float32)
    tw_cos, tw_sin = twist_rows(twist_ref, chans)
    turned = []
    for begin in (0, rows):
        real, imag = spread[0:half, begin : begin + rows], spread[half:, begin : begin + rows]
        turned.append([real * tw_cos + imag * tw_sin, imag * tw_cos - real * tw_sin])
    turned = jnp.concatenate([jnp.concatenate(pair, axis=1).astype(jnp.bfloat16) for pair in turned])
    spectra = jnp.dot(turned, inner, preferred_element_type=jnp.float32)
    real, imag = spectra[0:half, 0:rows], spectra[0:half, rows:]
    fil_re, fil_im = spectra[half:, 0:rows], spectra[half:, rows:]
    product = [real * fil_im + imag * fil_re, real * fil_re - imag * fil_im]
    product = jnp.concatenate(product, axis=1).astype(jnp.bfloat16)
    back = jnp.dot(product, inner, preferred_element_type=jnp.float32)
    imag, real = back[:, 0:rows], back[:, rows:]
    turned = jnp.concatenate([real * tw_cos - imag * tw_sin, imag * tw_cos + real * tw_sin])
    last = jnp.concatenate([first_ref[0:half, :].T, first_ref[half:, :].T], axis=1)
    conv = jnp.dot(last, turned.astype(jnp.bfloat16), preferred_element_type=jnp.float32)
    conv = jnp.concatenate([conv[:, 0:lane] * rim_query, conv[:, lane:] * scale], axis=1)
    out_ref[...] = conv.astype(jnp.bfloat16)
    if staged:
        put_routes(out_ref, None, *outs)


def output_body(query_ref, w_ref, *refs):
    if len(refs) > 5:
        keep_ref, got_ref, out_ref, conv_ref, result_ref, sems = refs
        take_routes(keep_ref, got_ref, conv_ref)
    else:
        conv_ref, out_ref, result_ref, sems = refs
    rows = query_ref.shape[0]
    copies = []
    for part in range(2):
        place = slice(part * rows // 2, (part + 1) * rows // 2)
        conv = conv_ref[:, place].T.astype(jnp.float32)
        mixed_out = (query_ref[place, :] * conv).astype(jnp.bfloat16)
        result = jnp.dot(mixed_out, w_ref[...], preferred_element_type=jnp.float32)
        result_ref[place, :] = result.astype(jnp.bfloat16)
        copies.append(pltpu.make_async_copy(result_ref.at[place], out_ref.at[place], sems.at[part]))
        copies[-1].start()
    for copy in copies:
        copy.wait()


def permute(array, partner):
    return lax.ppermute(array, seq, [(i, partner(i)) for i in range(lax.axis_size(seq))])


def bf16(*shape):
    return jax.ShapeDtypeStruct(shape, jnp.bfloat16)


def exchange(keep, give, near, home):
    turns, size = keep.shape[0], keep.shape[1] // 2 // chan_tile * chan_tile
    lanes, extra = keep.shape[2], keep.shape[1] - 2 * size
    got = permute(give, lambda i: i ^ 1)
    near = permute(near, lambda i: i ^ 2)
    far = call(
        functools.partial(merge_body, size),
        (bf16(4 * size + extra, lanes),) * turns,
        (keep, got),
        [pltpu.VMEM] * 2,
        moved=4 * keep.size,
    )
    routes = routes_of(lax.axis_size("chip"))
    far = [permute(part, lambda i: i ^ 2 * route[i % 2]) for part, route in zip(far, routes)]
    count = 2 * turns + 2
    half = bf16(count * size + count // 2 * extra, lanes)
    keep, give = call(
        functools.partial(split_body, size),
        (half, half),
        (*far, near, home),
        [pltpu.VMEM] * (turns + 2),
        moved=4 * keep.size,
    )
    return keep, permute(give, lambda i: i ^ 1)


def local(tokens, norm_gain, w_in, short_filter, long_filter, medium_filter, skip_gain, w_out):
    rows, width = tokens.shape
    devices, chips = lax.axis_size(seq), lax.axis_size("chip")
    chans = width // devices
    first, twist, inner = spectral_tables(devices, rows, chans)
    staged = chans == chan_tile and chips >= 4 and short_filter.shape[0] <= 3
    if staged:
        packed_shape = (2 * rows // lane * width, lane)
    else:
        packed_shape = (width, 2 * rows + lane)

    def pieces(shape, extra):
        if not staged:
            return (bf16(*shape),)
        size, turns = 2 * shape[0] // devices + extra, len(routes_of(chips))
        near = size + size - extra + chan_tile
        return (bf16(turns, size, shape[1]),) * 2 + (bf16(near, shape[1]), bf16(size, shape[1]))

    def scratch(*shapes):
        return [pltpu.VMEM(*shape) for shape in shapes] if staged else []

    def swap(parts):
        if staged:
            return exchange(*parts)
        (array,) = parts
        blocks = array.reshape(devices, -1, array.shape[-1])
        return (lax.all_to_all(blocks, seq, split_axis=0, concat_axis=0).reshape(array.shape),)

    query = call(
        query_body,
        jax.ShapeDtypeStruct((rows, width), jnp.float32),
        (tokens, norm_gain[None, :], w_in, short_filter),
        [pltpu.VMEM] * 4,
        flops=2 * rows * width * width,
        moved=800_000,
    )
    args = (tokens, norm_gain[None, :], w_in, short_filter, long_filter, medium_filter, skip_gain[None, :])
    args = tuple(pltpu.with_memory_space_constraint(arg, pltpu.HBM) for arg in args)
    packed = (packed_shape, jnp.bfloat16)
    parts = call(
        prepare_body,
        pieces(packed_shape, edge),
        args,
        [pltpu.HBM] * len(args),
        scratch(packed, ((chips, edge, lane), jnp.bfloat16))
        + [pltpu.VMEM(arg.shape, arg.dtype) for arg in args]
        + [pltpu.SemaphoreType.DMA((len(args),))],
        flops=2 * rows * width * 3 * width,
        moved=1_500_000,
    )
    conv = ((width, rows), jnp.bfloat16)
    parts = swap(parts)
    parts = call(
        functools.partial(convolve_body, chans, short_filter.shape[0] - 1),
        pieces((width, rows), 0),
        (first, twist, inner, *parts),
        [pltpu.VMEM] * (3 + len(parts)),
        scratch(packed, ((devices, edge, lane), jnp.float32), ((lane, lane), jnp.float32), conv),
        flops=18 * first.shape[0] * width * rows,
        moved=2_000_000,
    )
    parts = swap(parts)
    return call(
        output_body,
        bf16(rows, width),
        (query, w_out, *parts),
        [pltpu.VMEM] * (2 + len(parts)),
        scratch(conv) + [pltpu.VMEM((rows, width), jnp.bfloat16), pltpu.SemaphoreType.DMA((2,))],
        flops=2 * rows * width * width,
        moved=600_000,
        out_space=pltpu.HBM,
    )


def solution(mesh):
    groups, devices = mesh.devices.shape
    split = jax.sharding.Mesh(mesh.devices.reshape(groups, devices // 2, 2), ("groups", *seq))
    rows = P(("groups", *seq), None)
    placed = (rows, P(), P(), P(), P(seq, None), P(), P(), P())
    return jax.shard_map(local, mesh=split, in_specs=placed, out_specs=rows, check_vma=False)
```

```python
import functools
import math

import jax
import jax.numpy as jnp
import numpy as np
from jax import lax
from jax.experimental import pallas as pl
from jax.experimental.pallas import tpu as pltpu
from jax.sharding import PartitionSpec as P

epsilon = 1e-06
edge = 8
lane = 128
seq = ("chip", "core")
rim_step = 2 * edge
chan_tile = 16
vmem_bytes = 32 * 2**20


def whole(space):
    return pl.BlockSpec(memory_space=space)


def call(body, outs, args, spaces, scratch=(), flops=0, moved=0):
    return pl.pallas_call(
        body,
        out_shape=outs,
        in_specs=[whole(space) for space in spaces],
        out_specs=jax.tree.map(lambda _: whole(pltpu.VMEM), outs),
        scratch_shapes=list(scratch),
        compiler_params=pltpu.CompilerParams(vmem_limit_bytes=vmem_bytes),
        cost_estimate=pl.CostEstimate(flops=flops, bytes_accessed=moved, transcendentals=0),
    )(*args)


def spectral_tables(devices, rows, chans):
    full_len = devices * rows
    freqs = 4 * np.arange(devices) + 1
    eye = np.eye(chans)
    angle = 2.0 * math.pi / (4 * devices) * (freqs[:, None] * np.arange(devices)[None, :] % (4 * devices))
    cosine, sine = np.kron(np.cos(angle), eye), np.kron(np.sin(angle), eye)
    first = np.concatenate([cosine, -sine])
    offsets = np.arange(rows)
    twist = 2.0 * math.pi / (4 * full_len) * (freqs[:, None] * offsets[None, :] % (4 * full_len))
    twist = np.concatenate([np.cos(twist), np.sin(twist)])
    if chans % 8:
        twist = np.repeat(twist, chans, axis=0)
    turn = 2.0 * math.pi / rows * (offsets[:, None] * offsets[None, :] % rows)
    inner = np.concatenate([np.cos(turn), np.sin(turn)], axis=1)
    return (
        jnp.asarray(first, jnp.bfloat16),
        jnp.asarray(twist, jnp.float32),
        jnp.asarray(inner, jnp.bfloat16),
    )


def routes_of(chips, forward):
    far = sorted(range(2, chips, 2), key=lambda d: (-d.bit_length(), d))
    if forward:
        far = far[:1] + far[:0:-1]
    return [(d, d + 1) for d in far]


def carried(route, core):
    mine, others = route
    return jnp.where(core == 0, mine, others), jnp.where(core == 0, others, mine)


def put_routes(source_ref, rim_ref, keep_ref, give_ref, near_ref, home_ref):
    chip, core = lax.axis_index("chip"), lax.axis_index("core")
    size = source_ref.shape[0] // 2 // (lax.axis_size("chip"))
    extra = home_ref.shape[0] - 2 * size

    def put(out_ref, distance):
        start = pl.multiple_of((chip ^ distance) * 2 * size, 2 * size)
        out_ref[0 : 2 * size, :] = source_ref[pl.ds(start, 2 * size), :]
        if extra:
            out_ref[2 * size : 2 * size + extra, :] = rim_ref[chip ^ distance]

    for turn, route in enumerate(routes_of(lax.axis_size("chip"), extra > 0)):
        own, other = carried(route, core)
        put(keep_ref.at[turn], own)
        put(give_ref.at[turn], other)
    put(home_ref, 0)
    put(near_ref, 1)
    begin = 2 * size + extra
    near_ref[begin : begin + 2 * size, :] = home_ref[0 : 2 * size, :]
    near_ref[begin + 2 * size :, :] = home_ref[0:chan_tile, :]


def half_rims(first_ref, second_ref, begin):
    pair = [ref[begin : begin + edge, :].astype(jnp.float32) for ref in (first_ref, second_ref)]
    pair = [rims[0 : edge // 2] for rims in pair]
    return jnp.concatenate(pair).astype(jnp.bfloat16)


def merge_body(size, keep_ref, got_ref, *out_refs):
    for turn, out_ref in enumerate(out_refs):
        out_ref[0 : 2 * size, :] = keep_ref[turn, 0 : 2 * size, :]
        out_ref[2 * size : 4 * size, :] = got_ref[turn, 0 : 2 * size, :]
        if out_ref.shape[0] > 4 * size:
            out_ref[4 * size :, :] = half_rims(keep_ref.at[turn], got_ref.at[turn], 2 * size)


def split_body(size, *refs):
    far_refs, (near_ref, home_ref, keep_ref, give_ref) = refs[:-4], refs[-4:]
    core = lax.axis_index("core")
    sources = [(far_ref, 2 * sender) for far_ref in far_refs for sender in range(2)]
    sources += [(near_ref, 0), (home_ref, 0)]
    for out_ref, target in ((keep_ref, core), (give_ref, 1 - core)):
        for place, (source_ref, block) in enumerate(sources):
            start = pl.multiple_of((block + target) * size, size)
            out_ref[place * size : (place + 1) * size, :] = source_ref[pl.ds(start, size), :]
        begin = len(sources) * size
        if out_ref.shape[0] > begin:
            for far_ref in far_refs:
                out_ref[begin : begin + edge, :] = far_ref[4 * size :, :]
                begin += edge
            out_ref[begin:, :] = half_rims(near_ref, home_ref, 2 * size)


def take_routes(keep_ref, got_ref, target_ref, rim_ref=None):
    chip, core = lax.axis_index("chip"), lax.axis_index("core")
    routes = routes_of(lax.axis_size("chip"), rim_ref is not None)
    count = 2 * len(routes) + 2
    size = target_ref.shape[0] // (2 * lax.axis_size("chip"))
    places = [(*carried(route, core), sender) for route in routes for sender in range(2)]
    places += [(1, 1, 0), (0, 0, 0)]
    for place, (own, other, sender) in enumerate(places):
        for ref, distance, carrier in ((keep_ref, own, core), (got_ref, other, 1 - core)):
            device = (chip ^ distance) * 2 + (carrier if sender == 0 else 1 - carrier)
            start = pl.multiple_of(device * size, size)
            target_ref[pl.ds(start, size), :] = ref[place * size : (place + 1) * size, :]
            if rim_ref is not None:
                begin = count * size + place // 2 * edge
                rims = ref[begin : begin + edge, :].astype(jnp.float32)
                rim_ref[device, 0 : edge // 2, :] = rims[place % 2 * edge // 2 : (place % 2 + 1) * edge // 2]


def normed_of(tokens_ref, gain_ref):
    inputs = tokens_ref[...].astype(jnp.float32)
    mean_sq = jnp.mean(inputs * inputs, axis=-1, keepdims=True)
    return (inputs * lax.rsqrt(mean_sq + epsilon) * gain_ref[...]).astype(jnp.bfloat16)


def projected_of(normed, weights):
    projected = jnp.dot(normed, weights, preferred_element_type=jnp.float32)
    projected = projected.astype(jnp.bfloat16).astype(jnp.float32)
    return jnp.concatenate([projected, jnp.zeros((edge, projected.shape[1]), jnp.float32)])


def short_mix(projected, taps):
    acc = taps[0:1] * projected
    for tap_num in range(1, taps.shape[0]):
        acc = acc + taps[tap_num : tap_num + 1] * pltpu.roll(projected, tap_num, 0)
    return acc


def query_body(tokens_ref, gain_ref, w_ref, short_ref, query_ref):
    rows, width = tokens_ref.shape
    cols = slice(0, width)
    query = short_mix(projected_of(normed_of(tokens_ref, gain_ref), w_ref[:, cols]), short_ref[:, cols])
    query_ref[...] = query[0:rows]
    row = lax.broadcasted_iota(jnp.int32, (edge, width), 0)
    query_ref[0:edge, :] = jnp.where(row < short_ref.shape[0] - 1, 1.0, query[0:edge])


def prepare_body(*refs):
    hbm, outs, held, sems = refs[:7], refs[7:-8], refs[-8:-1], refs[-1]
    staged = len(outs) > 1
    outs, (packed_ref, rim_ref) = (outs[:-2], outs[-2:]) if staged else (outs, (outs[0], None))
    tokens_ref, gain_ref, w_ref, short_ref, long_ref, medium_ref, skip_ref = held
    rows, width = tokens_ref.shape
    copies = [pltpu.make_async_copy(h, v, sems.at[i]) for i, (h, v) in enumerate(zip(hbm, held))]
    for copy in copies:
        copy.start()
    copies[0].wait()
    copies[1].wait()
    normed = normed_of(tokens_ref, gain_ref)
    copies[2].wait()
    copies[3].wait()
    query_cols, cols = slice(0, width), slice(width, 3 * width)
    mixed = short_mix(projected_of(normed, w_ref[:, cols]), short_ref[:, cols])
    key, value = mixed[:, 0:width], mixed[:, width:]
    put_columns(packed_ref, 0, (key[0:rows] * value[0:rows]).astype(jnp.bfloat16).T)
    rims = [(key[0:edge], key[rows:]), (value[0:edge], value[rows:])]
    some = jnp.concatenate([normed[0 : 2 * edge], normed[rows - 2 * edge :]])
    some = short_mix(projected_of(some, w_ref[:, query_cols]), short_ref[:, query_cols])
    put_rim(packed_ref, rim_ref, [*rims, (some[0:edge], some[4 * edge :])])
    for copy in copies[4:]:
        copy.wait()
    med_len = medium_ref.shape[0]
    is_first = jnp.where(lax.axis_index(seq) == 0, 1.0, 0.0)
    head = long_ref[0:med_len, :] + is_first * medium_ref[...]
    head_row = lax.broadcasted_iota(jnp.int32, head.shape, 0)
    head = head + jnp.where(head_row == 0, is_first * skip_ref[...], 0.0)
    taps = jnp.concatenate([head, long_ref[med_len:, :]]).astype(jnp.bfloat16)
    put_columns(packed_ref, rows, taps.T)
    if staged:
        put_routes(packed_ref, rim_ref, *outs)


def put_columns(packed_ref, begin, values):
    if packed_ref.shape[1] > lane:
        packed_ref[:, begin : begin + values.shape[1]] = values
        return
    devices = lax.axis_size(seq)
    chans = values.shape[0] // devices
    size = packed_ref.shape[0] // devices
    for device in range(devices):
        for column in range(values.shape[1] // lane):
            start = device * size + (begin // lane + column) * chans
            packed_ref[start : start + chans, :] = values[
                device * chans : (device + 1) * chans, column * lane : (column + 1) * lane
            ]


def put_rim(packed_ref, rim_ref, parts):
    width = parts[0][0].shape[1]
    if rim_ref is None:
        rows = [row for part in parts for row in part]
        rows.append(jnp.zeros((lane - 3 * rim_step, width), jnp.float32))
        rim = jnp.concatenate(rows).T
        packed_ref[:, packed_ref.shape[1] - lane :] = rim.astype(jnp.bfloat16)
        return
    chips = rim_ref.shape[0]
    span = width // chips
    half = edge // 4
    group = lax.broadcasted_iota(jnp.int32, (edge // 2, lane), 1) // span
    parts = [jnp.concatenate([own[0:half], after[0:half]]) for own, after in parts]
    for chip in range(chips):
        begin = chip * span // lane * lane
        place = chip * span % lane
        rim = jnp.zeros((edge // 2, lane), jnp.float32)
        for index, part in enumerate(parts):
            shift = (index * span - place) % lane
            moved = part[:, begin : begin + lane]
            moved = pltpu.roll(moved, shift, 1) if shift else moved
            rim = jnp.where(group == index, moved, rim)
        rim = jnp.concatenate([rim, jnp.zeros((edge // 2, lane), jnp.float32)])
        rim_ref[chip] = rim.astype(jnp.bfloat16)


def columns_of(packed_ref, chans, rows):
    devices, count = lax.axis_size(seq), 2 * rows // lane
    blocks = packed_ref[...].reshape(devices, count * chans, lane)
    columns = [blocks[:, i * chans : (i + 1) * chans].reshape(-1, lane) for i in range(count)]
    return jnp.concatenate(columns, axis=1)


def rim_of(rim_ref, turned_ref, chans):
    span = 2 * chans
    rim = rim_ref[...].reshape(-1, lane)
    row = lax.broadcasted_iota(jnp.int32, rim.shape, 0)
    column = lax.broadcasted_iota(jnp.int32, rim.shape, 1)
    before = pltpu.roll(rim, edge - edge // 4, 0)
    rim = rim + jnp.where(row < edge, 0.0, before)
    signal = rim * pltpu.roll(rim, lane - span, 1)
    turned_ref[...] = jnp.where(column < span, signal, rim).T
    found = []
    for begin in (0, 2 * span):
        start = pl.multiple_of(begin + lax.axis_index("core") * chans, chans)
        part = turned_ref[pl.ds(start, chans), :]
        blocks = [part] + [pltpu.roll(part, lane - edge * k, 1) for k in range(1, rim_ref.shape[0])]
        found.append(jnp.concatenate(blocks))
    return found


def twist_rows(twist_ref, chans):
    half, rows = twist_ref.shape[0] // 2, twist_ref.shape[1]
    tables = twist_ref[0:half, :], twist_ref[half:, :]
    if chans % 8:
        return tables
    return tuple(
        jnp.broadcast_to(table[:, None, :], (half, chans, rows)).reshape(half * chans, rows)
        for table in tables
    )


def convolve_body(chans, rim_count, first_ref, twist_ref, inner_ref, *refs):
    rows = twist_ref.shape[1]
    half = first_ref.shape[0] // 2
    scale = chans / (half * rows)
    staged = len(refs) > 2
    if staged:
        keep_ref, got_ref, *outs, packed_ref, rim_ref, turned_ref, out_ref = refs
        rim_ref[...] = jnp.zeros_like(rim_ref)
        take_routes(keep_ref, got_ref, packed_ref, rim_ref)
        values = columns_of(packed_ref, chans, rows)
        rim_signal, rim_query = rim_of(rim_ref, turned_ref, chans)
    else:
        packed_ref, out_ref = refs
        values = packed_ref[:, : 2 * rows]
        rim = packed_ref[:, 2 * rows :].astype(jnp.float32)
        before = jnp.concatenate([jnp.zeros((chans, lane), jnp.float32), rim[:-chans]])
        rim = rim + pltpu.roll(before, lane - edge, 1)
        rim_signal = rim * pltpu.roll(rim, lane - rim_step, 1)
        rim_query = pltpu.roll(rim, lane - 2 * rim_step, 1)
    in_rim = lax.broadcasted_iota(jnp.int32, rim_signal.shape, 1) < rim_count
    rim_signal = rim_signal.astype(jnp.bfloat16)
    rim_query = scale * jnp.where(in_rim, rim_query, 1.0)
    values = jnp.concatenate(
        [jnp.where(in_rim, rim_signal, values[:, 0:lane]), values[:, lane:]], axis=1
    )
    cosine, sine = inner_ref[:, 0:rows], inner_ref[:, rows:]
    inner = jnp.concatenate(
        [jnp.concatenate([cosine, -sine], axis=1), jnp.concatenate([sine, cosine], axis=1)]
    )
    spread = jnp.dot(first_ref[...], values, preferred_element_type=jnp.float32)
    tw_cos, tw_sin = twist_rows(twist_ref, chans)
    turned = []
    for begin in (0, rows):
        real, imag = spread[0:half, begin : begin + rows], spread[half:, begin : begin + rows]
        turned.append([real * tw_cos + imag * tw_sin, imag * tw_cos - real * tw_sin])
    turned = jnp.concatenate([jnp.concatenate(pair, axis=1).astype(jnp.bfloat16) for pair in turned])
    spectra = jnp.dot(turned, inner, preferred_element_type=jnp.float32)
    real, imag = spectra[0:half, 0:rows], spectra[0:half, rows:]
    fil_re, fil_im = spectra[half:, 0:rows], spectra[half:, rows:]
    product = [real * fil_im + imag * fil_re, real * fil_re - imag * fil_im]
    product = jnp.concatenate(product, axis=1).astype(jnp.bfloat16)
    back = jnp.dot(product, inner, preferred_element_type=jnp.float32)
    imag, real = back[:, 0:rows], back[:, rows:]
    turned = jnp.concatenate([real * tw_cos - imag * tw_sin, imag * tw_cos + real * tw_sin])
    last = jnp.concatenate([first_ref[0:half, :].T, first_ref[half:, :].T], axis=1)
    conv = jnp.dot(last, turned.astype(jnp.bfloat16), preferred_element_type=jnp.float32)
    conv = jnp.concatenate([conv[:, 0:lane] * rim_query, conv[:, lane:] * scale], axis=1)
    out_ref[...] = conv.astype(jnp.bfloat16)
    if staged:
        put_routes(out_ref, None, *outs)


def output_body(query_ref, w_ref, *refs):
    if len(refs) > 2:
        keep_ref, got_ref, out_ref, conv_ref = refs
        take_routes(keep_ref, got_ref, conv_ref)
    else:
        conv_ref, out_ref = refs
    conv = conv_ref[...].T.astype(jnp.float32)
    mixed_out = (query_ref[...] * conv).astype(jnp.bfloat16)
    out_ref[...] = jnp.dot(mixed_out, w_ref[...], preferred_element_type=jnp.float32).astype(
        jnp.bfloat16
    )


def permute(array, partner):
    return lax.ppermute(array, seq, [(i, partner(i)) for i in range(lax.axis_size(seq))])


def bf16(*shape):
    return jax.ShapeDtypeStruct(shape, jnp.bfloat16)


def exchange(keep, give, near, home):
    turns, size = keep.shape[0], keep.shape[1] // 2 // chan_tile * chan_tile
    lanes, extra = keep.shape[2], keep.shape[1] - 2 * size
    got = permute(give, lambda i: i ^ 1)
    near = permute(near, lambda i: i ^ 2)
    far = call(
        functools.partial(merge_body, size),
        (bf16(4 * size + extra, lanes),) * turns,
        (keep, got),
        [pltpu.VMEM] * 2,
        moved=4 * keep.size,
    )
    routes = routes_of(lax.axis_size("chip"), extra > 0)
    far = [permute(part, lambda i: i ^ 2 * route[i % 2]) for part, route in zip(far, routes)]
    count = 2 * turns + 2
    half = bf16(count * size + count // 2 * extra, lanes)
    keep, give = call(
        functools.partial(split_body, size),
        (half, half),
        (*far, near, home),
        [pltpu.VMEM] * (turns + 2),
        moved=4 * keep.size,
    )
    return keep, permute(give, lambda i: i ^ 1)


def local(tokens, norm_gain, w_in, short_filter, long_filter, medium_filter, skip_gain, w_out):
    rows, width = tokens.shape
    devices, chips = lax.axis_size(seq), lax.axis_size("chip")
    chans = width // devices
    first, twist, inner = spectral_tables(devices, rows, chans)
    staged = chans == chan_tile and chips >= 4 and short_filter.shape[0] <= 3
    if staged:
        packed_shape = (2 * rows // lane * width, lane)
    else:
        packed_shape = (width, 2 * rows + lane)

    def pieces(shape, extra):
        if not staged:
            return (bf16(*shape),)
        size, turns = 2 * shape[0] // devices + extra, chips // 2 - 1
        near = size + size - extra + chan_tile
        return (bf16(turns, size, shape[1]),) * 2 + (bf16(near, shape[1]), bf16(size, shape[1]))

    def scratch(*shapes):
        return [pltpu.VMEM(*shape) for shape in shapes] if staged else []

    def swap(parts):
        if staged:
            return exchange(*parts)
        (array,) = parts
        blocks = array.reshape(devices, -1, array.shape[-1])
        return (lax.all_to_all(blocks, seq, split_axis=0, concat_axis=0).reshape(array.shape),)

    query = call(
        query_body,
        jax.ShapeDtypeStruct((rows, width), jnp.float32),
        (tokens, norm_gain[None, :], w_in, short_filter),
        [pltpu.VMEM] * 4,
        flops=2 * rows * width * width,
        moved=800_000,
    )
    args = (tokens, norm_gain[None, :], w_in, short_filter, long_filter, medium_filter, skip_gain[None, :])
    args = tuple(pltpu.with_memory_space_constraint(arg, pltpu.HBM) for arg in args)
    packed = (packed_shape, jnp.bfloat16)
    parts = call(
        prepare_body,
        pieces(packed_shape, edge),
        args,
        [pltpu.HBM] * len(args),
        scratch(packed, ((chips, edge, lane), jnp.bfloat16))
        + [pltpu.VMEM(arg.shape, arg.dtype) for arg in args]
        + [pltpu.SemaphoreType.DMA((len(args),))],
        flops=2 * rows * width * 3 * width,
        moved=1_500_000,
    )
    conv = ((width, rows), jnp.bfloat16)
    parts = swap(parts)
    parts = call(
        functools.partial(convolve_body, chans, short_filter.shape[0] - 1),
        pieces((width, rows), 0),
        (first, twist, inner, *parts),
        [pltpu.VMEM] * (3 + len(parts)),
        scratch(packed, ((devices, edge, lane), jnp.float32), ((lane, lane), jnp.float32), conv),
        flops=18 * first.shape[0] * width * rows,
        moved=2_000_000,
    )
    parts = swap(parts)
    return call(
        output_body,
        bf16(rows, width),
        (query, w_out, *parts),
        [pltpu.VMEM] * (2 + len(parts)),
        scratch(conv),
        flops=2 * rows * width * width,
        moved=600_000,
    )


def solution(mesh):
    groups, devices = mesh.devices.shape
    split = jax.sharding.Mesh(mesh.devices.reshape(groups, devices // 2, 2), ("groups", *seq))
    rows = P(("groups", *seq), None)
    placed = (rows, P(), P(), P(), P(seq, None), P(), P(), P())
    return jax.shard_map(local, mesh=split, in_specs=placed, out_specs=rows, check_vma=False)
```

```python
import functools
import math

import jax
import jax.numpy as jnp
import numpy as np
from jax import lax
from jax.experimental import pallas as pl
from jax.experimental.pallas import tpu as pltpu
from jax.sharding import PartitionSpec as P

epsilon = 1e-06
edge = 8
lane = 128
seq = ("chip", "core")
rim_step = 2 * edge
chan_tile = 16
vmem_bytes = 32 * 2**20


def whole(space):
    return pl.BlockSpec(memory_space=space)


def call(body, outs, args, spaces, scratch=(), flops=0, moved=0):
    return pl.pallas_call(
        body,
        out_shape=outs,
        in_specs=[whole(space) for space in spaces],
        out_specs=jax.tree.map(lambda _: whole(pltpu.VMEM), outs),
        scratch_shapes=list(scratch),
        compiler_params=pltpu.CompilerParams(vmem_limit_bytes=vmem_bytes),
        cost_estimate=pl.CostEstimate(flops=flops, bytes_accessed=moved, transcendentals=0),
    )(*args)


def spectral_tables(devices, rows, chans):
    full_len = devices * rows
    freqs = 4 * np.arange(devices) + 1
    eye = np.eye(chans)
    angle = 2.0 * math.pi / (4 * devices) * (freqs[:, None] * np.arange(devices)[None, :] % (4 * devices))
    cosine, sine = np.kron(np.cos(angle), eye), np.kron(np.sin(angle), eye)
    first = np.concatenate([cosine, -sine])
    offsets = np.arange(rows)
    twist = 2.0 * math.pi / (4 * full_len) * (freqs[:, None] * offsets[None, :] % (4 * full_len))
    twist = np.concatenate([np.cos(twist), np.sin(twist)])
    if chans % 8:
        twist = np.repeat(twist, chans, axis=0)
    turn = 2.0 * math.pi / rows * (offsets[:, None] * offsets[None, :] % rows)
    inner = np.concatenate([np.cos(turn), np.sin(turn)], axis=1)
    return (
        jnp.asarray(first, jnp.bfloat16),
        jnp.asarray(twist, jnp.float32),
        jnp.asarray(inner, jnp.bfloat16),
    )


def routes_of(chips):
    return [(d, d + 1) for d in range(chips - 2, 1, -2)]


def carried(route, core):
    mine, others = route
    return jnp.where(core == 0, mine, others), jnp.where(core == 0, others, mine)


def put_routes(source_ref, rim_ref, keep_ref, give_ref, near_ref, home_ref):
    chip, core = lax.axis_index("chip"), lax.axis_index("core")
    size = source_ref.shape[0] // 2 // (lax.axis_size("chip"))
    extra = home_ref.shape[0] - 2 * size

    def put(out_ref, distance):
        start = pl.multiple_of((chip ^ distance) * 2 * size, 2 * size)
        out_ref[0 : 2 * size, :] = source_ref[pl.ds(start, 2 * size), :]
        if extra:
            out_ref[2 * size : 2 * size + extra, :] = rim_ref[chip ^ distance]

    for turn, route in enumerate(routes_of(lax.axis_size("chip"))):
        own, other = carried(route, core)
        put(keep_ref.at[turn], own)
        put(give_ref.at[turn], other)
    put(home_ref, 0)
    put(near_ref, 1)
    begin = 2 * size + extra
    near_ref[begin : begin + 2 * size, :] = home_ref[0 : 2 * size, :]
    near_ref[begin + 2 * size :, :] = home_ref[0:chan_tile, :]


def half_rims(first_ref, second_ref, begin):
    pair = [ref[begin : begin + edge, :].astype(jnp.float32) for ref in (first_ref, second_ref)]
    pair = [rims[0 : edge // 2] for rims in pair]
    return jnp.concatenate(pair).astype(jnp.bfloat16)


def merge_body(size, keep_ref, got_ref, *out_refs):
    for turn, out_ref in enumerate(out_refs):
        out_ref[0 : 2 * size, :] = keep_ref[turn, 0 : 2 * size, :]
        out_ref[2 * size : 4 * size, :] = got_ref[turn, 0 : 2 * size, :]
        if out_ref.shape[0] > 4 * size:
            out_ref[4 * size :, :] = half_rims(keep_ref.at[turn], got_ref.at[turn], 2 * size)


def split_body(size, *refs):
    far_refs, (near_ref, home_ref, keep_ref, give_ref) = refs[:-4], refs[-4:]
    core = lax.axis_index("core")
    sources = [(far_ref, 2 * sender) for far_ref in far_refs for sender in range(2)]
    sources += [(near_ref, 0), (home_ref, 0)]
    for out_ref, target in ((keep_ref, core), (give_ref, 1 - core)):
        for place, (source_ref, block) in enumerate(sources):
            start = pl.multiple_of((block + target) * size, size)
            out_ref[place * size : (place + 1) * size, :] = source_ref[pl.ds(start, size), :]
        begin = len(sources) * size
        if out_ref.shape[0] > begin:
            for far_ref in far_refs:
                out_ref[begin : begin + edge, :] = far_ref[4 * size :, :]
                begin += edge
            out_ref[begin:, :] = half_rims(near_ref, home_ref, 2 * size)


def take_routes(keep_ref, got_ref, target_ref, rim_ref=None):
    chip, core = lax.axis_index("chip"), lax.axis_index("core")
    routes = routes_of(lax.axis_size("chip"))
    count = 2 * len(routes) + 2
    size = target_ref.shape[0] // (2 * lax.axis_size("chip"))
    places = [(*carried(route, core), sender) for route in routes for sender in range(2)]
    places += [(1, 1, 0), (0, 0, 0)]
    for place, (own, other, sender) in enumerate(places):
        for ref, distance, carrier in ((keep_ref, own, core), (got_ref, other, 1 - core)):
            device = (chip ^ distance) * 2 + (carrier if sender == 0 else 1 - carrier)
            start = pl.multiple_of(device * size, size)
            target_ref[pl.ds(start, size), :] = ref[place * size : (place + 1) * size, :]
            if rim_ref is not None:
                begin = count * size + place // 2 * edge
                rims = ref[begin : begin + edge, :].astype(jnp.float32)
                rim_ref[device, 0 : edge // 2, :] = rims[place % 2 * edge // 2 : (place % 2 + 1) * edge // 2]


def normed_of(tokens_ref, gain_ref):
    inputs = tokens_ref[...].astype(jnp.float32)
    mean_sq = jnp.mean(inputs * inputs, axis=-1, keepdims=True)
    return (inputs * lax.rsqrt(mean_sq + epsilon) * gain_ref[...]).astype(jnp.bfloat16)


def projected_of(normed, weights):
    projected = jnp.dot(normed, weights, preferred_element_type=jnp.float32)
    projected = projected.astype(jnp.bfloat16).astype(jnp.float32)
    return jnp.concatenate([projected, jnp.zeros((edge, projected.shape[1]), jnp.float32)])


def short_mix(projected, taps):
    acc = taps[0:1] * projected
    for tap_num in range(1, taps.shape[0]):
        acc = acc + taps[tap_num : tap_num + 1] * pltpu.roll(projected, tap_num, 0)
    return acc


def query_body(tokens_ref, gain_ref, w_ref, short_ref, query_ref):
    rows, width = tokens_ref.shape
    cols = slice(0, width)
    query = short_mix(projected_of(normed_of(tokens_ref, gain_ref), w_ref[:, cols]), short_ref[:, cols])
    query_ref[...] = query[0:rows]
    row = lax.broadcasted_iota(jnp.int32, (edge, width), 0)
    query_ref[0:edge, :] = jnp.where(row < short_ref.shape[0] - 1, 1.0, query[0:edge])


def prepare_body(*refs):
    hbm, outs, held, sems = refs[:7], refs[7:-8], refs[-8:-1], refs[-1]
    staged = len(outs) > 1
    outs, (packed_ref, rim_ref) = (outs[:-2], outs[-2:]) if staged else (outs, (outs[0], None))
    tokens_ref, gain_ref, w_ref, short_ref, long_ref, medium_ref, skip_ref = held
    rows, width = tokens_ref.shape
    copies = [pltpu.make_async_copy(h, v, sems.at[i]) for i, (h, v) in enumerate(zip(hbm, held))]
    for copy in copies:
        copy.start()
    copies[0].wait()
    copies[1].wait()
    normed = normed_of(tokens_ref, gain_ref)
    copies[2].wait()
    copies[3].wait()
    query_cols, cols = slice(0, width), slice(width, 3 * width)
    mixed = short_mix(projected_of(normed, w_ref[:, cols]), short_ref[:, cols])
    key, value = mixed[:, 0:width], mixed[:, width:]
    put_columns(packed_ref, 0, (key[0:rows] * value[0:rows]).astype(jnp.bfloat16).T)
    rims = [(key[0:edge], key[rows:]), (value[0:edge], value[rows:])]
    some = jnp.concatenate([normed[0 : 2 * edge], normed[rows - 2 * edge :]])
    some = short_mix(projected_of(some, w_ref[:, query_cols]), short_ref[:, query_cols])
    put_rim(packed_ref, rim_ref, [*rims, (some[0:edge], some[4 * edge :])])
    for copy in copies[4:]:
        copy.wait()
    med_len = medium_ref.shape[0]
    is_first = jnp.where(lax.axis_index(seq) == 0, 1.0, 0.0)
    head = long_ref[0:med_len, :] + is_first * medium_ref[...]
    head_row = lax.broadcasted_iota(jnp.int32, head.shape, 0)
    head = head + jnp.where(head_row == 0, is_first * skip_ref[...], 0.0)
    taps = jnp.concatenate([head, long_ref[med_len:, :]]).astype(jnp.bfloat16)
    put_columns(packed_ref, rows, taps.T)
    if staged:
        put_routes(packed_ref, rim_ref, *outs)


def put_columns(packed_ref, begin, values):
    if packed_ref.shape[1] > lane:
        packed_ref[:, begin : begin + values.shape[1]] = values
        return
    devices = lax.axis_size(seq)
    chans = values.shape[0] // devices
    size = packed_ref.shape[0] // devices
    for device in range(devices):
        for column in range(values.shape[1] // lane):
            start = device * size + (begin // lane + column) * chans
            packed_ref[start : start + chans, :] = values[
                device * chans : (device + 1) * chans, column * lane : (column + 1) * lane
            ]


def put_rim(packed_ref, rim_ref, parts):
    width = parts[0][0].shape[1]
    if rim_ref is None:
        rows = [row for part in parts for row in part]
        rows.append(jnp.zeros((lane - 3 * rim_step, width), jnp.float32))
        rim = jnp.concatenate(rows).T
        packed_ref[:, packed_ref.shape[1] - lane :] = rim.astype(jnp.bfloat16)
        return
    chips = rim_ref.shape[0]
    span = width // chips
    half = edge // 4
    group = lax.broadcasted_iota(jnp.int32, (edge // 2, lane), 1) // span
    parts = [jnp.concatenate([own[0:half], after[0:half]]) for own, after in parts]
    for chip in range(chips):
        begin = chip * span // lane * lane
        place = chip * span % lane
        rim = jnp.zeros((edge // 2, lane), jnp.float32)
        for index, part in enumerate(parts):
            shift = (index * span - place) % lane
            moved = part[:, begin : begin + lane]
            moved = pltpu.roll(moved, shift, 1) if shift else moved
            rim = jnp.where(group == index, moved, rim)
        rim = jnp.concatenate([rim, jnp.zeros((edge // 2, lane), jnp.float32)])
        rim_ref[chip] = rim.astype(jnp.bfloat16)


def columns_of(packed_ref, chans, rows):
    devices, count = lax.axis_size(seq), 2 * rows // lane
    blocks = packed_ref[...].reshape(devices, count * chans, lane)
    columns = [blocks[:, i * chans : (i + 1) * chans].reshape(-1, lane) for i in range(count)]
    return jnp.concatenate(columns, axis=1)


def rim_of(rim_ref, turned_ref, chans):
    span = 2 * chans
    rim = rim_ref[...].reshape(-1, lane)
    row = lax.broadcasted_iota(jnp.int32, rim.shape, 0)
    column = lax.broadcasted_iota(jnp.int32, rim.shape, 1)
    before = pltpu.roll(rim, edge - edge // 4, 0)
    rim = rim + jnp.where(row < edge, 0.0, before)
    signal = rim * pltpu.roll(rim, lane - span, 1)
    turned_ref[...] = jnp.where(column < span, signal, rim).T
    found = []
    for begin in (0, 2 * span):
        start = pl.multiple_of(begin + lax.axis_index("core") * chans, chans)
        part = turned_ref[pl.ds(start, chans), :]
        blocks = [part] + [pltpu.roll(part, lane - edge * k, 1) for k in range(1, rim_ref.shape[0])]
        found.append(jnp.concatenate(blocks))
    return found


def twist_rows(twist_ref, chans):
    half, rows = twist_ref.shape[0] // 2, twist_ref.shape[1]
    tables = twist_ref[0:half, :], twist_ref[half:, :]
    if chans % 8:
        return tables
    return tuple(
        jnp.broadcast_to(table[:, None, :], (half, chans, rows)).reshape(half * chans, rows)
        for table in tables
    )


def convolve_body(chans, rim_count, first_ref, twist_ref, inner_ref, *refs):
    rows = twist_ref.shape[1]
    half = first_ref.shape[0] // 2
    scale = chans / (half * rows)
    staged = len(refs) > 2
    if staged:
        keep_ref, got_ref, *outs, packed_ref, rim_ref, turned_ref, out_ref = refs
        rim_ref[...] = jnp.zeros_like(rim_ref)
        take_routes(keep_ref, got_ref, packed_ref, rim_ref)
        values = columns_of(packed_ref, chans, rows)
        rim_signal, rim_query = rim_of(rim_ref, turned_ref, chans)
    else:
        packed_ref, out_ref = refs
        values = packed_ref[:, : 2 * rows]
        rim = packed_ref[:, 2 * rows :].astype(jnp.float32)
        before = jnp.concatenate([jnp.zeros((chans, lane), jnp.float32), rim[:-chans]])
        rim = rim + pltpu.roll(before, lane - edge, 1)
        rim_signal = rim * pltpu.roll(rim, lane - rim_step, 1)
        rim_query = pltpu.roll(rim, lane - 2 * rim_step, 1)
    in_rim = lax.broadcasted_iota(jnp.int32, rim_signal.shape, 1) < rim_count
    rim_signal = rim_signal.astype(jnp.bfloat16)
    rim_query = scale * jnp.where(in_rim, rim_query, 1.0)
    values = jnp.concatenate(
        [jnp.where(in_rim, rim_signal, values[:, 0:lane]), values[:, lane:]], axis=1
    )
    cosine, sine = inner_ref[:, 0:rows], inner_ref[:, rows:]
    inner = jnp.concatenate(
        [jnp.concatenate([cosine, -sine], axis=1), jnp.concatenate([sine, cosine], axis=1)]
    )
    spread = jnp.dot(first_ref[...], values, preferred_element_type=jnp.float32)
    tw_cos, tw_sin = twist_rows(twist_ref, chans)
    turned = []
    for begin in (0, rows):
        real, imag = spread[0:half, begin : begin + rows], spread[half:, begin : begin + rows]
        turned.append([real * tw_cos + imag * tw_sin, imag * tw_cos - real * tw_sin])
    turned = jnp.concatenate([jnp.concatenate(pair, axis=1).astype(jnp.bfloat16) for pair in turned])
    spectra = jnp.dot(turned, inner, preferred_element_type=jnp.float32)
    real, imag = spectra[0:half, 0:rows], spectra[0:half, rows:]
    fil_re, fil_im = spectra[half:, 0:rows], spectra[half:, rows:]
    product = [real * fil_im + imag * fil_re, real * fil_re - imag * fil_im]
    product = jnp.concatenate(product, axis=1).astype(jnp.bfloat16)
    back = jnp.dot(product, inner, preferred_element_type=jnp.float32)
    imag, real = back[:, 0:rows], back[:, rows:]
    turned = jnp.concatenate([real * tw_cos - imag * tw_sin, imag * tw_cos + real * tw_sin])
    last = jnp.concatenate([first_ref[0:half, :].T, first_ref[half:, :].T], axis=1)
    conv = jnp.dot(last, turned.astype(jnp.bfloat16), preferred_element_type=jnp.float32)
    conv = jnp.concatenate([conv[:, 0:lane] * rim_query, conv[:, lane:] * scale], axis=1)
    out_ref[...] = conv.astype(jnp.bfloat16)
    if staged:
        put_routes(out_ref, None, *outs)


def output_body(query_ref, w_ref, *refs):
    if len(refs) > 2:
        keep_ref, got_ref, out_ref, conv_ref = refs
        take_routes(keep_ref, got_ref, conv_ref)
    else:
        conv_ref, out_ref = refs
    conv = conv_ref[...].T.astype(jnp.float32)
    mixed_out = (query_ref[...] * conv).astype(jnp.bfloat16)
    out_ref[...] = jnp.dot(mixed_out, w_ref[...], preferred_element_type=jnp.float32).astype(
        jnp.bfloat16
    )


def permute(array, partner):
    return lax.ppermute(array, seq, [(i, partner(i)) for i in range(lax.axis_size(seq))])


def bf16(*shape):
    return jax.ShapeDtypeStruct(shape, jnp.bfloat16)


def exchange(keep, give, near, home):
    turns, size = keep.shape[0], keep.shape[1] // 2 // chan_tile * chan_tile
    lanes, extra = keep.shape[2], keep.shape[1] - 2 * size
    got = permute(give, lambda i: i ^ 1)
    near = permute(near, lambda i: i ^ 2)
    far = call(
        functools.partial(merge_body, size),
        (bf16(4 * size + extra, lanes),) * turns,
        (keep, got),
        [pltpu.VMEM] * 2,
        moved=4 * keep.size,
    )
    routes = routes_of(lax.axis_size("chip"))
    far = [permute(part, lambda i: i ^ 2 * route[i % 2]) for part, route in zip(far, routes)]
    count = 2 * turns + 2
    half = bf16(count * size + count // 2 * extra, lanes)
    keep, give = call(
        functools.partial(split_body, size),
        (half, half),
        (*far, near, home),
        [pltpu.VMEM] * (turns + 2),
        moved=4 * keep.size,
    )
    return keep, permute(give, lambda i: i ^ 1)


def local(tokens, norm_gain, w_in, short_filter, long_filter, medium_filter, skip_gain, w_out):
    rows, width = tokens.shape
    devices, chips = lax.axis_size(seq), lax.axis_size("chip")
    chans = width // devices
    first, twist, inner = spectral_tables(devices, rows, chans)
    staged = chans == chan_tile and chips >= 4 and short_filter.shape[0] <= 3
    if staged:
        packed_shape = (2 * rows // lane * width, lane)
    else:
        packed_shape = (width, 2 * rows + lane)

    def pieces(shape, extra):
        if not staged:
            return (bf16(*shape),)
        size, turns = 2 * shape[0] // devices + extra, chips // 2 - 1
        near = size + size - extra + chan_tile
        return (bf16(turns, size, shape[1]),) * 2 + (bf16(near, shape[1]), bf16(size, shape[1]))

    def scratch(*shapes):
        return [pltpu.VMEM(*shape) for shape in shapes] if staged else []

    def swap(parts):
        if staged:
            return exchange(*parts)
        (array,) = parts
        blocks = array.reshape(devices, -1, array.shape[-1])
        return (lax.all_to_all(blocks, seq, split_axis=0, concat_axis=0).reshape(array.shape),)

    query = call(
        query_body,
        jax.ShapeDtypeStruct((rows, width), jnp.float32),
        (tokens, norm_gain[None, :], w_in, short_filter),
        [pltpu.VMEM] * 4,
        flops=2 * rows * width * width,
        moved=800_000,
    )
    args = (tokens, norm_gain[None, :], w_in, short_filter, long_filter, medium_filter, skip_gain[None, :])
    args = tuple(pltpu.with_memory_space_constraint(arg, pltpu.HBM) for arg in args)
    packed = (packed_shape, jnp.bfloat16)
    parts = call(
        prepare_body,
        pieces(packed_shape, edge),
        args,
        [pltpu.HBM] * len(args),
        scratch(packed, ((chips, edge, lane), jnp.bfloat16))
        + [pltpu.VMEM(arg.shape, arg.dtype) for arg in args]
        + [pltpu.SemaphoreType.DMA((len(args),))],
        flops=2 * rows * width * 3 * width,
        moved=1_500_000,
    )
    conv = ((width, rows), jnp.bfloat16)
    parts = swap(parts)
    parts = call(
        functools.partial(convolve_body, chans, short_filter.shape[0] - 1),
        pieces((width, rows), 0),
        (first, twist, inner, *parts),
        [pltpu.VMEM] * (3 + len(parts)),
        scratch(packed, ((devices, edge, lane), jnp.float32), ((lane, lane), jnp.float32), conv),
        flops=18 * first.shape[0] * width * rows,
        moved=2_000_000,
    )
    parts = swap(parts)
    return call(
        output_body,
        bf16(rows, width),
        (query, w_out, *parts),
        [pltpu.VMEM] * (2 + len(parts)),
        scratch(conv),
        flops=2 * rows * width * width,
        moved=600_000,
    )


def solution(mesh):
    groups, devices = mesh.devices.shape
    split = jax.sharding.Mesh(mesh.devices.reshape(groups, devices // 2, 2), ("groups", *seq))
    rows = P(("groups", *seq), None)
    placed = (rows, P(), P(), P(), P(seq, None), P(), P(), P())
    return jax.shard_map(local, mesh=split, in_specs=placed, out_specs=rows, check_vma=False)
```

```python
import functools
import math

import jax
import jax.numpy as jnp
import numpy as np
from jax import lax
from jax.experimental import pallas as pl
from jax.experimental.pallas import tpu as pltpu
from jax.sharding import PartitionSpec as P

epsilon = 1e-06
edge = 8
lane = 128
seq = ("chip", "core")
rim_step = 2 * edge
chan_tile = 16
vmem_bytes = 32 * 2**20


def whole(space):
    return pl.BlockSpec(memory_space=space)


def call(body, outs, args, spaces, scratch=(), flops=0, moved=0):
    return pl.pallas_call(
        body,
        out_shape=outs,
        in_specs=[whole(space) for space in spaces],
        out_specs=jax.tree.map(lambda _: whole(pltpu.VMEM), outs),
        scratch_shapes=list(scratch),
        compiler_params=pltpu.CompilerParams(vmem_limit_bytes=vmem_bytes),
        cost_estimate=pl.CostEstimate(flops=flops, bytes_accessed=moved, transcendentals=0),
    )(*args)


def spectral_tables(devices, rows, chans):
    full_len = devices * rows
    freqs = 4 * np.arange(devices) + 1
    eye = np.eye(chans)
    angle = 2.0 * math.pi / (4 * devices) * (freqs[:, None] * np.arange(devices)[None, :] % (4 * devices))
    cosine, sine = np.kron(np.cos(angle), eye), np.kron(np.sin(angle), eye)
    first = np.concatenate([cosine, -sine])
    offsets = np.arange(rows)
    twist = 2.0 * math.pi / (4 * full_len) * (freqs[:, None] * offsets[None, :] % (4 * full_len))
    twist = np.concatenate([np.cos(twist), np.sin(twist)])
    if chans % 8:
        twist = np.repeat(twist, chans, axis=0)
    turn = 2.0 * math.pi / rows * (offsets[:, None] * offsets[None, :] % rows)
    inner = np.concatenate([np.cos(turn), np.sin(turn)], axis=1)
    return (
        jnp.asarray(first, jnp.bfloat16),
        jnp.asarray(twist, jnp.float32),
        jnp.asarray(inner, jnp.bfloat16),
    )


def routes_of(chips):
    return [(d, d + 1) for d in range(chips - 2, 1, -2)]


def carried(route, core):
    mine, others = route
    return jnp.where(core == 0, mine, others), jnp.where(core == 0, others, mine)


def put_routes(source_ref, rim_ref, keep_ref, give_ref, near_ref, home_ref):
    chip, core = lax.axis_index("chip"), lax.axis_index("core")
    size = source_ref.shape[0] // 2 // (lax.axis_size("chip"))
    extra = home_ref.shape[0] - 2 * size

    def put(out_ref, distance):
        start = pl.multiple_of((chip ^ distance) * 2 * size, 2 * size)
        out_ref[0 : 2 * size, :] = source_ref[pl.ds(start, 2 * size), :]
        if extra:
            out_ref[2 * size : 2 * size + extra, :] = rim_ref[chip ^ distance]

    for turn, route in enumerate(routes_of(lax.axis_size("chip"))):
        own, other = carried(route, core)
        put(keep_ref.at[turn], own)
        put(give_ref.at[turn], other)
    put(home_ref, 0)
    put(near_ref, 1)
    if not extra:
        near_ref[2 * size : 4 * size, :] = home_ref[...]
        near_ref[4 * size :, :] = home_ref[0:chan_tile, :]


def half_rims(first_ref, second_ref, begin):
    pair = [ref[begin : begin + edge, :].astype(jnp.float32) for ref in (first_ref, second_ref)]
    pair = [rims[0 : edge // 2] for rims in pair]
    return jnp.concatenate(pair).astype(jnp.bfloat16)


def merge_body(size, keep_ref, got_ref, *out_refs):
    for turn, out_ref in enumerate(out_refs):
        out_ref[0 : 2 * size, :] = keep_ref[turn, 0 : 2 * size, :]
        out_ref[2 * size : 4 * size, :] = got_ref[turn, 0 : 2 * size, :]
        if out_ref.shape[0] > 4 * size:
            out_ref[4 * size :, :] = half_rims(keep_ref.at[turn], got_ref.at[turn], 2 * size)


def split_body(size, *refs):
    far_refs, (near_ref, home_ref, keep_ref, give_ref) = refs[:-4], refs[-4:]
    core = lax.axis_index("core")
    sources = [(far_ref, 2 * sender) for far_ref in far_refs for sender in range(2)]
    sources += [(near_ref, 0), (home_ref, 0)]
    for out_ref, target in ((keep_ref, core), (give_ref, 1 - core)):
        for place, (source_ref, block) in enumerate(sources):
            start = pl.multiple_of((block + target) * size, size)
            out_ref[place * size : (place + 1) * size, :] = source_ref[pl.ds(start, size), :]
        begin = len(sources) * size
        if out_ref.shape[0] > begin:
            for far_ref in far_refs:
                out_ref[begin : begin + edge, :] = far_ref[4 * size :, :]
                begin += edge
            out_ref[begin:, :] = half_rims(near_ref, home_ref, 2 * size)


def take_routes(keep_ref, got_ref, target_ref, rim_ref=None):
    chip, core = lax.axis_index("chip"), lax.axis_index("core")
    routes = routes_of(lax.axis_size("chip"))
    count = 2 * len(routes) + 2
    size = target_ref.shape[0] // (2 * lax.axis_size("chip"))
    places = [(*carried(route, core), sender) for route in routes for sender in range(2)]
    places += [(1, 1, 0), (0, 0, 0)]
    for place, (own, other, sender) in enumerate(places):
        for ref, distance, carrier in ((keep_ref, own, core), (got_ref, other, 1 - core)):
            device = (chip ^ distance) * 2 + (carrier if sender == 0 else 1 - carrier)
            start = pl.multiple_of(device * size, size)
            target_ref[pl.ds(start, size), :] = ref[place * size : (place + 1) * size, :]
            if rim_ref is not None:
                begin = count * size + place // 2 * edge
                rims = ref[begin : begin + edge, :].astype(jnp.float32)
                rim_ref[device, 0 : edge // 2, :] = rims[place % 2 * edge // 2 : (place % 2 + 1) * edge // 2]


def normed_of(tokens_ref, gain_ref):
    inputs = tokens_ref[...].astype(jnp.float32)
    mean_sq = jnp.mean(inputs * inputs, axis=-1, keepdims=True)
    return (inputs * lax.rsqrt(mean_sq + epsilon) * gain_ref[...]).astype(jnp.bfloat16)


def projected_of(normed, weights):
    projected = jnp.dot(normed, weights, preferred_element_type=jnp.float32)
    projected = projected.astype(jnp.bfloat16).astype(jnp.float32)
    return jnp.concatenate([projected, jnp.zeros((edge, projected.shape[1]), jnp.float32)])


def short_mix(projected, taps):
    acc = taps[0:1] * projected
    for tap_num in range(1, taps.shape[0]):
        acc = acc + taps[tap_num : tap_num + 1] * pltpu.roll(projected, tap_num, 0)
    return acc


def query_body(tokens_ref, gain_ref, w_ref, short_ref, query_ref):
    rows, width = tokens_ref.shape
    cols = slice(0, width)
    query = short_mix(projected_of(normed_of(tokens_ref, gain_ref), w_ref[:, cols]), short_ref[:, cols])
    query_ref[...] = query[0:rows]
    row = lax.broadcasted_iota(jnp.int32, (edge, width), 0)
    query_ref[0:edge, :] = jnp.where(row < short_ref.shape[0] - 1, 1.0, query[0:edge])


def prepare_body(*refs):
    hbm, outs, held, sems = refs[:7], refs[7:-8], refs[-8:-1], refs[-1]
    staged = len(outs) > 1
    outs, (packed_ref, rim_ref) = (outs[:-2], outs[-2:]) if staged else (outs, (outs[0], None))
    tokens_ref, gain_ref, w_ref, short_ref, long_ref, medium_ref, skip_ref = held
    rows, width = tokens_ref.shape
    copies = [pltpu.make_async_copy(h, v, sems.at[i]) for i, (h, v) in enumerate(zip(hbm, held))]
    for copy in copies:
        copy.start()
    copies[0].wait()
    copies[1].wait()
    normed = normed_of(tokens_ref, gain_ref)
    copies[2].wait()
    copies[3].wait()
    query_cols, cols = slice(0, width), slice(width, 3 * width)
    mixed = short_mix(projected_of(normed, w_ref[:, cols]), short_ref[:, cols])
    key, value = mixed[:, 0:width], mixed[:, width:]
    put_columns(packed_ref, 0, (key[0:rows] * value[0:rows]).astype(jnp.bfloat16).T)
    rims = [(key[0:edge], key[rows:]), (value[0:edge], value[rows:])]
    some = jnp.concatenate([normed[0 : 2 * edge], normed[rows - 2 * edge :]])
    some = short_mix(projected_of(some, w_ref[:, query_cols]), short_ref[:, query_cols])
    put_rim(packed_ref, rim_ref, [*rims, (some[0:edge], some[4 * edge :])])
    for copy in copies[4:]:
        copy.wait()
    med_len = medium_ref.shape[0]
    is_first = jnp.where(lax.axis_index(seq) == 0, 1.0, 0.0)
    head = long_ref[0:med_len, :] + is_first * medium_ref[...]
    head_row = lax.broadcasted_iota(jnp.int32, head.shape, 0)
    head = head + jnp.where(head_row == 0, is_first * skip_ref[...], 0.0)
    taps = jnp.concatenate([head, long_ref[med_len:, :]]).astype(jnp.bfloat16)
    put_columns(packed_ref, rows, taps.T)
    if staged:
        put_routes(packed_ref, rim_ref, *outs)


def put_columns(packed_ref, begin, values):
    if packed_ref.shape[1] > lane:
        packed_ref[:, begin : begin + values.shape[1]] = values
        return
    devices = lax.axis_size(seq)
    chans = values.shape[0] // devices
    size = packed_ref.shape[0] // devices
    for device in range(devices):
        for column in range(values.shape[1] // lane):
            start = device * size + (begin // lane + column) * chans
            packed_ref[start : start + chans, :] = values[
                device * chans : (device + 1) * chans, column * lane : (column + 1) * lane
            ]


def put_rim(packed_ref, rim_ref, parts):
    width = parts[0][0].shape[1]
    if rim_ref is None:
        rows = [row for part in parts for row in part]
        rows.append(jnp.zeros((lane - 3 * rim_step, width), jnp.float32))
        rim = jnp.concatenate(rows).T
        packed_ref[:, packed_ref.shape[1] - lane :] = rim.astype(jnp.bfloat16)
        return
    chips = rim_ref.shape[0]
    span = width // chips
    half = edge // 4
    group = lax.broadcasted_iota(jnp.int32, (edge // 2, lane), 1) // span
    parts = [jnp.concatenate([own[0:half], after[0:half]]) for own, after in parts]
    for chip in range(chips):
        begin = chip * span // lane * lane
        place = chip * span % lane
        rim = jnp.zeros((edge // 2, lane), jnp.float32)
        for index, part in enumerate(parts):
            shift = (index * span - place) % lane
            moved = part[:, begin : begin + lane]
            moved = pltpu.roll(moved, shift, 1) if shift else moved
            rim = jnp.where(group == index, moved, rim)
        rim = jnp.concatenate([rim, jnp.zeros((edge // 2, lane), jnp.float32)])
        rim_ref[chip] = rim.astype(jnp.bfloat16)


def columns_of(packed_ref, chans, rows):
    devices, count = lax.axis_size(seq), 2 * rows // lane
    blocks = packed_ref[...].reshape(devices, count * chans, lane)
    columns = [blocks[:, i * chans : (i + 1) * chans].reshape(-1, lane) for i in range(count)]
    return jnp.concatenate(columns, axis=1)


def rim_of(rim_ref, turned_ref, chans):
    span = 2 * chans
    rim = rim_ref[...].reshape(-1, lane)
    row = lax.broadcasted_iota(jnp.int32, rim.shape, 0)
    column = lax.broadcasted_iota(jnp.int32, rim.shape, 1)
    before = pltpu.roll(rim, edge - edge // 4, 0)
    rim = rim + jnp.where(row < edge, 0.0, before)
    signal = rim * pltpu.roll(rim, lane - span, 1)
    turned_ref[...] = jnp.where(column < span, signal, rim).T
    found = []
    for begin in (0, 2 * span):
        start = pl.multiple_of(begin + lax.axis_index("core") * chans, chans)
        part = turned_ref[pl.ds(start, chans), :]
        blocks = [part] + [pltpu.roll(part, lane - edge * k, 1) for k in range(1, rim_ref.shape[0])]
        found.append(jnp.concatenate(blocks))
    return found


def twist_rows(twist_ref, chans):
    half, rows = twist_ref.shape[0] // 2, twist_ref.shape[1]
    tables = twist_ref[0:half, :], twist_ref[half:, :]
    if chans % 8:
        return tables
    return tuple(
        jnp.broadcast_to(table[:, None, :], (half, chans, rows)).reshape(half * chans, rows)
        for table in tables
    )


def convolve_body(chans, rim_count, first_ref, twist_ref, inner_ref, *refs):
    rows = twist_ref.shape[1]
    half = first_ref.shape[0] // 2
    scale = chans / (half * rows)
    staged = len(refs) > 2
    if staged:
        keep_ref, got_ref, *outs, packed_ref, rim_ref, turned_ref, out_ref = refs
        rim_ref[...] = jnp.zeros_like(rim_ref)
        take_routes(keep_ref, got_ref, packed_ref, rim_ref)
        values = columns_of(packed_ref, chans, rows)
        rim_signal, rim_query = rim_of(rim_ref, turned_ref, chans)
    else:
        packed_ref, out_ref = refs
        values = packed_ref[:, : 2 * rows]
        rim = packed_ref[:, 2 * rows :].astype(jnp.float32)
        before = jnp.concatenate([jnp.zeros((chans, lane), jnp.float32), rim[:-chans]])
        rim = rim + pltpu.roll(before, lane - edge, 1)
        rim_signal = rim * pltpu.roll(rim, lane - rim_step, 1)
        rim_query = pltpu.roll(rim, lane - 2 * rim_step, 1)
    in_rim = lax.broadcasted_iota(jnp.int32, rim_signal.shape, 1) < rim_count
    rim_signal = rim_signal.astype(jnp.bfloat16)
    rim_query = scale * jnp.where(in_rim, rim_query, 1.0)
    values = jnp.concatenate(
        [jnp.where(in_rim, rim_signal, values[:, 0:lane]), values[:, lane:]], axis=1
    )
    cosine, sine = inner_ref[:, 0:rows], inner_ref[:, rows:]
    inner = jnp.concatenate(
        [jnp.concatenate([cosine, -sine], axis=1), jnp.concatenate([sine, cosine], axis=1)]
    )
    spread = jnp.dot(first_ref[...], values, preferred_element_type=jnp.float32)
    tw_cos, tw_sin = twist_rows(twist_ref, chans)
    turned = []
    for begin in (0, rows):
        real, imag = spread[0:half, begin : begin + rows], spread[half:, begin : begin + rows]
        turned.append([real * tw_cos + imag * tw_sin, imag * tw_cos - real * tw_sin])
    turned = jnp.concatenate([jnp.concatenate(pair, axis=1).astype(jnp.bfloat16) for pair in turned])
    spectra = jnp.dot(turned, inner, preferred_element_type=jnp.float32)
    real, imag = spectra[0:half, 0:rows], spectra[0:half, rows:]
    fil_re, fil_im = spectra[half:, 0:rows], spectra[half:, rows:]
    product = [real * fil_im + imag * fil_re, real * fil_re - imag * fil_im]
    product = jnp.concatenate(product, axis=1).astype(jnp.bfloat16)
    back = jnp.dot(product, inner, preferred_element_type=jnp.float32)
    imag, real = back[:, 0:rows], back[:, rows:]
    turned = jnp.concatenate([real * tw_cos - imag * tw_sin, imag * tw_cos + real * tw_sin])
    last = jnp.concatenate([first_ref[0:half, :].T, first_ref[half:, :].T], axis=1)
    conv = jnp.dot(last, turned.astype(jnp.bfloat16), preferred_element_type=jnp.float32)
    conv = jnp.concatenate([conv[:, 0:lane] * rim_query, conv[:, lane:] * scale], axis=1)
    out_ref[...] = conv.astype(jnp.bfloat16)
    if staged:
        put_routes(out_ref, None, *outs)


def output_body(query_ref, w_ref, *refs):
    if len(refs) > 2:
        keep_ref, got_ref, out_ref, conv_ref = refs
        take_routes(keep_ref, got_ref, conv_ref)
    else:
        conv_ref, out_ref = refs
    conv = conv_ref[...].T.astype(jnp.float32)
    mixed_out = (query_ref[...] * conv).astype(jnp.bfloat16)
    out_ref[...] = jnp.dot(mixed_out, w_ref[...], preferred_element_type=jnp.float32).astype(
        jnp.bfloat16
    )


def permute(array, partner):
    return lax.ppermute(array, seq, [(i, partner(i)) for i in range(lax.axis_size(seq))])


def bf16(*shape):
    return jax.ShapeDtypeStruct(shape, jnp.bfloat16)


def exchange(keep, give, near, home):
    turns, size = keep.shape[0], keep.shape[1] // 2 // chan_tile * chan_tile
    lanes, extra = keep.shape[2], keep.shape[1] - 2 * size
    got = permute(give, lambda i: i ^ 1)
    near = permute(near, lambda i: i ^ 2)
    far = call(
        functools.partial(merge_body, size),
        (bf16(4 * size + extra, lanes),) * turns,
        (keep, got),
        [pltpu.VMEM] * 2,
        moved=4 * keep.size,
    )
    routes = routes_of(lax.axis_size("chip"))
    far = [permute(part, lambda i: i ^ 2 * route[i % 2]) for part, route in zip(far, routes)]
    count = 2 * turns + 2
    half = bf16(count * size + count // 2 * extra, lanes)
    keep, give = call(
        functools.partial(split_body, size),
        (half, half),
        (*far, near, home),
        [pltpu.VMEM] * (turns + 2),
        moved=4 * keep.size,
    )
    return keep, permute(give, lambda i: i ^ 1)


def local(tokens, norm_gain, w_in, short_filter, long_filter, medium_filter, skip_gain, w_out):
    rows, width = tokens.shape
    devices, chips = lax.axis_size(seq), lax.axis_size("chip")
    chans = width // devices
    first, twist, inner = spectral_tables(devices, rows, chans)
    staged = chans == chan_tile and chips >= 4 and short_filter.shape[0] <= 3
    if staged:
        packed_shape = (2 * rows // lane * width, lane)
    else:
        packed_shape = (width, 2 * rows + lane)

    def pieces(shape, extra):
        if not staged:
            return (bf16(*shape),)
        size, turns = 2 * shape[0] // devices + extra, chips // 2 - 1
        near = size if extra else 2 * size + chan_tile
        return (bf16(turns, size, shape[1]),) * 2 + (bf16(near, shape[1]), bf16(size, shape[1]))

    def scratch(*shapes):
        return [pltpu.VMEM(*shape) for shape in shapes] if staged else []

    def swap(parts):
        if staged:
            return exchange(*parts)
        (array,) = parts
        blocks = array.reshape(devices, -1, array.shape[-1])
        return (lax.all_to_all(blocks, seq, split_axis=0, concat_axis=0).reshape(array.shape),)

    query = call(
        query_body,
        jax.ShapeDtypeStruct((rows, width), jnp.float32),
        (tokens, norm_gain[None, :], w_in, short_filter),
        [pltpu.VMEM] * 4,
        flops=2 * rows * width * width,
        moved=800_000,
    )
    args = (tokens, norm_gain[None, :], w_in, short_filter, long_filter, medium_filter, skip_gain[None, :])
    args = tuple(pltpu.with_memory_space_constraint(arg, pltpu.HBM) for arg in args)
    packed = (packed_shape, jnp.bfloat16)
    parts = call(
        prepare_body,
        pieces(packed_shape, edge),
        args,
        [pltpu.HBM] * len(args),
        scratch(packed, ((chips, edge, lane), jnp.bfloat16))
        + [pltpu.VMEM(arg.shape, arg.dtype) for arg in args]
        + [pltpu.SemaphoreType.DMA((len(args),))],
        flops=2 * rows * width * 3 * width,
        moved=1_500_000,
    )
    conv = ((width, rows), jnp.bfloat16)
    parts = swap(parts)
    parts = call(
        functools.partial(convolve_body, chans, short_filter.shape[0] - 1),
        pieces((width, rows), 0),
        (first, twist, inner, *parts),
        [pltpu.VMEM] * (3 + len(parts)),
        scratch(packed, ((devices, edge, lane), jnp.float32), ((lane, lane), jnp.float32), conv),
        flops=18 * first.shape[0] * width * rows,
        moved=2_000_000,
    )
    parts = swap(parts)
    return call(
        output_body,
        bf16(rows, width),
        (query, w_out, *parts),
        [pltpu.VMEM] * (2 + len(parts)),
        scratch(conv),
        flops=2 * rows * width * width,
        moved=600_000,
    )


def solution(mesh):
    groups, devices = mesh.devices.shape
    split = jax.sharding.Mesh(mesh.devices.reshape(groups, devices // 2, 2), ("groups", *seq))
    rows = P(("groups", *seq), None)
    placed = (rows, P(), P(), P(), P(seq, None), P(), P(), P())
    return jax.shard_map(local, mesh=split, in_specs=placed, out_specs=rows, check_vma=False)
```

```python
import functools
import math

import jax
import jax.numpy as jnp
import numpy as np
from jax import lax
from jax.experimental import pallas as pl
from jax.experimental.pallas import tpu as pltpu
from jax.sharding import PartitionSpec as P

epsilon = 1e-06
edge = 8
lane = 128
seq = ("chip", "core")
rim_step = 2 * edge
chan_tile = 16
vmem_bytes = 32 * 2**20


def whole(space):
    return pl.BlockSpec(memory_space=space)


def call(body, outs, args, spaces, scratch=(), flops=0, moved=0):
    return pl.pallas_call(
        body,
        out_shape=outs,
        in_specs=[whole(space) for space in spaces],
        out_specs=jax.tree.map(lambda _: whole(pltpu.VMEM), outs),
        scratch_shapes=list(scratch),
        compiler_params=pltpu.CompilerParams(vmem_limit_bytes=vmem_bytes),
        cost_estimate=pl.CostEstimate(flops=flops, bytes_accessed=moved, transcendentals=0),
    )(*args)


def spectral_tables(devices, rows, chans):
    full_len = devices * rows
    freqs = 4 * np.arange(devices) + 1
    eye = np.eye(chans)
    angle = 2.0 * math.pi / (4 * devices) * (freqs[:, None] * np.arange(devices)[None, :] % (4 * devices))
    cosine, sine = np.kron(np.cos(angle), eye), np.kron(np.sin(angle), eye)
    first = np.concatenate([cosine, -sine])
    offsets = np.arange(rows)
    twist = 2.0 * math.pi / (4 * full_len) * (freqs[:, None] * offsets[None, :] % (4 * full_len))
    twist = np.concatenate([np.cos(twist), np.sin(twist)])
    if chans % 8:
        twist = np.repeat(twist, chans, axis=0)
    turn = 2.0 * math.pi / rows * (offsets[:, None] * offsets[None, :] % rows)
    inner = np.concatenate([np.cos(turn), np.sin(turn)], axis=1)
    return (
        jnp.asarray(first, jnp.bfloat16),
        jnp.asarray(twist, jnp.float32),
        jnp.asarray(inner, jnp.bfloat16),
    )


def routes_of(chips):
    return [(d, d + 1) for d in range(chips - 2, 1, -2)]


def carried(route, core):
    mine, others = route
    return jnp.where(core == 0, mine, others), jnp.where(core == 0, others, mine)


def put_routes(source_ref, rim_ref, keep_ref, give_ref, near_ref, home_ref):
    chip, core = lax.axis_index("chip"), lax.axis_index("core")
    size = source_ref.shape[0] // 2 // (lax.axis_size("chip"))
    extra = home_ref.shape[0] - 2 * size

    def put(out_ref, distance):
        start = pl.multiple_of((chip ^ distance) * 2 * size, 2 * size)
        out_ref[0 : 2 * size, :] = source_ref[pl.ds(start, 2 * size), :]
        if extra:
            out_ref[2 * size : 2 * size + extra, :] = rim_ref[chip ^ distance]

    for turn, route in enumerate(routes_of(lax.axis_size("chip"))):
        own, other = carried(route, core)
        put(keep_ref.at[turn], own)
        put(give_ref.at[turn], other)
    put(home_ref, 0)
    put(near_ref, 1)
    begin = 2 * size + extra
    near_ref[begin : begin + 2 * size, :] = home_ref[0 : 2 * size, :]
    near_ref[begin + 2 * size :, :] = home_ref[0:chan_tile, :]


def half_rims(first_ref, second_ref, begin):
    pair = [ref[begin : begin + edge, :].astype(jnp.float32) for ref in (first_ref, second_ref)]
    pair = [rims[0 : edge // 2] for rims in pair]
    return jnp.concatenate(pair).astype(jnp.bfloat16)


def merge_body(size, keep_ref, got_ref, *out_refs):
    for turn, out_ref in enumerate(out_refs):
        out_ref[0 : 2 * size, :] = keep_ref[turn, 0 : 2 * size, :]
        out_ref[2 * size : 4 * size, :] = got_ref[turn, 0 : 2 * size, :]
        if out_ref.shape[0] > 4 * size:
            out_ref[4 * size :, :] = half_rims(keep_ref.at[turn], got_ref.at[turn], 2 * size)


def split_body(size, *refs):
    far_refs, (near_ref, home_ref, keep_ref, give_ref) = refs[:-4], refs[-4:]
    core = lax.axis_index("core")
    sources = [(far_ref, 2 * sender) for far_ref in far_refs for sender in range(2)]
    sources += [(near_ref, 0), (home_ref, 0)]
    for out_ref, target in ((keep_ref, core), (give_ref, 1 - core)):
        for place, (source_ref, block) in enumerate(sources):
            start = pl.multiple_of((block + target) * size, size)
            out_ref[place * size : (place + 1) * size, :] = source_ref[pl.ds(start, size), :]
        begin = len(sources) * size
        if out_ref.shape[0] > begin:
            for far_ref in far_refs:
                out_ref[begin : begin + edge, :] = far_ref[4 * size :, :]
                begin += edge
            out_ref[begin:, :] = half_rims(near_ref, home_ref, 2 * size)


def take_routes(keep_ref, got_ref, target_ref, rim_ref=None):
    chip, core = lax.axis_index("chip"), lax.axis_index("core")
    routes = routes_of(lax.axis_size("chip"))
    count = 2 * len(routes) + 2
    size = target_ref.shape[0] // (2 * lax.axis_size("chip"))
    places = [(*carried(route, core), sender) for route in routes for sender in range(2)]
    places += [(1, 1, 0), (0, 0, 0)]
    for place, (own, other, sender) in enumerate(places):
        for ref, distance, carrier in ((keep_ref, own, core), (got_ref, other, 1 - core)):
            device = (chip ^ distance) * 2 + (carrier if sender == 0 else 1 - carrier)
            start = pl.multiple_of(device * size, size)
            target_ref[pl.ds(start, size), :] = ref[place * size : (place + 1) * size, :]
            if rim_ref is not None:
                begin = count * size + place // 2 * edge
                rims = ref[begin : begin + edge, :].astype(jnp.float32)
                rim_ref[device, 0 : edge // 2, :] = rims[place % 2 * edge // 2 : (place % 2 + 1) * edge // 2]


def normed_of(tokens_ref, gain_ref):
    inputs = tokens_ref[...].astype(jnp.float32)
    mean_sq = jnp.mean(inputs * inputs, axis=-1, keepdims=True)
    return (inputs * lax.rsqrt(mean_sq + epsilon) * gain_ref[...]).astype(jnp.bfloat16)


def projected_of(normed, weights):
    projected = jnp.dot(normed, weights, preferred_element_type=jnp.float32)
    projected = projected.astype(jnp.bfloat16).astype(jnp.float32)
    return jnp.concatenate([projected, jnp.zeros((edge, projected.shape[1]), jnp.float32)])


def short_mix(projected, taps):
    acc = taps[0:1] * projected
    for tap_num in range(1, taps.shape[0]):
        acc = acc + taps[tap_num : tap_num + 1] * pltpu.roll(projected, tap_num, 0)
    return acc


def query_body(tokens_ref, gain_ref, w_ref, short_ref, query_ref):
    rows, width = tokens_ref.shape
    cols = slice(0, width)
    query = short_mix(projected_of(normed_of(tokens_ref, gain_ref), w_ref[:, cols]), short_ref[:, cols])
    query_ref[...] = query[0:rows]
    row = lax.broadcasted_iota(jnp.int32, (edge, width), 0)
    query_ref[0:edge, :] = jnp.where(row < short_ref.shape[0] - 1, 1.0, query[0:edge])


def prepare_body(*refs):
    hbm, outs, held, sems = refs[:7], refs[7:-8], refs[-8:-1], refs[-1]
    staged = len(outs) > 1
    outs, (packed_ref, rim_ref) = (outs[:-2], outs[-2:]) if staged else (outs, (outs[0], None))
    tokens_ref, gain_ref, w_ref, short_ref, long_ref, medium_ref, skip_ref = held
    rows, width = tokens_ref.shape
    copies = [pltpu.make_async_copy(h, v, sems.at[i]) for i, (h, v) in enumerate(zip(hbm, held))]
    for copy in copies:
        copy.start()
    copies[0].wait()
    copies[1].wait()
    normed = normed_of(tokens_ref, gain_ref)
    for copy in copies[2:]:
        copy.wait()
    query_cols, cols = slice(0, width), slice(width, 3 * width)
    mixed = short_mix(projected_of(normed, w_ref[:, cols]), short_ref[:, cols])
    key, value = mixed[:, 0:width], mixed[:, width:]
    put_columns(packed_ref, 0, (key[0:rows] * value[0:rows]).astype(jnp.bfloat16).T)
    rims = [(key[0:edge], key[rows:]), (value[0:edge], value[rows:])]
    some = jnp.concatenate([normed[0 : 2 * edge], normed[rows - 2 * edge :]])
    some = short_mix(projected_of(some, w_ref[:, query_cols]), short_ref[:, query_cols])
    put_rim(packed_ref, rim_ref, [*rims, (some[0:edge], some[4 * edge :])])
    med_len = medium_ref.shape[0]
    is_first = jnp.where(lax.axis_index(seq) == 0, 1.0, 0.0)
    head = long_ref[0:med_len, :] + is_first * medium_ref[...]
    head_row = lax.broadcasted_iota(jnp.int32, head.shape, 0)
    head = head + jnp.where(head_row == 0, is_first * skip_ref[...], 0.0)
    taps = jnp.concatenate([head, long_ref[med_len:, :]]).astype(jnp.bfloat16)
    put_columns(packed_ref, rows, taps.T)
    if staged:
        put_routes(packed_ref, rim_ref, *outs)


def put_columns(packed_ref, begin, values):
    if packed_ref.shape[1] > lane:
        packed_ref[:, begin : begin + values.shape[1]] = values
        return
    devices = lax.axis_size(seq)
    chans = values.shape[0] // devices
    size = packed_ref.shape[0] // devices
    for device in range(devices):
        for column in range(values.shape[1] // lane):
            start = device * size + (begin // lane + column) * chans
            packed_ref[start : start + chans, :] = values[
                device * chans : (device + 1) * chans, column * lane : (column + 1) * lane
            ]


def put_rim(packed_ref, rim_ref, parts):
    width = parts[0][0].shape[1]
    if rim_ref is None:
        rows = [row for part in parts for row in part]
        rows.append(jnp.zeros((lane - 3 * rim_step, width), jnp.float32))
        rim = jnp.concatenate(rows).T
        packed_ref[:, packed_ref.shape[1] - lane :] = rim.astype(jnp.bfloat16)
        return
    chips = rim_ref.shape[0]
    span = width // chips
    half = edge // 4
    group = lax.broadcasted_iota(jnp.int32, (edge // 2, lane), 1) // span
    parts = [jnp.concatenate([own[0:half], after[0:half]]) for own, after in parts]
    for chip in range(chips):
        begin = chip * span // lane * lane
        place = chip * span % lane
        rim = jnp.zeros((edge // 2, lane), jnp.float32)
        for index, part in enumerate(parts):
            shift = (index * span - place) % lane
            moved = part[:, begin : begin + lane]
            moved = pltpu.roll(moved, shift, 1) if shift else moved
            rim = jnp.where(group == index, moved, rim)
        rim = jnp.concatenate([rim, jnp.zeros((edge // 2, lane), jnp.float32)])
        rim_ref[chip] = rim.astype(jnp.bfloat16)


def columns_of(packed_ref, chans, rows):
    devices, count = lax.axis_size(seq), 2 * rows // lane
    blocks = packed_ref[...].reshape(devices, count * chans, lane)
    columns = [blocks[:, i * chans : (i + 1) * chans].reshape(-1, lane) for i in range(count)]
    return jnp.concatenate(columns, axis=1)


def rim_of(rim_ref, turned_ref, chans):
    span = 2 * chans
    rim = rim_ref[...].reshape(-1, lane)
    row = lax.broadcasted_iota(jnp.int32, rim.shape, 0)
    column = lax.broadcasted_iota(jnp.int32, rim.shape, 1)
    before = pltpu.roll(rim, edge - edge // 4, 0)
    rim = rim + jnp.where(row < edge, 0.0, before)
    signal = rim * pltpu.roll(rim, lane - span, 1)
    turned_ref[...] = jnp.where(column < span, signal, rim).T
    found = []
    for begin in (0, 2 * span):
        start = pl.multiple_of(begin + lax.axis_index("core") * chans, chans)
        part = turned_ref[pl.ds(start, chans), :]
        blocks = [part] + [pltpu.roll(part, lane - edge * k, 1) for k in range(1, rim_ref.shape[0])]
        found.append(jnp.concatenate(blocks))
    return found


def twist_rows(twist_ref, chans):
    half, rows = twist_ref.shape[0] // 2, twist_ref.shape[1]
    tables = twist_ref[0:half, :], twist_ref[half:, :]
    if chans % 8:
        return tables
    return tuple(
        jnp.broadcast_to(table[:, None, :], (half, chans, rows)).reshape(half * chans, rows)
        for table in tables
    )


def convolve_body(chans, rim_count, first_ref, twist_ref, inner_ref, *refs):
    rows = twist_ref.shape[1]
    half = first_ref.shape[0] // 2
    scale = chans / (half * rows)
    staged = len(refs) > 2
    if staged:
        keep_ref, got_ref, *outs, packed_ref, rim_ref, turned_ref, out_ref = refs
        rim_ref[...] = jnp.zeros_like(rim_ref)
        take_routes(keep_ref, got_ref, packed_ref, rim_ref)
        values = columns_of(packed_ref, chans, rows)
        rim_signal, rim_query = rim_of(rim_ref, turned_ref, chans)
    else:
        packed_ref, out_ref = refs
        values = packed_ref[:, : 2 * rows]
        rim = packed_ref[:, 2 * rows :].astype(jnp.float32)
        before = jnp.concatenate([jnp.zeros((chans, lane), jnp.float32), rim[:-chans]])
        rim = rim + pltpu.roll(before, lane - edge, 1)
        rim_signal = rim * pltpu.roll(rim, lane - rim_step, 1)
        rim_query = pltpu.roll(rim, lane - 2 * rim_step, 1)
    in_rim = lax.broadcasted_iota(jnp.int32, rim_signal.shape, 1) < rim_count
    rim_signal = rim_signal.astype(jnp.bfloat16)
    rim_query = scale * jnp.where(in_rim, rim_query, 1.0)
    signal = jnp.concatenate(
        [jnp.where(in_rim, rim_signal, values[:, 0:lane]), values[:, lane:rows]], axis=1
    )
    cosine, sine = inner_ref[:, 0:rows], inner_ref[:, rows:]
    inner = jnp.concatenate(
        [jnp.concatenate([cosine, -sine], axis=1), jnp.concatenate([sine, cosine], axis=1)]
    )
    spread_of = functools.partial(jnp.dot, first_ref[...], preferred_element_type=jnp.float32)
    spreads = [spread_of(values[:, rows : 2 * rows]), spread_of(signal)]
    tw_cos, tw_sin = twist_rows(twist_ref, chans)
    turned = []
    for spread in spreads:
        real, imag = spread[0:half], spread[half:]
        turned.append([real * tw_cos + imag * tw_sin, imag * tw_cos - real * tw_sin])
    turned = jnp.concatenate([jnp.concatenate(pair, axis=1).astype(jnp.bfloat16) for pair in turned])
    spectra = jnp.dot(turned, inner, preferred_element_type=jnp.float32)
    fil_re, fil_im = spectra[0:half, 0:rows], spectra[0:half, rows:]
    real, imag = spectra[half:, 0:rows], spectra[half:, rows:]
    product = [real * fil_im + imag * fil_re, real * fil_re - imag * fil_im]
    product = jnp.concatenate(product, axis=1).astype(jnp.bfloat16)
    back = jnp.dot(product, inner, preferred_element_type=jnp.float32)
    imag, real = back[:, 0:rows], back[:, rows:]
    turned = jnp.concatenate([real * tw_cos - imag * tw_sin, imag * tw_cos + real * tw_sin])
    last = jnp.concatenate([first_ref[0:half, :].T, first_ref[half:, :].T], axis=1)
    conv = jnp.dot(last, turned.astype(jnp.bfloat16), preferred_element_type=jnp.float32)
    conv = jnp.concatenate([conv[:, 0:lane] * rim_query, conv[:, lane:] * scale], axis=1)
    out_ref[...] = conv.astype(jnp.bfloat16)
    if staged:
        put_routes(out_ref, None, *outs)


def output_body(query_ref, w_ref, *refs):
    if len(refs) > 2:
        keep_ref, got_ref, out_ref, conv_ref = refs
        take_routes(keep_ref, got_ref, conv_ref)
    else:
        conv_ref, out_ref = refs
    conv = conv_ref[...].T.astype(jnp.float32)
    mixed_out = (query_ref[...] * conv).astype(jnp.bfloat16)
    out_ref[...] = jnp.dot(mixed_out, w_ref[...], preferred_element_type=jnp.float32).astype(
        jnp.bfloat16
    )


def permute(array, partner):
    return lax.ppermute(array, seq, [(i, partner(i)) for i in range(lax.axis_size(seq))])


def bf16(*shape):
    return jax.ShapeDtypeStruct(shape, jnp.bfloat16)


def exchange(keep, give, near, home):
    turns, size = keep.shape[0], keep.shape[1] // 2 // chan_tile * chan_tile
    lanes, extra = keep.shape[2], keep.shape[1] - 2 * size
    got = permute(give, lambda i: i ^ 1)
    near = permute(near, lambda i: i ^ 2)
    far = call(
        functools.partial(merge_body, size),
        (bf16(4 * size + extra, lanes),) * turns,
        (keep, got),
        [pltpu.VMEM] * 2,
        moved=4 * keep.size,
    )
    routes = routes_of(lax.axis_size("chip"))
    far = [permute(part, lambda i: i ^ 2 * route[i % 2]) for part, route in zip(far, routes)]
    count = 2 * turns + 2
    half = bf16(count * size + count // 2 * extra, lanes)
    keep, give = call(
        functools.partial(split_body, size),
        (half, half),
        (*far, near, home),
        [pltpu.VMEM] * (turns + 2),
        moved=4 * keep.size,
    )
    return keep, permute(give, lambda i: i ^ 1)


def local(tokens, norm_gain, w_in, short_filter, long_filter, medium_filter, skip_gain, w_out):
    rows, width = tokens.shape
    devices, chips = lax.axis_size(seq), lax.axis_size("chip")
    chans = width // devices
    first, twist, inner = spectral_tables(devices, rows, chans)
    staged = chans == chan_tile and chips >= 4 and short_filter.shape[0] <= 3
    if staged:
        packed_shape = (2 * rows // lane * width, lane)
    else:
        packed_shape = (width, 2 * rows + lane)

    def pieces(shape, extra):
        if not staged:
            return (bf16(*shape),)
        size, turns = 2 * shape[0] // devices + extra, chips // 2 - 1
        near = size + size - extra + chan_tile
        return (bf16(turns, size, shape[1]),) * 2 + (bf16(near, shape[1]), bf16(size, shape[1]))

    def scratch(*shapes):
        return [pltpu.VMEM(*shape) for shape in shapes] if staged else []

    def swap(parts):
        if staged:
            return exchange(*parts)
        (array,) = parts
        blocks = array.reshape(devices, -1, array.shape[-1])
        return (lax.all_to_all(blocks, seq, split_axis=0, concat_axis=0).reshape(array.shape),)

    query = call(
        query_body,
        jax.ShapeDtypeStruct((rows, width), jnp.float32),
        (tokens, norm_gain[None, :], w_in, short_filter),
        [pltpu.VMEM] * 4,
        flops=2 * rows * width * width,
        moved=800_000,
    )
    args = (tokens, norm_gain[None, :], w_in, short_filter, long_filter, medium_filter, skip_gain[None, :])
    args = tuple(pltpu.with_memory_space_constraint(arg, pltpu.HBM) for arg in args)
    packed = (packed_shape, jnp.bfloat16)
    parts = call(
        prepare_body,
        pieces(packed_shape, edge),
        args,
        [pltpu.HBM] * len(args),
        scratch(packed, ((chips, edge, lane), jnp.bfloat16))
        + [pltpu.VMEM(arg.shape, arg.dtype) for arg in args]
        + [pltpu.SemaphoreType.DMA((len(args),))],
        flops=2 * rows * width * 3 * width,
        moved=1_500_000,
    )
    conv = ((width, rows), jnp.bfloat16)
    parts = swap(parts)
    parts = call(
        functools.partial(convolve_body, chans, short_filter.shape[0] - 1),
        pieces((width, rows), 0),
        (first, twist, inner, *parts),
        [pltpu.VMEM] * (3 + len(parts)),
        scratch(packed, ((devices, edge, lane), jnp.float32), ((lane, lane), jnp.float32), conv),
        flops=18 * first.shape[0] * width * rows,
        moved=2_000_000,
    )
    parts = swap(parts)
    return call(
        output_body,
        bf16(rows, width),
        (query, w_out, *parts),
        [pltpu.VMEM] * (2 + len(parts)),
        scratch(conv),
        flops=2 * rows * width * width,
        moved=600_000,
    )


def solution(mesh):
    groups, devices = mesh.devices.shape
    split = jax.sharding.Mesh(mesh.devices.reshape(groups, devices // 2, 2), ("groups", *seq))
    rows = P(("groups", *seq), None)
    placed = (rows, P(), P(), P(), P(seq, None), P(), P(), P())
    return jax.shard_map(local, mesh=split, in_specs=placed, out_specs=rows, check_vma=False)
```

```python
import functools
import math

import jax
import jax.numpy as jnp
import numpy as np
from jax import lax
from jax.experimental import pallas as pl
from jax.experimental.pallas import tpu as pltpu
from jax.sharding import PartitionSpec as P

epsilon = 1e-06
edge = 8
lane = 128
seq = ("chip", "core")
rim_step = 2 * edge
chan_tile = 16
copy_parts = 4
vmem_bytes = 32 * 2**20


def whole(space):
    return pl.BlockSpec(memory_space=space)


def call(body, outs, args, spaces, scratch=(), flops=0, moved=0):
    return pl.pallas_call(
        body,
        out_shape=outs,
        in_specs=[whole(space) for space in spaces],
        out_specs=jax.tree.map(lambda _: whole(pltpu.VMEM), outs),
        scratch_shapes=list(scratch),
        compiler_params=pltpu.CompilerParams(vmem_limit_bytes=vmem_bytes),
        cost_estimate=pl.CostEstimate(flops=flops, bytes_accessed=moved, transcendentals=0),
    )(*args)


def spectral_tables(devices, rows, chans):
    full_len = devices * rows
    freqs = 4 * np.arange(devices) + 1
    eye = np.eye(chans)
    angle = 2.0 * math.pi / (4 * devices) * (freqs[:, None] * np.arange(devices)[None, :] % (4 * devices))
    cosine, sine = np.kron(np.cos(angle), eye), np.kron(np.sin(angle), eye)
    first = np.concatenate([cosine, -sine])
    offsets = np.arange(rows)
    twist = 2.0 * math.pi / (4 * full_len) * (freqs[:, None] * offsets[None, :] % (4 * full_len))
    twist = np.concatenate([np.cos(twist), np.sin(twist)])
    if chans % 8:
        twist = np.repeat(twist, chans, axis=0)
    turn = 2.0 * math.pi / rows * (offsets[:, None] * offsets[None, :] % rows)
    inner = np.concatenate([np.cos(turn), np.sin(turn)], axis=1)
    return (
        jnp.asarray(first, jnp.bfloat16),
        jnp.asarray(twist, jnp.float32),
        jnp.asarray(inner, jnp.bfloat16),
    )


def routes_of(chips):
    return [(d, d + 1) for d in range(chips - 2, 1, -2)]


def carried(route, core):
    mine, others = route
    return jnp.where(core == 0, mine, others), jnp.where(core == 0, others, mine)


def put_routes(source_ref, rim_ref, keep_ref, give_ref, near_ref, home_ref):
    chip, core = lax.axis_index("chip"), lax.axis_index("core")
    size = source_ref.shape[0] // 2 // (lax.axis_size("chip"))
    extra = home_ref.shape[0] - 2 * size

    def put(out_ref, distance):
        start = pl.multiple_of((chip ^ distance) * 2 * size, 2 * size)
        out_ref[0 : 2 * size, :] = source_ref[pl.ds(start, 2 * size), :]
        if extra:
            out_ref[2 * size : 2 * size + extra, :] = rim_ref[chip ^ distance]

    for turn, route in enumerate(routes_of(lax.axis_size("chip"))):
        own, other = carried(route, core)
        put(keep_ref.at[turn], own)
        put(give_ref.at[turn], other)
    put(home_ref, 0)
    put(near_ref, 1)
    begin = 2 * size + extra
    near_ref[begin : begin + 2 * size, :] = home_ref[0 : 2 * size, :]
    near_ref[begin + 2 * size :, :] = home_ref[0:chan_tile, :]


def half_rims(first_ref, second_ref, begin):
    pair = [ref[begin : begin + edge, :].astype(jnp.float32) for ref in (first_ref, second_ref)]
    pair = [rims[0 : edge // 2] for rims in pair]
    return jnp.concatenate(pair).astype(jnp.bfloat16)


def merge_body(size, keep_ref, got_ref, *out_refs):
    for turn, out_ref in enumerate(out_refs):
        out_ref[0 : 2 * size, :] = keep_ref[turn, 0 : 2 * size, :]
        out_ref[2 * size : 4 * size, :] = got_ref[turn, 0 : 2 * size, :]
        if out_ref.shape[0] > 4 * size:
            out_ref[4 * size :, :] = half_rims(keep_ref.at[turn], got_ref.at[turn], 2 * size)


def split_body(size, *refs):
    far_refs, (near_ref, home_ref, keep_ref, give_ref) = refs[:-4], refs[-4:]
    core = lax.axis_index("core")
    sources = [(far_ref, 2 * sender) for far_ref in far_refs for sender in range(2)]
    sources += [(near_ref, 0), (home_ref, 0)]
    for out_ref, target in ((keep_ref, core), (give_ref, 1 - core)):
        for place, (source_ref, block) in enumerate(sources):
            start = pl.multiple_of((block + target) * size, size)
            out_ref[place * size : (place + 1) * size, :] = source_ref[pl.ds(start, size), :]
        begin = len(sources) * size
        if out_ref.shape[0] > begin:
            for far_ref in far_refs:
                out_ref[begin : begin + edge, :] = far_ref[4 * size :, :]
                begin += edge
            out_ref[begin:, :] = half_rims(near_ref, home_ref, 2 * size)


def take_routes(keep_ref, got_ref, target_ref, rim_ref=None):
    chip, core = lax.axis_index("chip"), lax.axis_index("core")
    routes = routes_of(lax.axis_size("chip"))
    count = 2 * len(routes) + 2
    size = target_ref.shape[0] // (2 * lax.axis_size("chip"))
    places = [(*carried(route, core), sender) for route in routes for sender in range(2)]
    places += [(1, 1, 0), (0, 0, 0)]
    for place, (own, other, sender) in enumerate(places):
        for ref, distance, carrier in ((keep_ref, own, core), (got_ref, other, 1 - core)):
            device = (chip ^ distance) * 2 + (carrier if sender == 0 else 1 - carrier)
            start = pl.multiple_of(device * size, size)
            target_ref[pl.ds(start, size), :] = ref[place * size : (place + 1) * size, :]
            if rim_ref is not None:
                begin = count * size + place // 2 * edge
                rims = ref[begin : begin + edge, :].astype(jnp.float32)
                rim_ref[device, 0 : edge // 2, :] = rims[place % 2 * edge // 2 : (place % 2 + 1) * edge // 2]


def normed_of(tokens_ref, gain_ref):
    inputs = tokens_ref[...].astype(jnp.float32)
    mean_sq = jnp.mean(inputs * inputs, axis=-1, keepdims=True)
    return (inputs * lax.rsqrt(mean_sq + epsilon) * gain_ref[...]).astype(jnp.bfloat16)


def projected_of(normed, weights):
    projected = jnp.dot(normed, weights, preferred_element_type=jnp.float32)
    projected = projected.astype(jnp.bfloat16).astype(jnp.float32)
    return jnp.concatenate([projected, jnp.zeros((edge, projected.shape[1]), jnp.float32)])


def short_mix(projected, taps):
    acc = taps[0:1] * projected
    for tap_num in range(1, taps.shape[0]):
        acc = acc + taps[tap_num : tap_num + 1] * pltpu.roll(projected, tap_num, 0)
    return acc


def query_body(tokens_ref, gain_ref, w_ref, short_ref, query_ref):
    rows, width = tokens_ref.shape
    cols = slice(0, width)
    query = short_mix(projected_of(normed_of(tokens_ref, gain_ref), w_ref[:, cols]), short_ref[:, cols])
    query_ref[...] = query[0:rows]
    row = lax.broadcasted_iota(jnp.int32, (edge, width), 0)
    query_ref[0:edge, :] = jnp.where(row < short_ref.shape[0] - 1, 1.0, query[0:edge])


def prepare_body(*refs):
    hbm, outs, held, sems = refs[:7], refs[7:-8], refs[-8:-1], refs[-1]
    staged = len(outs) > 1
    outs, (packed_ref, rim_ref) = (outs[:-2], outs[-2:]) if staged else (outs, (outs[0], None))
    tokens_ref, gain_ref, w_ref, short_ref, long_ref, medium_ref, skip_ref = held
    rows, width = tokens_ref.shape
    copies = []
    for index, (source, target) in enumerate(zip(hbm, held)):
        parts = copy_parts if source.shape[0] % (16 * copy_parts) == 0 else 1
        step = source.shape[0] // parts
        places = [slice(part * step, (part + 1) * step) for part in range(parts)]
        copies.append(
            [
                pltpu.make_async_copy(source.at[place], target.at[place], sems.at[index, part])
                for part, place in enumerate(places)
            ]
        )
    for copy in sum(copies, []):
        copy.start()

    def wait_for(*operands):
        for operand in operands:
            for copy in copies[operand]:
                copy.wait()

    wait_for(0, 1)
    normed = normed_of(tokens_ref, gain_ref)
    wait_for(2, 3)
    query_cols, cols = slice(0, width), slice(width, 3 * width)
    mixed = short_mix(projected_of(normed, w_ref[:, cols]), short_ref[:, cols])
    key, value = mixed[:, 0:width], mixed[:, width:]
    put_columns(packed_ref, 0, (key[0:rows] * value[0:rows]).astype(jnp.bfloat16).T)
    rims = [(key[0:edge], key[rows:]), (value[0:edge], value[rows:])]
    some = jnp.concatenate([normed[0 : 2 * edge], normed[rows - 2 * edge :]])
    some = short_mix(projected_of(some, w_ref[:, query_cols]), short_ref[:, query_cols])
    put_rim(packed_ref, rim_ref, [*rims, (some[0:edge], some[4 * edge :])])
    wait_for(4, 5, 6)
    med_len = medium_ref.shape[0]
    is_first = jnp.where(lax.axis_index(seq) == 0, 1.0, 0.0)
    head = long_ref[0:med_len, :] + is_first * medium_ref[...]
    head_row = lax.broadcasted_iota(jnp.int32, head.shape, 0)
    head = head + jnp.where(head_row == 0, is_first * skip_ref[...], 0.0)
    taps = jnp.concatenate([head, long_ref[med_len:, :]]).astype(jnp.bfloat16)
    put_columns(packed_ref, rows, taps.T)
    if staged:
        put_routes(packed_ref, rim_ref, *outs)


def put_columns(packed_ref, begin, values):
    if packed_ref.shape[1] > lane:
        packed_ref[:, begin : begin + values.shape[1]] = values
        return
    devices = lax.axis_size(seq)
    chans = values.shape[0] // devices
    size = packed_ref.shape[0] // devices
    for device in range(devices):
        for column in range(values.shape[1] // lane):
            start = device * size + (begin // lane + column) * chans
            packed_ref[start : start + chans, :] = values[
                device * chans : (device + 1) * chans, column * lane : (column + 1) * lane
            ]


def put_rim(packed_ref, rim_ref, parts):
    width = parts[0][0].shape[1]
    if rim_ref is None:
        rows = [row for part in parts for row in part]
        rows.append(jnp.zeros((lane - 3 * rim_step, width), jnp.float32))
        rim = jnp.concatenate(rows).T
        packed_ref[:, packed_ref.shape[1] - lane :] = rim.astype(jnp.bfloat16)
        return
    chips = rim_ref.shape[0]
    span = width // chips
    half = edge // 4
    group = lax.broadcasted_iota(jnp.int32, (edge // 2, lane), 1) // span
    parts = [jnp.concatenate([own[0:half], after[0:half]]) for own, after in parts]
    for chip in range(chips):
        begin = chip * span // lane * lane
        place = chip * span % lane
        rim = jnp.zeros((edge // 2, lane), jnp.float32)
        for index, part in enumerate(parts):
            shift = (index * span - place) % lane
            moved = part[:, begin : begin + lane]
            moved = pltpu.roll(moved, shift, 1) if shift else moved
            rim = jnp.where(group == index, moved, rim)
        rim = jnp.concatenate([rim, jnp.zeros((edge // 2, lane), jnp.float32)])
        rim_ref[chip] = rim.astype(jnp.bfloat16)


def columns_of(packed_ref, chans, rows):
    devices, count = lax.axis_size(seq), 2 * rows // lane
    blocks = packed_ref[...].reshape(devices, count * chans, lane)
    columns = [blocks[:, i * chans : (i + 1) * chans].reshape(-1, lane) for i in range(count)]
    return jnp.concatenate(columns, axis=1)


def rim_of(rim_ref, turned_ref, chans):
    span = 2 * chans
    rim = rim_ref[...].reshape(-1, lane)
    row = lax.broadcasted_iota(jnp.int32, rim.shape, 0)
    column = lax.broadcasted_iota(jnp.int32, rim.shape, 1)
    before = pltpu.roll(rim, edge - edge // 4, 0)
    rim = rim + jnp.where(row < edge, 0.0, before)
    signal = rim * pltpu.roll(rim, lane - span, 1)
    turned_ref[...] = jnp.where(column < span, signal, rim).T
    found = []
    for begin in (0, 2 * span):
        start = pl.multiple_of(begin + lax.axis_index("core") * chans, chans)
        part = turned_ref[pl.ds(start, chans), :]
        blocks = [part] + [pltpu.roll(part, lane - edge * k, 1) for k in range(1, rim_ref.shape[0])]
        found.append(jnp.concatenate(blocks))
    return found


def twist_rows(twist_ref, chans):
    half, rows = twist_ref.shape[0] // 2, twist_ref.shape[1]
    tables = twist_ref[0:half, :], twist_ref[half:, :]
    if chans % 8:
        return tables
    return tuple(
        jnp.broadcast_to(table[:, None, :], (half, chans, rows)).reshape(half * chans, rows)
        for table in tables
    )


def convolve_body(chans, rim_count, first_ref, twist_ref, inner_ref, *refs):
    rows = twist_ref.shape[1]
    half = first_ref.shape[0] // 2
    scale = chans / (half * rows)
    staged = len(refs) > 2
    if staged:
        keep_ref, got_ref, *outs, packed_ref, rim_ref, turned_ref, out_ref = refs
        rim_ref[...] = jnp.zeros_like(rim_ref)
        take_routes(keep_ref, got_ref, packed_ref, rim_ref)
        values = columns_of(packed_ref, chans, rows)
        rim_signal, rim_query = rim_of(rim_ref, turned_ref, chans)
    else:
        packed_ref, out_ref = refs
        values = packed_ref[:, : 2 * rows]
        rim = packed_ref[:, 2 * rows :].astype(jnp.float32)
        before = jnp.concatenate([jnp.zeros((chans, lane), jnp.float32), rim[:-chans]])
        rim = rim + pltpu.roll(before, lane - edge, 1)
        rim_signal = rim * pltpu.roll(rim, lane - rim_step, 1)
        rim_query = pltpu.roll(rim, lane - 2 * rim_step, 1)
    in_rim = lax.broadcasted_iota(jnp.int32, rim_signal.shape, 1) < rim_count
    rim_signal = rim_signal.astype(jnp.bfloat16)
    rim_query = scale * jnp.where(in_rim, rim_query, 1.0)
    signal = jnp.concatenate(
        [jnp.where(in_rim, rim_signal, values[:, 0:lane]), values[:, lane:rows]], axis=1
    )
    cosine, sine = inner_ref[:, 0:rows], inner_ref[:, rows:]
    inner = jnp.concatenate(
        [jnp.concatenate([cosine, -sine], axis=1), jnp.concatenate([sine, cosine], axis=1)]
    )
    spread_of = functools.partial(jnp.dot, first_ref[...], preferred_element_type=jnp.float32)
    spreads = [spread_of(values[:, rows : 2 * rows]), spread_of(signal)]
    tw_cos, tw_sin = twist_rows(twist_ref, chans)
    turned = []
    for spread in spreads:
        real, imag = spread[0:half], spread[half:]
        turned.append([real * tw_cos + imag * tw_sin, imag * tw_cos - real * tw_sin])
    turned = jnp.concatenate([jnp.concatenate(pair, axis=1).astype(jnp.bfloat16) for pair in turned])
    spectra = jnp.dot(turned, inner, preferred_element_type=jnp.float32)
    fil_re, fil_im = spectra[0:half, 0:rows], spectra[0:half, rows:]
    real, imag = spectra[half:, 0:rows], spectra[half:, rows:]
    product = [real * fil_im + imag * fil_re, real * fil_re - imag * fil_im]
    product = jnp.concatenate(product, axis=1).astype(jnp.bfloat16)
    back = jnp.dot(product, inner, preferred_element_type=jnp.float32)
    imag, real = back[:, 0:rows], back[:, rows:]
    turned = jnp.concatenate([real * tw_cos - imag * tw_sin, imag * tw_cos + real * tw_sin])
    last = jnp.concatenate([first_ref[0:half, :].T, first_ref[half:, :].T], axis=1)
    conv = jnp.dot(last, turned.astype(jnp.bfloat16), preferred_element_type=jnp.float32)
    conv = jnp.concatenate([conv[:, 0:lane] * rim_query, conv[:, lane:] * scale], axis=1)
    out_ref[...] = conv.astype(jnp.bfloat16)
    if staged:
        put_routes(out_ref, None, *outs)


def output_body(query_ref, w_ref, *refs):
    if len(refs) > 2:
        keep_ref, got_ref, out_ref, conv_ref = refs
        take_routes(keep_ref, got_ref, conv_ref)
    else:
        conv_ref, out_ref = refs
    conv = conv_ref[...].T.astype(jnp.float32)
    mixed_out = (query_ref[...] * conv).astype(jnp.bfloat16)
    out_ref[...] = jnp.dot(mixed_out, w_ref[...], preferred_element_type=jnp.float32).astype(
        jnp.bfloat16
    )


def permute(array, partner):
    return lax.ppermute(array, seq, [(i, partner(i)) for i in range(lax.axis_size(seq))])


def bf16(*shape):
    return jax.ShapeDtypeStruct(shape, jnp.bfloat16)


def exchange(keep, give, near, home):
    turns, size = keep.shape[0], keep.shape[1] // 2 // chan_tile * chan_tile
    lanes, extra = keep.shape[2], keep.shape[1] - 2 * size
    got = permute(give, lambda i: i ^ 1)
    near = permute(near, lambda i: i ^ 2)
    far = call(
        functools.partial(merge_body, size),
        (bf16(4 * size + extra, lanes),) * turns,
        (keep, got),
        [pltpu.VMEM] * 2,
        moved=4 * keep.size,
    )
    routes = routes_of(lax.axis_size("chip"))
    far = [permute(part, lambda i: i ^ 2 * route[i % 2]) for part, route in zip(far, routes)]
    count = 2 * turns + 2
    half = bf16(count * size + count // 2 * extra, lanes)
    keep, give = call(
        functools.partial(split_body, size),
        (half, half),
        (*far, near, home),
        [pltpu.VMEM] * (turns + 2),
        moved=4 * keep.size,
    )
    return keep, permute(give, lambda i: i ^ 1)


def local(tokens, norm_gain, w_in, short_filter, long_filter, medium_filter, skip_gain, w_out):
    rows, width = tokens.shape
    devices, chips = lax.axis_size(seq), lax.axis_size("chip")
    chans = width // devices
    first, twist, inner = spectral_tables(devices, rows, chans)
    staged = chans == chan_tile and chips >= 4 and short_filter.shape[0] <= 3
    if staged:
        packed_shape = (2 * rows // lane * width, lane)
    else:
        packed_shape = (width, 2 * rows + lane)

    def pieces(shape, extra):
        if not staged:
            return (bf16(*shape),)
        size, turns = 2 * shape[0] // devices + extra, chips // 2 - 1
        near = size + size - extra + chan_tile
        return (bf16(turns, size, shape[1]),) * 2 + (bf16(near, shape[1]), bf16(size, shape[1]))

    def scratch(*shapes):
        return [pltpu.VMEM(*shape) for shape in shapes] if staged else []

    def swap(parts):
        if staged:
            return exchange(*parts)
        (array,) = parts
        blocks = array.reshape(devices, -1, array.shape[-1])
        return (lax.all_to_all(blocks, seq, split_axis=0, concat_axis=0).reshape(array.shape),)

    query = call(
        query_body,
        jax.ShapeDtypeStruct((rows, width), jnp.float32),
        (tokens, norm_gain[None, :], w_in, short_filter),
        [pltpu.VMEM] * 4,
        flops=2 * rows * width * width,
        moved=800_000,
    )
    args = (tokens, norm_gain[None, :], w_in, short_filter, long_filter, medium_filter, skip_gain[None, :])
    args = tuple(pltpu.with_memory_space_constraint(arg, pltpu.HBM) for arg in args)
    packed = (packed_shape, jnp.bfloat16)
    parts = call(
        prepare_body,
        pieces(packed_shape, edge),
        args,
        [pltpu.HBM] * len(args),
        scratch(packed, ((chips, edge, lane), jnp.bfloat16))
        + [pltpu.VMEM(arg.shape, arg.dtype) for arg in args]
        + [pltpu.SemaphoreType.DMA((len(args), copy_parts))],
        flops=2 * rows * width * 3 * width,
        moved=1_500_000,
    )
    conv = ((width, rows), jnp.bfloat16)
    parts = swap(parts)
    parts = call(
        functools.partial(convolve_body, chans, short_filter.shape[0] - 1),
        pieces((width, rows), 0),
        (first, twist, inner, *parts),
        [pltpu.VMEM] * (3 + len(parts)),
        scratch(packed, ((devices, edge, lane), jnp.float32), ((lane, lane), jnp.float32), conv),
        flops=18 * first.shape[0] * width * rows,
        moved=2_000_000,
    )
    parts = swap(parts)
    return call(
        output_body,
        bf16(rows, width),
        (query, w_out, *parts),
        [pltpu.VMEM] * (2 + len(parts)),
        scratch(conv),
        flops=2 * rows * width * width,
        moved=600_000,
    )


def solution(mesh):
    groups, devices = mesh.devices.shape
    split = jax.sharding.Mesh(mesh.devices.reshape(groups, devices // 2, 2), ("groups", *seq))
    rows = P(("groups", *seq), None)
    placed = (rows, P(), P(), P(), P(seq, None), P(), P(), P())
    return jax.shard_map(local, mesh=split, in_specs=placed, out_specs=rows, check_vma=False)
```

```python
import functools
import math

import jax
import jax.numpy as jnp
import numpy as np
from jax import lax
from jax.experimental import pallas as pl
from jax.experimental.pallas import tpu as pltpu
from jax.sharding import PartitionSpec as P

epsilon = 1e-06
edge = 8
lane = 128
seq = ("chip", "core")
rim_step = 2 * edge
chan_tile = 16
vmem_bytes = 32 * 2**20


def whole(space):
    return pl.BlockSpec(memory_space=space)


def call(body, outs, args, spaces, scratch=(), flops=0, moved=0):
    return pl.pallas_call(
        body,
        out_shape=outs,
        in_specs=[whole(space) for space in spaces],
        out_specs=jax.tree.map(lambda _: whole(pltpu.VMEM), outs),
        scratch_shapes=list(scratch),
        compiler_params=pltpu.CompilerParams(vmem_limit_bytes=vmem_bytes),
        cost_estimate=pl.CostEstimate(flops=flops, bytes_accessed=moved, transcendentals=0),
    )(*args)


def spectral_tables(devices, rows, chans):
    full_len = devices * rows
    freqs = 4 * np.arange(devices) + 1
    eye = np.eye(chans)
    angle = 2.0 * math.pi / (4 * devices) * (freqs[:, None] * np.arange(devices)[None, :] % (4 * devices))
    cosine, sine = np.kron(np.cos(angle), eye), np.kron(np.sin(angle), eye)
    first = np.concatenate([cosine, -sine])
    offsets = np.arange(rows)
    twist = 2.0 * math.pi / (4 * full_len) * (freqs[:, None] * offsets[None, :] % (4 * full_len))
    twist = np.concatenate([np.cos(twist), np.sin(twist)])
    if chans % 8:
        twist = np.repeat(twist, chans, axis=0)
    turn = 2.0 * math.pi / rows * (offsets[:, None] * offsets[None, :] % rows)
    inner = np.concatenate([np.cos(turn), np.sin(turn)], axis=1)
    return (
        jnp.asarray(first, jnp.bfloat16),
        jnp.asarray(twist, jnp.float32),
        jnp.asarray(inner, jnp.bfloat16),
    )


def routes_of(chips):
    return [(d, d + 1) for d in range(chips - 2, 1, -2)]


def carried(route, core):
    mine, others = route
    return jnp.where(core == 0, mine, others), jnp.where(core == 0, others, mine)


def put_routes(source_ref, rim_ref, keep_ref, give_ref, near_ref, home_ref):
    chip, core = lax.axis_index("chip"), lax.axis_index("core")
    size = source_ref.shape[0] // 2 // (lax.axis_size("chip"))
    extra = home_ref.shape[0] - 2 * size

    def put(out_ref, distance):
        start = pl.multiple_of((chip ^ distance) * 2 * size, 2 * size)
        out_ref[0 : 2 * size, :] = source_ref[pl.ds(start, 2 * size), :]
        if extra:
            out_ref[2 * size : 2 * size + extra, :] = rim_ref[chip ^ distance]

    for turn, route in enumerate(routes_of(lax.axis_size("chip"))):
        own, other = carried(route, core)
        put(keep_ref.at[turn], own)
        put(give_ref.at[turn], other)
    put(home_ref, 0)
    put(near_ref, 1)
    begin = 2 * size + extra
    near_ref[begin : begin + 2 * size, :] = home_ref[0 : 2 * size, :]
    near_ref[begin + 2 * size :, :] = home_ref[0:chan_tile, :]


def half_rims(first_ref, second_ref, begin):
    pair = [ref[begin : begin + edge, :].astype(jnp.float32) for ref in (first_ref, second_ref)]
    pair = [rims[0 : edge // 2] for rims in pair]
    return jnp.concatenate(pair).astype(jnp.bfloat16)


def merge_body(size, keep_ref, got_ref, *out_refs):
    for turn, out_ref in enumerate(out_refs):
        out_ref[0 : 2 * size, :] = keep_ref[turn, 0 : 2 * size, :]
        out_ref[2 * size : 4 * size, :] = got_ref[turn, 0 : 2 * size, :]
        if out_ref.shape[0] > 4 * size:
            out_ref[4 * size :, :] = half_rims(keep_ref.at[turn], got_ref.at[turn], 2 * size)


def split_body(size, *refs):
    far_refs, (near_ref, home_ref, keep_ref, give_ref) = refs[:-4], refs[-4:]
    core = lax.axis_index("core")
    sources = [(far_ref, 2 * sender) for far_ref in far_refs for sender in range(2)]
    sources += [(near_ref, 0), (home_ref, 0)]
    for out_ref, target in ((keep_ref, core), (give_ref, 1 - core)):
        for place, (source_ref, block) in enumerate(sources):
            start = pl.multiple_of((block + target) * size, size)
            out_ref[place * size : (place + 1) * size, :] = source_ref[pl.ds(start, size), :]
        begin = len(sources) * size
        if out_ref.shape[0] > begin:
            for far_ref in far_refs:
                out_ref[begin : begin + edge, :] = far_ref[4 * size :, :]
                begin += edge
            out_ref[begin:, :] = half_rims(near_ref, home_ref, 2 * size)


def take_routes(keep_ref, got_ref, target_ref, rim_ref=None):
    chip, core = lax.axis_index("chip"), lax.axis_index("core")
    routes = routes_of(lax.axis_size("chip"))
    count = 2 * len(routes) + 2
    size = target_ref.shape[0] // (2 * lax.axis_size("chip"))
    places = [(*carried(route, core), sender) for route in routes for sender in range(2)]
    places += [(1, 1, 0), (0, 0, 0)]
    for place, (own, other, sender) in enumerate(places):
        for ref, distance, carrier in ((keep_ref, own, core), (got_ref, other, 1 - core)):
            device = (chip ^ distance) * 2 + (carrier if sender == 0 else 1 - carrier)
            start = pl.multiple_of(device * size, size)
            target_ref[pl.ds(start, size), :] = ref[place * size : (place + 1) * size, :]
            if rim_ref is not None:
                begin = count * size + place // 2 * edge
                rims = ref[begin : begin + edge, :].astype(jnp.float32)
                rim_ref[device, 0 : edge // 2, :] = rims[place % 2 * edge // 2 : (place % 2 + 1) * edge // 2]


def normed_of(tokens_ref, gain_ref):
    inputs = tokens_ref[...].astype(jnp.float32)
    mean_sq = jnp.mean(inputs * inputs, axis=-1, keepdims=True)
    return (inputs * lax.rsqrt(mean_sq + epsilon) * gain_ref[...]).astype(jnp.bfloat16)


def projected_of(normed, weights):
    projected = jnp.dot(normed, weights, preferred_element_type=jnp.float32)
    projected = projected.astype(jnp.bfloat16).astype(jnp.float32)
    return jnp.concatenate([projected, jnp.zeros((edge, projected.shape[1]), jnp.float32)])


def short_mix(projected, taps):
    acc = taps[0:1] * projected
    for tap_num in range(1, taps.shape[0]):
        acc = acc + taps[tap_num : tap_num + 1] * pltpu.roll(projected, tap_num, 0)
    return acc


def query_body(tokens_ref, gain_ref, w_ref, short_ref, query_ref):
    rows, width = tokens_ref.shape
    cols = slice(0, width)
    query = short_mix(projected_of(normed_of(tokens_ref, gain_ref), w_ref[:, cols]), short_ref[:, cols])
    query_ref[...] = query[0:rows]
    row = lax.broadcasted_iota(jnp.int32, (edge, width), 0)
    query_ref[0:edge, :] = jnp.where(row < short_ref.shape[0] - 1, 1.0, query[0:edge])


def prepare_body(*refs):
    hbm, outs, held, sems = refs[:7], refs[7:-8], refs[-8:-1], refs[-1]
    staged = len(outs) > 1
    outs, (packed_ref, rim_ref) = (outs[:-2], outs[-2:]) if staged else (outs, (outs[0], None))
    tokens_ref, gain_ref, w_ref, short_ref, long_ref, medium_ref, skip_ref = held
    rows, width = tokens_ref.shape
    copies = [pltpu.make_async_copy(h, v, sems.at[i]) for i, (h, v) in enumerate(zip(hbm, held))]
    for copy in copies:
        copy.start()
    copies[0].wait()
    copies[1].wait()
    normed = normed_of(tokens_ref, gain_ref)
    copies[2].wait()
    copies[3].wait()
    query_cols, cols = slice(0, width), slice(width, 3 * width)
    mixed = short_mix(projected_of(normed, w_ref[:, cols]), short_ref[:, cols])
    key, value = mixed[:, 0:width], mixed[:, width:]
    put_columns(packed_ref, 0, (key[0:rows] * value[0:rows]).astype(jnp.bfloat16).T)
    rims = [(key[0:edge], key[rows:]), (value[0:edge], value[rows:])]
    some = jnp.concatenate([normed[0 : 2 * edge], normed[rows - 2 * edge :]])
    some = short_mix(projected_of(some, w_ref[:, query_cols]), short_ref[:, query_cols])
    put_rim(packed_ref, rim_ref, [*rims, (some[0:edge], some[4 * edge :])])
    for copy in copies[4:]:
        copy.wait()
    med_len = medium_ref.shape[0]
    is_first = jnp.where(lax.axis_index(seq) == 0, 1.0, 0.0)
    head = long_ref[0:med_len, :] + is_first * medium_ref[...]
    row = lax.broadcasted_iota(jnp.int32, (edge, width), 0)
    top = head[0:edge] + jnp.where(row == 0, is_first * skip_ref[...], 0.0)
    taps = jnp.concatenate([top, head[edge:], long_ref[med_len:, :]]).astype(jnp.bfloat16)
    put_columns(packed_ref, rows, taps.T)
    if staged:
        put_routes(packed_ref, rim_ref, *outs)


def put_columns(packed_ref, begin, values):
    if packed_ref.shape[1] > lane:
        packed_ref[:, begin : begin + values.shape[1]] = values
        return
    devices = lax.axis_size(seq)
    chans = values.shape[0] // devices
    size = packed_ref.shape[0] // devices
    for device in range(devices):
        for column in range(values.shape[1] // lane):
            start = device * size + (begin // lane + column) * chans
            packed_ref[start : start + chans, :] = values[
                device * chans : (device + 1) * chans, column * lane : (column + 1) * lane
            ]


def put_rim(packed_ref, rim_ref, parts):
    width = parts[0][0].shape[1]
    if rim_ref is None:
        rows = [row for part in parts for row in part]
        rows.append(jnp.zeros((lane - 3 * rim_step, width), jnp.float32))
        rim = jnp.concatenate(rows).T
        packed_ref[:, packed_ref.shape[1] - lane :] = rim.astype(jnp.bfloat16)
        return
    chips = rim_ref.shape[0]
    span = width // chips
    half = edge // 4
    group = lax.broadcasted_iota(jnp.int32, (edge // 2, lane), 1) // span
    parts = [jnp.concatenate([own[0:half], after[0:half]]) for own, after in parts]
    for chip in range(chips):
        begin = chip * span // lane * lane
        place = chip * span % lane
        rim = jnp.zeros((edge // 2, lane), jnp.float32)
        for index, part in enumerate(parts):
            shift = (index * span - place) % lane
            moved = part[:, begin : begin + lane]
            moved = pltpu.roll(moved, shift, 1) if shift else moved
            rim = jnp.where(group == index, moved, rim)
        rim = jnp.concatenate([rim, jnp.zeros((edge // 2, lane), jnp.float32)])
        rim_ref[chip] = rim.astype(jnp.bfloat16)


def columns_of(packed_ref, chans, rows):
    devices, count = lax.axis_size(seq), 2 * rows // lane
    blocks = packed_ref[...].reshape(devices, count * chans, lane)
    columns = [blocks[:, i * chans : (i + 1) * chans].reshape(-1, lane) for i in range(count)]
    return jnp.concatenate(columns, axis=1)


def rim_of(rim_ref, turned_ref, chans):
    span = 2 * chans
    rim = rim_ref[...].reshape(-1, lane)
    row = lax.broadcasted_iota(jnp.int32, rim.shape, 0)
    column = lax.broadcasted_iota(jnp.int32, rim.shape, 1)
    before = pltpu.roll(rim, edge - edge // 4, 0)
    rim = rim + jnp.where(row < edge, 0.0, before)
    signal = rim * pltpu.roll(rim, lane - span, 1)
    turned_ref[...] = jnp.where(column < span, signal, rim).T
    found = []
    for begin in (0, 2 * span):
        start = pl.multiple_of(begin + lax.axis_index("core") * chans, chans)
        part = turned_ref[pl.ds(start, chans), :]
        blocks = [part] + [pltpu.roll(part, lane - edge * k, 1) for k in range(1, rim_ref.shape[0])]
        found.append(jnp.concatenate(blocks))
    return found


def twist_rows(twist_ref, chans):
    half, rows = twist_ref.shape[0] // 2, twist_ref.shape[1]
    tables = twist_ref[0:half, :], twist_ref[half:, :]
    if chans % 8:
        return tables
    return tuple(
        jnp.broadcast_to(table[:, None, :], (half, chans, rows)).reshape(half * chans, rows)
        for table in tables
    )


def convolve_body(chans, rim_count, first_ref, twist_ref, inner_ref, *refs):
    rows = twist_ref.shape[1]
    half = first_ref.shape[0] // 2
    scale = chans / (half * rows)
    staged = len(refs) > 2
    if staged:
        keep_ref, got_ref, *outs, packed_ref, rim_ref, turned_ref, out_ref = refs
        rim_ref[...] = jnp.zeros_like(rim_ref)
        take_routes(keep_ref, got_ref, packed_ref, rim_ref)
        values = columns_of(packed_ref, chans, rows)
        rim_signal, rim_query = rim_of(rim_ref, turned_ref, chans)
    else:
        packed_ref, out_ref = refs
        values = packed_ref[:, : 2 * rows]
        rim = packed_ref[:, 2 * rows :].astype(jnp.float32)
        before = jnp.concatenate([jnp.zeros((chans, lane), jnp.float32), rim[:-chans]])
        rim = rim + pltpu.roll(before, lane - edge, 1)
        rim_signal = rim * pltpu.roll(rim, lane - rim_step, 1)
        rim_query = pltpu.roll(rim, lane - 2 * rim_step, 1)
    in_rim = lax.broadcasted_iota(jnp.int32, rim_signal.shape, 1) < rim_count
    rim_signal = rim_signal.astype(jnp.bfloat16)
    rim_query = scale * jnp.where(in_rim, rim_query, 1.0)
    signal = jnp.concatenate(
        [jnp.where(in_rim, rim_signal, values[:, 0:lane]), values[:, lane:rows]], axis=1
    )
    cosine, sine = inner_ref[:, 0:rows], inner_ref[:, rows:]
    inner = jnp.concatenate(
        [jnp.concatenate([cosine, -sine], axis=1), jnp.concatenate([sine, cosine], axis=1)]
    )
    spread_of = functools.partial(jnp.dot, first_ref[...], preferred_element_type=jnp.float32)
    spreads = [spread_of(values[:, rows : 2 * rows]), spread_of(signal)]
    tw_cos, tw_sin = twist_rows(twist_ref, chans)
    turned = []
    for spread in spreads:
        real, imag = spread[0:half], spread[half:]
        turned.append([real * tw_cos + imag * tw_sin, imag * tw_cos - real * tw_sin])
    turned = jnp.concatenate([jnp.concatenate(pair, axis=1).astype(jnp.bfloat16) for pair in turned])
    spectra = jnp.dot(turned, inner, preferred_element_type=jnp.float32)
    fil_re, fil_im = spectra[0:half, 0:rows], spectra[0:half, rows:]
    real, imag = spectra[half:, 0:rows], spectra[half:, rows:]
    product = [real * fil_im + imag * fil_re, real * fil_re - imag * fil_im]
    product = jnp.concatenate(product, axis=1).astype(jnp.bfloat16)
    back = jnp.dot(product, inner, preferred_element_type=jnp.float32)
    imag, real = back[:, 0:rows], back[:, rows:]
    turned = jnp.concatenate([real * tw_cos - imag * tw_sin, imag * tw_cos + real * tw_sin])
    last = jnp.concatenate([first_ref[0:half, :].T, first_ref[half:, :].T], axis=1)
    conv = jnp.dot(last, turned.astype(jnp.bfloat16), preferred_element_type=jnp.float32)
    conv = jnp.concatenate([conv[:, 0:lane] * rim_query, conv[:, lane:] * scale], axis=1)
    out_ref[...] = conv.astype(jnp.bfloat16)
    if staged:
        put_routes(out_ref, None, *outs)


def output_body(query_ref, w_ref, *refs):
    if len(refs) > 2:
        keep_ref, got_ref, out_ref, conv_ref = refs
        take_routes(keep_ref, got_ref, conv_ref)
    else:
        conv_ref, out_ref = refs
    conv = conv_ref[...].T.astype(jnp.float32)
    mixed_out = (query_ref[...] * conv).astype(jnp.bfloat16)
    out_ref[...] = jnp.dot(mixed_out, w_ref[...], preferred_element_type=jnp.float32).astype(
        jnp.bfloat16
    )


def permute(array, partner):
    return lax.ppermute(array, seq, [(i, partner(i)) for i in range(lax.axis_size(seq))])


def bf16(*shape):
    return jax.ShapeDtypeStruct(shape, jnp.bfloat16)


def exchange(keep, give, near, home):
    turns, size = keep.shape[0], keep.shape[1] // 2 // chan_tile * chan_tile
    lanes, extra = keep.shape[2], keep.shape[1] - 2 * size
    got = permute(give, lambda i: i ^ 1)
    near = permute(near, lambda i: i ^ 2)
    far = call(
        functools.partial(merge_body, size),
        (bf16(4 * size + extra, lanes),) * turns,
        (keep, got),
        [pltpu.VMEM] * 2,
        moved=4 * keep.size,
    )
    routes = routes_of(lax.axis_size("chip"))
    far = [permute(part, lambda i: i ^ 2 * route[i % 2]) for part, route in zip(far, routes)]
    count = 2 * turns + 2
    half = bf16(count * size + count // 2 * extra, lanes)
    keep, give = call(
        functools.partial(split_body, size),
        (half, half),
        (*far, near, home),
        [pltpu.VMEM] * (turns + 2),
        moved=4 * keep.size,
    )
    return keep, permute(give, lambda i: i ^ 1)


def local(tokens, norm_gain, w_in, short_filter, long_filter, medium_filter, skip_gain, w_out):
    rows, width = tokens.shape
    devices, chips = lax.axis_size(seq), lax.axis_size("chip")
    chans = width // devices
    first, twist, inner = spectral_tables(devices, rows, chans)
    staged = chans == chan_tile and chips >= 4 and short_filter.shape[0] <= 3
    if staged:
        packed_shape = (2 * rows // lane * width, lane)
    else:
        packed_shape = (width, 2 * rows + lane)

    def pieces(shape, extra):
        if not staged:
            return (bf16(*shape),)
        size, turns = 2 * shape[0] // devices + extra, chips // 2 - 1
        near = size + size - extra + chan_tile
        return (bf16(turns, size, shape[1]),) * 2 + (bf16(near, shape[1]), bf16(size, shape[1]))

    def scratch(*shapes):
        return [pltpu.VMEM(*shape) for shape in shapes] if staged else []

    def swap(parts):
        if staged:
            return exchange(*parts)
        (array,) = parts
        blocks = array.reshape(devices, -1, array.shape[-1])
        return (lax.all_to_all(blocks, seq, split_axis=0, concat_axis=0).reshape(array.shape),)

    query = call(
        query_body,
        jax.ShapeDtypeStruct((rows, width), jnp.float32),
        (tokens, norm_gain[None, :], w_in, short_filter),
        [pltpu.VMEM] * 4,
        flops=2 * rows * width * width,
        moved=800_000,
    )
    args = (tokens, norm_gain[None, :], w_in, short_filter, long_filter, medium_filter, skip_gain[None, :])
    args = tuple(pltpu.with_memory_space_constraint(arg, pltpu.HBM) for arg in args)
    packed = (packed_shape, jnp.bfloat16)
    parts = call(
        prepare_body,
        pieces(packed_shape, edge),
        args,
        [pltpu.HBM] * len(args),
        scratch(packed, ((chips, edge, lane), jnp.bfloat16))
        + [pltpu.VMEM(arg.shape, arg.dtype) for arg in args]
        + [pltpu.SemaphoreType.DMA((len(args),))],
        flops=2 * rows * width * 3 * width,
        moved=1_500_000,
    )
    conv = ((width, rows), jnp.bfloat16)
    parts = swap(parts)
    parts = call(
        functools.partial(convolve_body, chans, short_filter.shape[0] - 1),
        pieces((width, rows), 0),
        (first, twist, inner, *parts),
        [pltpu.VMEM] * (3 + len(parts)),
        scratch(packed, ((devices, edge, lane), jnp.float32), ((lane, lane), jnp.float32), conv),
        flops=18 * first.shape[0] * width * rows,
        moved=2_000_000,
    )
    parts = swap(parts)
    return call(
        output_body,
        bf16(rows, width),
        (query, w_out, *parts),
        [pltpu.VMEM] * (2 + len(parts)),
        scratch(conv),
        flops=2 * rows * width * width,
        moved=600_000,
    )


def solution(mesh):
    groups, devices = mesh.devices.shape
    split = jax.sharding.Mesh(mesh.devices.reshape(groups, devices // 2, 2), ("groups", *seq))
    rows = P(("groups", *seq), None)
    placed = (rows, P(), P(), P(), P(seq, None), P(), P(), P())
    return jax.shard_map(local, mesh=split, in_specs=placed, out_specs=rows, check_vma=False)
```

```python
import functools
import math

import jax
import jax.numpy as jnp
import numpy as np
from jax import lax
from jax.experimental import pallas as pl
from jax.experimental.pallas import tpu as pltpu
from jax.sharding import PartitionSpec as P

epsilon = 1e-06
edge = 8
lane = 128
seq = ("chip", "core")
rim_step = 2 * edge
chan_tile = 16
vmem_bytes = 32 * 2**20


def whole(space):
    return pl.BlockSpec(memory_space=space)


def call(body, outs, args, spaces, scratch=(), flops=0, moved=0):
    return pl.pallas_call(
        body,
        out_shape=outs,
        in_specs=[whole(space) for space in spaces],
        out_specs=jax.tree.map(lambda _: whole(pltpu.VMEM), outs),
        scratch_shapes=list(scratch),
        compiler_params=pltpu.CompilerParams(vmem_limit_bytes=vmem_bytes),
        cost_estimate=pl.CostEstimate(flops=flops, bytes_accessed=moved, transcendentals=0),
    )(*args)


def spectral_tables(devices, rows, chans):
    full_len = devices * rows
    freqs = 4 * np.arange(devices) + 1
    eye = np.eye(chans)
    angle = 2.0 * math.pi / (4 * devices) * (freqs[:, None] * np.arange(devices)[None, :] % (4 * devices))
    cosine, sine = np.kron(np.cos(angle), eye), np.kron(np.sin(angle), eye)
    first = np.concatenate([cosine, -sine])
    offsets = np.arange(rows)
    twist = 2.0 * math.pi / (4 * full_len) * (freqs[:, None] * offsets[None, :] % (4 * full_len))
    twist = np.concatenate([np.cos(twist), np.sin(twist)])
    if chans % 8:
        twist = np.repeat(twist, chans, axis=0)
    turn = 2.0 * math.pi / rows * (offsets[:, None] * offsets[None, :] % rows)
    inner = np.concatenate([np.cos(turn), np.sin(turn)], axis=1)
    return (
        jnp.asarray(first, jnp.bfloat16),
        jnp.asarray(twist, jnp.float32),
        jnp.asarray(inner, jnp.bfloat16),
    )


def routes_of(chips):
    return [(d, d + 1) for d in range(chips - 2, 1, -2)]


def carried(route, core):
    mine, others = route
    return jnp.where(core == 0, mine, others), jnp.where(core == 0, others, mine)


def put_routes(source_ref, rim_ref, keep_ref, give_ref, near_ref, home_ref):
    chip, core = lax.axis_index("chip"), lax.axis_index("core")
    size = source_ref.shape[0] // 2 // (lax.axis_size("chip"))
    extra = home_ref.shape[0] - 2 * size

    def put(out_ref, distance):
        start = pl.multiple_of((chip ^ distance) * 2 * size, 2 * size)
        out_ref[0 : 2 * size, :] = source_ref[pl.ds(start, 2 * size), :]
        if extra:
            out_ref[2 * size : 2 * size + extra, :] = rim_ref[chip ^ distance]

    for turn, route in enumerate(routes_of(lax.axis_size("chip"))):
        own, other = carried(route, core)
        put(keep_ref.at[turn], own)
        put(give_ref.at[turn], other)
    put(home_ref, 0)
    put(near_ref, 1)
    begin = 2 * size
    if extra:
        rim = rim_ref[chip ^ 1].astype(jnp.float32)
        near_ref[begin : begin + chan_tile, :] = jnp.concatenate([rim, rim]).astype(jnp.bfloat16)
        begin += chan_tile
    near_ref[begin : begin + 2 * size, :] = home_ref[0 : 2 * size, :]
    begin += 2 * size
    near_ref[begin:, :] = home_ref[0 : near_ref.shape[0] - begin, :]


def half_rims(first_ref, second_ref, begin):
    pair = [ref[begin : begin + edge, :].astype(jnp.float32) for ref in (first_ref, second_ref)]
    return jnp.concatenate([rims[0 : edge // 2] for rims in pair])


def merge_body(size, keep_ref, got_ref, *out_refs):
    for turn, out_ref in enumerate(out_refs):
        out_ref[0 : 2 * size, :] = keep_ref[turn, 0 : 2 * size, :]
        out_ref[2 * size : 4 * size, :] = got_ref[turn, 0 : 2 * size, :]
        if out_ref.shape[0] > 4 * size:
            rims = half_rims(keep_ref.at[turn], got_ref.at[turn], 2 * size)
            out_ref[4 * size :, :] = rims.astype(jnp.bfloat16)


def split_body(size, *refs):
    far_refs, (near_ref, home_ref, keep_ref, give_ref) = refs[:-4], refs[-4:]
    core = lax.axis_index("core")
    sources = [(far_ref, 2 * sender) for far_ref in far_refs for sender in range(2)]
    sources += [(near_ref, 0), (home_ref, 0)]
    for out_ref, target in ((keep_ref, core), (give_ref, 1 - core)):
        for place, (source_ref, block) in enumerate(sources):
            start = pl.multiple_of((block + target) * size, size)
            out_ref[place * size : (place + 1) * size, :] = source_ref[pl.ds(start, size), :]
        begin = len(sources) * size
        if out_ref.shape[0] > begin:
            rims = [far_ref[4 * size :, :].astype(jnp.float32) for far_ref in far_refs]
            rims.append(half_rims(near_ref, home_ref, 2 * size))
            out_ref[begin:, :] = jnp.concatenate(rims).astype(jnp.bfloat16)


def take_routes(keep_ref, got_ref, target_ref, rim_ref=None):
    chip, core = lax.axis_index("chip"), lax.axis_index("core")
    routes = routes_of(lax.axis_size("chip"))
    count = 2 * len(routes) + 2
    size = target_ref.shape[0] // (2 * lax.axis_size("chip"))
    places = [(*carried(route, core), sender) for route in routes for sender in range(2)]
    places += [(1, 1, 0), (0, 0, 0)]
    for place, (own, other, sender) in enumerate(places):
        for ref, distance, carrier in ((keep_ref, own, core), (got_ref, other, 1 - core)):
            device = (chip ^ distance) * 2 + (carrier if sender == 0 else 1 - carrier)
            start = pl.multiple_of(device * size, size)
            target_ref[pl.ds(start, size), :] = ref[place * size : (place + 1) * size, :]
            if rim_ref is not None:
                begin = place * edge // 2
                rims = ref[count * size :, :].astype(jnp.float32)
                rim_ref[device, 0 : edge // 2, :] = rims[begin : begin + edge // 2]


def normed_of(tokens_ref, gain_ref):
    inputs = tokens_ref[...].astype(jnp.float32)
    mean_sq = jnp.mean(inputs * inputs, axis=-1, keepdims=True)
    return (inputs * lax.rsqrt(mean_sq + epsilon) * gain_ref[...]).astype(jnp.bfloat16)


def projected_of(normed, weights):
    projected = jnp.dot(normed, weights, preferred_element_type=jnp.float32)
    projected = projected.astype(jnp.bfloat16).astype(jnp.float32)
    return jnp.concatenate([projected, jnp.zeros((edge, projected.shape[1]), jnp.float32)])


def short_mix(projected, taps):
    acc = taps[0:1] * projected
    for tap_num in range(1, taps.shape[0]):
        acc = acc + taps[tap_num : tap_num + 1] * pltpu.roll(projected, tap_num, 0)
    return acc


def query_body(tokens_ref, gain_ref, w_ref, short_ref, query_ref):
    rows, width = tokens_ref.shape
    cols = slice(0, width)
    query = short_mix(projected_of(normed_of(tokens_ref, gain_ref), w_ref[:, cols]), short_ref[:, cols])
    query_ref[...] = query[0:rows]
    row = lax.broadcasted_iota(jnp.int32, (edge, width), 0)
    query_ref[0:edge, :] = jnp.where(row < short_ref.shape[0] - 1, 1.0, query[0:edge])


def prepare_body(*refs):
    hbm, outs, held, sems = refs[:7], refs[7:-8], refs[-8:-1], refs[-1]
    staged = len(outs) > 1
    outs, (packed_ref, rim_ref) = (outs[:-2], outs[-2:]) if staged else (outs, (outs[0], None))
    tokens_ref, gain_ref, w_ref, short_ref, long_ref, medium_ref, skip_ref = held
    rows, width = tokens_ref.shape
    copies = [pltpu.make_async_copy(h, v, sems.at[i]) for i, (h, v) in enumerate(zip(hbm, held))]
    for copy in copies:
        copy.start()
    copies[0].wait()
    copies[1].wait()
    normed = normed_of(tokens_ref, gain_ref)
    copies[2].wait()
    copies[3].wait()
    query_cols, cols = slice(0, width), slice(width, 3 * width)
    mixed = short_mix(projected_of(normed, w_ref[:, cols]), short_ref[:, cols])
    key, value = mixed[:, 0:width], mixed[:, width:]
    put_columns(packed_ref, 0, (key[0:rows] * value[0:rows]).astype(jnp.bfloat16).T)
    rims = [(key[0:edge], key[rows:]), (value[0:edge], value[rows:])]
    some = jnp.concatenate([normed[0 : 2 * edge], normed[rows - 2 * edge :]])
    some = short_mix(projected_of(some, w_ref[:, query_cols]), short_ref[:, query_cols])
    put_rim(packed_ref, rim_ref, [*rims, (some[0:edge], some[4 * edge :])])
    for copy in copies[4:]:
        copy.wait()
    med_len = medium_ref.shape[0]
    is_first = jnp.where(lax.axis_index(seq) == 0, 1.0, 0.0)
    head = long_ref[0:med_len, :] + is_first * medium_ref[...]
    row = lax.broadcasted_iota(jnp.int32, (edge, width), 0)
    top = head[0:edge] + jnp.where(row == 0, is_first * skip_ref[...], 0.0)
    taps = jnp.concatenate([top, head[edge:], long_ref[med_len:, :]]).astype(jnp.bfloat16)
    put_columns(packed_ref, rows, taps.T)
    if staged:
        put_routes(packed_ref, rim_ref, *outs)


def put_columns(packed_ref, begin, values):
    if packed_ref.shape[1] > lane:
        packed_ref[:, begin : begin + values.shape[1]] = values
        return
    devices = lax.axis_size(seq)
    chans = values.shape[0] // devices
    size = packed_ref.shape[0] // devices
    for device in range(devices):
        for column in range(values.shape[1] // lane):
            start = device * size + (begin // lane + column) * chans
            packed_ref[start : start + chans, :] = values[
                device * chans : (device + 1) * chans, column * lane : (column + 1) * lane
            ]


def put_rim(packed_ref, rim_ref, parts):
    width = parts[0][0].shape[1]
    if rim_ref is None:
        rows = [row for part in parts for row in part]
        rows.append(jnp.zeros((lane - 3 * rim_step, width), jnp.float32))
        rim = jnp.concatenate(rows).T
        packed_ref[:, packed_ref.shape[1] - lane :] = rim.astype(jnp.bfloat16)
        return
    chips = rim_ref.shape[0]
    span = width // chips
    half = edge // 4
    group = lax.broadcasted_iota(jnp.int32, (edge // 2, lane), 1) // span
    parts = [jnp.concatenate([own[0:half], after[0:half]]) for own, after in parts]
    for chip in range(chips):
        begin = chip * span // lane * lane
        place = chip * span % lane
        rim = jnp.zeros((edge // 2, lane), jnp.float32)
        for index, part in enumerate(parts):
            shift = (index * span - place) % lane
            moved = part[:, begin : begin + lane]
            moved = pltpu.roll(moved, shift, 1) if shift else moved
            rim = jnp.where(group == index, moved, rim)
        rim = jnp.concatenate([rim, jnp.zeros((edge // 2, lane), jnp.float32)])
        rim_ref[chip] = rim.astype(jnp.bfloat16)


def columns_of(packed_ref, chans, rows):
    devices, count = lax.axis_size(seq), 2 * rows // lane
    blocks = packed_ref[...].reshape(devices, count * chans, lane)
    columns = [blocks[:, i * chans : (i + 1) * chans].reshape(-1, lane) for i in range(count)]
    return jnp.concatenate(columns, axis=1)


def rim_of(rim_ref, turned_ref, chans):
    span = 2 * chans
    rim = rim_ref[...].reshape(-1, lane)
    row = lax.broadcasted_iota(jnp.int32, rim.shape, 0)
    column = lax.broadcasted_iota(jnp.int32, rim.shape, 1)
    before = pltpu.roll(rim, edge - edge // 4, 0)
    rim = rim + jnp.where(row < edge, 0.0, before)
    signal = rim * pltpu.roll(rim, lane - span, 1)
    turned_ref[...] = jnp.where(column < span, signal, rim).T
    found = []
    for begin in (0, 2 * span):
        start = pl.multiple_of(begin + lax.axis_index("core") * chans, chans)
        part = turned_ref[pl.ds(start, chans), :]
        blocks = [part] + [pltpu.roll(part, lane - edge * k, 1) for k in range(1, rim_ref.shape[0])]
        found.append(jnp.concatenate(blocks))
    return found


def twist_rows(twist_ref, chans):
    half, rows = twist_ref.shape[0] // 2, twist_ref.shape[1]
    tables = twist_ref[0:half, :], twist_ref[half:, :]
    if chans % 8:
        return tables
    return tuple(
        jnp.broadcast_to(table[:, None, :], (half, chans, rows)).reshape(half * chans, rows)
        for table in tables
    )


def convolve_body(chans, rim_count, first_ref, twist_ref, inner_ref, *refs):
    rows = twist_ref.shape[1]
    half = first_ref.shape[0] // 2
    scale = chans / (half * rows)
    staged = len(refs) > 2
    if staged:
        keep_ref, got_ref, *outs, packed_ref, rim_ref, turned_ref, out_ref = refs
        rim_ref[...] = jnp.zeros_like(rim_ref)
        take_routes(keep_ref, got_ref, packed_ref, rim_ref)
        values = columns_of(packed_ref, chans, rows)
        rim_signal, rim_query = rim_of(rim_ref, turned_ref, chans)
    else:
        packed_ref, out_ref = refs
        values = packed_ref[:, : 2 * rows]
        rim = packed_ref[:, 2 * rows :].astype(jnp.float32)
        before = jnp.concatenate([jnp.zeros((chans, lane), jnp.float32), rim[:-chans]])
        rim = rim + pltpu.roll(before, lane - edge, 1)
        rim_signal = rim * pltpu.roll(rim, lane - rim_step, 1)
        rim_query = pltpu.roll(rim, lane - 2 * rim_step, 1)
    in_rim = lax.broadcasted_iota(jnp.int32, rim_signal.shape, 1) < rim_count
    rim_signal = rim_signal.astype(jnp.bfloat16)
    rim_query = scale * jnp.where(in_rim, rim_query, 1.0)
    signal = jnp.concatenate(
        [jnp.where(in_rim, rim_signal, values[:, 0:lane]), values[:, lane:rows]], axis=1
    )
    cosine, sine = inner_ref[:, 0:rows], inner_ref[:, rows:]
    inner = jnp.concatenate(
        [jnp.concatenate([cosine, -sine], axis=1), jnp.concatenate([sine, cosine], axis=1)]
    )
    spread_of = functools.partial(jnp.dot, first_ref[...], preferred_element_type=jnp.float32)
    spreads = [spread_of(values[:, rows : 2 * rows]), spread_of(signal)]
    tw_cos, tw_sin = twist_rows(twist_ref, chans)
    turned = []
    for spread in spreads:
        real, imag = spread[0:half], spread[half:]
        turned.append([real * tw_cos + imag * tw_sin, imag * tw_cos - real * tw_sin])
    turned = jnp.concatenate([jnp.concatenate(pair, axis=1).astype(jnp.bfloat16) for pair in turned])
    spectra = jnp.dot(turned, inner, preferred_element_type=jnp.float32)
    fil_re, fil_im = spectra[0:half, 0:rows], spectra[0:half, rows:]
    real, imag = spectra[half:, 0:rows], spectra[half:, rows:]
    product = [real * fil_im + imag * fil_re, real * fil_re - imag * fil_im]
    product = jnp.concatenate(product, axis=1).astype(jnp.bfloat16)
    back = jnp.dot(product, inner, preferred_element_type=jnp.float32)
    imag, real = back[:, 0:rows], back[:, rows:]
    turned = jnp.concatenate([real * tw_cos - imag * tw_sin, imag * tw_cos + real * tw_sin])
    last = jnp.concatenate([first_ref[0:half, :].T, first_ref[half:, :].T], axis=1)
    conv = jnp.dot(last, turned.astype(jnp.bfloat16), preferred_element_type=jnp.float32)
    conv = jnp.concatenate([conv[:, 0:lane] * rim_query, conv[:, lane:] * scale], axis=1)
    out_ref[...] = conv.astype(jnp.bfloat16)
    if staged:
        put_routes(out_ref, None, *outs)


def output_body(query_ref, w_ref, *refs):
    if len(refs) > 2:
        keep_ref, got_ref, out_ref, conv_ref = refs
        take_routes(keep_ref, got_ref, conv_ref)
    else:
        conv_ref, out_ref = refs
    conv = conv_ref[...].T.astype(jnp.float32)
    mixed_out = (query_ref[...] * conv).astype(jnp.bfloat16)
    out_ref[...] = jnp.dot(mixed_out, w_ref[...], preferred_element_type=jnp.float32).astype(
        jnp.bfloat16
    )


def permute(array, partner):
    return lax.ppermute(array, seq, [(i, partner(i)) for i in range(lax.axis_size(seq))])


def bf16(*shape):
    return jax.ShapeDtypeStruct(shape, jnp.bfloat16)


def exchange(keep, give, near, home):
    turns, size = keep.shape[0], keep.shape[1] // 2 // chan_tile * chan_tile
    lanes, extra = keep.shape[2], keep.shape[1] - 2 * size
    got = permute(give, lambda i: i ^ 1)
    near = permute(near, lambda i: i ^ 2)
    far = call(
        functools.partial(merge_body, size),
        (bf16(4 * size + extra, lanes),) * turns,
        (keep, got),
        [pltpu.VMEM] * 2,
        moved=4 * keep.size,
    )
    routes = routes_of(lax.axis_size("chip"))
    far = [permute(part, lambda i: i ^ 2 * route[i % 2]) for part, route in zip(far, routes)]
    count = 2 * turns + 2
    half = bf16(count * size + count // 2 * extra, lanes)
    keep, give = call(
        functools.partial(split_body, size),
        (half, half),
        (*far, near, home),
        [pltpu.VMEM] * (turns + 2),
        moved=4 * keep.size,
    )
    return keep, permute(give, lambda i: i ^ 1)


def local(tokens, norm_gain, w_in, short_filter, long_filter, medium_filter, skip_gain, w_out):
    rows, width = tokens.shape
    devices, chips = lax.axis_size(seq), lax.axis_size("chip")
    chans = width // devices
    first, twist, inner = spectral_tables(devices, rows, chans)
    staged = chans == chan_tile and chips >= 4 and short_filter.shape[0] <= 3
    if staged:
        packed_shape = (2 * rows // lane * width, lane)
    else:
        packed_shape = (width, 2 * rows + lane)

    def pieces(shape, extra):
        if not staged:
            return (bf16(*shape),)
        size, turns = 2 * shape[0] // devices + extra, chips // 2 - 1
        near = size + size - extra + chan_tile
        return (bf16(turns, size, shape[1]),) * 2 + (bf16(near, shape[1]), bf16(size, shape[1]))

    def scratch(*shapes):
        return [pltpu.VMEM(*shape) for shape in shapes] if staged else []

    def swap(parts):
        if staged:
            return exchange(*parts)
        (array,) = parts
        blocks = array.reshape(devices, -1, array.shape[-1])
        return (lax.all_to_all(blocks, seq, split_axis=0, concat_axis=0).reshape(array.shape),)

    query = call(
        query_body,
        jax.ShapeDtypeStruct((rows, width), jnp.float32),
        (tokens, norm_gain[None, :], w_in, short_filter),
        [pltpu.VMEM] * 4,
        flops=2 * rows * width * width,
        moved=800_000,
    )
    args = (tokens, norm_gain[None, :], w_in, short_filter, long_filter, medium_filter, skip_gain[None, :])
    args = tuple(pltpu.with_memory_space_constraint(arg, pltpu.HBM) for arg in args)
    packed = (packed_shape, jnp.bfloat16)
    parts = call(
        prepare_body,
        pieces(packed_shape, edge),
        args,
        [pltpu.HBM] * len(args),
        scratch(packed, ((chips, edge, lane), jnp.bfloat16))
        + [pltpu.VMEM(arg.shape, arg.dtype) for arg in args]
        + [pltpu.SemaphoreType.DMA((len(args),))],
        flops=2 * rows * width * 3 * width,
        moved=1_500_000,
    )
    conv = ((width, rows), jnp.bfloat16)
    parts = swap(parts)
    parts = call(
        functools.partial(convolve_body, chans, short_filter.shape[0] - 1),
        pieces((width, rows), 0),
        (first, twist, inner, *parts),
        [pltpu.VMEM] * (3 + len(parts)),
        scratch(packed, ((devices, edge, lane), jnp.float32), ((lane, lane), jnp.float32), conv),
        flops=18 * first.shape[0] * width * rows,
        moved=2_000_000,
    )
    parts = swap(parts)
    return call(
        output_body,
        bf16(rows, width),
        (query, w_out, *parts),
        [pltpu.VMEM] * (2 + len(parts)),
        scratch(conv),
        flops=2 * rows * width * width,
        moved=600_000,
    )


def solution(mesh):
    groups, devices = mesh.devices.shape
    split = jax.sharding.Mesh(mesh.devices.reshape(groups, devices // 2, 2), ("groups", *seq))
    rows = P(("groups", *seq), None)
    placed = (rows, P(), P(), P(), P(seq, None), P(), P(), P())
    return jax.shard_map(local, mesh=split, in_specs=placed, out_specs=rows, check_vma=False)
```

```python
import functools
import math

import jax
import jax.numpy as jnp
import numpy as np
from jax import lax
from jax.experimental import pallas as pl
from jax.experimental.pallas import tpu as pltpu
from jax.sharding import PartitionSpec as P

epsilon = 1e-06
edge = 8
lane = 128
seq = ("chip", "core")
rim_step = 2 * edge
chan_tile = 16
vmem_bytes = 32 * 2**20


def whole(space):
    return pl.BlockSpec(memory_space=space)


def call(body, outs, args, spaces, scratch=(), flops=0, moved=0):
    return pl.pallas_call(
        body,
        out_shape=outs,
        in_specs=[whole(space) for space in spaces],
        out_specs=jax.tree.map(lambda _: whole(pltpu.VMEM), outs),
        scratch_shapes=list(scratch),
        compiler_params=pltpu.CompilerParams(vmem_limit_bytes=vmem_bytes),
        cost_estimate=pl.CostEstimate(flops=flops, bytes_accessed=moved, transcendentals=0),
    )(*args)


def spectral_tables(devices, rows, chans):
    full_len = devices * rows
    freqs = 4 * np.arange(devices) + 1
    eye = np.eye(chans)
    angle = 2.0 * math.pi / (4 * devices) * (freqs[:, None] * np.arange(devices)[None, :] % (4 * devices))
    cosine, sine = np.kron(np.cos(angle), eye), np.kron(np.sin(angle), eye)
    first = np.concatenate([cosine, -sine])
    offsets = np.arange(rows)
    twist = 2.0 * math.pi / (4 * full_len) * (freqs[:, None] * offsets[None, :] % (4 * full_len))
    twist = np.concatenate([np.cos(twist), np.sin(twist)])
    if chans % 8:
        twist = np.repeat(twist, chans, axis=0)
    turn = 2.0 * math.pi / rows * (offsets[:, None] * offsets[None, :] % rows)
    inner = np.concatenate([np.cos(turn), np.sin(turn)], axis=1)
    return (
        jnp.asarray(first, jnp.bfloat16),
        jnp.asarray(twist, jnp.float32),
        jnp.asarray(inner, jnp.bfloat16),
    )


def routes_of(chips):
    return [(d, d + 1) for d in range(chips - 2, 1, -2)]


def carried(route, core):
    mine, others = route
    return jnp.where(core == 0, mine, others), jnp.where(core == 0, others, mine)


def put_routes(source_ref, rim_ref, keep_ref, give_ref, near_ref, home_ref):
    chip, core = lax.axis_index("chip"), lax.axis_index("core")
    size = source_ref.shape[0] // 2 // (lax.axis_size("chip"))
    extra = home_ref.shape[0] - 2 * size

    def put(out_ref, distance):
        start = pl.multiple_of((chip ^ distance) * 2 * size, 2 * size)
        out_ref[0 : 2 * size, :] = source_ref[pl.ds(start, 2 * size), :]
        if extra:
            out_ref[2 * size : 2 * size + extra, :] = rim_ref[chip ^ distance]

    for turn, route in enumerate(routes_of(lax.axis_size("chip"))):
        own, other = carried(route, core)
        put(keep_ref.at[turn], own)
        put(give_ref.at[turn], other)
    put(home_ref, 0)
    put(near_ref, 1)
    begin = 2 * size
    if extra:
        rim = rim_ref[chip ^ 1].astype(jnp.float32)
        near_ref[begin : begin + chan_tile, :] = jnp.concatenate([rim, rim]).astype(jnp.bfloat16)
        begin += chan_tile
    near_ref[begin : begin + 2 * size, :] = home_ref[0 : 2 * size, :]
    begin += 2 * size
    near_ref[begin:, :] = home_ref[0 : near_ref.shape[0] - begin, :]


def half_rims(first_ref, second_ref, begin):
    pair = [ref[begin : begin + edge, :].astype(jnp.float32) for ref in (first_ref, second_ref)]
    return jnp.concatenate([rims[0 : edge // 2] for rims in pair])


def merge_body(size, keep_ref, got_ref, *out_refs):
    for turn, out_ref in enumerate(out_refs):
        out_ref[0 : 2 * size, :] = keep_ref[turn, 0 : 2 * size, :]
        out_ref[2 * size : 4 * size, :] = got_ref[turn, 0 : 2 * size, :]
        if out_ref.shape[0] > 4 * size:
            rims = half_rims(keep_ref.at[turn], got_ref.at[turn], 2 * size)
            out_ref[4 * size :, :] = rims.astype(jnp.bfloat16)


def split_body(size, *refs):
    far_refs, (near_ref, home_ref, keep_ref, give_ref) = refs[:-4], refs[-4:]
    core = lax.axis_index("core")
    sources = [(far_ref, 2 * sender) for far_ref in far_refs for sender in range(2)]
    sources += [(near_ref, 0), (home_ref, 0)]
    for out_ref, target in ((keep_ref, core), (give_ref, 1 - core)):
        for place, (source_ref, block) in enumerate(sources):
            start = pl.multiple_of((block + target) * size, size)
            out_ref[place * size : (place + 1) * size, :] = source_ref[pl.ds(start, size), :]
        begin = len(sources) * size
        if out_ref.shape[0] > begin:
            rims = [far_ref[4 * size :, :].astype(jnp.float32) for far_ref in far_refs]
            rims.append(half_rims(near_ref, home_ref, 2 * size))
            out_ref[begin:, :] = jnp.concatenate(rims).astype(jnp.bfloat16)


def take_routes(keep_ref, got_ref, target_ref, rim_ref=None):
    chip, core = lax.axis_index("chip"), lax.axis_index("core")
    routes = routes_of(lax.axis_size("chip"))
    count = 2 * len(routes) + 2
    size = target_ref.shape[0] // (2 * lax.axis_size("chip"))
    places = [(*carried(route, core), sender) for route in routes for sender in range(2)]
    places += [(1, 1, 0), (0, 0, 0)]
    for place, (own, other, sender) in enumerate(places):
        for ref, distance, carrier in ((keep_ref, own, core), (got_ref, other, 1 - core)):
            device = (chip ^ distance) * 2 + (carrier if sender == 0 else 1 - carrier)
            start = pl.multiple_of(device * size, size)
            target_ref[pl.ds(start, size), :] = ref[place * size : (place + 1) * size, :]
            if rim_ref is not None:
                begin = place * edge // 2
                rims = ref[count * size :, :].astype(jnp.float32)
                rim_ref[device, 0 : edge // 2, :] = rims[begin : begin + edge // 2]


def scaled_of(tokens_ref, gain_ref):
    inputs = tokens_ref[...].astype(jnp.float32)
    mean_sq = jnp.mean(inputs * inputs, axis=-1, keepdims=True)
    return (inputs * gain_ref[...]).astype(jnp.bfloat16), lax.rsqrt(mean_sq + epsilon)


def projected_of(scaled, factor, weights):
    projected = jnp.dot(scaled, weights, preferred_element_type=jnp.float32) * factor
    projected = projected.astype(jnp.bfloat16).astype(jnp.float32)
    return jnp.concatenate([projected, jnp.zeros((edge, projected.shape[1]), jnp.float32)])


def short_mix(projected, taps):
    acc = taps[0:1] * projected
    for tap_num in range(1, taps.shape[0]):
        acc = acc + taps[tap_num : tap_num + 1] * pltpu.roll(projected, tap_num, 0)
    return acc


def query_body(tokens_ref, gain_ref, w_ref, short_ref, query_ref):
    rows, width = tokens_ref.shape
    cols = slice(0, width)
    projected = projected_of(*scaled_of(tokens_ref, gain_ref), w_ref[:, cols])
    query = short_mix(projected, short_ref[:, cols])
    query_ref[...] = query[0:rows]
    row = lax.broadcasted_iota(jnp.int32, (edge, width), 0)
    query_ref[0:edge, :] = jnp.where(row < short_ref.shape[0] - 1, 1.0, query[0:edge])


def prepare_body(*refs):
    hbm, outs, held, sems = refs[:7], refs[7:-8], refs[-8:-1], refs[-1]
    staged = len(outs) > 1
    outs, (packed_ref, rim_ref) = (outs[:-2], outs[-2:]) if staged else (outs, (outs[0], None))
    tokens_ref, gain_ref, w_ref, short_ref, long_ref, medium_ref, skip_ref = held
    rows, width = tokens_ref.shape
    copies = [pltpu.make_async_copy(h, v, sems.at[i]) for i, (h, v) in enumerate(zip(hbm, held))]
    for copy in copies:
        copy.start()
    copies[0].wait()
    copies[1].wait()
    scaled, factor = scaled_of(tokens_ref, gain_ref)
    copies[2].wait()
    copies[3].wait()
    query_cols, cols = slice(0, width), slice(width, 3 * width)
    mixed = short_mix(projected_of(scaled, factor, w_ref[:, cols]), short_ref[:, cols])
    key, value = mixed[:, 0:width], mixed[:, width:]
    put_columns(packed_ref, 0, (key[0:rows] * value[0:rows]).astype(jnp.bfloat16).T)
    rims = [(key[0:edge], key[rows:]), (value[0:edge], value[rows:])]
    some, some_factor = (
        jnp.concatenate([part[0 : 2 * edge], part[rows - 2 * edge :]]) for part in (scaled, factor)
    )
    some = short_mix(projected_of(some, some_factor, w_ref[:, query_cols]), short_ref[:, query_cols])
    put_rim(packed_ref, rim_ref, [*rims, (some[0:edge], some[4 * edge :])])
    for copy in copies[4:]:
        copy.wait()
    med_len = medium_ref.shape[0]
    is_first = jnp.where(lax.axis_index(seq) == 0, 1.0, 0.0)
    head = long_ref[0:med_len, :] + is_first * medium_ref[...]
    row = lax.broadcasted_iota(jnp.int32, (edge, width), 0)
    top = head[0:edge] + jnp.where(row == 0, is_first * skip_ref[...], 0.0)
    taps = jnp.concatenate([top, head[edge:], long_ref[med_len:, :]]).astype(jnp.bfloat16)
    put_columns(packed_ref, rows, taps.T)
    if staged:
        put_routes(packed_ref, rim_ref, *outs)


def put_columns(packed_ref, begin, values):
    if packed_ref.shape[1] > lane:
        packed_ref[:, begin : begin + values.shape[1]] = values
        return
    devices = lax.axis_size(seq)
    chans = values.shape[0] // devices
    size = packed_ref.shape[0] // devices
    for device in range(devices):
        for column in range(values.shape[1] // lane):
            start = device * size + (begin // lane + column) * chans
            packed_ref[start : start + chans, :] = values[
                device * chans : (device + 1) * chans, column * lane : (column + 1) * lane
            ]


def put_rim(packed_ref, rim_ref, parts):
    width = parts[0][0].shape[1]
    if rim_ref is None:
        rows = [row for part in parts for row in part]
        rows.append(jnp.zeros((lane - 3 * rim_step, width), jnp.float32))
        rim = jnp.concatenate(rows).T
        packed_ref[:, packed_ref.shape[1] - lane :] = rim.astype(jnp.bfloat16)
        return
    chips = rim_ref.shape[0]
    span = width // chips
    half = edge // 4
    group = lax.broadcasted_iota(jnp.int32, (edge // 2, lane), 1) // span
    parts = [jnp.concatenate([own[0:half], after[0:half]]) for own, after in parts]
    for chip in range(chips):
        begin = chip * span // lane * lane
        place = chip * span % lane
        rim = jnp.zeros((edge // 2, lane), jnp.float32)
        for index, part in enumerate(parts):
            shift = (index * span - place) % lane
            moved = part[:, begin : begin + lane]
            moved = pltpu.roll(moved, shift, 1) if shift else moved
            rim = jnp.where(group == index, moved, rim)
        rim = jnp.concatenate([rim, jnp.zeros((edge // 2, lane), jnp.float32)])
        rim_ref[chip] = rim.astype(jnp.bfloat16)


def columns_of(packed_ref, chans, rows):
    devices, count = lax.axis_size(seq), 2 * rows // lane
    blocks = packed_ref[...].reshape(devices, count * chans, lane)
    columns = [blocks[:, i * chans : (i + 1) * chans].reshape(-1, lane) for i in range(count)]
    return jnp.concatenate(columns, axis=1)


def rim_of(rim_ref, turned_ref, chans):
    span = 2 * chans
    rim = rim_ref[...].reshape(-1, lane)
    row = lax.broadcasted_iota(jnp.int32, rim.shape, 0)
    column = lax.broadcasted_iota(jnp.int32, rim.shape, 1)
    before = pltpu.roll(rim, edge - edge // 4, 0)
    rim = rim + jnp.where(row < edge, 0.0, before)
    signal = rim * pltpu.roll(rim, lane - span, 1)
    turned_ref[...] = jnp.where(column < span, signal, rim).T
    found = []
    for begin in (0, 2 * span):
        start = pl.multiple_of(begin + lax.axis_index("core") * chans, chans)
        part = turned_ref[pl.ds(start, chans), :]
        blocks = [part] + [pltpu.roll(part, lane - edge * k, 1) for k in range(1, rim_ref.shape[0])]
        found.append(jnp.concatenate(blocks))
    return found


def twist_rows(twist_ref, chans):
    half, rows = twist_ref.shape[0] // 2, twist_ref.shape[1]
    tables = twist_ref[0:half, :], twist_ref[half:, :]
    if chans % 8:
        return tables
    return tuple(
        jnp.broadcast_to(table[:, None, :], (half, chans, rows)).reshape(half * chans, rows)
        for table in tables
    )


def convolve_body(chans, rim_count, first_ref, twist_ref, inner_ref, *refs):
    rows = twist_ref.shape[1]
    half = first_ref.shape[0] // 2
    scale = chans / (half * rows)
    staged = len(refs) > 2
    if staged:
        keep_ref, got_ref, *outs, packed_ref, rim_ref, turned_ref, out_ref = refs
        rim_ref[...] = jnp.zeros_like(rim_ref)
        take_routes(keep_ref, got_ref, packed_ref, rim_ref)
        values = columns_of(packed_ref, chans, rows)
        rim_signal, rim_query = rim_of(rim_ref, turned_ref, chans)
    else:
        packed_ref, out_ref = refs
        values = packed_ref[:, : 2 * rows]
        rim = packed_ref[:, 2 * rows :].astype(jnp.float32)
        before = jnp.concatenate([jnp.zeros((chans, lane), jnp.float32), rim[:-chans]])
        rim = rim + pltpu.roll(before, lane - edge, 1)
        rim_signal = rim * pltpu.roll(rim, lane - rim_step, 1)
        rim_query = pltpu.roll(rim, lane - 2 * rim_step, 1)
    in_rim = lax.broadcasted_iota(jnp.int32, rim_signal.shape, 1) < rim_count
    rim_signal = rim_signal.astype(jnp.bfloat16)
    rim_query = scale * jnp.where(in_rim, rim_query, 1.0)
    signal = jnp.concatenate(
        [jnp.where(in_rim, rim_signal, values[:, 0:lane]), values[:, lane:rows]], axis=1
    )
    cosine, sine = inner_ref[:, 0:rows], inner_ref[:, rows:]
    inner = jnp.concatenate(
        [jnp.concatenate([cosine, -sine], axis=1), jnp.concatenate([sine, cosine], axis=1)]
    )
    spread_of = functools.partial(jnp.dot, first_ref[...], preferred_element_type=jnp.float32)
    spreads = [spread_of(values[:, rows : 2 * rows]), spread_of(signal)]
    tw_cos, tw_sin = twist_rows(twist_ref, chans)
    turned = []
    for spread in spreads:
        real, imag = spread[0:half], spread[half:]
        turned.append([real * tw_cos + imag * tw_sin, imag * tw_cos - real * tw_sin])
    turned = jnp.concatenate([jnp.concatenate(pair, axis=1).astype(jnp.bfloat16) for pair in turned])
    spectra = jnp.dot(turned, inner, preferred_element_type=jnp.float32)
    fil_re, fil_im = spectra[0:half, 0:rows], spectra[0:half, rows:]
    real, imag = spectra[half:, 0:rows], spectra[half:, rows:]
    product = [real * fil_im + imag * fil_re, real * fil_re - imag * fil_im]
    product = jnp.concatenate(product, axis=1).astype(jnp.bfloat16)
    back = jnp.dot(product, inner, preferred_element_type=jnp.float32)
    imag, real = back[:, 0:rows], back[:, rows:]
    turned = jnp.concatenate([real * tw_cos - imag * tw_sin, imag * tw_cos + real * tw_sin])
    last = jnp.concatenate([first_ref[0:half, :].T, first_ref[half:, :].T], axis=1)
    conv = jnp.dot(last, turned.astype(jnp.bfloat16), preferred_element_type=jnp.float32)
    conv = jnp.concatenate([conv[:, 0:lane] * rim_query, conv[:, lane:] * scale], axis=1)
    out_ref[...] = conv.astype(jnp.bfloat16)
    if staged:
        put_routes(out_ref, None, *outs)


def output_body(query_ref, w_ref, *refs):
    if len(refs) > 2:
        keep_ref, got_ref, out_ref, conv_ref = refs
        take_routes(keep_ref, got_ref, conv_ref)
    else:
        conv_ref, out_ref = refs
    conv = conv_ref[...].T.astype(jnp.float32)
    mixed_out = (query_ref[...] * conv).astype(jnp.bfloat16)
    out_ref[...] = jnp.dot(mixed_out, w_ref[...], preferred_element_type=jnp.float32).astype(
        jnp.bfloat16
    )


def permute(array, partner):
    return lax.ppermute(array, seq, [(i, partner(i)) for i in range(lax.axis_size(seq))])


def bf16(*shape):
    return jax.ShapeDtypeStruct(shape, jnp.bfloat16)


def exchange(keep, give, near, home):
    turns, size = keep.shape[0], keep.shape[1] // 2 // chan_tile * chan_tile
    lanes, extra = keep.shape[2], keep.shape[1] - 2 * size
    got = permute(give, lambda i: i ^ 1)
    near = permute(near, lambda i: i ^ 2)
    far = call(
        functools.partial(merge_body, size),
        (bf16(4 * size + extra, lanes),) * turns,
        (keep, got),
        [pltpu.VMEM] * 2,
        moved=4 * keep.size,
    )
    routes = routes_of(lax.axis_size("chip"))
    far = [permute(part, lambda i: i ^ 2 * route[i % 2]) for part, route in zip(far, routes)]
    count = 2 * turns + 2
    half = bf16(count * size + count // 2 * extra, lanes)
    keep, give = call(
        functools.partial(split_body, size),
        (half, half),
        (*far, near, home),
        [pltpu.VMEM] * (turns + 2),
        moved=4 * keep.size,
    )
    return keep, permute(give, lambda i: i ^ 1)


def local(tokens, norm_gain, w_in, short_filter, long_filter, medium_filter, skip_gain, w_out):
    rows, width = tokens.shape
    devices, chips = lax.axis_size(seq), lax.axis_size("chip")
    chans = width // devices
    first, twist, inner = spectral_tables(devices, rows, chans)
    staged = chans == chan_tile and chips >= 4 and short_filter.shape[0] <= 3
    if staged:
        packed_shape = (2 * rows // lane * width, lane)
    else:
        packed_shape = (width, 2 * rows + lane)

    def pieces(shape, extra):
        if not staged:
            return (bf16(*shape),)
        size, turns = 2 * shape[0] // devices + extra, chips // 2 - 1
        near = size + size - extra + chan_tile
        return (bf16(turns, size, shape[1]),) * 2 + (bf16(near, shape[1]), bf16(size, shape[1]))

    def scratch(*shapes):
        return [pltpu.VMEM(*shape) for shape in shapes] if staged else []

    def swap(parts):
        if staged:
            return exchange(*parts)
        (array,) = parts
        blocks = array.reshape(devices, -1, array.shape[-1])
        return (lax.all_to_all(blocks, seq, split_axis=0, concat_axis=0).reshape(array.shape),)

    query = call(
        query_body,
        jax.ShapeDtypeStruct((rows, width), jnp.float32),
        (tokens, norm_gain[None, :], w_in, short_filter),
        [pltpu.VMEM] * 4,
        flops=2 * rows * width * width,
        moved=800_000,
    )
    args = (tokens, norm_gain[None, :], w_in, short_filter, long_filter, medium_filter, skip_gain[None, :])
    args = tuple(pltpu.with_memory_space_constraint(arg, pltpu.HBM) for arg in args)
    packed = (packed_shape, jnp.bfloat16)
    parts = call(
        prepare_body,
        pieces(packed_shape, edge),
        args,
        [pltpu.HBM] * len(args),
        scratch(packed, ((chips, edge, lane), jnp.bfloat16))
        + [pltpu.VMEM(arg.shape, arg.dtype) for arg in args]
        + [pltpu.SemaphoreType.DMA((len(args),))],
        flops=2 * rows * width * 3 * width,
        moved=1_500_000,
    )
    conv = ((width, rows), jnp.bfloat16)
    parts = swap(parts)
    parts = call(
        functools.partial(convolve_body, chans, short_filter.shape[0] - 1),
        pieces((width, rows), 0),
        (first, twist, inner, *parts),
        [pltpu.VMEM] * (3 + len(parts)),
        scratch(packed, ((devices, edge, lane), jnp.float32), ((lane, lane), jnp.float32), conv),
        flops=18 * first.shape[0] * width * rows,
        moved=2_000_000,
    )
    parts = swap(parts)
    return call(
        output_body,
        bf16(rows, width),
        (query, w_out, *parts),
        [pltpu.VMEM] * (2 + len(parts)),
        scratch(conv),
        flops=2 * rows * width * width,
        moved=600_000,
    )


def solution(mesh):
    groups, devices = mesh.devices.shape
    split = jax.sharding.Mesh(mesh.devices.reshape(groups, devices // 2, 2), ("groups", *seq))
    rows = P(("groups", *seq), None)
    placed = (rows, P(), P(), P(), P(seq, None), P(), P(), P())
    return jax.shard_map(local, mesh=split, in_specs=placed, out_specs=rows, check_vma=False)
```

```python
import functools
import math

import jax
import jax.numpy as jnp
import numpy as np
from jax import lax
from jax.experimental import pallas as pl
from jax.experimental.pallas import tpu as pltpu
from jax.sharding import PartitionSpec as P

epsilon = 1e-06
edge = 8
lane = 128
seq = ("chip", "core")
rim_step = 2 * edge
chan_tile = 16
vmem_bytes = 32 * 2**20


def whole(space):
    return pl.BlockSpec(memory_space=space)


def call(body, outs, args, spaces, scratch=(), flops=0, moved=0):
    return pl.pallas_call(
        body,
        out_shape=outs,
        in_specs=[whole(space) for space in spaces],
        out_specs=jax.tree.map(lambda _: whole(pltpu.VMEM), outs),
        scratch_shapes=list(scratch),
        compiler_params=pltpu.CompilerParams(vmem_limit_bytes=vmem_bytes),
        cost_estimate=pl.CostEstimate(flops=flops, bytes_accessed=moved, transcendentals=0),
    )(*args)


def spectral_tables(devices, rows, chans):
    full_len = devices * rows
    freqs = 4 * np.arange(devices) + 1
    eye = np.eye(chans)
    angle = 2.0 * math.pi / (4 * devices) * (freqs[:, None] * np.arange(devices)[None, :] % (4 * devices))
    cosine, sine = np.kron(np.cos(angle), eye), np.kron(np.sin(angle), eye)
    first = np.concatenate([cosine, -sine])
    offsets = np.arange(rows)
    twist = 2.0 * math.pi / (4 * full_len) * (freqs[:, None] * offsets[None, :] % (4 * full_len))
    twist = np.concatenate([np.cos(twist), np.sin(twist)])
    if chans % 8:
        twist = np.repeat(twist, chans, axis=0)
    turn = 2.0 * math.pi / rows * (offsets[:, None] * offsets[None, :] % rows)
    inner = np.concatenate([np.cos(turn), np.sin(turn)], axis=1)
    return (
        jnp.asarray(first, jnp.bfloat16),
        jnp.asarray(twist, jnp.float32),
        jnp.asarray(inner, jnp.bfloat16),
    )


def routes_of(chips, forward):
    far = list(range(chips - 2, 1, -2))
    if forward:
        far = far[:1] + far[:0:-1]
    return [(d, d + 1) for d in far]


def carried(route, core):
    mine, others = route
    return jnp.where(core == 0, mine, others), jnp.where(core == 0, others, mine)


def put_routes(source_ref, rim_ref, keep_ref, give_ref, near_ref, home_ref):
    chip, core = lax.axis_index("chip"), lax.axis_index("core")
    size = source_ref.shape[0] // 2 // (lax.axis_size("chip"))
    extra = home_ref.shape[0] - 2 * size

    def put(out_ref, distance):
        start = pl.multiple_of((chip ^ distance) * 2 * size, 2 * size)
        out_ref[0 : 2 * size, :] = source_ref[pl.ds(start, 2 * size), :]
        if extra:
            out_ref[2 * size : 2 * size + extra, :] = rim_ref[chip ^ distance]

    for turn, route in enumerate(routes_of(lax.axis_size("chip"), extra > 0)):
        own, other = carried(route, core)
        put(keep_ref.at[turn], own)
        put(give_ref.at[turn], other)
    put(home_ref, 0)
    put(near_ref, 1)
    begin = 2 * size
    if extra:
        rim = rim_ref[chip ^ 1].astype(jnp.float32)
        near_ref[begin : begin + chan_tile, :] = jnp.concatenate([rim, rim]).astype(jnp.bfloat16)
        begin += chan_tile
    near_ref[begin : begin + 2 * size, :] = home_ref[0 : 2 * size, :]
    begin += 2 * size
    near_ref[begin:, :] = home_ref[0 : near_ref.shape[0] - begin, :]


def half_rims(first_ref, second_ref, begin):
    pair = [ref[begin : begin + edge, :].astype(jnp.float32) for ref in (first_ref, second_ref)]
    return jnp.concatenate([rims[0 : edge // 2] for rims in pair])


def merge_body(size, keep_ref, got_ref, *out_refs):
    for turn, out_ref in enumerate(out_refs):
        out_ref[0 : 2 * size, :] = keep_ref[turn, 0 : 2 * size, :]
        out_ref[2 * size : 4 * size, :] = got_ref[turn, 0 : 2 * size, :]
        if out_ref.shape[0] > 4 * size:
            rims = half_rims(keep_ref.at[turn], got_ref.at[turn], 2 * size)
            out_ref[4 * size :, :] = rims.astype(jnp.bfloat16)


def split_body(size, *refs):
    far_refs, (near_ref, home_ref, keep_ref, give_ref) = refs[:-4], refs[-4:]
    core = lax.axis_index("core")
    sources = [(far_ref, 2 * sender) for far_ref in far_refs for sender in range(2)]
    sources += [(near_ref, 0), (home_ref, 0)]
    for out_ref, target in ((keep_ref, core), (give_ref, 1 - core)):
        for place, (source_ref, block) in enumerate(sources):
            start = pl.multiple_of((block + target) * size, size)
            out_ref[place * size : (place + 1) * size, :] = source_ref[pl.ds(start, size), :]
        begin = len(sources) * size
        if out_ref.shape[0] > begin:
            rims = [far_ref[4 * size :, :].astype(jnp.float32) for far_ref in far_refs]
            rims.append(half_rims(near_ref, home_ref, 2 * size))
            out_ref[begin:, :] = jnp.concatenate(rims).astype(jnp.bfloat16)


def take_routes(keep_ref, got_ref, target_ref, rim_ref=None):
    chip, core = lax.axis_index("chip"), lax.axis_index("core")
    routes = routes_of(lax.axis_size("chip"), rim_ref is not None)
    count = 2 * len(routes) + 2
    size = target_ref.shape[0] // (2 * lax.axis_size("chip"))
    places = [(*carried(route, core), sender) for route in routes for sender in range(2)]
    places += [(1, 1, 0), (0, 0, 0)]
    for place, (own, other, sender) in enumerate(places):
        for ref, distance, carrier in ((keep_ref, own, core), (got_ref, other, 1 - core)):
            device = (chip ^ distance) * 2 + (carrier if sender == 0 else 1 - carrier)
            start = pl.multiple_of(device * size, size)
            target_ref[pl.ds(start, size), :] = ref[place * size : (place + 1) * size, :]
            if rim_ref is not None:
                begin = place * edge // 2
                rims = ref[count * size :, :].astype(jnp.float32)
                rim_ref[device, 0 : edge // 2, :] = rims[begin : begin + edge // 2]


def normed_of(tokens_ref, gain_ref):
    inputs = tokens_ref[...].astype(jnp.float32)
    mean_sq = jnp.mean(inputs * inputs, axis=-1, keepdims=True)
    return (inputs * lax.rsqrt(mean_sq + epsilon) * gain_ref[...]).astype(jnp.bfloat16)


def projected_of(normed, weights):
    projected = jnp.dot(normed, weights, preferred_element_type=jnp.float32)
    projected = projected.astype(jnp.bfloat16).astype(jnp.float32)
    return jnp.concatenate([projected, jnp.zeros((edge, projected.shape[1]), jnp.float32)])


def short_mix(projected, taps):
    acc = taps[0:1] * projected
    for tap_num in range(1, taps.shape[0]):
        acc = acc + taps[tap_num : tap_num + 1] * pltpu.roll(projected, tap_num, 0)
    return acc


def query_body(tokens_ref, gain_ref, w_ref, short_ref, query_ref):
    rows, width = tokens_ref.shape
    cols = slice(0, width)
    query = short_mix(projected_of(normed_of(tokens_ref, gain_ref), w_ref[:, cols]), short_ref[:, cols])
    query_ref[...] = query[0:rows]
    row = lax.broadcasted_iota(jnp.int32, (edge, width), 0)
    query_ref[0:edge, :] = jnp.where(row < short_ref.shape[0] - 1, 1.0, query[0:edge])


def prepare_body(*refs):
    hbm, outs, held, sems = refs[:7], refs[7:-8], refs[-8:-1], refs[-1]
    staged = len(outs) > 1
    outs, (packed_ref, rim_ref) = (outs[:-2], outs[-2:]) if staged else (outs, (outs[0], None))
    tokens_ref, gain_ref, w_ref, short_ref, long_ref, medium_ref, skip_ref = held
    rows, width = tokens_ref.shape
    copies = [pltpu.make_async_copy(h, v, sems.at[i]) for i, (h, v) in enumerate(zip(hbm, held))]
    for copy in copies:
        copy.start()
    copies[0].wait()
    copies[1].wait()
    normed = normed_of(tokens_ref, gain_ref)
    copies[2].wait()
    copies[3].wait()
    query_cols, cols = slice(0, width), slice(width, 3 * width)
    mixed = short_mix(projected_of(normed, w_ref[:, cols]), short_ref[:, cols])
    key, value = mixed[:, 0:width], mixed[:, width:]
    put_columns(packed_ref, 0, (key[0:rows] * value[0:rows]).astype(jnp.bfloat16).T)
    rims = [(key[0:edge], key[rows:]), (value[0:edge], value[rows:])]
    some = jnp.concatenate([normed[0 : 2 * edge], normed[rows - 2 * edge :]])
    some = short_mix(projected_of(some, w_ref[:, query_cols]), short_ref[:, query_cols])
    put_rim(packed_ref, rim_ref, [*rims, (some[0:edge], some[4 * edge :])])
    for copy in copies[4:]:
        copy.wait()
    med_len = medium_ref.shape[0]
    is_first = jnp.where(lax.axis_index(seq) == 0, 1.0, 0.0)
    head = long_ref[0:med_len, :] + is_first * medium_ref[...]
    row = lax.broadcasted_iota(jnp.int32, (edge, width), 0)
    top = head[0:edge] + jnp.where(row == 0, is_first * skip_ref[...], 0.0)
    taps = jnp.concatenate([top, head[edge:], long_ref[med_len:, :]]).astype(jnp.bfloat16)
    put_columns(packed_ref, rows, taps.T)
    if staged:
        put_routes(packed_ref, rim_ref, *outs)


def put_columns(packed_ref, begin, values):
    if packed_ref.shape[1] > lane:
        packed_ref[:, begin : begin + values.shape[1]] = values
        return
    devices = lax.axis_size(seq)
    chans = values.shape[0] // devices
    size = packed_ref.shape[0] // devices
    for device in range(devices):
        for column in range(values.shape[1] // lane):
            start = device * size + (begin // lane + column) * chans
            packed_ref[start : start + chans, :] = values[
                device * chans : (device + 1) * chans, column * lane : (column + 1) * lane
            ]


def put_rim(packed_ref, rim_ref, parts):
    width = parts[0][0].shape[1]
    if rim_ref is None:
        rows = [row for part in parts for row in part]
        rows.append(jnp.zeros((lane - 3 * rim_step, width), jnp.float32))
        rim = jnp.concatenate(rows).T
        packed_ref[:, packed_ref.shape[1] - lane :] = rim.astype(jnp.bfloat16)
        return
    chips = rim_ref.shape[0]
    span = width // chips
    half = edge // 4
    group = lax.broadcasted_iota(jnp.int32, (edge // 2, lane), 1) // span
    parts = [jnp.concatenate([own[0:half], after[0:half]]) for own, after in parts]
    for chip in range(chips):
        begin = chip * span // lane * lane
        place = chip * span % lane
        rim = jnp.zeros((edge // 2, lane), jnp.float32)
        for index, part in enumerate(parts):
            shift = (index * span - place) % lane
            moved = part[:, begin : begin + lane]
            moved = pltpu.roll(moved, shift, 1) if shift else moved
            rim = jnp.where(group == index, moved, rim)
        rim = jnp.concatenate([rim, jnp.zeros((edge // 2, lane), jnp.float32)])
        rim_ref[chip] = rim.astype(jnp.bfloat16)


def columns_of(packed_ref, chans, rows):
    devices, count = lax.axis_size(seq), 2 * rows // lane
    blocks = packed_ref[...].reshape(devices, count * chans, lane)
    columns = [blocks[:, i * chans : (i + 1) * chans].reshape(-1, lane) for i in range(count)]
    return jnp.concatenate(columns, axis=1)


def rim_of(rim_ref, turned_ref, chans):
    span = 2 * chans
    rim = rim_ref[...].reshape(-1, lane)
    row = lax.broadcasted_iota(jnp.int32, rim.shape, 0)
    column = lax.broadcasted_iota(jnp.int32, rim.shape, 1)
    before = pltpu.roll(rim, edge - edge // 4, 0)
    rim = rim + jnp.where(row < edge, 0.0, before)
    signal = rim * pltpu.roll(rim, lane - span, 1)
    turned_ref[...] = jnp.where(column < span, signal, rim).T
    found = []
    for begin in (0, 2 * span):
        start = pl.multiple_of(begin + lax.axis_index("core") * chans, chans)
        part = turned_ref[pl.ds(start, chans), :]
        blocks = [part] + [pltpu.roll(part, lane - edge * k, 1) for k in range(1, rim_ref.shape[0])]
        found.append(jnp.concatenate(blocks))
    return found


def twist_rows(twist_ref, chans):
    half, rows = twist_ref.shape[0] // 2, twist_ref.shape[1]
    tables = twist_ref[0:half, :], twist_ref[half:, :]
    if chans % 8:
        return tables
    return tuple(
        jnp.broadcast_to(table[:, None, :], (half, chans, rows)).reshape(half * chans, rows)
        for table in tables
    )


def convolve_body(chans, rim_count, first_ref, twist_ref, inner_ref, *refs):
    rows = twist_ref.shape[1]
    half = first_ref.shape[0] // 2
    scale = chans / (half * rows)
    staged = len(refs) > 2
    if staged:
        keep_ref, got_ref, *outs, packed_ref, rim_ref, turned_ref, out_ref = refs
        rim_ref[...] = jnp.zeros_like(rim_ref)
        take_routes(keep_ref, got_ref, packed_ref, rim_ref)
        values = columns_of(packed_ref, chans, rows)
        rim_signal, rim_query = rim_of(rim_ref, turned_ref, chans)
    else:
        packed_ref, out_ref = refs
        values = packed_ref[:, : 2 * rows]
        rim = packed_ref[:, 2 * rows :].astype(jnp.float32)
        before = jnp.concatenate([jnp.zeros((chans, lane), jnp.float32), rim[:-chans]])
        rim = rim + pltpu.roll(before, lane - edge, 1)
        rim_signal = rim * pltpu.roll(rim, lane - rim_step, 1)
        rim_query = pltpu.roll(rim, lane - 2 * rim_step, 1)
    in_rim = lax.broadcasted_iota(jnp.int32, rim_signal.shape, 1) < rim_count
    rim_signal = rim_signal.astype(jnp.bfloat16)
    rim_query = scale * jnp.where(in_rim, rim_query, 1.0)
    signal = jnp.concatenate(
        [jnp.where(in_rim, rim_signal, values[:, 0:lane]), values[:, lane:rows]], axis=1
    )
    cosine, sine = inner_ref[:, 0:rows], inner_ref[:, rows:]
    inner = jnp.concatenate(
        [jnp.concatenate([cosine, -sine], axis=1), jnp.concatenate([sine, cosine], axis=1)]
    )
    spread_of = functools.partial(jnp.dot, first_ref[...], preferred_element_type=jnp.float32)
    spreads = [spread_of(values[:, rows : 2 * rows]), spread_of(signal)]
    tw_cos, tw_sin = twist_rows(twist_ref, chans)
    turned = []
    for spread in spreads:
        real, imag = spread[0:half], spread[half:]
        turned.append([real * tw_cos + imag * tw_sin, imag * tw_cos - real * tw_sin])
    turned = jnp.concatenate([jnp.concatenate(pair, axis=1).astype(jnp.bfloat16) for pair in turned])
    spectra = jnp.dot(turned, inner, preferred_element_type=jnp.float32)
    fil_re, fil_im = spectra[0:half, 0:rows], spectra[0:half, rows:]
    real, imag = spectra[half:, 0:rows], spectra[half:, rows:]
    product = [real * fil_im + imag * fil_re, real * fil_re - imag * fil_im]
    product = jnp.concatenate(product, axis=1).astype(jnp.bfloat16)
    back = jnp.dot(product, inner, preferred_element_type=jnp.float32)
    imag, real = back[:, 0:rows], back[:, rows:]
    turned = jnp.concatenate([real * tw_cos - imag * tw_sin, imag * tw_cos + real * tw_sin])
    last = jnp.concatenate([first_ref[0:half, :].T, first_ref[half:, :].T], axis=1)
    conv = jnp.dot(last, turned.astype(jnp.bfloat16), preferred_element_type=jnp.float32)
    conv = jnp.concatenate([conv[:, 0:lane] * rim_query, conv[:, lane:] * scale], axis=1)
    out_ref[...] = conv.astype(jnp.bfloat16)
    if staged:
        put_routes(out_ref, None, *outs)


def output_body(query_ref, w_ref, *refs):
    if len(refs) > 2:
        keep_ref, got_ref, out_ref, conv_ref = refs
        take_routes(keep_ref, got_ref, conv_ref)
    else:
        conv_ref, out_ref = refs
    conv = conv_ref[...].T.astype(jnp.float32)
    mixed_out = (query_ref[...] * conv).astype(jnp.bfloat16)
    out_ref[...] = jnp.dot(mixed_out, w_ref[...], preferred_element_type=jnp.float32).astype(
        jnp.bfloat16
    )


def permute(array, partner):
    return lax.ppermute(array, seq, [(i, partner(i)) for i in range(lax.axis_size(seq))])


def bf16(*shape):
    return jax.ShapeDtypeStruct(shape, jnp.bfloat16)


def exchange(keep, give, near, home):
    turns, size = keep.shape[0], keep.shape[1] // 2 // chan_tile * chan_tile
    lanes, extra = keep.shape[2], keep.shape[1] - 2 * size
    got = permute(give, lambda i: i ^ 1)
    near = permute(near, lambda i: i ^ 2)
    far = call(
        functools.partial(merge_body, size),
        (bf16(4 * size + extra, lanes),) * turns,
        (keep, got),
        [pltpu.VMEM] * 2,
        moved=4 * keep.size,
    )
    routes = routes_of(lax.axis_size("chip"), extra > 0)
    far = [permute(part, lambda i: i ^ 2 * route[i % 2]) for part, route in zip(far, routes)]
    count = 2 * turns + 2
    half = bf16(count * size + count // 2 * extra, lanes)
    keep, give = call(
        functools.partial(split_body, size),
        (half, half),
        (*far, near, home),
        [pltpu.VMEM] * (turns + 2),
        moved=4 * keep.size,
    )
    return keep, permute(give, lambda i: i ^ 1)


def local(tokens, norm_gain, w_in, short_filter, long_filter, medium_filter, skip_gain, w_out):
    rows, width = tokens.shape
    devices, chips = lax.axis_size(seq), lax.axis_size("chip")
    chans = width // devices
    first, twist, inner = spectral_tables(devices, rows, chans)
    staged = chans == chan_tile and chips >= 4 and short_filter.shape[0] <= 3
    if staged:
        packed_shape = (2 * rows // lane * width, lane)
    else:
        packed_shape = (width, 2 * rows + lane)

    def pieces(shape, extra):
        if not staged:
            return (bf16(*shape),)
        size, turns = 2 * shape[0] // devices + extra, chips // 2 - 1
        near = size + size - extra + chan_tile
        return (bf16(turns, size, shape[1]),) * 2 + (bf16(near, shape[1]), bf16(size, shape[1]))

    def scratch(*shapes):
        return [pltpu.VMEM(*shape) for shape in shapes] if staged else []

    def swap(parts):
        if staged:
            return exchange(*parts)
        (array,) = parts
        blocks = array.reshape(devices, -1, array.shape[-1])
        return (lax.all_to_all(blocks, seq, split_axis=0, concat_axis=0).reshape(array.shape),)

    query = call(
        query_body,
        jax.ShapeDtypeStruct((rows, width), jnp.float32),
        (tokens, norm_gain[None, :], w_in, short_filter),
        [pltpu.VMEM] * 4,
        flops=2 * rows * width * width,
        moved=800_000,
    )
    args = (tokens, norm_gain[None, :], w_in, short_filter, long_filter, medium_filter, skip_gain[None, :])
    args = tuple(pltpu.with_memory_space_constraint(arg, pltpu.HBM) for arg in args)
    packed = (packed_shape, jnp.bfloat16)
    parts = call(
        prepare_body,
        pieces(packed_shape, edge),
        args,
        [pltpu.HBM] * len(args),
        scratch(packed, ((chips, edge, lane), jnp.bfloat16))
        + [pltpu.VMEM(arg.shape, arg.dtype) for arg in args]
        + [pltpu.SemaphoreType.DMA((len(args),))],
        flops=2 * rows * width * 3 * width,
        moved=1_500_000,
    )
    conv = ((width, rows), jnp.bfloat16)
    parts = swap(parts)
    parts = call(
        functools.partial(convolve_body, chans, short_filter.shape[0] - 1),
        pieces((width, rows), 0),
        (first, twist, inner, *parts),
        [pltpu.VMEM] * (3 + len(parts)),
        scratch(packed, ((devices, edge, lane), jnp.float32), ((lane, lane), jnp.float32), conv),
        flops=18 * first.shape[0] * width * rows,
        moved=2_000_000,
    )
    parts = swap(parts)
    return call(
        output_body,
        bf16(rows, width),
        (query, w_out, *parts),
        [pltpu.VMEM] * (2 + len(parts)),
        scratch(conv),
        flops=2 * rows * width * width,
        moved=600_000,
    )


def solution(mesh):
    groups, devices = mesh.devices.shape
    split = jax.sharding.Mesh(mesh.devices.reshape(groups, devices // 2, 2), ("groups", *seq))
    rows = P(("groups", *seq), None)
    placed = (rows, P(), P(), P(), P(seq, None), P(), P(), P())
    return jax.shard_map(local, mesh=split, in_specs=placed, out_specs=rows, check_vma=False)
```

```python
import functools
import math

import jax
import jax.numpy as jnp
import numpy as np
from jax import lax
from jax.experimental import pallas as pl
from jax.experimental.pallas import tpu as pltpu
from jax.sharding import PartitionSpec as P

epsilon = 1e-06
edge = 8
lane = 128
seq = ("chip", "core")
rim_step = 2 * edge
chan_tile = 16
vmem_bytes = 32 * 2**20


def whole(space):
    return pl.BlockSpec(memory_space=space)


def call(body, outs, args, spaces, scratch=(), flops=0, moved=0):
    return pl.pallas_call(
        body,
        out_shape=outs,
        in_specs=[whole(space) for space in spaces],
        out_specs=jax.tree.map(lambda _: whole(pltpu.VMEM), outs),
        scratch_shapes=list(scratch),
        compiler_params=pltpu.CompilerParams(vmem_limit_bytes=vmem_bytes),
        cost_estimate=pl.CostEstimate(flops=flops, bytes_accessed=moved, transcendentals=0),
    )(*args)


def spectral_tables(devices, rows, chans):
    full_len = devices * rows
    freqs = 4 * np.arange(devices) + 1
    eye = np.eye(chans)
    angle = 2.0 * math.pi / (4 * devices) * (freqs[:, None] * np.arange(devices)[None, :] % (4 * devices))
    cosine, sine = np.kron(np.cos(angle), eye), np.kron(np.sin(angle), eye)
    first = np.concatenate([cosine, -sine])
    offsets = np.arange(rows)
    twist = 2.0 * math.pi / (4 * full_len) * (freqs[:, None] * offsets[None, :] % (4 * full_len))
    twist = np.concatenate([np.cos(twist), np.sin(twist)])
    if chans % 8:
        twist = np.repeat(twist, chans, axis=0)
    turn = 2.0 * math.pi / rows * (offsets[:, None] * offsets[None, :] % rows)
    inner = np.concatenate([np.cos(turn), np.sin(turn)], axis=1)
    return (
        jnp.asarray(first, jnp.bfloat16),
        jnp.asarray(twist, jnp.float32),
        jnp.asarray(inner, jnp.bfloat16),
    )


def routes_of(chips):
    far = list(range(chips - 2, 1, -2))
    others = far[1::-1] + far[2:]
    return [(mine, other + 1) for mine, other in zip(far, others)]


def carried(route, core):
    mine, others = route
    return jnp.where(core == 0, mine, others), jnp.where(core == 0, others, mine)


def put_routes(source_ref, rim_ref, keep_ref, give_ref, near_ref, home_ref):
    chip, core = lax.axis_index("chip"), lax.axis_index("core")
    size = source_ref.shape[0] // 2 // (lax.axis_size("chip"))
    extra = home_ref.shape[0] - 2 * size

    def put(out_ref, distance):
        start = pl.multiple_of((chip ^ distance) * 2 * size, 2 * size)
        out_ref[0 : 2 * size, :] = source_ref[pl.ds(start, 2 * size), :]
        if extra:
            out_ref[2 * size : 2 * size + extra, :] = rim_ref[chip ^ distance]

    for turn, route in enumerate(routes_of(lax.axis_size("chip"))):
        own, other = carried(route, core)
        put(keep_ref.at[turn], own)
        put(give_ref.at[turn], other)
    put(home_ref, 0)
    put(near_ref, 1)
    begin = 2 * size
    if extra:
        rim = rim_ref[chip ^ 1].astype(jnp.float32)
        near_ref[begin : begin + chan_tile, :] = jnp.concatenate([rim, rim]).astype(jnp.bfloat16)
        begin += chan_tile
    near_ref[begin : begin + 2 * size, :] = home_ref[0 : 2 * size, :]
    begin += 2 * size
    near_ref[begin:, :] = home_ref[0 : near_ref.shape[0] - begin, :]


def half_rims(first_ref, second_ref, begin):
    pair = [ref[begin : begin + edge, :].astype(jnp.float32) for ref in (first_ref, second_ref)]
    return jnp.concatenate([rims[0 : edge // 2] for rims in pair])


def merge_body(size, keep_ref, got_ref, *out_refs):
    for turn, out_ref in enumerate(out_refs):
        out_ref[0 : 2 * size, :] = keep_ref[turn, 0 : 2 * size, :]
        out_ref[2 * size : 4 * size, :] = got_ref[turn, 0 : 2 * size, :]
        if out_ref.shape[0] > 4 * size:
            rims = half_rims(keep_ref.at[turn], got_ref.at[turn], 2 * size)
            out_ref[4 * size :, :] = rims.astype(jnp.bfloat16)


def split_body(size, *refs):
    far_refs, (near_ref, home_ref, keep_ref, give_ref) = refs[:-4], refs[-4:]
    core = lax.axis_index("core")
    sources = [(far_ref, 2 * sender) for far_ref in far_refs for sender in range(2)]
    sources += [(near_ref, 0), (home_ref, 0)]
    for out_ref, target in ((keep_ref, core), (give_ref, 1 - core)):
        for place, (source_ref, block) in enumerate(sources):
            start = pl.multiple_of((block + target) * size, size)
            out_ref[place * size : (place + 1) * size, :] = source_ref[pl.ds(start, size), :]
        begin = len(sources) * size
        if out_ref.shape[0] > begin:
            rims = [far_ref[4 * size :, :].astype(jnp.float32) for far_ref in far_refs]
            rims.append(half_rims(near_ref, home_ref, 2 * size))
            out_ref[begin:, :] = jnp.concatenate(rims).astype(jnp.bfloat16)


def take_routes(keep_ref, got_ref, target_ref, rim_ref=None):
    chip, core = lax.axis_index("chip"), lax.axis_index("core")
    routes = routes_of(lax.axis_size("chip"))
    count = 2 * len(routes) + 2
    size = target_ref.shape[0] // (2 * lax.axis_size("chip"))
    places = [(*carried(route, core), sender) for route in routes for sender in range(2)]
    places += [(1, 1, 0), (0, 0, 0)]
    for place, (own, other, sender) in enumerate(places):
        for ref, distance, carrier in ((keep_ref, own, core), (got_ref, other, 1 - core)):
            device = (chip ^ distance) * 2 + (carrier if sender == 0 else 1 - carrier)
            start = pl.multiple_of(device * size, size)
            target_ref[pl.ds(start, size), :] = ref[place * size : (place + 1) * size, :]
            if rim_ref is not None:
                begin = place * edge // 2
                rims = ref[count * size :, :].astype(jnp.float32)
                rim_ref[device, 0 : edge // 2, :] = rims[begin : begin + edge // 2]


def normed_of(tokens_ref, gain_ref):
    inputs = tokens_ref[...].astype(jnp.float32)
    mean_sq = jnp.mean(inputs * inputs, axis=-1, keepdims=True)
    return (inputs * lax.rsqrt(mean_sq + epsilon) * gain_ref[...]).astype(jnp.bfloat16)


def projected_of(normed, weights):
    projected = jnp.dot(normed, weights, preferred_element_type=jnp.float32)
    projected = projected.astype(jnp.bfloat16).astype(jnp.float32)
    return jnp.concatenate([projected, jnp.zeros((edge, projected.shape[1]), jnp.float32)])


def short_mix(projected, taps):
    acc = taps[0:1] * projected
    for tap_num in range(1, taps.shape[0]):
        acc = acc + taps[tap_num : tap_num + 1] * pltpu.roll(projected, tap_num, 0)
    return acc


def query_body(tokens_ref, gain_ref, w_ref, short_ref, query_ref):
    rows, width = tokens_ref.shape
    cols = slice(0, width)
    query = short_mix(projected_of(normed_of(tokens_ref, gain_ref), w_ref[:, cols]), short_ref[:, cols])
    query_ref[...] = query[0:rows]
    row = lax.broadcasted_iota(jnp.int32, (edge, width), 0)
    query_ref[0:edge, :] = jnp.where(row < short_ref.shape[0] - 1, 1.0, query[0:edge])


def prepare_body(*refs):
    hbm, outs, held, sems = refs[:7], refs[7:-8], refs[-8:-1], refs[-1]
    staged = len(outs) > 1
    outs, (packed_ref, rim_ref) = (outs[:-2], outs[-2:]) if staged else (outs, (outs[0], None))
    tokens_ref, gain_ref, w_ref, short_ref, long_ref, medium_ref, skip_ref = held
    rows, width = tokens_ref.shape
    copies = [pltpu.make_async_copy(h, v, sems.at[i]) for i, (h, v) in enumerate(zip(hbm, held))]
    for copy in copies:
        copy.start()
    copies[0].wait()
    copies[1].wait()
    normed = normed_of(tokens_ref, gain_ref)
    copies[2].wait()
    copies[3].wait()
    query_cols, cols = slice(0, width), slice(width, 3 * width)
    mixed = short_mix(projected_of(normed, w_ref[:, cols]), short_ref[:, cols])
    key, value = mixed[:, 0:width], mixed[:, width:]
    put_columns(packed_ref, 0, (key[0:rows] * value[0:rows]).astype(jnp.bfloat16).T)
    rims = [(key[0:edge], key[rows:]), (value[0:edge], value[rows:])]
    some = jnp.concatenate([normed[0 : 2 * edge], normed[rows - 2 * edge :]])
    some = short_mix(projected_of(some, w_ref[:, query_cols]), short_ref[:, query_cols])
    put_rim(packed_ref, rim_ref, [*rims, (some[0:edge], some[4 * edge :])])
    for copy in copies[4:]:
        copy.wait()
    med_len = medium_ref.shape[0]
    is_first = jnp.where(lax.axis_index(seq) == 0, 1.0, 0.0)
    head = long_ref[0:med_len, :] + is_first * medium_ref[...]
    row = lax.broadcasted_iota(jnp.int32, (edge, width), 0)
    top = head[0:edge] + jnp.where(row == 0, is_first * skip_ref[...], 0.0)
    taps = jnp.concatenate([top, head[edge:], long_ref[med_len:, :]]).astype(jnp.bfloat16)
    put_columns(packed_ref, rows, taps.T)
    if staged:
        put_routes(packed_ref, rim_ref, *outs)


def put_columns(packed_ref, begin, values):
    if packed_ref.shape[1] > lane:
        packed_ref[:, begin : begin + values.shape[1]] = values
        return
    devices = lax.axis_size(seq)
    chans = values.shape[0] // devices
    size = packed_ref.shape[0] // devices
    for device in range(devices):
        for column in range(values.shape[1] // lane):
            start = device * size + (begin // lane + column) * chans
            packed_ref[start : start + chans, :] = values[
                device * chans : (device + 1) * chans, column * lane : (column + 1) * lane
            ]


def put_rim(packed_ref, rim_ref, parts):
    width = parts[0][0].shape[1]
    if rim_ref is None:
        rows = [row for part in parts for row in part]
        rows.append(jnp.zeros((lane - 3 * rim_step, width), jnp.float32))
        rim = jnp.concatenate(rows).T
        packed_ref[:, packed_ref.shape[1] - lane :] = rim.astype(jnp.bfloat16)
        return
    chips = rim_ref.shape[0]
    span = width // chips
    half = edge // 4
    group = lax.broadcasted_iota(jnp.int32, (edge // 2, lane), 1) // span
    parts = [jnp.concatenate([own[0:half], after[0:half]]) for own, after in parts]
    for chip in range(chips):
        begin = chip * span // lane * lane
        place = chip * span % lane
        rim = jnp.zeros((edge // 2, lane), jnp.float32)
        for index, part in enumerate(parts):
            shift = (index * span - place) % lane
            moved = part[:, begin : begin + lane]
            moved = pltpu.roll(moved, shift, 1) if shift else moved
            rim = jnp.where(group == index, moved, rim)
        rim = jnp.concatenate([rim, jnp.zeros((edge // 2, lane), jnp.float32)])
        rim_ref[chip] = rim.astype(jnp.bfloat16)


def columns_of(packed_ref, chans, rows):
    devices, count = lax.axis_size(seq), 2 * rows // lane
    blocks = packed_ref[...].reshape(devices, count * chans, lane)
    columns = [blocks[:, i * chans : (i + 1) * chans].reshape(-1, lane) for i in range(count)]
    return jnp.concatenate(columns, axis=1)


def rim_of(rim_ref, turned_ref, chans):
    span = 2 * chans
    rim = rim_ref[...].reshape(-1, lane)
    row = lax.broadcasted_iota(jnp.int32, rim.shape, 0)
    column = lax.broadcasted_iota(jnp.int32, rim.shape, 1)
    before = pltpu.roll(rim, edge - edge // 4, 0)
    rim = rim + jnp.where(row < edge, 0.0, before)
    signal = rim * pltpu.roll(rim, lane - span, 1)
    turned_ref[...] = jnp.where(column < span, signal, rim).T
    found = []
    for begin in (0, 2 * span):
        start = pl.multiple_of(begin + lax.axis_index("core") * chans, chans)
        part = turned_ref[pl.ds(start, chans), :]
        blocks = [part] + [pltpu.roll(part, lane - edge * k, 1) for k in range(1, rim_ref.shape[0])]
        found.append(jnp.concatenate(blocks))
    return found


def twist_rows(twist_ref, chans):
    half, rows = twist_ref.shape[0] // 2, twist_ref.shape[1]
    tables = twist_ref[0:half, :], twist_ref[half:, :]
    if chans % 8:
        return tables
    return tuple(
        jnp.broadcast_to(table[:, None, :], (half, chans, rows)).reshape(half * chans, rows)
        for table in tables
    )


def convolve_body(chans, rim_count, first_ref, twist_ref, inner_ref, *refs):
    rows = twist_ref.shape[1]
    half = first_ref.shape[0] // 2
    scale = chans / (half * rows)
    staged = len(refs) > 2
    if staged:
        keep_ref, got_ref, *outs, packed_ref, rim_ref, turned_ref, out_ref = refs
        rim_ref[...] = jnp.zeros_like(rim_ref)
        take_routes(keep_ref, got_ref, packed_ref, rim_ref)
        values = columns_of(packed_ref, chans, rows)
        rim_signal, rim_query = rim_of(rim_ref, turned_ref, chans)
    else:
        packed_ref, out_ref = refs
        values = packed_ref[:, : 2 * rows]
        rim = packed_ref[:, 2 * rows :].astype(jnp.float32)
        before = jnp.concatenate([jnp.zeros((chans, lane), jnp.float32), rim[:-chans]])
        rim = rim + pltpu.roll(before, lane - edge, 1)
        rim_signal = rim * pltpu.roll(rim, lane - rim_step, 1)
        rim_query = pltpu.roll(rim, lane - 2 * rim_step, 1)
    in_rim = lax.broadcasted_iota(jnp.int32, rim_signal.shape, 1) < rim_count
    rim_signal = rim_signal.astype(jnp.bfloat16)
    rim_query = scale * jnp.where(in_rim, rim_query, 1.0)
    signal = jnp.concatenate(
        [jnp.where(in_rim, rim_signal, values[:, 0:lane]), values[:, lane:rows]], axis=1
    )
    cosine, sine = inner_ref[:, 0:rows], inner_ref[:, rows:]
    inner = jnp.concatenate(
        [jnp.concatenate([cosine, -sine], axis=1), jnp.concatenate([sine, cosine], axis=1)]
    )
    spread_of = functools.partial(jnp.dot, first_ref[...], preferred_element_type=jnp.float32)
    spreads = [spread_of(values[:, rows : 2 * rows]), spread_of(signal)]
    tw_cos, tw_sin = twist_rows(twist_ref, chans)
    turned = []
    for spread in spreads:
        real, imag = spread[0:half], spread[half:]
        turned.append([real * tw_cos + imag * tw_sin, imag * tw_cos - real * tw_sin])
    turned = jnp.concatenate([jnp.concatenate(pair, axis=1).astype(jnp.bfloat16) for pair in turned])
    spectra = jnp.dot(turned, inner, preferred_element_type=jnp.float32)
    fil_re, fil_im = spectra[0:half, 0:rows], spectra[0:half, rows:]
    real, imag = spectra[half:, 0:rows], spectra[half:, rows:]
    product = [real * fil_im + imag * fil_re, real * fil_re - imag * fil_im]
    product = jnp.concatenate(product, axis=1).astype(jnp.bfloat16)
    back = jnp.dot(product, inner, preferred_element_type=jnp.float32)
    imag, real = back[:, 0:rows], back[:, rows:]
    turned = jnp.concatenate([real * tw_cos - imag * tw_sin, imag * tw_cos + real * tw_sin])
    last = jnp.concatenate([first_ref[0:half, :].T, first_ref[half:, :].T], axis=1)
    conv = jnp.dot(last, turned.astype(jnp.bfloat16), preferred_element_type=jnp.float32)
    conv = jnp.concatenate([conv[:, 0:lane] * rim_query, conv[:, lane:] * scale], axis=1)
    out_ref[...] = conv.astype(jnp.bfloat16)
    if staged:
        put_routes(out_ref, None, *outs)


def output_body(query_ref, w_ref, *refs):
    if len(refs) > 2:
        keep_ref, got_ref, out_ref, conv_ref = refs
        take_routes(keep_ref, got_ref, conv_ref)
    else:
        conv_ref, out_ref = refs
    conv = conv_ref[...].T.astype(jnp.float32)
    mixed_out = (query_ref[...] * conv).astype(jnp.bfloat16)
    out_ref[...] = jnp.dot(mixed_out, w_ref[...], preferred_element_type=jnp.float32).astype(
        jnp.bfloat16
    )


def permute(array, partner):
    return lax.ppermute(array, seq, [(i, partner(i)) for i in range(lax.axis_size(seq))])


def bf16(*shape):
    return jax.ShapeDtypeStruct(shape, jnp.bfloat16)


def exchange(keep, give, near, home):
    turns, size = keep.shape[0], keep.shape[1] // 2 // chan_tile * chan_tile
    lanes, extra = keep.shape[2], keep.shape[1] - 2 * size
    got = permute(give, lambda i: i ^ 1)
    near = permute(near, lambda i: i ^ 2)
    far = call(
        functools.partial(merge_body, size),
        (bf16(4 * size + extra, lanes),) * turns,
        (keep, got),
        [pltpu.VMEM] * 2,
        moved=4 * keep.size,
    )
    routes = routes_of(lax.axis_size("chip"))
    far = [permute(part, lambda i: i ^ 2 * route[i % 2]) for part, route in zip(far, routes)]
    count = 2 * turns + 2
    half = bf16(count * size + count // 2 * extra, lanes)
    keep, give = call(
        functools.partial(split_body, size),
        (half, half),
        (*far, near, home),
        [pltpu.VMEM] * (turns + 2),
        moved=4 * keep.size,
    )
    return keep, permute(give, lambda i: i ^ 1)


def local(tokens, norm_gain, w_in, short_filter, long_filter, medium_filter, skip_gain, w_out):
    rows, width = tokens.shape
    devices, chips = lax.axis_size(seq), lax.axis_size("chip")
    chans = width // devices
    first, twist, inner = spectral_tables(devices, rows, chans)
    staged = chans == chan_tile and chips >= 4 and short_filter.shape[0] <= 3
    if staged:
        packed_shape = (2 * rows // lane * width, lane)
    else:
        packed_shape = (width, 2 * rows + lane)

    def pieces(shape, extra):
        if not staged:
            return (bf16(*shape),)
        size, turns = 2 * shape[0] // devices + extra, chips // 2 - 1
        near = size + size - extra + chan_tile
        return (bf16(turns, size, shape[1]),) * 2 + (bf16(near, shape[1]), bf16(size, shape[1]))

    def scratch(*shapes):
        return [pltpu.VMEM(*shape) for shape in shapes] if staged else []

    def swap(parts):
        if staged:
            return exchange(*parts)
        (array,) = parts
        blocks = array.reshape(devices, -1, array.shape[-1])
        return (lax.all_to_all(blocks, seq, split_axis=0, concat_axis=0).reshape(array.shape),)

    query = call(
        query_body,
        jax.ShapeDtypeStruct((rows, width), jnp.float32),
        (tokens, norm_gain[None, :], w_in, short_filter),
        [pltpu.VMEM] * 4,
        flops=2 * rows * width * width,
        moved=800_000,
    )
    args = (tokens, norm_gain[None, :], w_in, short_filter, long_filter, medium_filter, skip_gain[None, :])
    args = tuple(pltpu.with_memory_space_constraint(arg, pltpu.HBM) for arg in args)
    packed = (packed_shape, jnp.bfloat16)
    parts = call(
        prepare_body,
        pieces(packed_shape, edge),
        args,
        [pltpu.HBM] * len(args),
        scratch(packed, ((chips, edge, lane), jnp.bfloat16))
        + [pltpu.VMEM(arg.shape, arg.dtype) for arg in args]
        + [pltpu.SemaphoreType.DMA((len(args),))],
        flops=2 * rows * width * 3 * width,
        moved=1_500_000,
    )
    conv = ((width, rows), jnp.bfloat16)
    parts = swap(parts)
    parts = call(
        functools.partial(convolve_body, chans, short_filter.shape[0] - 1),
        pieces((width, rows), 0),
        (first, twist, inner, *parts),
        [pltpu.VMEM] * (3 + len(parts)),
        scratch(packed, ((devices, edge, lane), jnp.float32), ((lane, lane), jnp.float32), conv),
        flops=18 * first.shape[0] * width * rows,
        moved=2_000_000,
    )
    parts = swap(parts)
    return call(
        output_body,
        bf16(rows, width),
        (query, w_out, *parts),
        [pltpu.VMEM] * (2 + len(parts)),
        scratch(conv),
        flops=2 * rows * width * width,
        moved=600_000,
    )


def solution(mesh):
    groups, devices = mesh.devices.shape
    split = jax.sharding.Mesh(mesh.devices.reshape(groups, devices // 2, 2), ("groups", *seq))
    rows = P(("groups", *seq), None)
    placed = (rows, P(), P(), P(), P(seq, None), P(), P(), P())
    return jax.shard_map(local, mesh=split, in_specs=placed, out_specs=rows, check_vma=False)
```

```python
import functools
import math

import jax
import jax.numpy as jnp
import numpy as np
from jax import lax
from jax.experimental import pallas as pl
from jax.experimental.pallas import tpu as pltpu
from jax.sharding import PartitionSpec as P

epsilon = 1e-06
edge = 8
lane = 128
seq = ("chip", "core")
rim_step = 2 * edge
chan_tile = 16
vmem_bytes = 32 * 2**20


def whole(space):
    return pl.BlockSpec(memory_space=space)


def call(body, outs, args, spaces, scratch=(), flops=0, moved=0):
    return pl.pallas_call(
        body,
        out_shape=outs,
        in_specs=[whole(space) for space in spaces],
        out_specs=jax.tree.map(lambda _: whole(pltpu.VMEM), outs),
        scratch_shapes=list(scratch),
        compiler_params=pltpu.CompilerParams(vmem_limit_bytes=vmem_bytes),
        cost_estimate=pl.CostEstimate(flops=flops, bytes_accessed=moved, transcendentals=0),
    )(*args)


def spectral_tables(devices, rows, chans):
    full_len = devices * rows
    freqs = 4 * np.arange(devices) + 1
    eye = np.eye(chans)
    angle = 2.0 * math.pi / (4 * devices) * (freqs[:, None] * np.arange(devices)[None, :] % (4 * devices))
    cosine, sine = np.kron(np.cos(angle), eye), np.kron(np.sin(angle), eye)
    first = np.concatenate([cosine, -sine])
    offsets = np.arange(rows)
    twist = 2.0 * math.pi / (4 * full_len) * (freqs[:, None] * offsets[None, :] % (4 * full_len))
    twist = np.concatenate([np.cos(twist), np.sin(twist)])
    if chans % 8:
        twist = np.repeat(twist, chans, axis=0)
    turn = 2.0 * math.pi / rows * (offsets[:, None] * offsets[None, :] % rows)
    inner = np.concatenate([np.cos(turn), np.sin(turn)], axis=1)
    return (
        jnp.asarray(first, jnp.bfloat16),
        jnp.asarray(twist, jnp.float32),
        jnp.asarray(inner, jnp.bfloat16),
    )


def routes_of(chips):
    return [(d, d + 1) for d in range(chips - 2, 1, -2)]


def carried(route, core):
    mine, others = route
    return jnp.where(core == 0, mine, others), jnp.where(core == 0, others, mine)


def put_routes(source_ref, rim_ref, keep_ref, give_ref, near_ref, home_ref):
    chip, core = lax.axis_index("chip"), lax.axis_index("core")
    size = source_ref.shape[0] // 2 // (lax.axis_size("chip"))
    extra = home_ref.shape[0] - 2 * size

    def put(out_ref, distance):
        start = pl.multiple_of((chip ^ distance) * 2 * size, 2 * size)
        out_ref[0 : 2 * size, :] = source_ref[pl.ds(start, 2 * size), :]
        if extra:
            out_ref[2 * size : 2 * size + extra, :] = rim_ref[chip ^ distance]

    for turn, route in enumerate(routes_of(lax.axis_size("chip"))):
        own, other = carried(route, core)
        put(keep_ref.at[turn], own)
        put(give_ref.at[turn], other)
    put(home_ref, 0)
    put(near_ref, 1)
    begin = 2 * size
    if extra:
        rim = rim_ref[chip ^ 1].astype(jnp.float32)
        near_ref[begin : begin + chan_tile, :] = jnp.concatenate([rim, rim]).astype(jnp.bfloat16)
        begin += chan_tile
    near_ref[begin : begin + 2 * size, :] = home_ref[0 : 2 * size, :]
    begin += 2 * size
    near_ref[begin:, :] = home_ref[0 : near_ref.shape[0] - begin, :]


def half_rims(first_ref, second_ref, begin):
    pair = [ref[begin : begin + edge, :].astype(jnp.float32) for ref in (first_ref, second_ref)]
    return jnp.concatenate([rims[0 : edge // 2] for rims in pair])


def merge_body(size, keep_ref, got_ref, *out_refs):
    for turn, out_ref in enumerate(out_refs):
        out_ref[0 : 2 * size, :] = keep_ref[turn, 0 : 2 * size, :]
        out_ref[2 * size : 4 * size, :] = got_ref[turn, 0 : 2 * size, :]
        if out_ref.shape[0] > 4 * size:
            rims = half_rims(keep_ref.at[turn], got_ref.at[turn], 2 * size)
            out_ref[4 * size :, :] = rims.astype(jnp.bfloat16)


def split_body(size, *refs):
    far_refs, (near_ref, home_ref, keep_ref, give_ref) = refs[:-4], refs[-4:]
    core = lax.axis_index("core")
    sources = [(far_ref, 2 * sender) for far_ref in far_refs for sender in range(2)]
    sources += [(near_ref, 0), (home_ref, 0)]
    for out_ref, target in ((keep_ref, core), (give_ref, 1 - core)):
        for place, (source_ref, block) in enumerate(sources):
            start = pl.multiple_of((block + target) * size, size)
            out_ref[place * size : (place + 1) * size, :] = source_ref[pl.ds(start, size), :]
        begin = len(sources) * size
        if out_ref.shape[0] > begin:
            rims = [far_ref[4 * size :, :].astype(jnp.float32) for far_ref in far_refs]
            rims.append(half_rims(near_ref, home_ref, 2 * size))
            out_ref[begin:, :] = jnp.concatenate(rims).astype(jnp.bfloat16)


def take_routes(keep_ref, got_ref, target_ref, rim_ref=None):
    chip, core = lax.axis_index("chip"), lax.axis_index("core")
    routes = routes_of(lax.axis_size("chip"))
    count = 2 * len(routes) + 2
    size = target_ref.shape[0] // (2 * lax.axis_size("chip"))
    places = [(*carried(route, core), sender) for route in routes for sender in range(2)]
    places += [(1, 1, 0), (0, 0, 0)]
    for place, (own, other, sender) in enumerate(places):
        for ref, distance, carrier in ((keep_ref, own, core), (got_ref, other, 1 - core)):
            device = (chip ^ distance) * 2 + (carrier if sender == 0 else 1 - carrier)
            start = pl.multiple_of(device * size, size)
            target_ref[pl.ds(start, size), :] = ref[place * size : (place + 1) * size, :]
            if rim_ref is not None:
                begin = place * edge // 2
                rims = ref[count * size :, :].astype(jnp.float32)
                rim_ref[device, 0 : edge // 2, :] = rims[begin : begin + edge // 2]


def normed_of(tokens_ref, gain_ref):
    inputs = tokens_ref[...].astype(jnp.float32)
    mean_sq = jnp.mean(inputs * inputs, axis=-1, keepdims=True)
    return (inputs * lax.rsqrt(mean_sq + epsilon) * gain_ref[...]).astype(jnp.bfloat16)


def projected_of(normed, weights):
    projected = jnp.dot(normed, weights, preferred_element_type=jnp.float32)
    projected = projected.astype(jnp.bfloat16).astype(jnp.float32)
    return jnp.concatenate([projected, jnp.zeros((edge, projected.shape[1]), jnp.float32)])


def short_mix(projected, taps):
    acc = taps[0:1] * projected
    for tap_num in range(1, taps.shape[0]):
        acc = acc + taps[tap_num : tap_num + 1] * pltpu.roll(projected, tap_num, 0)
    return acc


def query_body(tokens_ref, gain_ref, w_ref, short_ref, query_ref):
    rows, width = tokens_ref.shape
    cols = slice(0, width)
    query = short_mix(projected_of(normed_of(tokens_ref, gain_ref), w_ref[:, cols]), short_ref[:, cols])
    query_ref[...] = query[0:rows]
    row = lax.broadcasted_iota(jnp.int32, (edge, width), 0)
    query_ref[0:edge, :] = jnp.where(row < short_ref.shape[0] - 1, 1.0, query[0:edge])


def prepare_body(*refs):
    hbm, outs, held, sems = refs[:7], refs[7:-8], refs[-8:-1], refs[-1]
    staged = len(outs) > 1
    outs, (packed_ref, rim_ref) = (outs[:-2], outs[-2:]) if staged else (outs, (outs[0], None))
    tokens_ref, gain_ref, w_ref, short_ref, long_ref, medium_ref, skip_ref = held
    rows, width = tokens_ref.shape
    copies = [pltpu.make_async_copy(h, v, sems.at[i]) for i, (h, v) in enumerate(zip(hbm, held))]
    for index in (2, 0, 1, 3, 4, 5, 6):
        copies[index].start()
    copies[0].wait()
    copies[1].wait()
    normed = normed_of(tokens_ref, gain_ref)
    copies[2].wait()
    copies[3].wait()
    query_cols, cols = slice(0, width), slice(width, 3 * width)
    mixed = short_mix(projected_of(normed, w_ref[:, cols]), short_ref[:, cols])
    key, value = mixed[:, 0:width], mixed[:, width:]
    put_columns(packed_ref, 0, (key[0:rows] * value[0:rows]).astype(jnp.bfloat16).T)
    rims = [(key[0:edge], key[rows:]), (value[0:edge], value[rows:])]
    some = jnp.concatenate([normed[0 : 2 * edge], normed[rows - 2 * edge :]])
    some = short_mix(projected_of(some, w_ref[:, query_cols]), short_ref[:, query_cols])
    put_rim(packed_ref, rim_ref, [*rims, (some[0:edge], some[4 * edge :])])
    for copy in copies[4:]:
        copy.wait()
    med_len = medium_ref.shape[0]
    is_first = jnp.where(lax.axis_index(seq) == 0, 1.0, 0.0)
    head = long_ref[0:med_len, :] + is_first * medium_ref[...]
    row = lax.broadcasted_iota(jnp.int32, (edge, width), 0)
    top = head[0:edge] + jnp.where(row == 0, is_first * skip_ref[...], 0.0)
    taps = jnp.concatenate([top, head[edge:], long_ref[med_len:, :]]).astype(jnp.bfloat16)
    put_columns(packed_ref, rows, taps.T)
    if staged:
        put_routes(packed_ref, rim_ref, *outs)


def put_columns(packed_ref, begin, values):
    if packed_ref.shape[1] > lane:
        packed_ref[:, begin : begin + values.shape[1]] = values
        return
    devices = lax.axis_size(seq)
    chans = values.shape[0] // devices
    size = packed_ref.shape[0] // devices
    for device in range(devices):
        for column in range(values.shape[1] // lane):
            start = device * size + (begin // lane + column) * chans
            packed_ref[start : start + chans, :] = values[
                device * chans : (device + 1) * chans, column * lane : (column + 1) * lane
            ]


def put_rim(packed_ref, rim_ref, parts):
    width = parts[0][0].shape[1]
    if rim_ref is None:
        rows = [row for part in parts for row in part]
        rows.append(jnp.zeros((lane - 3 * rim_step, width), jnp.float32))
        rim = jnp.concatenate(rows).T
        packed_ref[:, packed_ref.shape[1] - lane :] = rim.astype(jnp.bfloat16)
        return
    chips = rim_ref.shape[0]
    span = width // chips
    half = edge // 4
    group = lax.broadcasted_iota(jnp.int32, (edge // 2, lane), 1) // span
    parts = [jnp.concatenate([own[0:half], after[0:half]]) for own, after in parts]
    for chip in range(chips):
        begin = chip * span // lane * lane
        place = chip * span % lane
        rim = jnp.zeros((edge // 2, lane), jnp.float32)
        for index, part in enumerate(parts):
            shift = (index * span - place) % lane
            moved = part[:, begin : begin + lane]
            moved = pltpu.roll(moved, shift, 1) if shift else moved
            rim = jnp.where(group == index, moved, rim)
        rim = jnp.concatenate([rim, jnp.zeros((edge // 2, lane), jnp.float32)])
        rim_ref[chip] = rim.astype(jnp.bfloat16)


def columns_of(packed_ref, chans, rows):
    devices, count = lax.axis_size(seq), 2 * rows // lane
    blocks = packed_ref[...].reshape(devices, count * chans, lane)
    columns = [blocks[:, i * chans : (i + 1) * chans].reshape(-1, lane) for i in range(count)]
    return jnp.concatenate(columns, axis=1)


def rim_of(rim_ref, turned_ref, chans):
    span = 2 * chans
    rim = rim_ref[...].reshape(-1, lane)
    row = lax.broadcasted_iota(jnp.int32, rim.shape, 0)
    column = lax.broadcasted_iota(jnp.int32, rim.shape, 1)
    before = pltpu.roll(rim, edge - edge // 4, 0)
    rim = rim + jnp.where(row < edge, 0.0, before)
    signal = rim * pltpu.roll(rim, lane - span, 1)
    turned_ref[...] = jnp.where(column < span, signal, rim).T
    found = []
    for begin in (0, 2 * span):
        start = pl.multiple_of(begin + lax.axis_index("core") * chans, chans)
        part = turned_ref[pl.ds(start, chans), :]
        blocks = [part] + [pltpu.roll(part, lane - edge * k, 1) for k in range(1, rim_ref.shape[0])]
        found.append(jnp.concatenate(blocks))
    return found


def twist_rows(twist_ref, chans):
    half, rows = twist_ref.shape[0] // 2, twist_ref.shape[1]
    tables = twist_ref[0:half, :], twist_ref[half:, :]
    if chans % 8:
        return tables
    return tuple(
        jnp.broadcast_to(table[:, None, :], (half, chans, rows)).reshape(half * chans, rows)
        for table in tables
    )


def convolve_body(chans, rim_count, first_ref, twist_ref, inner_ref, *refs):
    rows = twist_ref.shape[1]
    half = first_ref.shape[0] // 2
    scale = chans / (half * rows)
    staged = len(refs) > 2
    if staged:
        keep_ref, got_ref, *outs, packed_ref, rim_ref, turned_ref, out_ref = refs
        rim_ref[...] = jnp.zeros_like(rim_ref)
        take_routes(keep_ref, got_ref, packed_ref, rim_ref)
        values = columns_of(packed_ref, chans, rows)
        rim_signal, rim_query = rim_of(rim_ref, turned_ref, chans)
    else:
        packed_ref, out_ref = refs
        values = packed_ref[:, : 2 * rows]
        rim = packed_ref[:, 2 * rows :].astype(jnp.float32)
        before = jnp.concatenate([jnp.zeros((chans, lane), jnp.float32), rim[:-chans]])
        rim = rim + pltpu.roll(before, lane - edge, 1)
        rim_signal = rim * pltpu.roll(rim, lane - rim_step, 1)
        rim_query = pltpu.roll(rim, lane - 2 * rim_step, 1)
    in_rim = lax.broadcasted_iota(jnp.int32, rim_signal.shape, 1) < rim_count
    rim_signal = rim_signal.astype(jnp.bfloat16)
    rim_query = scale * jnp.where(in_rim, rim_query, 1.0)
    signal = jnp.concatenate(
        [jnp.where(in_rim, rim_signal, values[:, 0:lane]), values[:, lane:rows]], axis=1
    )
    cosine, sine = inner_ref[:, 0:rows], inner_ref[:, rows:]
    inner = jnp.concatenate(
        [jnp.concatenate([cosine, -sine], axis=1), jnp.concatenate([sine, cosine], axis=1)]
    )
    spread_of = functools.partial(jnp.dot, first_ref[...], preferred_element_type=jnp.float32)
    spreads = [spread_of(values[:, rows : 2 * rows]), spread_of(signal)]
    tw_cos, tw_sin = twist_rows(twist_ref, chans)
    turned = []
    for spread in spreads:
        real, imag = spread[0:half], spread[half:]
        turned.append([real * tw_cos + imag * tw_sin, imag * tw_cos - real * tw_sin])
    turned = jnp.concatenate([jnp.concatenate(pair, axis=1).astype(jnp.bfloat16) for pair in turned])
    spectra = jnp.dot(turned, inner, preferred_element_type=jnp.float32)
    fil_re, fil_im = spectra[0:half, 0:rows], spectra[0:half, rows:]
    real, imag = spectra[half:, 0:rows], spectra[half:, rows:]
    product = [real * fil_im + imag * fil_re, real * fil_re - imag * fil_im]
    product = jnp.concatenate(product, axis=1).astype(jnp.bfloat16)
    back = jnp.dot(product, inner, preferred_element_type=jnp.float32)
    imag, real = back[:, 0:rows], back[:, rows:]
    turned = jnp.concatenate([real * tw_cos - imag * tw_sin, imag * tw_cos + real * tw_sin])
    last = jnp.concatenate([first_ref[0:half, :].T, first_ref[half:, :].T], axis=1)
    conv = jnp.dot(last, turned.astype(jnp.bfloat16), preferred_element_type=jnp.float32)
    conv = jnp.concatenate([conv[:, 0:lane] * rim_query, conv[:, lane:] * scale], axis=1)
    out_ref[...] = conv.astype(jnp.bfloat16)
    if staged:
        put_routes(out_ref, None, *outs)


def output_body(query_ref, w_ref, *refs):
    if len(refs) > 2:
        keep_ref, got_ref, out_ref, conv_ref = refs
        take_routes(keep_ref, got_ref, conv_ref)
    else:
        conv_ref, out_ref = refs
    conv = conv_ref[...].T.astype(jnp.float32)
    mixed_out = (query_ref[...] * conv).astype(jnp.bfloat16)
    out_ref[...] = jnp.dot(mixed_out, w_ref[...], preferred_element_type=jnp.float32).astype(
        jnp.bfloat16
    )


def permute(array, partner):
    return lax.ppermute(array, seq, [(i, partner(i)) for i in range(lax.axis_size(seq))])


def bf16(*shape):
    return jax.ShapeDtypeStruct(shape, jnp.bfloat16)


def exchange(keep, give, near, home):
    turns, size = keep.shape[0], keep.shape[1] // 2 // chan_tile * chan_tile
    lanes, extra = keep.shape[2], keep.shape[1] - 2 * size
    got = permute(give, lambda i: i ^ 1)
    near = permute(near, lambda i: i ^ 2)
    far = call(
        functools.partial(merge_body, size),
        (bf16(4 * size + extra, lanes),) * turns,
        (keep, got),
        [pltpu.VMEM] * 2,
        moved=4 * keep.size,
    )
    routes = routes_of(lax.axis_size("chip"))
    far = [permute(part, lambda i: i ^ 2 * route[i % 2]) for part, route in zip(far, routes)]
    count = 2 * turns + 2
    half = bf16(count * size + count // 2 * extra, lanes)
    keep, give = call(
        functools.partial(split_body, size),
        (half, half),
        (*far, near, home),
        [pltpu.VMEM] * (turns + 2),
        moved=4 * keep.size,
    )
    return keep, permute(give, lambda i: i ^ 1)


def local(tokens, norm_gain, w_in, short_filter, long_filter, medium_filter, skip_gain, w_out):
    rows, width = tokens.shape
    devices, chips = lax.axis_size(seq), lax.axis_size("chip")
    chans = width // devices
    first, twist, inner = spectral_tables(devices, rows, chans)
    staged = chans == chan_tile and chips >= 4 and short_filter.shape[0] <= 3
    if staged:
        packed_shape = (2 * rows // lane * width, lane)
    else:
        packed_shape = (width, 2 * rows + lane)

    def pieces(shape, extra):
        if not staged:
            return (bf16(*shape),)
        size, turns = 2 * shape[0] // devices + extra, chips // 2 - 1
        near = size + size - extra + chan_tile
        return (bf16(turns, size, shape[1]),) * 2 + (bf16(near, shape[1]), bf16(size, shape[1]))

    def scratch(*shapes):
        return [pltpu.VMEM(*shape) for shape in shapes] if staged else []

    def swap(parts):
        if staged:
            return exchange(*parts)
        (array,) = parts
        blocks = array.reshape(devices, -1, array.shape[-1])
        return (lax.all_to_all(blocks, seq, split_axis=0, concat_axis=0).reshape(array.shape),)

    query = call(
        query_body,
        jax.ShapeDtypeStruct((rows, width), jnp.float32),
        (tokens, norm_gain[None, :], w_in, short_filter),
        [pltpu.VMEM] * 4,
        flops=2 * rows * width * width,
        moved=800_000,
    )
    args = (tokens, norm_gain[None, :], w_in, short_filter, long_filter, medium_filter, skip_gain[None, :])
    args = tuple(pltpu.with_memory_space_constraint(arg, pltpu.HBM) for arg in args)
    packed = (packed_shape, jnp.bfloat16)
    parts = call(
        prepare_body,
        pieces(packed_shape, edge),
        args,
        [pltpu.HBM] * len(args),
        scratch(packed, ((chips, edge, lane), jnp.bfloat16))
        + [pltpu.VMEM(arg.shape, arg.dtype) for arg in args]
        + [pltpu.SemaphoreType.DMA((len(args),))],
        flops=2 * rows * width * 3 * width,
        moved=1_500_000,
    )
    conv = ((width, rows), jnp.bfloat16)
    parts = swap(parts)
    parts = call(
        functools.partial(convolve_body, chans, short_filter.shape[0] - 1),
        pieces((width, rows), 0),
        (first, twist, inner, *parts),
        [pltpu.VMEM] * (3 + len(parts)),
        scratch(packed, ((devices, edge, lane), jnp.float32), ((lane, lane), jnp.float32), conv),
        flops=18 * first.shape[0] * width * rows,
        moved=2_000_000,
    )
    parts = swap(parts)
    return call(
        output_body,
        bf16(rows, width),
        (query, w_out, *parts),
        [pltpu.VMEM] * (2 + len(parts)),
        scratch(conv),
        flops=2 * rows * width * width,
        moved=600_000,
    )


def solution(mesh):
    groups, devices = mesh.devices.shape
    split = jax.sharding.Mesh(mesh.devices.reshape(groups, devices // 2, 2), ("groups", *seq))
    rows = P(("groups", *seq), None)
    placed = (rows, P(), P(), P(), P(seq, None), P(), P(), P())
    return jax.shard_map(local, mesh=split, in_specs=placed, out_specs=rows, check_vma=False)
```

```python
import functools
import math

import jax
import jax.numpy as jnp
import numpy as np
from jax import lax
from jax.experimental import pallas as pl
from jax.experimental.pallas import tpu as pltpu
from jax.sharding import PartitionSpec as P

epsilon = 1e-06
edge = 8
lane = 128
seq = ("chip", "core")
rim_step = 2 * edge
chan_tile = 16
vmem_bytes = 32 * 2**20


def whole(space):
    return pl.BlockSpec(memory_space=space)


def call(body, outs, args, spaces, scratch=(), flops=0, moved=0):
    return pl.pallas_call(
        body,
        out_shape=outs,
        in_specs=[whole(space) for space in spaces],
        out_specs=jax.tree.map(lambda _: whole(pltpu.VMEM), outs),
        scratch_shapes=list(scratch),
        compiler_params=pltpu.CompilerParams(vmem_limit_bytes=vmem_bytes),
        cost_estimate=pl.CostEstimate(flops=flops, bytes_accessed=moved, transcendentals=0),
    )(*args)


def spectral_tables(devices, rows, chans):
    full_len = devices * rows
    freqs = 4 * np.arange(devices) + 1
    eye = np.eye(chans)
    angle = 2.0 * math.pi / (4 * devices) * (freqs[:, None] * np.arange(devices)[None, :] % (4 * devices))
    cosine, sine = np.kron(np.cos(angle), eye), np.kron(np.sin(angle), eye)
    first = np.concatenate([cosine, -sine])
    offsets = np.arange(rows)
    twist = 2.0 * math.pi / (4 * full_len) * (freqs[:, None] * offsets[None, :] % (4 * full_len))
    twist = np.concatenate([np.cos(twist), np.sin(twist)])
    if chans % 8:
        twist = np.repeat(twist, chans, axis=0)
    turn = 2.0 * math.pi / rows * (offsets[:, None] * offsets[None, :] % rows)
    inner = np.concatenate([np.cos(turn), np.sin(turn)], axis=1)
    return (
        jnp.asarray(first, jnp.bfloat16),
        jnp.asarray(twist, jnp.float32),
        jnp.asarray(inner, jnp.bfloat16),
    )


def routes_of(chips):
    return [(d, d + 1) for d in range(chips - 2, 1, -2)]


def carried(route, core):
    mine, others = route
    return jnp.where(core == 0, mine, others), jnp.where(core == 0, others, mine)


def put_routes(source_ref, rim_ref, keep_ref, give_ref, near_ref, home_ref):
    chip, core = lax.axis_index("chip"), lax.axis_index("core")
    size = source_ref.shape[0] // 2 // (lax.axis_size("chip"))
    extra = home_ref.shape[0] - 2 * size

    def put(out_ref, distance):
        start = pl.multiple_of((chip ^ distance) * 2 * size, 2 * size)
        out_ref[0 : 2 * size, :] = source_ref[pl.ds(start, 2 * size), :]
        if extra:
            out_ref[2 * size : 2 * size + extra, :] = rim_ref[chip ^ distance]

    for turn, route in enumerate(routes_of(lax.axis_size("chip"))):
        own, other = carried(route, core)
        put(keep_ref.at[turn], own)
        put(give_ref.at[turn], other)
    put(home_ref, 0)
    put(near_ref, 1)
    begin = 2 * size
    if extra:
        rim = rim_ref[chip ^ 1].astype(jnp.float32)
        near_ref[begin : begin + chan_tile, :] = jnp.concatenate([rim, rim]).astype(jnp.bfloat16)
        begin += chan_tile
    near_ref[begin : begin + 2 * size, :] = home_ref[0 : 2 * size, :]
    begin += 2 * size
    near_ref[begin:, :] = home_ref[0 : near_ref.shape[0] - begin, :]


def half_rims(first_ref, second_ref, begin):
    pair = [ref[begin : begin + edge, :].astype(jnp.float32) for ref in (first_ref, second_ref)]
    return jnp.concatenate([rims[0 : edge // 2] for rims in pair])


def merge_body(size, keep_ref, got_ref, *out_refs):
    for turn, out_ref in enumerate(out_refs):
        out_ref[0 : 2 * size, :] = keep_ref[turn, 0 : 2 * size, :]
        out_ref[2 * size : 4 * size, :] = got_ref[turn, 0 : 2 * size, :]
        if out_ref.shape[0] > 4 * size:
            rims = half_rims(keep_ref.at[turn], got_ref.at[turn], 2 * size)
            out_ref[4 * size :, :] = rims.astype(jnp.bfloat16)


def split_body(size, *refs):
    far_refs, (near_ref, home_ref, keep_ref, give_ref) = refs[:-4], refs[-4:]
    core = lax.axis_index("core")
    sources = [(far_ref, 2 * sender) for far_ref in far_refs for sender in range(2)]
    sources += [(near_ref, 0), (home_ref, 0)]
    for out_ref, target in ((keep_ref, core), (give_ref, 1 - core)):
        for place, (source_ref, block) in enumerate(sources):
            start = pl.multiple_of((block + target) * size, size)
            out_ref[place * size : (place + 1) * size, :] = source_ref[pl.ds(start, size), :]
        begin = len(sources) * size
        if out_ref.shape[0] > begin:
            rims = [far_ref[4 * size :, :].astype(jnp.float32) for far_ref in far_refs]
            rims.append(half_rims(near_ref, home_ref, 2 * size))
            out_ref[begin:, :] = jnp.concatenate(rims).astype(jnp.bfloat16)


def take_routes(keep_ref, got_ref, target_ref, rim_ref=None):
    chip, core = lax.axis_index("chip"), lax.axis_index("core")
    routes = routes_of(lax.axis_size("chip"))
    count = 2 * len(routes) + 2
    size = target_ref.shape[0] // (2 * lax.axis_size("chip"))
    places = [(*carried(route, core), sender) for route in routes for sender in range(2)]
    places += [(1, 1, 0), (0, 0, 0)]
    for place, (own, other, sender) in enumerate(places):
        for ref, distance, carrier in ((keep_ref, own, core), (got_ref, other, 1 - core)):
            device = (chip ^ distance) * 2 + (carrier if sender == 0 else 1 - carrier)
            start = pl.multiple_of(device * size, size)
            target_ref[pl.ds(start, size), :] = ref[place * size : (place + 1) * size, :]
            if rim_ref is not None:
                begin = place * edge // 2
                rims = ref[count * size :, :].astype(jnp.float32)
                rim_ref[device, 0 : edge // 2, :] = rims[begin : begin + edge // 2]


def normed_of(tokens_ref, gain_ref):
    inputs = tokens_ref[...].astype(jnp.float32)
    mean_sq = jnp.mean(inputs * inputs, axis=-1, keepdims=True)
    return (inputs * lax.rsqrt(mean_sq + epsilon) * gain_ref[...]).astype(jnp.bfloat16)


def projected_of(normed, weights):
    projected = jnp.dot(normed, weights, preferred_element_type=jnp.float32)
    projected = projected.astype(jnp.bfloat16).astype(jnp.float32)
    return jnp.concatenate([projected, jnp.zeros((edge, projected.shape[1]), jnp.float32)])


def short_mix(projected, taps):
    acc = taps[0:1] * projected
    for tap_num in range(1, taps.shape[0]):
        acc = acc + taps[tap_num : tap_num + 1] * pltpu.roll(projected, tap_num, 0)
    return acc


def query_body(tokens_ref, gain_ref, w_ref, short_ref, query_ref):
    rows, width = tokens_ref.shape
    cols = slice(0, width)
    query = short_mix(projected_of(normed_of(tokens_ref, gain_ref), w_ref[:, cols]), short_ref[:, cols])
    query_ref[...] = query[0:rows]
    row = lax.broadcasted_iota(jnp.int32, (edge, width), 0)
    query_ref[0:edge, :] = jnp.where(row < short_ref.shape[0] - 1, 1.0, query[0:edge])


def prepare_body(*refs):
    hbm, outs, held, sems = refs[:7], refs[7:-8], refs[-8:-1], refs[-1]
    staged = len(outs) > 1
    outs, (packed_ref, rim_ref) = (outs[:-2], outs[-2:]) if staged else (outs, (outs[0], None))
    tokens_ref, gain_ref, w_ref, short_ref, long_ref, medium_ref, skip_ref = held
    rows, width = tokens_ref.shape
    copies = [pltpu.make_async_copy(h, v, sems.at[i]) for i, (h, v) in enumerate(zip(hbm, held))]
    for copy in copies:
        copy.start()
    copies[0].wait()
    copies[1].wait()
    normed = normed_of(tokens_ref, gain_ref)
    copies[2].wait()
    copies[3].wait()
    query_cols, cols = slice(0, width), slice(width, 3 * width)
    mixed = short_mix(projected_of(normed, w_ref[:, cols]), short_ref[:, cols])
    key, value = mixed[:, 0:width], mixed[:, width:]
    put_columns(packed_ref, 0, (key[0:rows] * value[0:rows]).astype(jnp.bfloat16).T)
    rims = [(key[0:edge], key[rows:]), (value[0:edge], value[rows:])]
    some = jnp.concatenate([normed[0 : 2 * edge], normed[rows - 2 * edge :]])
    some = short_mix(projected_of(some, w_ref[:, query_cols]), short_ref[:, query_cols])
    put_rim(packed_ref, rim_ref, [*rims, (some[0:edge], some[4 * edge :])])
    for copy in copies[4:]:
        copy.wait()
    med_len = medium_ref.shape[0]
    is_first = jnp.where(lax.axis_index(seq) == 0, 1.0, 0.0)
    head = long_ref[0:med_len, :] + is_first * medium_ref[...]
    row = lax.broadcasted_iota(jnp.int32, (edge, width), 0)
    top = head[0:edge] + jnp.where(row == 0, is_first * skip_ref[...], 0.0)
    taps = jnp.concatenate([top, head[edge:], long_ref[med_len:, :]]).astype(jnp.bfloat16)
    put_columns(packed_ref, rows, taps.T)
    if staged:
        put_routes(packed_ref, rim_ref, *outs)


def put_columns(packed_ref, begin, values):
    if packed_ref.shape[1] > lane:
        packed_ref[:, begin : begin + values.shape[1]] = values
        return
    devices = lax.axis_size(seq)
    chans = values.shape[0] // devices
    size = packed_ref.shape[0] // devices
    for device in range(devices):
        for column in range(values.shape[1] // lane):
            start = device * size + (begin // lane + column) * chans
            packed_ref[start : start + chans, :] = values[
                device * chans : (device + 1) * chans, column * lane : (column + 1) * lane
            ]


def put_rim(packed_ref, rim_ref, parts):
    width = parts[0][0].shape[1]
    if rim_ref is None:
        rows = [row for part in parts for row in part]
        rows.append(jnp.zeros((lane - 3 * rim_step, width), jnp.float32))
        rim = jnp.concatenate(rows).T
        packed_ref[:, packed_ref.shape[1] - lane :] = rim.astype(jnp.bfloat16)
        return
    chips = rim_ref.shape[0]
    span = width // chips
    half = edge // 4
    group = lax.broadcasted_iota(jnp.int32, (edge // 2, lane), 1) // span
    parts = [jnp.concatenate([own[0:half], after[0:half]]) for own, after in parts]
    for chip in range(chips):
        begin = chip * span // lane * lane
        place = chip * span % lane
        rim = jnp.zeros((edge // 2, lane), jnp.float32)
        for index, part in enumerate(parts):
            shift = (index * span - place) % lane
            moved = part[:, begin : begin + lane]
            moved = pltpu.roll(moved, shift, 1) if shift else moved
            rim = jnp.where(group == index, moved, rim)
        rim = jnp.concatenate([rim, jnp.zeros((edge // 2, lane), jnp.float32)])
        rim_ref[chip] = rim.astype(jnp.bfloat16)


def columns_of(packed_ref, chans, rows):
    devices, count = lax.axis_size(seq), 2 * rows // lane
    blocks = packed_ref[...].reshape(devices, count * chans, lane)
    columns = [blocks[:, i * chans : (i + 1) * chans].reshape(-1, lane) for i in range(count)]
    return jnp.concatenate(columns, axis=1)


def rim_of(rim_ref, turned_ref, chans):
    span = 2 * chans
    rim = rim_ref[...].reshape(-1, lane)
    row = lax.broadcasted_iota(jnp.int32, rim.shape, 0)
    column = lax.broadcasted_iota(jnp.int32, rim.shape, 1)
    before = pltpu.roll(rim, edge - edge // 4, 0)
    rim = rim + jnp.where(row < edge, 0.0, before)
    signal = rim * pltpu.roll(rim, lane - span, 1)
    turned_ref[...] = jnp.where(column < span, signal, rim).T
    found = []
    for begin in (0, 2 * span):
        start = pl.multiple_of(begin + lax.axis_index("core") * chans, chans)
        part = turned_ref[pl.ds(start, chans), :]
        blocks = [part] + [pltpu.roll(part, lane - edge * k, 1) for k in range(1, rim_ref.shape[0])]
        found.append(jnp.concatenate(blocks))
    return found


def twist_rows(twist_ref, chans):
    half, rows = twist_ref.shape[0] // 2, twist_ref.shape[1]
    tables = twist_ref[0:half, :], twist_ref[half:, :]
    if chans % 8:
        return tables
    return tuple(
        jnp.broadcast_to(table[:, None, :], (half, chans, rows)).reshape(half * chans, rows)
        for table in tables
    )


def convolve_body(chans, rim_count, first_ref, twist_ref, inner_ref, *refs):
    rows = twist_ref.shape[1]
    half = first_ref.shape[0] // 2
    scale = chans / (half * rows)
    staged = len(refs) > 2
    if staged:
        keep_ref, got_ref, *outs, packed_ref, rim_ref, turned_ref, out_ref = refs
        rim_ref[...] = jnp.zeros_like(rim_ref)
        take_routes(keep_ref, got_ref, packed_ref, rim_ref)
        values = columns_of(packed_ref, chans, rows)
        rim_signal, rim_query = rim_of(rim_ref, turned_ref, chans)
    else:
        packed_ref, out_ref = refs
        values = packed_ref[:, : 2 * rows]
        rim = packed_ref[:, 2 * rows :].astype(jnp.float32)
        before = jnp.concatenate([jnp.zeros((chans, lane), jnp.float32), rim[:-chans]])
        rim = rim + pltpu.roll(before, lane - edge, 1)
        rim_signal = rim * pltpu.roll(rim, lane - rim_step, 1)
        rim_query = pltpu.roll(rim, lane - 2 * rim_step, 1)
    in_rim = lax.broadcasted_iota(jnp.int32, rim_signal.shape, 1) < rim_count
    rim_signal = rim_signal.astype(jnp.bfloat16)
    rim_query = scale * jnp.where(in_rim, rim_query, 1.0)
    signal = jnp.concatenate(
        [jnp.where(in_rim, rim_signal, values[:, 0:lane]), values[:, lane:rows]], axis=1
    )
    cosine, sine = inner_ref[:, 0:rows], inner_ref[:, rows:]
    inner = jnp.concatenate(
        [jnp.concatenate([cosine, -sine], axis=1), jnp.concatenate([sine, cosine], axis=1)]
    )
    spread_of = functools.partial(jnp.dot, first_ref[...], preferred_element_type=jnp.float32)
    spreads = [spread_of(values[:, rows : 2 * rows]), spread_of(signal)]
    tw_cos, tw_sin = twist_rows(twist_ref, chans)
    turned = []
    for spread in spreads:
        real, imag = spread[0:half], spread[half:]
        turned.append([real * tw_cos + imag * tw_sin, imag * tw_cos - real * tw_sin])
    turned = jnp.concatenate([jnp.concatenate(pair, axis=1).astype(jnp.bfloat16) for pair in turned])
    spectra = jnp.dot(turned, inner, preferred_element_type=jnp.float32)
    fil_re, fil_im = spectra[0:half, 0:rows], spectra[0:half, rows:]
    real, imag = spectra[half:, 0:rows], spectra[half:, rows:]
    product = [real * fil_im + imag * fil_re, real * fil_re - imag * fil_im]
    product = jnp.concatenate(product, axis=1).astype(jnp.bfloat16)
    back = jnp.dot(product, inner, preferred_element_type=jnp.float32)
    imag, real = back[:, 0:rows], back[:, rows:]
    turned = jnp.concatenate([real * tw_cos - imag * tw_sin, imag * tw_cos + real * tw_sin])
    last = jnp.concatenate([first_ref[0:half, :].T, first_ref[half:, :].T], axis=1)
    conv = jnp.dot(last, turned.astype(jnp.bfloat16), preferred_element_type=jnp.float32)
    conv = jnp.concatenate([conv[:, 0:lane] * rim_query, conv[:, lane:] * scale], axis=1)
    out_ref[...] = conv.astype(jnp.bfloat16)
    if staged:
        put_routes(out_ref, None, *outs)


def output_body(query_ref, w_ref, *refs):
    if len(refs) > 2:
        keep_ref, got_ref, out_ref, conv_ref = refs
        take_routes(keep_ref, got_ref, conv_ref)
    else:
        conv_ref, out_ref = refs
    conv = conv_ref[...].T.astype(jnp.float32)
    mixed_out = (query_ref[...] * conv).astype(jnp.bfloat16)
    out_ref[...] = jnp.dot(mixed_out, w_ref[...], preferred_element_type=jnp.float32).astype(
        jnp.bfloat16
    )


def permute(array, partner):
    return lax.ppermute(array, seq, [(i, partner(i)) for i in range(lax.axis_size(seq))])


def bf16(*shape):
    return jax.ShapeDtypeStruct(shape, jnp.bfloat16)


def exchange(keep, give, near, home):
    turns, size = keep.shape[0], keep.shape[1] // 2 // chan_tile * chan_tile
    lanes, extra = keep.shape[2], keep.shape[1] - 2 * size
    got = permute(give, lambda i: i ^ 1)
    near = permute(near, lambda i: i ^ 2)
    far = call(
        functools.partial(merge_body, size),
        (bf16(4 * size + extra, lanes),) * turns,
        (keep, got),
        [pltpu.VMEM] * 2,
        moved=4 * keep.size,
    )
    routes = routes_of(lax.axis_size("chip"))
    far = [permute(part, lambda i: i ^ 2 * route[i % 2]) for part, route in zip(far, routes)]
    count = 2 * turns + 2
    half = bf16(count * size + count // 2 * extra, lanes)
    keep, give = call(
        functools.partial(split_body, size),
        (half, half),
        (*far, near, home),
        [pltpu.VMEM] * (turns + 2),
        moved=4 * keep.size,
    )
    return keep, permute(give, lambda i: i ^ 1)


def local(tokens, norm_gain, w_in, short_filter, long_filter, medium_filter, skip_gain, w_out):
    rows, width = tokens.shape
    devices, chips = lax.axis_size(seq), lax.axis_size("chip")
    chans = width // devices
    first, twist, inner = spectral_tables(devices, rows, chans)
    staged = chans == chan_tile and chips >= 4 and short_filter.shape[0] <= 3
    if staged:
        packed_shape = (2 * rows // lane * width, lane)
    else:
        packed_shape = (width, 2 * rows + lane)

    def pieces(shape, extra):
        if not staged:
            return (bf16(*shape),)
        size, turns = 2 * shape[0] // devices + extra, chips // 2 - 1
        near = size + size - extra + chan_tile
        return (bf16(turns, size, shape[1]),) * 2 + (bf16(near, shape[1]), bf16(size, shape[1]))

    def scratch(*shapes):
        return [pltpu.VMEM(*shape) for shape in shapes] if staged else []

    def swap(parts):
        if staged:
            return exchange(*parts)
        (array,) = parts
        blocks = array.reshape(devices, -1, array.shape[-1])
        return (lax.all_to_all(blocks, seq, split_axis=0, concat_axis=0).reshape(array.shape),)

    query = call(
        query_body,
        jax.ShapeDtypeStruct((rows, width), jnp.float32),
        (tokens, norm_gain[None, :], w_in, short_filter),
        [pltpu.VMEM] * 4,
        flops=2 * rows * width * width,
        moved=800_000,
    )
    args = (tokens, norm_gain[None, :], w_in, short_filter, long_filter, medium_filter, skip_gain[None, :])
    args = tuple(pltpu.with_memory_space_constraint(arg, pltpu.HBM) for arg in args)
    packed = (packed_shape, jnp.bfloat16)
    parts = call(
        prepare_body,
        pieces(packed_shape, edge),
        args,
        [pltpu.HBM] * len(args),
        scratch(packed, ((chips, edge, lane), jnp.bfloat16))
        + [pltpu.VMEM(arg.shape, arg.dtype) for arg in args]
        + [pltpu.SemaphoreType.DMA((len(args),))],
        flops=2 * rows * width * 3 * width,
        moved=1_500_000,
    )
    conv = ((width, rows), jnp.bfloat16)
    parts, query = lax.optimization_barrier((swap(parts), query))
    parts = call(
        functools.partial(convolve_body, chans, short_filter.shape[0] - 1),
        pieces((width, rows), 0),
        (first, twist, inner, *parts),
        [pltpu.VMEM] * (3 + len(parts)),
        scratch(packed, ((devices, edge, lane), jnp.float32), ((lane, lane), jnp.float32), conv),
        flops=18 * first.shape[0] * width * rows,
        moved=2_000_000,
    )
    parts = swap(parts)
    return call(
        output_body,
        bf16(rows, width),
        (query, w_out, *parts),
        [pltpu.VMEM] * (2 + len(parts)),
        scratch(conv),
        flops=2 * rows * width * width,
        moved=600_000,
    )


def solution(mesh):
    groups, devices = mesh.devices.shape
    split = jax.sharding.Mesh(mesh.devices.reshape(groups, devices // 2, 2), ("groups", *seq))
    rows = P(("groups", *seq), None)
    placed = (rows, P(), P(), P(), P(seq, None), P(), P(), P())
    return jax.shard_map(local, mesh=split, in_specs=placed, out_specs=rows, check_vma=False)
```

```python
import functools
import math

import jax
import jax.numpy as jnp
import numpy as np
from jax import lax
from jax.experimental import pallas as pl
from jax.experimental.pallas import tpu as pltpu
from jax.sharding import PartitionSpec as P

epsilon = 1e-06
edge = 8
lane = 128
seq = ("chip", "core")
rim_step = 2 * edge
chan_tile = 16
vmem_bytes = 32 * 2**20


def whole(space):
    return pl.BlockSpec(memory_space=space)


def call(body, outs, args, spaces, scratch=(), flops=0, moved=0):
    return pl.pallas_call(
        body,
        out_shape=outs,
        in_specs=[whole(space) for space in spaces],
        out_specs=jax.tree.map(lambda _: whole(pltpu.VMEM), outs),
        scratch_shapes=list(scratch),
        compiler_params=pltpu.CompilerParams(vmem_limit_bytes=vmem_bytes),
        cost_estimate=pl.CostEstimate(flops=flops, bytes_accessed=moved, transcendentals=0),
    )(*args)


def spectral_tables(devices, rows, chans):
    full_len = devices * rows
    freqs = 4 * np.arange(devices) + 1
    eye = np.eye(chans)
    angle = 2.0 * math.pi / (4 * devices) * (freqs[:, None] * np.arange(devices)[None, :] % (4 * devices))
    cosine, sine = np.kron(np.cos(angle), eye), np.kron(np.sin(angle), eye)
    first = np.concatenate([cosine, -sine])
    offsets = np.arange(rows)
    twist = 2.0 * math.pi / (4 * full_len) * (freqs[:, None] * offsets[None, :] % (4 * full_len))
    twist = np.concatenate([np.cos(twist), np.sin(twist)])
    if chans % 8:
        twist = np.repeat(twist, chans, axis=0)
    turn = 2.0 * math.pi / rows * (offsets[:, None] * offsets[None, :] % rows)
    inner = np.concatenate([np.cos(turn), np.sin(turn)], axis=1)
    return (
        jnp.asarray(first, jnp.bfloat16),
        jnp.asarray(twist, jnp.float32),
        jnp.asarray(inner, jnp.bfloat16),
    )


def routes_of(chips):
    return [(d, d + 1) for d in range(chips - 2, 2, -2)] + [(3, 2)]


def carried(route, core):
    mine, others = route
    return jnp.where(core == 0, mine, others), jnp.where(core == 0, others, mine)


def put_routes(source_ref, rim_ref, keep_ref, give_ref, near_ref, home_ref):
    chip, core = lax.axis_index("chip"), lax.axis_index("core")
    size = source_ref.shape[0] // 2 // (lax.axis_size("chip"))
    extra = home_ref.shape[0] - 2 * size

    def put(out_ref, distance):
        start = pl.multiple_of((chip ^ distance) * 2 * size, 2 * size)
        out_ref[0 : 2 * size, :] = source_ref[pl.ds(start, 2 * size), :]
        if extra:
            out_ref[2 * size : 2 * size + extra, :] = rim_ref[chip ^ distance]

    for turn, route in enumerate(routes_of(lax.axis_size("chip"))):
        own, other = carried(route, core)
        put(keep_ref.at[turn], own)
        put(give_ref.at[turn], other)
    put(home_ref, 0)
    put(near_ref, 1)
    begin = 2 * size
    if extra:
        rim = rim_ref[chip ^ 1].astype(jnp.float32)
        near_ref[begin : begin + chan_tile, :] = jnp.concatenate([rim, rim]).astype(jnp.bfloat16)
        begin += chan_tile
    near_ref[begin : begin + 2 * size, :] = home_ref[0 : 2 * size, :]
    begin += 2 * size
    near_ref[begin:, :] = home_ref[0 : near_ref.shape[0] - begin, :]


def half_rims(first_ref, second_ref, begin):
    pair = [ref[begin : begin + edge, :].astype(jnp.float32) for ref in (first_ref, second_ref)]
    return jnp.concatenate([rims[0 : edge // 2] for rims in pair])


def merge_body(size, keep_ref, got_ref, *out_refs):
    for turn, out_ref in enumerate(out_refs):
        out_ref[0 : 2 * size, :] = keep_ref[turn, 0 : 2 * size, :]
        out_ref[2 * size : 4 * size, :] = got_ref[turn, 0 : 2 * size, :]
        if out_ref.shape[0] > 4 * size:
            rims = half_rims(keep_ref.at[turn], got_ref.at[turn], 2 * size)
            out_ref[4 * size :, :] = rims.astype(jnp.bfloat16)


def split_body(size, *refs):
    far_refs, (near_ref, home_ref, keep_ref, give_ref) = refs[:-4], refs[-4:]
    core = lax.axis_index("core")
    sources = [(far_ref, 2 * sender) for far_ref in far_refs for sender in range(2)]
    sources += [(near_ref, 0), (home_ref, 0)]
    for out_ref, target in ((keep_ref, core), (give_ref, 1 - core)):
        for place, (source_ref, block) in enumerate(sources):
            start = pl.multiple_of((block + target) * size, size)
            out_ref[place * size : (place + 1) * size, :] = source_ref[pl.ds(start, size), :]
        begin = len(sources) * size
        if out_ref.shape[0] > begin:
            rims = [far_ref[4 * size :, :].astype(jnp.float32) for far_ref in far_refs]
            rims.append(half_rims(near_ref, home_ref, 2 * size))
            out_ref[begin:, :] = jnp.concatenate(rims).astype(jnp.bfloat16)


def take_routes(keep_ref, got_ref, target_ref, rim_ref=None):
    chip, core = lax.axis_index("chip"), lax.axis_index("core")
    routes = routes_of(lax.axis_size("chip"))
    count = 2 * len(routes) + 2
    size = target_ref.shape[0] // (2 * lax.axis_size("chip"))
    places = [(*carried(route, core), sender) for route in routes for sender in range(2)]
    places += [(1, 1, 0), (0, 0, 0)]
    for place, (own, other, sender) in enumerate(places):
        for ref, distance, carrier in ((keep_ref, own, core), (got_ref, other, 1 - core)):
            device = (chip ^ distance) * 2 + (carrier if sender == 0 else 1 - carrier)
            start = pl.multiple_of(device * size, size)
            target_ref[pl.ds(start, size), :] = ref[place * size : (place + 1) * size, :]
            if rim_ref is not None:
                begin = place * edge // 2
                rims = ref[count * size :, :].astype(jnp.float32)
                rim_ref[device, 0 : edge // 2, :] = rims[begin : begin + edge // 2]


def normed_of(tokens_ref, gain_ref):
    inputs = tokens_ref[...].astype(jnp.float32)
    mean_sq = jnp.mean(inputs * inputs, axis=-1, keepdims=True)
    return (inputs * lax.rsqrt(mean_sq + epsilon) * gain_ref[...]).astype(jnp.bfloat16)


def projected_of(normed, weights):
    projected = jnp.dot(normed, weights, preferred_element_type=jnp.float32)
    projected = projected.astype(jnp.bfloat16).astype(jnp.float32)
    return jnp.concatenate([projected, jnp.zeros((edge, projected.shape[1]), jnp.float32)])


def short_mix(projected, taps):
    acc = taps[0:1] * projected
    for tap_num in range(1, taps.shape[0]):
        acc = acc + taps[tap_num : tap_num + 1] * pltpu.roll(projected, tap_num, 0)
    return acc


def query_body(tokens_ref, gain_ref, w_ref, short_ref, query_ref):
    rows, width = tokens_ref.shape
    cols = slice(0, width)
    query = short_mix(projected_of(normed_of(tokens_ref, gain_ref), w_ref[:, cols]), short_ref[:, cols])
    query_ref[...] = query[0:rows]
    row = lax.broadcasted_iota(jnp.int32, (edge, width), 0)
    query_ref[0:edge, :] = jnp.where(row < short_ref.shape[0] - 1, 1.0, query[0:edge])


def prepare_body(*refs):
    hbm, outs, held, sems = refs[:7], refs[7:-8], refs[-8:-1], refs[-1]
    staged = len(outs) > 1
    outs, (packed_ref, rim_ref) = (outs[:-2], outs[-2:]) if staged else (outs, (outs[0], None))
    tokens_ref, gain_ref, w_ref, short_ref, long_ref, medium_ref, skip_ref = held
    rows, width = tokens_ref.shape
    copies = [pltpu.make_async_copy(h, v, sems.at[i]) for i, (h, v) in enumerate(zip(hbm, held))]
    for copy in copies:
        copy.start()
    copies[0].wait()
    copies[1].wait()
    normed = normed_of(tokens_ref, gain_ref)
    copies[2].wait()
    copies[3].wait()
    query_cols, cols = slice(0, width), slice(width, 3 * width)
    mixed = short_mix(projected_of(normed, w_ref[:, cols]), short_ref[:, cols])
    key, value = mixed[:, 0:width], mixed[:, width:]
    put_columns(packed_ref, 0, (key[0:rows] * value[0:rows]).astype(jnp.bfloat16).T)
    rims = [(key[0:edge], key[rows:]), (value[0:edge], value[rows:])]
    some = jnp.concatenate([normed[0 : 2 * edge], normed[rows - 2 * edge :]])
    some = short_mix(projected_of(some, w_ref[:, query_cols]), short_ref[:, query_cols])
    put_rim(packed_ref, rim_ref, [*rims, (some[0:edge], some[4 * edge :])])
    for copy in copies[4:]:
        copy.wait()
    med_len = medium_ref.shape[0]
    is_first = jnp.where(lax.axis_index(seq) == 0, 1.0, 0.0)
    head = long_ref[0:med_len, :] + is_first * medium_ref[...]
    row = lax.broadcasted_iota(jnp.int32, (edge, width), 0)
    top = head[0:edge] + jnp.where(row == 0, is_first * skip_ref[...], 0.0)
    taps = jnp.concatenate([top, head[edge:], long_ref[med_len:, :]]).astype(jnp.bfloat16)
    put_columns(packed_ref, rows, taps.T)
    if staged:
        put_routes(packed_ref, rim_ref, *outs)


def put_columns(packed_ref, begin, values):
    if packed_ref.shape[1] > lane:
        packed_ref[:, begin : begin + values.shape[1]] = values
        return
    devices = lax.axis_size(seq)
    chans = values.shape[0] // devices
    size = packed_ref.shape[0] // devices
    for device in range(devices):
        for column in range(values.shape[1] // lane):
            start = device * size + (begin // lane + column) * chans
            packed_ref[start : start + chans, :] = values[
                device * chans : (device + 1) * chans, column * lane : (column + 1) * lane
            ]


def put_rim(packed_ref, rim_ref, parts):
    width = parts[0][0].shape[1]
    if rim_ref is None:
        rows = [row for part in parts for row in part]
        rows.append(jnp.zeros((lane - 3 * rim_step, width), jnp.float32))
        rim = jnp.concatenate(rows).T
        packed_ref[:, packed_ref.shape[1] - lane :] = rim.astype(jnp.bfloat16)
        return
    chips = rim_ref.shape[0]
    span = width // chips
    half = edge // 4
    group = lax.broadcasted_iota(jnp.int32, (edge // 2, lane), 1) // span
    parts = [jnp.concatenate([own[0:half], after[0:half]]) for own, after in parts]
    for chip in range(chips):
        begin = chip * span // lane * lane
        place = chip * span % lane
        rim = jnp.zeros((edge // 2, lane), jnp.float32)
        for index, part in enumerate(parts):
            shift = (index * span - place) % lane
            moved = part[:, begin : begin + lane]
            moved = pltpu.roll(moved, shift, 1) if shift else moved
            rim = jnp.where(group == index, moved, rim)
        rim = jnp.concatenate([rim, jnp.zeros((edge // 2, lane), jnp.float32)])
        rim_ref[chip] = rim.astype(jnp.bfloat16)


def columns_of(packed_ref, chans, rows):
    devices, count = lax.axis_size(seq), 2 * rows // lane
    blocks = packed_ref[...].reshape(devices, count * chans, lane)
    columns = [blocks[:, i * chans : (i + 1) * chans].reshape(-1, lane) for i in range(count)]
    return jnp.concatenate(columns, axis=1)


def rim_of(rim_ref, turned_ref, chans):
    span = 2 * chans
    rim = rim_ref[...].reshape(-1, lane)
    row = lax.broadcasted_iota(jnp.int32, rim.shape, 0)
    column = lax.broadcasted_iota(jnp.int32, rim.shape, 1)
    before = pltpu.roll(rim, edge - edge // 4, 0)
    rim = rim + jnp.where(row < edge, 0.0, before)
    signal = rim * pltpu.roll(rim, lane - span, 1)
    turned_ref[...] = jnp.where(column < span, signal, rim).T
    found = []
    for begin in (0, 2 * span):
        start = pl.multiple_of(begin + lax.axis_index("core") * chans, chans)
        part = turned_ref[pl.ds(start, chans), :]
        blocks = [part] + [pltpu.roll(part, lane - edge * k, 1) for k in range(1, rim_ref.shape[0])]
        found.append(jnp.concatenate(blocks))
    return found


def twist_rows(twist_ref, chans):
    half, rows = twist_ref.shape[0] // 2, twist_ref.shape[1]
    tables = twist_ref[0:half, :], twist_ref[half:, :]
    if chans % 8:
        return tables
    return tuple(
        jnp.broadcast_to(table[:, None, :], (half, chans, rows)).reshape(half * chans, rows)
        for table in tables
    )


def convolve_body(chans, rim_count, first_ref, twist_ref, inner_ref, *refs):
    rows = twist_ref.shape[1]
    half = first_ref.shape[0] // 2
    scale = chans / (half * rows)
    staged = len(refs) > 2
    if staged:
        keep_ref, got_ref, *outs, packed_ref, rim_ref, turned_ref, out_ref = refs
        rim_ref[...] = jnp.zeros_like(rim_ref)
        take_routes(keep_ref, got_ref, packed_ref, rim_ref)
        values = columns_of(packed_ref, chans, rows)
        rim_signal, rim_query = rim_of(rim_ref, turned_ref, chans)
    else:
        packed_ref, out_ref = refs
        values = packed_ref[:, : 2 * rows]
        rim = packed_ref[:, 2 * rows :].astype(jnp.float32)
        before = jnp.concatenate([jnp.zeros((chans, lane), jnp.float32), rim[:-chans]])
        rim = rim + pltpu.roll(before, lane - edge, 1)
        rim_signal = rim * pltpu.roll(rim, lane - rim_step, 1)
        rim_query = pltpu.roll(rim, lane - 2 * rim_step, 1)
    in_rim = lax.broadcasted_iota(jnp.int32, rim_signal.shape, 1) < rim_count
    rim_signal = rim_signal.astype(jnp.bfloat16)
    rim_query = scale * jnp.where(in_rim, rim_query, 1.0)
    signal = jnp.concatenate(
        [jnp.where(in_rim, rim_signal, values[:, 0:lane]), values[:, lane:rows]], axis=1
    )
    cosine, sine = inner_ref[:, 0:rows], inner_ref[:, rows:]
    inner = jnp.concatenate(
        [jnp.concatenate([cosine, -sine], axis=1), jnp.concatenate([sine, cosine], axis=1)]
    )
    spread_of = functools.partial(jnp.dot, first_ref[...], preferred_element_type=jnp.float32)
    spreads = [spread_of(values[:, rows : 2 * rows]), spread_of(signal)]
    tw_cos, tw_sin = twist_rows(twist_ref, chans)
    turned = []
    for spread in spreads:
        real, imag = spread[0:half], spread[half:]
        turned.append([real * tw_cos + imag * tw_sin, imag * tw_cos - real * tw_sin])
    turned = jnp.concatenate([jnp.concatenate(pair, axis=1).astype(jnp.bfloat16) for pair in turned])
    spectra = jnp.dot(turned, inner, preferred_element_type=jnp.float32)
    fil_re, fil_im = spectra[0:half, 0:rows], spectra[0:half, rows:]
    real, imag = spectra[half:, 0:rows], spectra[half:, rows:]
    product = [real * fil_im + imag * fil_re, real * fil_re - imag * fil_im]
    product = jnp.concatenate(product, axis=1).astype(jnp.bfloat16)
    back = jnp.dot(product, inner, preferred_element_type=jnp.float32)
    imag, real = back[:, 0:rows], back[:, rows:]
    turned = jnp.concatenate([real * tw_cos - imag * tw_sin, imag * tw_cos + real * tw_sin])
    last = jnp.concatenate([first_ref[0:half, :].T, first_ref[half:, :].T], axis=1)
    conv = jnp.dot(last, turned.astype(jnp.bfloat16), preferred_element_type=jnp.float32)
    conv = jnp.concatenate([conv[:, 0:lane] * rim_query, conv[:, lane:] * scale], axis=1)
    out_ref[...] = conv.astype(jnp.bfloat16)
    if staged:
        put_routes(out_ref, None, *outs)


def output_body(query_ref, w_ref, *refs):
    if len(refs) > 2:
        keep_ref, got_ref, out_ref, conv_ref = refs
        take_routes(keep_ref, got_ref, conv_ref)
    else:
        conv_ref, out_ref = refs
    conv = conv_ref[...].T.astype(jnp.float32)
    mixed_out = (query_ref[...] * conv).astype(jnp.bfloat16)
    out_ref[...] = jnp.dot(mixed_out, w_ref[...], preferred_element_type=jnp.float32).astype(
        jnp.bfloat16
    )


def permute(array, partner):
    return lax.ppermute(array, seq, [(i, partner(i)) for i in range(lax.axis_size(seq))])


def bf16(*shape):
    return jax.ShapeDtypeStruct(shape, jnp.bfloat16)


def exchange(keep, give, near, home):
    turns, size = keep.shape[0], keep.shape[1] // 2 // chan_tile * chan_tile
    lanes, extra = keep.shape[2], keep.shape[1] - 2 * size
    got = permute(give, lambda i: i ^ 1)
    near = permute(near, lambda i: i ^ 2)
    far = call(
        functools.partial(merge_body, size),
        (bf16(4 * size + extra, lanes),) * turns,
        (keep, got),
        [pltpu.VMEM] * 2,
        moved=4 * keep.size,
    )
    routes = routes_of(lax.axis_size("chip"))
    far = [permute(part, lambda i: i ^ 2 * route[i % 2]) for part, route in zip(far, routes)]
    count = 2 * turns + 2
    half = bf16(count * size + count // 2 * extra, lanes)
    keep, give = call(
        functools.partial(split_body, size),
        (half, half),
        (*far, near, home),
        [pltpu.VMEM] * (turns + 2),
        moved=4 * keep.size,
    )
    return keep, permute(give, lambda i: i ^ 1)


def local(tokens, norm_gain, w_in, short_filter, long_filter, medium_filter, skip_gain, w_out):
    rows, width = tokens.shape
    devices, chips = lax.axis_size(seq), lax.axis_size("chip")
    chans = width // devices
    first, twist, inner = spectral_tables(devices, rows, chans)
    staged = chans == chan_tile and chips >= 4 and short_filter.shape[0] <= 3
    if staged:
        packed_shape = (2 * rows // lane * width, lane)
    else:
        packed_shape = (width, 2 * rows + lane)

    def pieces(shape, extra):
        if not staged:
            return (bf16(*shape),)
        size, turns = 2 * shape[0] // devices + extra, chips // 2 - 1
        near = size + size - extra + chan_tile
        return (bf16(turns, size, shape[1]),) * 2 + (bf16(near, shape[1]), bf16(size, shape[1]))

    def scratch(*shapes):
        return [pltpu.VMEM(*shape) for shape in shapes] if staged else []

    def swap(parts):
        if staged:
            return exchange(*parts)
        (array,) = parts
        blocks = array.reshape(devices, -1, array.shape[-1])
        return (lax.all_to_all(blocks, seq, split_axis=0, concat_axis=0).reshape(array.shape),)

    query = call(
        query_body,
        jax.ShapeDtypeStruct((rows, width), jnp.float32),
        (tokens, norm_gain[None, :], w_in, short_filter),
        [pltpu.VMEM] * 4,
        flops=2 * rows * width * width,
        moved=800_000,
    )
    args = (tokens, norm_gain[None, :], w_in, short_filter, long_filter, medium_filter, skip_gain[None, :])
    args = tuple(pltpu.with_memory_space_constraint(arg, pltpu.HBM) for arg in args)
    packed = (packed_shape, jnp.bfloat16)
    parts = call(
        prepare_body,
        pieces(packed_shape, edge),
        args,
        [pltpu.HBM] * len(args),
        scratch(packed, ((chips, edge, lane), jnp.bfloat16))
        + [pltpu.VMEM(arg.shape, arg.dtype) for arg in args]
        + [pltpu.SemaphoreType.DMA((len(args),))],
        flops=2 * rows * width * 3 * width,
        moved=1_500_000,
    )
    conv = ((width, rows), jnp.bfloat16)
    parts = swap(parts)
    parts = call(
        functools.partial(convolve_body, chans, short_filter.shape[0] - 1),
        pieces((width, rows), 0),
        (first, twist, inner, *parts),
        [pltpu.VMEM] * (3 + len(parts)),
        scratch(packed, ((devices, edge, lane), jnp.float32), ((lane, lane), jnp.float32), conv),
        flops=18 * first.shape[0] * width * rows,
        moved=2_000_000,
    )
    parts = swap(parts)
    return call(
        output_body,
        bf16(rows, width),
        (query, w_out, *parts),
        [pltpu.VMEM] * (2 + len(parts)),
        scratch(conv),
        flops=2 * rows * width * width,
        moved=600_000,
    )


def solution(mesh):
    groups, devices = mesh.devices.shape
    split = jax.sharding.Mesh(mesh.devices.reshape(groups, devices // 2, 2), ("groups", *seq))
    rows = P(("groups", *seq), None)
    placed = (rows, P(), P(), P(), P(seq, None), P(), P(), P())
    return jax.shard_map(local, mesh=split, in_specs=placed, out_specs=rows, check_vma=False)
```
